32 devices in a mesh: section: 2 (over x), fsdp: 4 (over y, core), rep: 4 (over z).
Axes of the slice: x: 2, y: 2, z: 4, core: 2. Of those that a mesh axis runs over, the one named last changes fastest.
Arguments:
- inputs: bfloat16 [64, 256, 1024], P(('fsdp', 'rep')), may hold values from -6 to 6
- teacher: bfloat16 [64, 256, 1024], P(('fsdp', 'rep')), may hold values from -6 to 6
- lengths: int32 [64], replicated, may hold values from 1 to 256, as said below
- order: int32 [64], replicated, may hold values from 0 to 63, as said below
- loss_scale: float32 [], replicated, may hold values from 131072 to 524288
- norm_gain1: bfloat16 [2, 1024], P('section', 'fsdp'), may hold values from 0.5 to 1.5
- w_query: bfloat16 [2, 1024, 512], P('section', 'fsdp'), may hold values from -0.1875 to 0.1875
- w_key: bfloat16 [2, 1024, 128], P('section', 'fsdp'), may hold values from -0.1875 to 0.1875
- w_value: bfloat16 [2, 1024, 128], P('section', 'fsdp'), may hold values from -0.1875 to 0.1875
- w_attn_out: bfloat16 [2, 512, 1024], P('section', 'fsdp'), may hold values from -1 to 1
- w_ssm_gate: bfloat16 [2, 1024, 1536], P('section', 'fsdp'), may hold values from -0.1875 to 0.1875
- w_conv_in: bfloat16 [2, 1024, 1792], P('section', 'fsdp'), may hold values from -0.1875 to 0.1875
- w_step: bfloat16 [2, 1024, 24], P('section', 'fsdp'), may hold values from -0.046875 to 0.046875
- conv_kernel: bfloat16 [2, 4, 1792], P('section', None, 'fsdp'), may hold values from -3 to 3
- conv_bias: bfloat16 [2, 1792], P('section', 'fsdp'), may hold values from -3 to 3
- step_bias: float32 [2, 24], P('section'), may hold values from -6 to -2.5
- decay_log: float32 [2, 24], P('section'), may hold values from 0 to 1.4
- skip_gain: float32 [2, 24], P('section'), may hold values from 0.5 to 1.5
- ssm_norm_gain: bfloat16 [2, 1536], P('section', 'fsdp'), may hold values from 0.5 to 1.5
- w_ssm_out: bfloat16 [2, 1536, 1024], P('section', 'fsdp'), may hold values from -0.15625 to 0.15625
- norm_gain2: bfloat16 [2, 1024], P('section', 'fsdp'), may hold values from 0.5 to 1.5
- w_gate: bfloat16 [2, 1024, 2048], P('section', 'fsdp'), may hold values from -0.1875 to 0.1875
- w_up: bfloat16 [2, 1024, 2048], P('section', 'fsdp'), may hold values from -0.1875 to 0.1875
- w_down: bfloat16 [2, 2048, 1024], P('section', 'fsdp'), may hold values from -0.125 to 0.125
Outputs:
- activations: bfloat16 [2, 64, 256, 1024], P('section', ('fsdp', 'rep'))
- gradients: bfloat16 [2, 64, 256, 1024], P('section', ('fsdp', 'rep'))
- loss: float32 [], replicated
- grad_norm_gain1: float32 [2, 1024], P('section', 'fsdp')
- grad_w_query: float32 [2, 1024, 512], P('section', 'fsdp')
- grad_w_key: float32 [2, 1024, 128], P('section', 'fsdp')
- grad_w_value: float32 [2, 1024, 128], P('section', 'fsdp')
- grad_w_attn_out: float32 [2, 512, 1024], P('section', 'fsdp')
- grad_w_ssm_gate: float32 [2, 1024, 1536], P('section', 'fsdp')
- grad_w_conv_in: float32 [2, 1024, 1792], P('section', 'fsdp')
- grad_w_step: float32 [2, 1024, 24], P('section', 'fsdp')
- grad_conv_kernel: float32 [2, 4, 1792], P('section', None, 'fsdp')
- grad_conv_bias: float32 [2, 1792], P('section', 'fsdp')
- grad_step_bias: float32 [2, 24], P('section')
- grad_decay_log: float32 [2, 24], P('section')
- grad_skip_gain: float32 [2, 24], P('section')
- grad_ssm_norm_gain: float32 [2, 1536], P('section', 'fsdp')
- grad_w_ssm_out: float32 [2, 1536, 1024], P('section', 'fsdp')
- grad_norm_gain2: float32 [2, 1024], P('section', 'fsdp')
- grad_w_gate: float32 [2, 1024, 2048], P('section', 'fsdp')
- grad_w_up: float32 [2, 1024, 2048], P('section', 'fsdp')
- grad_w_down: float32 [2, 2048, 1024], P('section', 'fsdp')
The draws below stay inside these ranges and needn't reach their ends.
Inputs may be any that keep to these rules, and one draw needn't show every extreme that they name: `lengths`: valid tokens fill the first positions of a sequence; the last sequence holds 256. `order`: A permutation; dealt positions are numbered as the rows of the sharded layout, 4 to a device. A sequence stays among the 4 devices that share its fsdp index, and each device sends exactly one of its sequences to each of them.
All inputs are finite; a program needn't handle non-finite values.
Results may differ from the reference program's by a relative error of at most 0.022.
Values may be sent and summed in bfloat16 or wider, within the bound.
No kernel may reach another device: no remote copies, remote signals or barrier semaphores. Data moves between devices by JAX's collectives and lax.ppermute only.
A program may use at most 448 MiB of HBM per device.

```python
import math
import jax
import jax.numpy as jnp
from jax import lax

D = 1024
NH = 8
KVH = 2
HD = 64
MH = 24
KC = 4
FF = 2048
LEN = 256
DSSM = 1536
CONVC = 1792
MB = 4
SEQS = 64
N_SECTION = 2


def draw_lengths(key, part):
    key = jax.random.fold_in(key, 11)
    device_count = SEQS // MB
    position = jnp.arange(SEQS, dtype=jnp.int32) // MB
    lowest = 1 + LEN * position // (2 * (device_count - 1))
    highest = LEN // 2 + LEN * position // (2 * (device_count - 1))
    raw_draw = jax.random.randint(key, (SEQS,), 0, 1 << 20, dtype=jnp.int32)
    drawn = lowest + raw_draw % (highest - lowest + 1)
    return jnp.where(jnp.arange(SEQS, dtype=jnp.int32) == SEQS - 1, LEN, drawn).astype(jnp.int32)


def draw_order(key, part):
    key = jax.random.fold_in(key, 23)
    group_count = SEQS // (MB * MB)
    sending_key, placing_key = jax.random.split(key)
    ramp = jnp.arange(MB, dtype=jnp.int32)
    sending = jnp.argsort(jax.random.randint(sending_key, (group_count, MB, MB), 0, 1 << 20, dtype=jnp.int32) * MB + ramp, axis=-1).astype(jnp.int32)
    placing = jnp.argsort(jax.random.randint(placing_key, (group_count, MB, MB), 0, 1 << 20, dtype=jnp.int32) * MB + ramp, axis=-1).astype(jnp.int32)
    placing_turned = jnp.transpose(placing, (0, 2, 1))
    arrival = jnp.take_along_axis(placing_turned, sending, axis=2)
    group_index = jnp.arange(group_count, dtype=jnp.int32)[:, None, None]
    dealt_position = (group_index * MB + sending) * MB + arrival
    return dealt_position.reshape(SEQS).astype(jnp.int32)


def level_of(stream_key, extent, shards, smallest, largest):
    def one(dim, shards_of):
        heights = jax.random.uniform(jax.random.fold_in(jax.random.fold_in(stream_key, 6), dim), (shards_of,), jnp.float32, smallest / len(shards), largest / len(shards))
        return jnp.repeat(jnp.exp(heights), extent[dim] // shards_of).reshape((-1,) + (1,) * (len(extent) - dim - 1))

    loudness = one(*shards[0])
    for cut in shards[1:]:
        loudness = loudness * one(*cut)
    return loudness


def scatter_about(stream_key, extent, deviation, bound, cuts=(), kind=jnp.bfloat16):
    values = deviation * jax.random.normal(stream_key, extent, jnp.float32)
    if cuts:
        values = values * level_of(stream_key, extent, cuts, -0.22, 0.18)
    return jnp.clip(values, -bound, bound).astype(kind)


def setup_inputs(seed: int = 0) -> dict:
    streams_of = jax.random.split(jax.random.key(seed), 25)
    return {
        "inputs": scatter_about(streams_of[0], (SEQS, LEN, D), 1.0, 6.0, ((0, 16),)),
        "teacher": scatter_about(streams_of[1], (SEQS, LEN, D), 1.0, 6.0, ((0, 16),)),
        "lengths": draw_lengths(jax.random.fold_in(streams_of[24], 71), 0),
        "order": draw_order(jax.random.fold_in(streams_of[24], 71), 0),
        "loss_scale": jnp.clip(jnp.exp(jax.random.uniform(streams_of[4], (), jnp.float32, math.log(131072.0), math.log(524288.0))), 131072.0, 524288.0),
        "norm_gain1": jnp.clip(1.0 + 0.1 * jax.random.normal(streams_of[5], (N_SECTION, D), jnp.float32), 0.5, 1.5).astype(jnp.bfloat16),
        "w_query": scatter_about(streams_of[6], (N_SECTION, D, NH * HD), D ** -0.5, 0.1875, ((0, 2), (1, 4))),
        "w_key": scatter_about(streams_of[7], (N_SECTION, D, KVH * HD), D ** -0.5, 0.1875, ((0, 2), (1, 4))),
        "w_value": scatter_about(streams_of[8], (N_SECTION, D, KVH * HD), D ** -0.5, 0.1875, ((0, 2), (1, 4))),
        "w_attn_out": scatter_about(streams_of[9], (N_SECTION, NH * HD, D), (NH * HD // 16) ** -0.5, 1.0, ((0, 2), (1, 4))),
        "w_ssm_gate": scatter_about(streams_of[10], (N_SECTION, D, DSSM), D ** -0.5, 0.1875, ((0, 2), (1, 4))),
        "w_conv_in": scatter_about(streams_of[11], (N_SECTION, D, CONVC), D ** -0.5, 0.1875, ((0, 2), (1, 4))),
        "w_step": scatter_about(streams_of[12], (N_SECTION, D, MH), (16 * D) ** -0.5, 0.046875, ((0, 2), (1, 4))),
        "conv_kernel": scatter_about(streams_of[13], (N_SECTION, KC, CONVC), KC ** -0.5, 3.0, ((0, 2), (2, 4))),
        "conv_bias": scatter_about(streams_of[14], (N_SECTION, CONVC), 0.5, 3.0, ((0, 2), (1, 4))),
        "step_bias": jnp.clip(-6.0 + 3.5 * jax.random.uniform(streams_of[15], (N_SECTION, MH), jnp.float32) ** level_of(streams_of[15], (N_SECTION, MH), ((0, 2),), -0.2, 0.2), -6.0, -2.5),
        "decay_log": jnp.clip(1.4 * jax.random.uniform(streams_of[16], (N_SECTION, MH), jnp.float32) ** level_of(streams_of[16], (N_SECTION, MH), ((0, 2),), -0.2, 0.2), 0.0, 1.4),
        "skip_gain": jnp.clip(0.5 + 1.0 * jax.random.uniform(streams_of[17], (N_SECTION, MH), jnp.float32) ** level_of(streams_of[17], (N_SECTION, MH), ((0, 2),), -0.2, 0.2), 0.5, 1.5),
        "ssm_norm_gain": jnp.clip(1.0 + 0.1 * jax.random.normal(streams_of[18], (N_SECTION, DSSM), jnp.float32), 0.5, 1.5).astype(jnp.bfloat16),
        "w_ssm_out": scatter_about(streams_of[19], (N_SECTION, DSSM, D), DSSM ** -0.5, 0.15625, ((0, 2), (1, 4))),
        "norm_gain2": jnp.clip(1.0 + 0.1 * jax.random.normal(streams_of[20], (N_SECTION, D), jnp.float32), 0.5, 1.5).astype(jnp.bfloat16),
        "w_gate": scatter_about(streams_of[21], (N_SECTION, D, FF), D ** -0.5, 0.1875, ((0, 2), (1, 4))),
        "w_up": scatter_about(streams_of[22], (N_SECTION, D, FF), D ** -0.5, 0.1875, ((0, 2), (1, 4))),
        "w_down": scatter_about(streams_of[23], (N_SECTION, FF, D), FF ** -0.5, 0.125, ((0, 2), (1, 4))),
    }


EPSILON = 1e-05
ROPE_BASE = 100000000000.0
MASKED = -1e+30
HIGHEST = lax.Precision.HIGHEST

@jax.custom_vjp
def low(v):
    return lax.optimization_barrier(v.astype(jnp.bfloat16)).astype(jnp.float32)

@jax.custom_vjp
def low_back(v):
    return v

def low_keep(v):
    return (low(v), None)

def low_pass(kept, grad):
    return (grad,)

def back_keep(v):
    return (v, None)

def back_low(kept, grad):
    return (low(grad),)
low.defvjp(low_keep, low_pass)
low_back.defvjp(back_keep, back_low)

def product(left_side, right_side):
    return jnp.dot(left_side, right_side, precision=HIGHEST, preferred_element_type=jnp.float32)

def norm_rows(values, gain_row):
    return values * lax.rsqrt(lax.optimization_barrier(jnp.mean(values * values, axis=-1, keepdims=True)) + EPSILON) * gain_row

def rope_tables(length, head_size):
    halves = head_size // 2
    inverse = jnp.exp(jnp.arange(halves, dtype=jnp.float32) * (-2.0 * math.log(ROPE_BASE) / head_size))
    angles = jnp.arange(length, dtype=jnp.float32)[:, None] * inverse[None, :]
    return (jnp.cos(angles)[:, None, :], jnp.sin(angles)[:, None, :])

def rotate(values, cosine, sine_table):
    halves = values.shape[-1] // 2
    former = values[..., :halves]
    latter = values[..., halves:]
    return jnp.concatenate([former * cosine - latter * sine_table, latter * cosine + former * sine_table], axis=-1)

def soft_plus(values):
    return jnp.log1p(jnp.exp(values))

def swish(values):
    return values * jax.nn.sigmoid(values)

def swiglu(gate_value, up_value):
    return swish(gate_value) * up_value

def mixer_core(gate_raw, conv_raw, step_raw, kernel, conv_bias, step_bias, decay_log, skip_gain, gain_row):
    length = conv_raw.shape[0]
    kernel_taps = kernel.shape[0]
    head_count = step_raw.shape[1]
    inner_width = gate_raw.shape[1]
    state_width = (conv_raw.shape[1] - inner_width) // 2
    padded = jnp.pad(conv_raw, ((kernel_taps - 1, 0), (0, 0)))
    convolved = conv_bias[None, :]
    for offset in range(kernel_taps):
        convolved = convolved + kernel[offset][None, :] * padded[offset:offset + length]
    convolved = swish(convolved)
    states_in = convolved[:, :inner_width].reshape(length, head_count, inner_width // head_count)
    inputs_b = convolved[:, inner_width:inner_width + state_width]
    inputs_c = convolved[:, inner_width + state_width:]
    step_size = soft_plus(step_raw + step_bias[None, :])
    running = jnp.cumsum(-step_size * jnp.exp(decay_log)[None, :], axis=0).T
    row_index = lax.broadcasted_iota(jnp.int32, (length, length), 0)
    col_index = lax.broadcasted_iota(jnp.int32, (length, length), 1)
    causal = (col_index <= row_index)[None]
    decay_matrix = jnp.exp(jnp.where(causal, running[:, :, None] - running[:, None, :], MASKED))
    intersection = jnp.dot(inputs_c, inputs_b.T, precision=HIGHEST, preferred_element_type=jnp.float32)
    weights = decay_matrix * intersection[None]
    scaled = step_size[:, :, None] * states_in
    mixed_heads = jnp.einsum('hts,shp->thp', weights, scaled, precision=HIGHEST, preferred_element_type=jnp.float32)
    mixed_heads = mixed_heads + skip_gain[None, :, None] * states_in
    gated_rows = mixed_heads.reshape(length, inner_width) * swish(gate_raw)
    return norm_rows(gated_rows, gain_row)

def layer(seq_in, params, valid_rows):
    gain_one, w_query, w_key, w_value, w_attn_out, w_ssm_gate, w_conv_in, w_step, conv_kernel, conv_bias, step_bias, decay_log, skip_gain, ssm_gain, w_ssm_out, gain_two, w_gate, w_up, w_down = params
    length = seq_in.shape[0]
    head_count = w_query.shape[1] // HD
    key_heads = w_key.shape[1] // HD
    cosine, sine_table = rope_tables(length, HD)
    row_index = lax.broadcasted_iota(jnp.int32, (length, length), 0)
    col_index = lax.broadcasted_iota(jnp.int32, (length, length), 1)
    causal = col_index <= row_index
    normed = low(norm_rows(seq_in, gain_one))
    query_pre = low_back(product(normed, w_query))
    key_pre = low_back(product(normed, w_key))
    values_low = low(low_back(product(normed, w_value))).reshape(length, key_heads, HD)
    query_low = low(rotate(query_pre.reshape(length, head_count, HD), cosine, sine_table))
    query_low = query_low.reshape(length, key_heads, head_count // key_heads, HD)
    keys_low = low(rotate(key_pre.reshape(length, key_heads, HD), cosine, sine_table))
    scores = low_back(jnp.einsum('qgrd,kgd->grqk', query_low, keys_low, precision=HIGHEST) * HD ** (-0.5))
    scores = jnp.where(causal, scores, MASKED)
    row_top = lax.optimization_barrier(jnp.max(scores, axis=-1, keepdims=True))
    exp_scores = jnp.exp(scores - row_top)
    attn_probs = exp_scores / lax.optimization_barrier(jnp.sum(exp_scores, axis=-1, keepdims=True))
    attn_mixed = jnp.einsum('grqk,kgd->qgrd', low(attn_probs), values_low, precision=HIGHEST)
    attn_mixed = attn_mixed.reshape(length, head_count * HD)
    attention = low_back(product(low(low_back(attn_mixed)), w_attn_out))
    ssm_out = mixer_core(low_back(product(normed, w_ssm_gate)), low_back(product(normed, w_conv_in)), low_back(product(normed, w_step)), conv_kernel, conv_bias, step_bias, decay_log, skip_gain, ssm_gain)
    ssm_branch = low_back(product(low(ssm_out), w_ssm_out))
    hidden = seq_in + attention + ssm_branch
    normed_two = low(norm_rows(hidden, gain_two))
    act_low = low(swiglu(low_back(product(normed_two, w_gate)), low_back(product(normed_two, w_up))))
    return (hidden + low_back(product(act_low, w_down))) * valid_rows[:, None]

def reference(inputs, teacher, lengths, order, loss_scale, norm_gain1, w_query, w_key, w_value, w_attn_out, w_ssm_gate, w_conv_in, w_step, conv_kernel, conv_bias, step_bias, decay_log, skip_gain, ssm_norm_gain, w_ssm_out, norm_gain2, w_gate, w_up, w_down):
    weights = (norm_gain1, w_query, w_key, w_value, w_attn_out, w_ssm_gate, w_conv_in, w_step, conv_kernel, conv_bias, step_bias, decay_log, skip_gain, ssm_norm_gain, w_ssm_out, norm_gain2, w_gate, w_up, w_down)
    first_params = tuple((item[0].astype(jnp.float32) for item in weights))
    second = tuple((item[1].astype(jnp.float32) for item in weights))
    valid_count = jnp.sum(lengths).astype(jnp.float32)
    factor = loss_scale.astype(jnp.float32) / (valid_count * D)
    valid_all = (jnp.arange(LEN, dtype=jnp.int32)[None, :] < lengths[:, None]).astype(jnp.float32)
    group_size = math.gcd(SEQS, max(1, 4096 // LEN))
    blocks = SEQS // group_size
    seq_blocks = inputs.reshape(blocks, group_size, LEN, D)
    target_blocks = teacher.reshape(blocks, group_size, LEN, D)
    valid_blocks = valid_all.reshape(blocks, group_size, LEN)
    section_layer = jax.vmap(layer, in_axes=(0, None, 0))

    def one_group(carry_in, block_data):
        loss_sum, first_sum, second_sum = carry_in
        seq_block, target_block, valid_block = block_data
        seq_block = seq_block.astype(jnp.float32)
        target_block = target_block.astype(jnp.float32)

        def forward(seq_values, probe, params_one, params_two):
            boundary = low(section_layer(seq_values, params_one, valid_block))
            final = section_layer(low_back(boundary) + probe, params_two, valid_block)
            misfit = final - target_block
            partial_sum = jnp.sum(valid_block[:, :, None] * misfit * misfit)
            return (partial_sum * factor, (boundary, final, partial_sum))
        scaled_loss, pullback, extras = jax.vjp(forward, seq_block, jnp.zeros_like(seq_block), first_params, second, has_aux=True)
        d_seq, d_probe, d_first, d_second = pullback(jnp.ones_like(scaled_loss))
        boundary, final, partial_sum = extras
        first_sum = jax.tree.map(lambda total, extra: total + extra, first_sum, d_first)
        second_sum = jax.tree.map(lambda total, extra: total + extra, second_sum, d_second)
        outputs = (boundary.astype(jnp.bfloat16), final.astype(jnp.bfloat16), d_seq.astype(jnp.bfloat16), d_probe.astype(jnp.bfloat16))
        return ((loss_sum + partial_sum, first_sum, second_sum), outputs)
    initial = (jnp.zeros((), jnp.float32), tuple((jnp.zeros_like(item) for item in first_params)), tuple((jnp.zeros_like(item) for item in second)))
    carried, stacked = lax.scan(one_group, initial, (seq_blocks, target_blocks, valid_blocks))
    loss_sum, first_grads, second_grads = carried
    boundaries, finals, d_inputs, d_boundary = stacked
    full_shape = (SEQS, LEN, D)
    inverse = jnp.argsort(order).astype(jnp.int32)
    activations = jnp.stack([boundaries.reshape(full_shape)[inverse], finals.reshape(full_shape)])
    gradients = jnp.stack([d_inputs.reshape(full_shape), d_boundary.reshape(full_shape)[inverse]])
    loss_value = loss_sum / (valid_count * D)
    stacked_grads = [jnp.stack([grad_one, grad_two]) for grad_one, grad_two in zip(first_grads, second_grads)]
    return (activations, gradients, loss_value, stacked_grads[0], stacked_grads[1], stacked_grads[2], stacked_grads[3], stacked_grads[4], stacked_grads[5], stacked_grads[6], stacked_grads[7], stacked_grads[8], stacked_grads[9], stacked_grads[10], stacked_grads[11], stacked_grads[12], stacked_grads[13], stacked_grads[14], stacked_grads[15], stacked_grads[16], stacked_grads[17], stacked_grads[18])
```

```python
import math
import functools

import jax
import jax.numpy as jnp
from jax import lax
from jax.experimental import pallas as pl
from jax.experimental.pallas import tpu as pltpu
from jax.sharding import PartitionSpec as P

HD = 64
EPSILON = 1e-05
ROPE_BASE = 100000000000.0
MASKED = -1e30
F32 = jnp.float32
BF = jnp.bfloat16
TILE = 256
HALF = 128
ANY = pl.BlockSpec(memory_space=pl.ANY)
VM = pl.BlockSpec(memory_space=pltpu.VMEM)
SM = pl.BlockSpec(memory_space=pltpu.SMEM)


def dot(a, b):
    return jnp.dot(a, b, preferred_element_type=F32)


def dot_nt(a, b):
    return lax.dot_general(a, b, (((1,), (1,)), ((), ())), preferred_element_type=F32)


def dot_tn(a, b):
    return lax.dot_general(a, b, (((0,), (0,)), ((), ())), preferred_element_type=F32)


def sigmoid(v):
    return 0.5 * jnp.tanh(0.5 * v) + 0.5


def lanes(i, width=TILE):
    return pl.ds(pl.multiple_of(i * width, width), width)


def iota(shape, axis):
    return lax.broadcasted_iota(jnp.int32, shape, axis)


def split2(v):
    hi = v.astype(BF)
    return hi, (v - hi.astype(F32)).astype(BF)


def split3(v):
    hi = v.astype(BF)
    rest = v - hi.astype(F32)
    mid = rest.astype(BF)
    return hi, mid, (rest - mid.astype(F32)).astype(BF)


def expand_matrix(tile):
    row = jnp.bitwise_and(iota((TILE, TILE), 0), HALF - 1)
    col = jnp.right_shift(iota((TILE, TILE), 1), 6) + tile * (TILE // HD)
    return jnp.where(row == col, 1.0, 0.0).astype(BF)


def reduce_matrix(tile):
    row = jnp.right_shift(iota((TILE, HALF), 0), 6) + tile * (TILE // HD)
    col = iota((TILE, HALF), 1)
    return jnp.where(row == col, 1.0, 0.0).astype(BF)


def both(v):
    return jnp.concatenate(split2(v), axis=1)


def rope(v, cosine, sine, first):
    turned = jnp.where(first, pltpu.roll(v, HALF - HD // 2, 1), pltpu.roll(v, HD // 2, 1))
    return v * cosine + turned * sine


def copies_in(pairs, sems):
    copies = [pltpu.make_async_copy(a, b, sems.at[i]) for i, (a, b) in enumerate(pairs)]
    for copy in copies:
        copy.start()
    return copies


V_TAP, V_CBIAS, V_GS, V_SKIP, V_G1, V_G2, V_SBIAS, V_DECAY = 0, 4, 5, 6, 7, 8, 9, 10


def scan_terms(step_raw, vec_ref, heads):
    lane = iota(step_raw.shape, 1)
    pre = step_raw + vec_ref[V_SBIAS : V_SBIAS + 1, :HALF]
    soft = jnp.maximum(pre, 0.0) + jnp.log1p(jnp.exp(-jnp.abs(pre)))
    step = jnp.where(lane < heads, soft, 0.0)
    change = step * vec_ref[V_DECAY : V_DECAY + 1, :HALF]
    length = step.shape[0]
    lower = jnp.where(
        iota((length, length), 0) >= iota((length, length), 1), 1.0, 0.0
    ).astype(BF)
    run = sum(dot(lower, part) for part in split3(change))
    middle = run[HALF - 1 : HALF, :]
    bend = jnp.where(iota(run.shape, 0) < HALF, middle - run, run - middle)
    bend = jnp.exp(jnp.minimum(bend, 0.0))
    return pre, step, change, run, bend


def broadcast_runs(run, run_wide, heads):
    for h in range(heads):
        run_wide[:, h * HALF : (h + 1) * HALF] = jnp.broadcast_to(
            run[:, h : h + 1], (run.shape[0], HALF)
        )


def mix_forward(
    slot_ref, x_ref, vec_ref, cos_ref, sin_ref, win_hbm, wout_hbm, *rest, n_stack, widths
):
    ci, mi, qw, kw, heads = widths
    outs = rest[n_stack : 2 * n_stack + 1]
    stacks, hidden_ref = outs[:n_stack], outs[n_stack]
    (win, wout, normed, conv_raw, z, xbc, gate_raw, qkv, step_raw, probs, branch, y, gated,
     run_wide, run_row, step_two, bend_two, in_sem, out_sem) = rest[2 * n_stack + 1 :]
    (s_normed, s_conv, s_z, s_gate, s_qkv, s_step, s_probs, s_branch, s_y, s_hidden, s_x) = stacks
    slot, active = slot_ref[0], slot_ref[1] > 0
    g0 = ci
    q0 = ci + mi
    total = win.shape[1]
    load = copies_in(
        [
            (win_hbm.at[:, q0:total], win.at[:, q0:total]),
            (win_hbm.at[:, 0:ci], win.at[:, 0:ci]),
            (win_hbm.at[:, g0:q0], win.at[:, g0:q0]),
            (wout_hbm, wout),
        ],
        in_sem,
    )
    stores = []

    def save(buffer, stack):
        copy = pltpu.make_async_copy(buffer, stack.at[slot], out_sem.at[len(stores)])
        pl.when(active)(copy.start)
        stores.append(copy)

    length = x_ref.shape[0]
    x = x_ref[...].astype(F32)
    rate = lax.rsqrt(jnp.mean(x * x, axis=-1, keepdims=True) + EPSILON)
    normed[...] = (x * rate * vec_ref[V_G1 : V_G1 + 1, : x.shape[1]]).astype(BF)
    save(normed, s_normed)
    lane_first = jnp.bitwise_and(iota((length, HALF), 1), HD - 1) < HD // 2
    half_low = iota((length, HALF), 1) < HD

    load[0].wait()
    cosine, sine = cos_ref[...], sin_ref[...]
    n_rope = (qw + kw) // HALF
    for t in range((total - q0) // HALF // 2):
        raw = dot(normed[...], win[:, q0 + t * TILE : q0 + (t + 1) * TILE])
        for part in range(2):
            c = 2 * t + part
            piece = raw[:, part * HALF : (part + 1) * HALF]
            if c < n_rope:
                piece = rope(piece, cosine, sine, lane_first)
            if c < n_rope + kw // HALF:
                qkv[:, c * HALF : (c + 1) * HALF] = piece.astype(BF)
            else:
                step_raw[...] = piece
    if ((total - q0) // HALF) % 2:
        step_raw[...] = dot(normed[...], win[:, total - HALF : total])
    save(qkv, s_qkv)
    save(step_raw, s_step)

    load[1].wait()
    row = iota((length, TILE), 0)

    def conv_tile(t, carry):
        cols = lanes(t)
        raw = dot(normed[...], win[:, cols])
        conv_raw[:, cols] = raw.astype(BF)
        total_z = vec_ref[V_CBIAS : V_CBIAS + 1, cols] + raw * vec_ref[3:4, cols]
        for back in range(1, 4):
            moved = jnp.where(row >= back, pltpu.roll(raw, back, 0), 0.0)
            total_z = total_z + moved * vec_ref[3 - back : 4 - back, cols]
        z[:, cols] = total_z.astype(BF)
        xbc[:, cols] = (total_z * sigmoid(total_z)).astype(BF)
        return carry

    lax.fori_loop(0, ci // TILE, conv_tile, 0)
    save(conv_raw, s_conv)
    save(z, s_z)

    load[2].wait()

    def gate_tile(t, carry):
        raw = dot(normed[...], win[:, pl.ds(pl.multiple_of(g0 + t * TILE, TILE), TILE)])
        gate_raw[:, lanes(t)] = raw.astype(BF)
        return carry

    lax.fori_loop(0, mi // TILE, gate_tile, 0)
    save(gate_raw, s_gate)

    keys, values = qkv[:, qw : qw + kw], qkv[:, qw + kw : qw + 2 * kw]
    keys_far, values_far = pltpu.roll(keys.astype(F32), HD, 1).astype(BF), pltpu.roll(
        values.astype(F32), HD, 1
    ).astype(BF)
    causal_top = iota((HALF, HALF), 1) <= iota((HALF, HALF), 0)
    causal_low = iota((HALF, length), 1) <= iota((HALF, length), 0) + HALF
    pairs = qw // HALF
    groups = kw // HD
    probs_zero = jnp.zeros((HALF, HALF), BF)
    for pair in range(pairs):
        group = pair // (pairs // groups)
        keep = half_low if group == 0 else jnp.logical_not(half_low)
        keys_two = jnp.where(keep, keys, keys_far)
        values_two = jnp.where(keep, values, values_far)
        query = qkv[:, pair * HALF : (pair + 1) * HALF] * jnp.asarray(HD ** (-0.5), BF)
        results = []
        for side in range(2):
            own = half_low if side == 0 else jnp.logical_not(half_low)
            q = jnp.where(own, query, jnp.zeros_like(query))
            at = (2 * pair + side) * length
            out = []
            for lo, causal in ((0, causal_top), (1, causal_low)):
                width = HALF if lo == 0 else length
                scores = dot_nt(q[lo * HALF : (lo + 1) * HALF], keys_two[:width])
                scores = jnp.where(causal, scores, MASKED)
                top = jnp.max(scores, axis=-1, keepdims=True)
                weights = jnp.exp(scores - top)
                weights = weights / jnp.sum(weights, axis=-1, keepdims=True)
                weights = weights.astype(BF)
                if lo == 0:
                    probs[at : at + HALF, :HALF] = weights
                    probs[at : at + HALF, HALF:] = probs_zero
                else:
                    probs[at + HALF : at + length, :] = weights
                out.append(dot(weights, values_two[:width]))
            results.append(jnp.concatenate(out, axis=0))
        mixed = jnp.where(half_low, results[0], results[1])
        branch[:, mi + pair * HALF : mi + (pair + 1) * HALF] = mixed.astype(BF)
    save(probs, s_probs)

    pre, step, change, run, bend = scan_terms(step_raw[...], vec_ref, heads)
    turned = run.T
    run_row[:HALF, :] = turned[:, :HALF]
    run_row[HALF:, :] = turned[:, HALF:]
    broadcast_runs(run, run_wide, heads)
    step_two[...] = both(step)
    bend_two[...] = both(bend)
    b_in, c_in = xbc[:, mi : mi + HALF], xbc[:, mi + HALF : mi + 2 * HALF]
    tops = [dot_nt(c_in[c * HALF : (c + 1) * HALF], b_in[c * HALF : (c + 1) * HALF]) for c in (0, 1)]
    cross = dot_nt(c_in[HALF:], b_in[:HALF]).astype(BF)
    pair_low = iota((HALF, HALF), 1) < HD
    tops = [jnp.where(causal_top, t, 0.0) for t in tops]

    def mix_tile(t, squares):
        cols = lanes(t)
        spread = expand_matrix(t)
        x_in = xbc[:, cols].astype(F32)
        scaled = (dot(step_two[...], spread) * x_in).astype(BF)
        bends = dot(bend_two[...], spread)
        u = (bends[:HALF] * scaled[:HALF].astype(F32)).astype(BF)
        far = dot(cross, u) * bends[HALF:]
        parts = []
        for p in range(TILE // HALF):
            block = []
            for c in range(2):
                rows = slice(c * HALF, (c + 1) * HALF)
                weights = []
                for side in range(2):
                    h = t * (TILE // HD) + 2 * p + side
                    wide = run_wide[rows, lanes(h, HALF)]
                    line = run_row[pl.ds(c * HALF + h, 1), :]
                    decay = jnp.exp(jnp.minimum(wide - line, 0.0))
                    weights.append((decay * tops[c]).astype(BF))
                xs = scaled[rows, p * HALF : (p + 1) * HALF]
                zero = jnp.zeros_like(xs)
                right = jnp.concatenate(
                    [jnp.where(pair_low, xs, zero), jnp.where(pair_low, zero, xs)], axis=0
                )
                block.append(dot(jnp.concatenate(weights, axis=1), right))
            parts.append(jnp.concatenate(block, axis=0))
        out = jnp.concatenate(parts, axis=1)
        out = out + jnp.concatenate([jnp.zeros_like(far), far], axis=0)
        out = out + vec_ref[V_SKIP : V_SKIP + 1, cols] * x_in
        y[:, cols] = out.astype(BF)
        g = gate_raw[:, cols].astype(F32)
        out = out * (g * sigmoid(g))
        gated[:, cols] = out
        return squares + jnp.sum(out * out, axis=-1, keepdims=True)

    squares = lax.fori_loop(0, mi // TILE, mix_tile, jnp.zeros((length, 1), F32))
    save(y, s_y)
    rate = lax.rsqrt(squares * (1.0 / mi) + EPSILON)
    branch[:, :mi] = (gated[...] * rate * vec_ref[V_GS : V_GS + 1, :mi]).astype(BF)
    save(branch, s_branch)

    load[3].wait()

    def out_tile(t, carry):
        cols = lanes(t)
        hidden_ref[:, cols] = x_ref[:, cols].astype(F32) + dot(branch[...], wout[:, cols])
        return carry

    lax.fori_loop(0, wout.shape[1] // TILE, out_tile, 0)
    save(hidden_ref, s_hidden)
    save(x_ref, s_x)
    for copy in stores:
        pl.when(active)(copy.wait)


def mixer_forward_call(slot, x, vec, cosine, sine, win, wout, stacks, widths):
    ci, mi, qw, kw, heads = widths
    length, width = x.shape
    n_stack = len(stacks)
    scratch = [
        pltpu.VMEM(win.shape, BF),
        pltpu.VMEM(wout.shape, BF),
        pltpu.VMEM((length, width), BF),
        pltpu.VMEM((length, ci), BF),
        pltpu.VMEM((length, ci), BF),
        pltpu.VMEM((length, ci), BF),
        pltpu.VMEM((length, mi), BF),
        pltpu.VMEM((length, qw + 2 * kw), BF),
        pltpu.VMEM((length, HALF), F32),
        pltpu.VMEM((qw // HD * length, length), BF),
        pltpu.VMEM((length, mi + qw), BF),
        pltpu.VMEM((length, mi), BF),
        pltpu.VMEM((length, mi), F32),
        pltpu.VMEM((length, heads * HALF), F32),
        pltpu.VMEM((length, HALF), F32),
        pltpu.VMEM((length, 2 * HALF), BF),
        pltpu.VMEM((length, 2 * HALF), BF),
        pltpu.SemaphoreType.DMA((4,)),
        pltpu.SemaphoreType.DMA((n_stack,)),
    ]
    out = pl.pallas_call(
        functools.partial(mix_forward, n_stack=n_stack, widths=widths),
        out_shape=[jax.ShapeDtypeStruct(s.shape, s.dtype) for s in stacks]
        + [jax.ShapeDtypeStruct((length, width), F32)],
        in_specs=[SM, VM, VM, VM, VM, ANY, ANY] + [ANY] * n_stack,
        out_specs=[ANY] * n_stack + [VM],
        scratch_shapes=scratch,
        input_output_aliases={7 + i: i for i in range(n_stack)},
        compiler_params=pltpu.CompilerParams(vmem_limit_bytes=44 * 1024 * 1024),
        cost_estimate=pl.CostEstimate(
            flops=2 * length * (win.size + wout.size), bytes_accessed=24000000, transcendentals=0
        ),
        name="mixer_forward",
    )(slot, x, vec, cosine, sine, win, wout, *stacks)
    return list(out[:n_stack]), out[n_stack]


def mlp_forward(slot_ref, hidden_ref, valid_ref, vec_ref, wgu_hbm, wdown_hbm, *rest, n_stack):
    outs = rest[n_stack : 2 * n_stack + 1]
    stacks, low_ref = outs[:n_stack], outs[n_stack]
    wgu, wdown, normed, gu, act, final, in_sem, out_sem = rest[2 * n_stack + 1 :]
    s_normed, s_gu, s_act, s_final, s_low = stacks
    slot, active = slot_ref[0], slot_ref[1] > 0
    ff = wdown.shape[0]
    parts = 4
    step = ff // parts
    pairs = []
    for i in range(parts):
        a = slice(i * step, (i + 1) * step)
        b = slice(ff + i * step, ff + (i + 1) * step)
        pairs += [(wgu_hbm.at[:, a], wgu.at[:, a]), (wgu_hbm.at[:, b], wgu.at[:, b])]
    pairs.append((wdown_hbm, wdown))
    load = copies_in(pairs, in_sem)
    stores = []

    def save(buffer, stack):
        copy = pltpu.make_async_copy(buffer, stack.at[slot], out_sem.at[len(stores)])
        pl.when(active)(copy.start)
        stores.append(copy)

    hidden = hidden_ref[...]
    rate = lax.rsqrt(jnp.mean(hidden * hidden, axis=-1, keepdims=True) + EPSILON)
    normed[...] = (hidden * rate * vec_ref[V_G2 : V_G2 + 1, : hidden.shape[1]]).astype(BF)
    save(normed, s_normed)
    for i in range(parts):
        load[2 * i].wait()
        load[2 * i + 1].wait()

        def up_tile(t, carry):
            a = pl.ds(pl.multiple_of(i * step + t * TILE, TILE), TILE)
            b = pl.ds(pl.multiple_of(ff + i * step + t * TILE, TILE), TILE)
            gate = dot(normed[...], wgu[:, a])
            up = dot(normed[...], wgu[:, b])
            gu[:, a] = gate.astype(BF)
            gu[:, b] = up.astype(BF)
            act[:, a] = (gate * sigmoid(gate) * up).astype(BF)
            return carry

        lax.fori_loop(0, step // TILE, up_tile, 0)
    save(gu, s_gu)
    save(act, s_act)
    load[2 * parts].wait()

    def down_tile(t, carry):
        cols = lanes(t)
        out = (hidden_ref[:, cols] + dot(act[...], wdown[:, cols])) * valid_ref[...]
        final[:, cols] = out
        low_ref[:, cols] = out.astype(BF)
        return carry

    lax.fori_loop(0, wdown.shape[1] // TILE, down_tile, 0)
    save(final, s_final)
    save(low_ref, s_low)
    for copy in stores:
        pl.when(active)(copy.wait)


def mlp_forward_call(slot, hidden, valid, vec, wgu, wdown, stacks):
    length, width = hidden.shape
    ff = wdown.shape[0]
    n_stack = len(stacks)
    scratch = [
        pltpu.VMEM(wgu.shape, BF),
        pltpu.VMEM(wdown.shape, BF),
        pltpu.VMEM((length, width), BF),
        pltpu.VMEM((length, 2 * ff), BF),
        pltpu.VMEM((length, ff), BF),
        pltpu.VMEM((length, width), F32),
        pltpu.SemaphoreType.DMA((9,)),
        pltpu.SemaphoreType.DMA((n_stack,)),
    ]
    out = pl.pallas_call(
        functools.partial(mlp_forward, n_stack=n_stack),
        out_shape=[jax.ShapeDtypeStruct(s.shape, s.dtype) for s in stacks]
        + [jax.ShapeDtypeStruct((length, width), BF)],
        in_specs=[SM, VM, VM, VM, ANY, ANY] + [ANY] * n_stack,
        out_specs=[ANY] * n_stack + [VM],
        scratch_shapes=scratch,
        input_output_aliases={6 + i: i for i in range(n_stack)},
        compiler_params=pltpu.CompilerParams(vmem_limit_bytes=32 * 1024 * 1024),
        cost_estimate=pl.CostEstimate(
            flops=2 * length * (wgu.size + wdown.size), bytes_accessed=19000000, transcendentals=0
        ),
        name="mlp_forward",
    )(slot, hidden, valid, vec, wgu, wdown, *stacks)
    return list(out[:n_stack]), out[n_stack]


def mlp_backward(
    slot_ref, mix_ref, target_ref, valid_ref, vec_ref, wgu_hbm, wdown_hbm, s_final, s_hidden, s_gu,
    *rest, n_stack
):
    outs = rest[n_stack : 2 * n_stack + 1]
    stacks, d_hidden_ref = outs[:n_stack], outs[n_stack]
    (wgu, wdown, final, hidden, gu, d_mlp, d_gu, d_sum, d_normed, small, in_sem, out_sem) = rest[
        2 * n_stack + 1 :
    ]
    s_dmlp, s_dgu, s_small = stacks
    slot, active = slot_ref[0], slot_ref[1] > 0
    ff = wdown.shape[0]
    load = copies_in(
        [
            (s_final.at[slot], final),
            (s_gu.at[slot], gu),
            (wdown_hbm, wdown),
            (wgu_hbm, wgu),
            (s_hidden.at[slot], hidden),
        ],
        in_sem,
    )
    stores = []

    def save(buffer, stack):
        copy = pltpu.make_async_copy(buffer, stack.at[slot], out_sem.at[len(stores)])
        pl.when(active)(copy.start)
        stores.append(copy)

    load[0].wait()
    target = target_ref[...].astype(F32)
    valid = valid_ref[...]
    misfit = final[...] - target
    loss = jnp.sum(valid * misfit * misfit, axis=0, keepdims=True)
    seed = valid * jnp.where(mix_ref[0] > 0.5, target, mix_ref[1] * misfit)
    d_sum[...] = seed
    d_mlp[...] = seed.astype(BF)
    save(d_mlp, s_dmlp)
    load[1].wait()
    load[2].wait()

    def act_tile(t, carry):
        a = lanes(t)
        b = pl.ds(pl.multiple_of(ff + t * TILE, TILE), TILE)
        d_act = dot_nt(d_mlp[...], wdown[a, :])
        gate, up = gu[:, a].astype(F32), gu[:, b].astype(F32)
        s = sigmoid(gate)
        swish = gate * s
        d_gu[:, a] = (d_act * up * (s + swish - swish * s)).astype(BF)
        d_gu[:, b] = (d_act * swish).astype(BF)
        return carry

    lax.fori_loop(0, ff // TILE, act_tile, 0)
    save(d_gu, s_dgu)
    load[3].wait()

    def back_tile(t, carry):
        rows = lanes(t)
        d_normed[:, rows] = dot_nt(d_gu[...], wgu[rows, :])
        return carry

    lax.fori_loop(0, wgu.shape[0] // TILE, back_tile, 0)
    load[4].wait()
    h = hidden[...]
    width = h.shape[1]
    rate = lax.rsqrt(jnp.mean(h * h, axis=-1, keepdims=True) + EPSILON)
    unit = h * rate
    d_n = d_normed[...]
    small[...] = jnp.zeros_like(small)
    small[0:1, :width] = jnp.sum(d_n * unit, axis=0, keepdims=True)
    small[1:2, :width] = loss
    save(small, s_small)
    d_n = d_n * vec_ref[V_G2 : V_G2 + 1, :width]
    d_hidden_ref[...] = d_sum[...] + rate * (
        d_n - unit * jnp.mean(d_n * unit, axis=-1, keepdims=True)
    )
    for copy in stores:
        pl.when(active)(copy.wait)


def mlp_backward_call(slot, mix, target, valid, vec, wgu, wdown, reads, stacks):
    length, width = target.shape
    ff = wdown.shape[0]
    n_stack = len(stacks)
    scratch = [
        pltpu.VMEM(wgu.shape, BF),
        pltpu.VMEM(wdown.shape, BF),
        pltpu.VMEM((length, width), F32),
        pltpu.VMEM((length, width), F32),
        pltpu.VMEM((length, 2 * ff), BF),
        pltpu.VMEM((length, width), BF),
        pltpu.VMEM((length, 2 * ff), BF),
        pltpu.VMEM((length, width), F32),
        pltpu.VMEM((length, width), F32),
        pltpu.VMEM(stacks[2].shape[1:], F32),
        pltpu.SemaphoreType.DMA((5,)),
        pltpu.SemaphoreType.DMA((n_stack,)),
    ]
    out = pl.pallas_call(
        functools.partial(mlp_backward, n_stack=n_stack),
        out_shape=[jax.ShapeDtypeStruct(s.shape, s.dtype) for s in stacks]
        + [jax.ShapeDtypeStruct((length, width), F32)],
        in_specs=[SM, SM, VM, VM, VM, ANY, ANY, ANY, ANY, ANY] + [ANY] * n_stack,
        out_specs=[ANY] * n_stack + [VM],
        scratch_shapes=scratch,
        input_output_aliases={10 + i: i for i in range(n_stack)},
        compiler_params=pltpu.CompilerParams(vmem_limit_bytes=40 * 1024 * 1024),
        cost_estimate=pl.CostEstimate(
            flops=2 * length * (wgu.size + wdown.size), bytes_accessed=20000000, transcendentals=0
        ),
        name="mlp_backward",
    )(slot, mix, target, valid, vec, wgu, wdown, *reads, *stacks)
    return list(out[:n_stack]), out[n_stack]


def column_sum(v):
    return jnp.sum(v, axis=0, keepdims=True)


def mix_backward(
    slot_ref, d_hidden_ref, vec_ref, cos_ref, sin_ref, win_hbm, wout_hbm,
    s_conv, s_z, s_gate, s_qkv, s_step, s_probs, s_y, s_x, *rest, n_stack, widths
):
    ci, mi, qw, kw, heads = widths
    outs = rest[n_stack : 2 * n_stack + 1]
    stacks, d_input_ref = outs[:n_stack], outs[n_stack]
    (win, wout, conv_raw, z, gate_raw, qkv, step_raw, probs, y, x_low, d_branch, d_proj, d_mixed,
     d_ssm, d_z, d_normed, run_wide, run_row, step_two, bend_two, tops, d_tops, run_acc, step_acc,
     small, in_sem, out_sem) = rest[2 * n_stack + 1 :]
    s_dbranch, s_dproj, s_small = stacks
    slot, active = slot_ref[0], slot_ref[1] > 0
    g0, q0 = ci, ci + mi
    s0 = q0 + qw + 2 * kw
    total = win.shape[1]
    length, width = d_hidden_ref.shape
    load = copies_in(
        [
            (wout_hbm, wout),
            (s_probs.at[slot], probs),
            (s_qkv.at[slot], qkv),
            (s_step.at[slot], step_raw),
            (s_gate.at[slot], gate_raw),
            (s_y.at[slot], y),
            (s_z.at[slot], z),
            (s_conv.at[slot], conv_raw),
            (win_hbm, win),
            (s_x.at[slot], x_low),
        ],
        in_sem,
    )
    stores = []

    def save(buffer, stack):
        copy = pltpu.make_async_copy(buffer, stack.at[slot], out_sem.at[len(stores)])
        pl.when(active)(copy.start)
        stores.append(copy)

    small[...] = jnp.zeros_like(small)
    d_branch[...] = d_hidden_ref[...].astype(BF)
    save(d_branch, s_dbranch)
    load[0].wait()
    for t in range(qw // TILE):
        rows = slice(mi + t * TILE, mi + (t + 1) * TILE)
        d_mixed[:, t * TILE : (t + 1) * TILE] = dot_nt(d_branch[...], wout[rows, :]).astype(BF)

    lane_first = jnp.bitwise_and(iota((length, HALF), 1), HD - 1) < HD // 2
    half_low = iota((length, HALF), 1) < HD
    cosine, sine = cos_ref[...], -sin_ref[...]
    load[1].wait()
    load[2].wait()
    keys, values = qkv[:, qw : qw + kw], qkv[:, qw + kw : qw + 2 * kw]
    keys_far, values_far = pltpu.roll(keys.astype(F32), HD, 1).astype(BF), pltpu.roll(
        values.astype(F32), HD, 1
    ).astype(BF)
    pairs = qw // HALF
    groups = kw // HD
    scale = HD ** (-0.5)
    d_keys = [jnp.zeros((length, HALF), F32) for _ in range(groups)]
    d_values = [jnp.zeros((length, HALF), F32) for _ in range(groups)]
    for pair in range(pairs):
        group = pair // (pairs // groups)
        keep = half_low if group == 0 else jnp.logical_not(half_low)
        keys_two = jnp.where(keep, keys, keys_far)
        values_two = jnp.where(keep, values, values_far)
        cols = slice(pair * HALF, (pair + 1) * HALF)
        query, d_out = qkv[:, cols], d_mixed[:, cols]
        results = []
        for side in range(2):
            own = half_low if side == 0 else jnp.logical_not(half_low)
            q = jnp.where(own, query, jnp.zeros_like(query))
            d_o = jnp.where(own, d_out, jnp.zeros_like(d_out))
            at = (2 * pair + side) * length
            weights = probs[at : at + length, :]
            wide = weights.astype(F32)
            d_weights = dot_nt(d_o, values_two)
            inner = wide * d_weights
            d_scores = (inner - wide * jnp.sum(inner, axis=-1, keepdims=True)).astype(BF)
            results.append(dot(d_scores, keys_two))
            d_keys[group] = d_keys[group] + dot_tn(d_scores, q)
            d_values[group] = d_values[group] + dot_tn(weights, d_o)
        d_q = jnp.where(half_low, results[0], results[1]) * scale
        d_proj[:, q0 + pair * HALF : q0 + (pair + 1) * HALF] = rope(
            d_q, cosine, sine, lane_first
        ).astype(BF)
    folded = [v + pltpu.roll(v, HD, 1) for v in d_keys]
    d_k = jnp.where(half_low, folded[0], folded[1]) * scale
    d_proj[:, q0 + qw : q0 + qw + kw] = rope(d_k, cosine, sine, lane_first).astype(BF)
    folded = [v + pltpu.roll(v, HD, 1) for v in d_values]
    d_proj[:, q0 + qw + kw : s0] = jnp.where(half_low, folded[0], folded[1]).astype(BF)

    load[3].wait()
    load[4].wait()
    load[5].wait()

    def norm_tile(t, sums):
        cols = lanes(t)
        d_s = dot_nt(d_branch[...], wout[cols, :])
        d_ssm[:, cols] = d_s
        g = gate_raw[:, cols].astype(F32)
        gated = y[:, cols].astype(F32) * (g * sigmoid(g))
        d_n = d_s * vec_ref[V_GS : V_GS + 1, cols]
        return (
            sums[0] + jnp.sum(gated * gated, axis=-1, keepdims=True),
            sums[1] + jnp.sum(gated * d_n, axis=-1, keepdims=True),
        )

    zero_col = jnp.zeros((length, 1), F32)
    squares, along = lax.fori_loop(0, mi // TILE, norm_tile, (zero_col, zero_col))
    rate = lax.rsqrt(squares * (1.0 / mi) + EPSILON)
    along = along * (rate * rate) * (1.0 / mi)

    pre, step, change, run, bend = scan_terms(step_raw[...], vec_ref, heads)
    turned = run.T
    run_row[:HALF, :] = turned[:, :HALF]
    run_row[HALF:, :] = turned[:, HALF:]
    broadcast_runs(run, run_wide, heads)
    step_two[...] = both(step)
    bend_two[...] = both(bend)
    load[6].wait()
    zb = z[:, mi : mi + 2 * HALF].astype(F32)
    sb = sigmoid(zb)
    bc = (zb * sb).astype(BF)
    b_in, c_in = bc[:, :HALF], bc[:, HALF:]
    causal = iota((HALF, HALF), 1) <= iota((HALF, HALF), 0)
    for c in range(2):
        rows = slice(c * HALF, (c + 1) * HALF)
        tops[rows, :] = jnp.where(causal, dot_nt(c_in[rows], b_in[rows]), 0.0)
    cross = dot_nt(c_in[HALF:], b_in[:HALF])
    cross_turned = cross.T.astype(BF)
    cross = cross.astype(BF)
    pair_low = iota((HALF, HALF), 1) < HD
    d_tops[...] = jnp.zeros_like(d_tops)
    run_acc[...] = jnp.zeros_like(run_acc)
    step_acc[...] = jnp.zeros_like(step_acc)

    def mix_tile(t, carry):
        cols = lanes(t)
        g = gate_raw[:, cols].astype(F32)
        s = sigmoid(g)
        swish = g * s
        y_in = y[:, cols].astype(F32)
        gated = y_in * swish
        d_s = d_ssm[:, cols]
        small[V_GS : V_GS + 1, cols] = column_sum(d_s * gated * rate)
        d_gated = rate * (d_s * vec_ref[V_GS : V_GS + 1, cols]) - gated * (along * rate)
        d_proj[:, pl.ds(pl.multiple_of(g0 + t * TILE, TILE), TILE)] = (
            d_gated * y_in * (s + swish - swish * s)
        ).astype(BF)
        d_y = d_gated * swish
        z_in = z[:, cols].astype(F32)
        s = sigmoid(z_in)
        x_in = z_in * s
        slope = s + x_in - x_in * s
        spread = expand_matrix(t)
        steps = dot(step_two[...], spread)
        bends = dot(bend_two[...], spread)
        scaled = (steps * x_in).astype(BF)
        d_low = d_y.astype(BF)
        u = (bends[:HALF] * scaled[:HALF].astype(F32)).astype(BF)
        v = (bends[HALF:] * d_y[HALF:]).astype(BF)
        far = dot(cross, u)
        back = dot(cross_turned, v)
        d_tops[2 * HALF :, :] += dot_nt(v, u)
        mixed_parts, back_parts = [], []
        for p in range(TILE // HALF):
            mixed_block, back_block = [], []
            for c in range(2):
                rows = slice(c * HALF, (c + 1) * HALF)
                xs = scaled[rows, p * HALF : (p + 1) * HALF]
                dy = d_low[rows, p * HALF : (p + 1) * HALF]
                zero = jnp.zeros_like(xs)
                xs_two = [jnp.where(pair_low, xs, zero), jnp.where(pair_low, zero, xs)]
                dy_two = [jnp.where(pair_low, dy, zero), jnp.where(pair_low, zero, dy)]
                weights = []
                d_top = jnp.zeros((HALF, HALF), F32)
                for side in range(2):
                    h = t * (TILE // HD) + 2 * p + side
                    wide = run_wide[rows, lanes(h, HALF)]
                    line = run_row[pl.ds(c * HALF + h, 1), :]
                    decay = jnp.exp(jnp.minimum(wide - line, 0.0))
                    weights.append((decay * tops[rows, :]).astype(BF))
                    d_top = d_top + decay * dot_nt(dy_two[side], xs)
                d_tops[rows, :] += d_top
                mixed_block.append(
                    dot(jnp.concatenate(weights, axis=1), jnp.concatenate(xs_two, axis=0))
                )
                back_block.append(
                    dot_tn(jnp.concatenate(weights, axis=0), jnp.concatenate(dy_two, axis=0))
                )
            mixed_parts.append(jnp.concatenate(mixed_block, axis=0))
            back_parts.append(jnp.concatenate(back_block, axis=0))
        mixed = jnp.concatenate(mixed_parts, axis=1)
        d_scaled = jnp.concatenate(back_parts, axis=1)
        crossing = jnp.concatenate(
            [-(u.astype(F32) * back), v.astype(F32) * far], axis=0
        )
        runs = d_low.astype(F32) * mixed - scaled.astype(F32) * d_scaled + crossing
        d_scaled = d_scaled + jnp.concatenate([bends[:HALF] * back, jnp.zeros_like(back)], axis=0)
        gather = reduce_matrix(t)
        run_acc[...] += sum(dot(part, gather) for part in split2(runs))
        step_acc[...] += sum(dot(part, gather) for part in split2(x_in * d_scaled))
        small[V_SKIP : V_SKIP + 1, cols] = column_sum(d_y * x_in)
        d_x = steps * d_scaled + vec_ref[V_SKIP : V_SKIP + 1, cols] * d_y
        d_z[:, cols] = d_x * slope
        return carry

    lax.fori_loop(0, mi // TILE, mix_tile, 0)
    d_top = [
        jnp.where(causal, d_tops[c * HALF : (c + 1) * HALF, :], 0.0).astype(BF) for c in range(2)
    ]
    d_cross = d_tops[2 * HALF :, :].astype(BF)
    d_c = jnp.concatenate(
        [dot(d_top[0], b_in[:HALF]), dot(d_cross, b_in[:HALF]) + dot(d_top[1], b_in[HALF:])], axis=0
    )
    d_b = jnp.concatenate(
        [dot_tn(d_top[0], c_in[:HALF]) + dot_tn(d_cross, c_in[HALF:]), dot_tn(d_top[1], c_in[HALF:])],
        axis=0,
    )
    xb = zb * sb
    d_z[:, mi : mi + 2 * HALF] = jnp.concatenate([d_b, d_c], axis=1) * (sb + xb - xb * sb)
    upper = jnp.where(
        iota((length, length), 0) <= iota((length, length), 1), 1.0, 0.0
    ).astype(BF)
    d_change = sum(dot(upper, part) for part in split3(run_acc[...]))
    d_pre = (step_acc[...] + d_change * vec_ref[V_DECAY : V_DECAY + 1, :HALF]) * sigmoid(pre)
    d_pre = jnp.where(iota(d_pre.shape, 1) < heads, d_pre, 0.0)
    d_proj[:, s0:total] = d_pre.astype(BF)
    small[V_SBIAS : V_SBIAS + 1, :HALF] = column_sum(d_pre)
    small[V_DECAY : V_DECAY + 1, :HALF] = column_sum(d_change * change)

    load[7].wait()
    row = iota((length, TILE), 0)

    def conv_tile(t, carry):
        cols = lanes(t)
        d = d_z[:, cols]
        raw = conv_raw[:, cols].astype(F32)
        small[V_CBIAS : V_CBIAS + 1, cols] = column_sum(d)
        small[3:4, cols] = column_sum(d * raw)
        out = d * vec_ref[3:4, cols]
        for ahead in range(1, 4):
            moved = jnp.where(row < length - ahead, pltpu.roll(d, length - ahead, 0), 0.0)
            small[3 - ahead : 4 - ahead, cols] = column_sum(moved * raw)
            out = out + moved * vec_ref[3 - ahead : 4 - ahead, cols]
        d_proj[:, cols] = out.astype(BF)
        return carry

    lax.fori_loop(0, ci // TILE, conv_tile, 0)
    save(d_proj, s_dproj)

    load[8].wait()

    def back_tile(t, carry):
        rows = lanes(t)
        d_normed[:, rows] = dot_nt(d_proj[...], win[rows, :])
        return carry

    lax.fori_loop(0, width // TILE, back_tile, 0)
    load[9].wait()
    x = x_low[...].astype(F32)
    rate_one = lax.rsqrt(jnp.mean(x * x, axis=-1, keepdims=True) + EPSILON)
    unit = x * rate_one
    d_n = d_normed[...]
    small[V_G1 : V_G1 + 1, :width] = column_sum(d_n * unit)
    save(small, s_small)
    d_n = d_n * vec_ref[V_G1 : V_G1 + 1, :width]
    d_input_ref[...] = (
        d_hidden_ref[...]
        + rate_one * (d_n - unit * jnp.mean(d_n * unit, axis=-1, keepdims=True))
    ).astype(BF)
    for copy in stores:
        pl.when(active)(copy.wait)


def mixer_backward_call(slot, d_hidden, vec, cosine, sine, win, wout, reads, stacks, widths):
    ci, mi, qw, kw, heads = widths
    length, width = d_hidden.shape
    n_stack = len(stacks)
    n_read = len(reads)
    scratch = [
        pltpu.VMEM(win.shape, BF),
        pltpu.VMEM(wout.shape, BF),
        pltpu.VMEM((length, ci), BF),
        pltpu.VMEM((length, ci), BF),
        pltpu.VMEM((length, mi), BF),
        pltpu.VMEM((length, qw + 2 * kw), BF),
        pltpu.VMEM((length, HALF), F32),
        pltpu.VMEM((qw // HD * length, length), BF),
        pltpu.VMEM((length, mi), BF),
        pltpu.VMEM((length, width), BF),
        pltpu.VMEM((length, width), BF),
        pltpu.VMEM((length, win.shape[1]), BF),
        pltpu.VMEM((length, qw), BF),
        pltpu.VMEM((length, mi), F32),
        pltpu.VMEM((length, ci), F32),
        pltpu.VMEM((length, width), F32),
        pltpu.VMEM((length, heads * HALF), F32),
        pltpu.VMEM((length, HALF), F32),
        pltpu.VMEM((length, 2 * HALF), BF),
        pltpu.VMEM((length, 2 * HALF), BF),
        pltpu.VMEM((2 * HALF, HALF), F32),
        pltpu.VMEM((3 * HALF, HALF), F32),
        pltpu.VMEM((length, HALF), F32),
        pltpu.VMEM((length, HALF), F32),
        pltpu.VMEM(stacks[2].shape[1:], F32),
        pltpu.SemaphoreType.DMA((10,)),
        pltpu.SemaphoreType.DMA((n_stack,)),
    ]
    out = pl.pallas_call(
        functools.partial(mix_backward, n_stack=n_stack, widths=widths),
        out_shape=[jax.ShapeDtypeStruct(s.shape, s.dtype) for s in stacks]
        + [jax.ShapeDtypeStruct((length, width), BF)],
        in_specs=[SM, VM, VM, VM, VM, ANY, ANY] + [ANY] * (n_read + n_stack),
        out_specs=[ANY] * n_stack + [VM],
        scratch_shapes=scratch,
        input_output_aliases={7 + n_read + i: i for i in range(n_stack)},
        compiler_params=pltpu.CompilerParams(vmem_limit_bytes=48 * 1024 * 1024),
        cost_estimate=pl.CostEstimate(
            flops=2 * length * (win.size + wout.size), bytes_accessed=24000000, transcendentals=0
        ),
        name="mixer_backward",
    )(slot, d_hidden, vec, cosine, sine, win, wout, *reads, *stacks)
    return list(out[:n_stack]), out[n_stack]


def rope_tables(length):
    halves = HD // 2
    inverse = jnp.exp(jnp.arange(halves, dtype=F32) * (-2.0 * math.log(ROPE_BASE) / HD))
    angles = jnp.arange(length, dtype=F32)[:, None] * inverse[None, :]
    cosine, sine = jnp.cos(angles), jnp.sin(angles)
    return (
        jnp.concatenate([cosine] * 4, axis=1),
        jnp.concatenate([-sine, sine, -sine, sine], axis=1),
    )


def swap(block, axis, bit):
    return lax.ppermute(block, axis, [(i, i ^ bit) for i in range(lax.axis_size(axis))])


def place(full, piece, row):
    return lax.dynamic_update_slice(full, piece, (row, 0))


def quick_links():
    return lax.axis_size("fsdp") == 4 and lax.axis_size("rep") == 4


def gather_rows(shard):
    if not quick_links():
        return lax.all_gather(shard, "fsdp", axis=0, tiled=True)
    me = lax.axis_index("fsdp")
    parity = lax.axis_index("rep") % 2
    rows = shard.shape[0]
    half = rows // 2
    first = lax.dynamic_slice_in_dim(shard, parity * half, half, 0)
    far_one = swap(first, "fsdp", 2)
    far_two = swap(far_one, "rep", 1)
    near = swap(shard, "fsdp", 1)
    full = jnp.zeros((rows * 4, shard.shape[1]), shard.dtype)
    full = place(full, shard, me * rows)
    full = place(full, near, (me ^ 1) * rows)
    for piece, at in ((far_one, parity * half), (far_two, (1 - parity) * half)):
        full = place(full, piece, (me ^ 2) * rows + at)
        full = place(full, swap(piece, "fsdp", 1), (me ^ 3) * rows + at)
    return full


def plus(a, b):
    return (a.astype(F32) + b.astype(F32)).astype(BF)


def reduce_rows(grad):
    n = lax.axis_size("fsdp")
    if not quick_links():
        own = lax.psum_scatter(grad, "fsdp", scatter_dimension=0, tiled=True)
        return lax.psum(own, "rep").astype(F32)
    me, rank = lax.axis_index("fsdp"), lax.axis_index("rep")
    core, chip = me % 2, me // 2
    rows = grad.shape[0] // n
    blocks = grad.reshape(2, 2, rows, grad.shape[1])
    away = lax.dynamic_index_in_dim(blocks, 1 - core, 1, keepdims=False)
    stay = lax.dynamic_index_in_dim(blocks, core, 1, keepdims=False)
    pair = plus(stay, swap(away, "fsdp", 1))
    away = lax.dynamic_index_in_dim(pair, 1 - chip, 0, keepdims=False)
    stay = lax.dynamic_index_in_dim(pair, chip, 0, keepdims=False)
    own = plus(stay, swap(away, "fsdp", 2))
    inner = jnp.logical_or(rank == 1, rank == 2)
    own = plus(own, lax.ppermute(own, "rep", [(0, 1), (3, 2)]))
    total = plus(own, lax.ppermute(own, "rep", [(1, 2), (2, 1)]))
    outer = lax.ppermute(total, "rep", [(1, 0), (2, 3)])
    return jnp.where(inner, total, outer).astype(F32)


def weight_grad(left, right):
    return lax.dot_general(
        left, right, (((0, 1), (0, 1)), ((), ())), preferred_element_type=F32
    ).astype(BF)


def body(
    inputs,
    teacher,
    lengths,
    order,
    loss_scale,
    norm_gain1,
    w_query,
    w_key,
    w_value,
    w_attn_out,
    w_ssm_gate,
    w_conv_in,
    w_step,
    conv_kernel,
    conv_bias,
    step_bias,
    decay_log,
    skip_gain,
    ssm_norm_gain,
    w_ssm_out,
    norm_gain2,
    w_gate,
    w_up,
    w_down,
):
    n_rep = lax.axis_size("rep")
    n_fsdp = lax.axis_size("fsdp")
    rank = lax.axis_index("rep")
    section = lax.axis_index("section")
    first = section == 0
    device = lax.axis_index("fsdp") * n_rep + rank
    count, length, width = inputs.shape
    ci, mi, qw, kw = (w.shape[2] for w in (w_conv_in, w_ssm_gate, w_query, w_key))
    heads = w_step.shape[2]
    ff = w_up.shape[2]
    widths = (ci, mi, qw, kw, heads)
    taps = conv_kernel.shape[1]
    rows = width // n_fsdp

    def columns(flat):
        wide = -(-flat.size // rows)
        return jnp.pad(flat, (0, wide * rows - flat.size)).reshape(rows, wide)

    convs = jnp.concatenate([conv_kernel[0], conv_bias], axis=0)
    riders = [norm_gain1[0][:, None], norm_gain2[0][:, None], columns(convs.reshape(-1)), columns(ssm_norm_gain[0])]
    used = sum(r.shape[1] for r in riders)
    shard_in = jnp.concatenate(
        [w_conv_in[0], w_ssm_gate[0], w_query[0], w_key[0], w_value[0], w_step[0]]
        + riders
        + [jnp.zeros((rows, HALF - heads - used), BF)],
        axis=1,
    )
    win = gather_rows(shard_in)
    wout = jnp.concatenate([gather_rows(w_ssm_out[0]), gather_rows(w_attn_out[0])], axis=0)
    wgu = gather_rows(jnp.concatenate([w_gate[0], w_up[0]], axis=1))
    wdown = gather_rows(w_down[0])

    at = ci + mi + qw + 2 * kw + heads
    ridden = win[:, at : at + used].reshape(n_fsdp, rows, used)
    wide = riders[2].shape[1]
    conv_all = ridden[:, :, 2 : 2 + wide].reshape(n_fsdp, -1)[:, : (taps + 1) * ci // n_fsdp]
    conv_all = conv_all.reshape(n_fsdp, taps + 1, ci // n_fsdp).transpose(1, 0, 2).reshape(taps + 1, ci)
    ssm_gain = ridden[:, :, 2 + wide :].reshape(n_fsdp, -1)[:, : mi // n_fsdp].reshape(1, mi)

    def table_row(v):
        v = v.astype(F32)
        return jnp.pad(v, ((0, 0), (0, ci - v.shape[1])))

    vec = jnp.concatenate(
        [
            table_row(v)
            for v in (
                conv_all,
                ssm_gain,
                jnp.repeat(skip_gain, HD, axis=1),
                ridden[:, :, 0].reshape(1, width),
                ridden[:, :, 1].reshape(1, width),
                step_bias,
                -jnp.exp(decay_log),
                jnp.zeros((16 - taps - 7, 1), F32),
            )
        ],
        axis=0,
    )
    cosine, sine = rope_tables(length)

    inverse_order = jnp.argsort(order)
    target = lax.dynamic_slice_in_dim(order, device * count, count) // count % n_rep
    sources = lax.dynamic_slice_in_dim(inverse_order, device * count, count)
    anchor = sources // count % n_rep
    own_data = jnp.where(first, inputs, teacher)
    turns = jnp.arange(count, dtype=jnp.int32)
    send_at = jnp.argsort(target ^ rank)
    keep_at = jnp.argsort(anchor ^ rank)
    dealt = []
    for j in range(count):
        piece = lax.dynamic_index_in_dim(own_data, send_at[j], 0, keepdims=False)
        dealt.append(swap(piece, "rep", j) if j else piece)
    own_lengths = jnp.take(lengths, jnp.take(sources, keep_at))
    positions = jnp.arange(length, dtype=jnp.int32)
    valid_all = (positions[None, :] < own_lengths[:, None]).astype(F32)[:, :, None]
    valid_count = jnp.sum(lengths).astype(F32)
    factor = loss_scale / (valid_count * width)

    def stack(*shape, kind=BF):
        return jnp.zeros((count,) + shape, kind)

    mix_stacks = [
        stack(length, width),
        stack(length, ci),
        stack(length, ci),
        stack(length, mi),
        stack(length, qw + 2 * kw),
        stack(length, HALF, kind=F32),
        stack(qw // HD * length, length),
        stack(length, mi + qw),
        stack(length, mi),
        stack(length, width, kind=F32),
        stack(length, width),
    ]
    mlp_stacks = [
        stack(length, width),
        stack(length, 2 * ff),
        stack(length, ff),
        stack(length, width, kind=F32),
        stack(length, width),
    ]
    skew = 2

    def slot_of(raw):
        inside = jnp.logical_and(raw >= 0, raw < count).astype(jnp.int32)
        return jnp.clip(raw, 0, count - 1), inside

    received = []
    for tick in range(count + skew):
        slot, inside = slot_of(tick - skew * section)
        if tick < skew:
            seq_in = dealt[tick]
        elif tick < count:
            seq_in = jnp.where(first, dealt[tick], received[tick - skew])
        else:
            seq_in = received[tick - skew]
        slots = jnp.stack([slot, inside])
        mix_stacks, hidden = mixer_forward_call(
            slots, seq_in, vec, cosine, sine, win, wout, mix_stacks, widths
        )
        valid = lax.dynamic_index_in_dim(valid_all, slot, 0, keepdims=False)
        mlp_stacks, low = mlp_forward_call(slots, hidden, valid, vec, wgu, wdown, mlp_stacks)
        if tick < count:
            received.append(lax.ppermute(low, "section", [(0, 1)]))

    (s_normed, s_conv, s_z, s_gate, s_qkv, s_step, s_probs, s_branch, s_y, s_hidden, s_x) = mix_stacks
    s_normed2, s_gu, s_act, s_final, s_low = mlp_stacks
    mlp_grads = [stack(length, width), stack(length, 2 * ff), stack(8, width, kind=F32)]
    mix_grads = [stack(length, width), stack(length, win.shape[1]), stack(16, ci, kind=F32)]
    mix = jnp.stack([jnp.where(first, 1.0, 0.0), 2.0 * factor])
    incoming, returned, d_inputs = [], [None] * count, [None] * count
    for turn in range(count + skew):
        slot, inside = slot_of(count - 1 - turn + skew * (1 - section))
        if turn < skew:
            seed = dealt[count - 1 - turn]
        elif turn < count:
            seed = jnp.where(first, incoming[turn - skew], dealt[count - 1 - turn])
        else:
            seed = incoming[turn - skew]
        slots = jnp.stack([slot, inside])
        valid = lax.dynamic_index_in_dim(valid_all, slot, 0, keepdims=False)
        mlp_grads, d_hidden = mlp_backward_call(
            slots, mix, seed, valid, vec, wgu, wdown, [s_final, s_hidden, s_gu], mlp_grads
        )
        mix_grads, d_input = mixer_backward_call(
            slots,
            d_hidden,
            vec,
            cosine,
            sine,
            win,
            wout,
            [s_conv, s_z, s_gate, s_qkv, s_step, s_probs, s_y, s_x],
            mix_grads,
            widths,
        )
        if turn < count:
            incoming.append(lax.ppermute(d_input, "section", [(1, 0)]))
            d_inputs[count - 1 - turn] = d_input
        if turn >= skew:
            j = count - 1 - turn + skew
            back = jnp.where(first, d_input, s_low[j])
            returned[j] = swap(back, "rep", j) if j else back

    s_dmlp, s_dgu, small_mlp = mlp_grads
    s_dbranch, s_dproj, small_mix = mix_grads
    grad_gu = reduce_rows(weight_grad(s_normed2, s_dgu))
    grad_down = reduce_rows(weight_grad(s_act, s_dmlp))
    grad_out = weight_grad(s_branch, s_dbranch)
    grad_ssm_out = reduce_rows(grad_out[:mi])
    grad_attn_out = reduce_rows(grad_out[mi:])
    grad_in = reduce_rows(weight_grad(s_normed, s_dproj))

    mix_sum = jnp.sum(small_mix, axis=0)
    mlp_sum = jnp.sum(small_mlp, axis=0)
    loss_part = jnp.where(first, 0.0, jnp.sum(mlp_sum[1]))
    flat = jnp.concatenate(
        [
            mix_sum[:5].reshape(-1),
            mix_sum[V_GS, :mi],
            mix_sum[V_G1, :width],
            mlp_sum[0],
            mix_sum[V_SBIAS, :heads],
            mix_sum[V_DECAY, :heads],
            jnp.sum(mix_sum[V_SKIP, :mi].reshape(heads, HD), axis=1),
        ]
    )
    slots = jnp.arange(lax.axis_size("section"), dtype=jnp.int32) == section
    flat = jnp.where(slots[:, None], flat[None], 0.0)
    loss_total, flat = lax.psum((loss_part, flat), ("section", "fsdp", "rep"))
    flat = lax.dynamic_index_in_dim(flat, section, 0, keepdims=False)
    cuts = [taps * ci, ci, mi, width, width, heads, heads, heads]
    parts, begin = [], 0
    for cut in cuts:
        parts.append(flat[begin : begin + cut])
        begin += cut
    fsdp = lax.axis_index("fsdp")

    def own(v):
        size = v.shape[-1] // n_fsdp
        return lax.dynamic_slice_in_dim(v, fsdp * size, size, v.ndim - 1)[None]

    returned = jnp.stack(returned)
    restored = jnp.take(returned, target ^ rank, axis=0)
    dealt_acts = jnp.take(s_low, anchor ^ rank, axis=0)
    dealt_grads = jnp.take(jnp.stack(d_inputs), anchor ^ rank, axis=0)
    activations = jnp.where(first, dealt_acts, restored)[None]
    gradients = jnp.where(first, restored, dealt_grads)[None]
    q0 = ci + mi
    s0 = q0 + qw + 2 * kw
    return (
        activations,
        gradients,
        loss_total / (valid_count * width),
        own(parts[3]),
        grad_in[None, :, q0 : q0 + qw],
        grad_in[None, :, q0 + qw : q0 + qw + kw],
        grad_in[None, :, q0 + qw + kw : s0],
        grad_attn_out[None],
        grad_in[None, :, ci:q0],
        grad_in[None, :, :ci],
        grad_in[None, :, s0 : s0 + heads],
        own(parts[0].reshape(taps, ci)),
        own(parts[1]),
        parts[5][None],
        parts[6][None],
        parts[7][None],
        own(parts[2]),
        grad_ssm_out[None],
        own(parts[4]),
        grad_gu[None, :, :ff],
        grad_gu[None, :, ff:],
        grad_down[None],
    )


def solution(mesh):
    rows3 = P("section", "fsdp", None)
    pair = P("section", "fsdp")
    one = P("section", None)
    data = P(("fsdp", "rep"), None, None)
    taps = P("section", None, "fsdp")
    in_specs = (data, data, P(), P(), P(), pair) + (rows3,) * 7
    in_specs += (taps, pair, one, one, one, pair, rows3, pair, rows3, rows3, rows3)
    placed = P("section", ("fsdp", "rep"), None, None)
    out_specs = (placed, placed, P(), pair) + (rows3,) * 7
    out_specs += (taps, pair, one, one, one, pair, rows3, pair, rows3, rows3, rows3)
    return jax.shard_map(body, mesh=mesh, in_specs=in_specs, out_specs=out_specs, check_vma=False)
```

```python
import math
import functools

import jax
import jax.numpy as jnp
from jax import lax
from jax.experimental import pallas as pl
from jax.experimental.pallas import tpu as pltpu
from jax.sharding import PartitionSpec as P

HD = 64
EPSILON = 1e-05
ROPE_BASE = 100000000000.0
MASKED = -1e30
F32 = jnp.float32
BF = jnp.bfloat16
TILE = 256
HALF = 128
HB = pl.BlockSpec(memory_space=pltpu.HBM)
VM = pl.BlockSpec(memory_space=pltpu.VMEM)
SM = pl.BlockSpec(memory_space=pltpu.SMEM)


def dot(a, b):
    return jnp.dot(a, b, preferred_element_type=F32)


def dot_nt(a, b):
    return lax.dot_general(a, b, (((1,), (1,)), ((), ())), preferred_element_type=F32)


def dot_tn(a, b):
    return lax.dot_general(a, b, (((0,), (0,)), ((), ())), preferred_element_type=F32)


def sigmoid(v):
    return 0.5 * jnp.tanh(0.5 * v) + 0.5


def lanes(i, width=TILE):
    return pl.ds(pl.multiple_of(i * width, width), width)


def iota(shape, axis):
    return lax.broadcasted_iota(jnp.int32, shape, axis)


def split2(v):
    hi = v.astype(BF)
    return hi, (v - hi.astype(F32)).astype(BF)


def split3(v):
    hi = v.astype(BF)
    rest = v - hi.astype(F32)
    mid = rest.astype(BF)
    return hi, mid, (rest - mid.astype(F32)).astype(BF)


def expand_matrix(tile):
    row = jnp.bitwise_and(iota((TILE, TILE), 0), HALF - 1)
    col = jnp.right_shift(iota((TILE, TILE), 1), 6) + tile * (TILE // HD)
    return jnp.where(row == col, 1.0, 0.0).astype(BF)


def reduce_matrix(tile):
    row = jnp.right_shift(iota((TILE, HALF), 0), 6) + tile * (TILE // HD)
    col = iota((TILE, HALF), 1)
    return jnp.where(row == col, 1.0, 0.0).astype(BF)


def both(v):
    return jnp.concatenate(split2(v), axis=1)


def rope(v, cosine, sine, first):
    turned = jnp.where(first, pltpu.roll(v, HALF - HD // 2, 1), pltpu.roll(v, HD // 2, 1))
    return v * cosine + turned * sine


def start_all(groups, sems):
    waits, at = [], 0
    for group in groups:
        copies = []
        for source, target in group:
            copies.append(pltpu.make_async_copy(source, target, sems.at[at]))
            at += 1
        for copy in copies:
            copy.start()
        waits.append(copies)

    def wait(i):
        for copy in waits[i]:
            copy.wait()

    return wait


def row_pieces(pieces, spots, scratch, columns):
    if len(pieces) == 1:
        return [(pieces[0].at[:, a], scratch.at[:, b]) for a, b in columns]
    unit = pieces[-1].shape[0]
    if len(pieces) == 4:
        places = [jnp.right_shift(spots[i], 1) for i in (0, 1, 2, 4)]
    else:
        places = [spots[i] for i in range(6)]
    out = []
    for a, b in columns:
        for place, piece in zip(places, pieces):
            rows = pl.ds(pl.multiple_of(place * unit, unit), piece.shape[0])
            out.append((piece.at[:, a], scratch.at[rows, b]))
    return out


def out_pieces(pieces, spots, scratch, inner):
    if len(pieces) == 1:
        return [(pieces[0], scratch)]
    total, width = scratch.shape
    n = total // pieces[0].shape[0]
    cut, rest = inner // n, (total - inner) // n
    out = []
    for i, piece in enumerate(pieces):
        block, side = jnp.right_shift(spots[i], 1), jnp.bitwise_and(spots[i], 1)
        span = piece.shape[1]
        cols = slice(0, width)
        if span < width:
            cols = pl.ds(pl.multiple_of(side * span, span), span)
        upper = pl.ds(pl.multiple_of(block * cut, cut), cut)
        lower = pl.ds(pl.multiple_of(inner + block * rest, rest), rest)
        out.append((piece.at[:cut, :], scratch.at[upper, cols]))
        out.append((piece.at[cut:, :], scratch.at[lower, cols]))
    return out


def saver(slot, active, sems):
    stores = []

    def save(buffer, stack, at=slot):
        copy = pltpu.make_async_copy(buffer, stack.at[at], sems.at[len(stores)])
        pl.when(active)(copy.start)
        stores.append(copy)

    def finish():
        for copy in stores:
            pl.when(active)(copy.wait)

    return save, finish


def in_hbm(a):
    return pltpu.with_memory_space_constraint(a, pltpu.HBM)


def call(body, name, scalars, spots, ordinary, weights, reads, stacks, result, scratch, limit, work):
    fresh = isinstance(stacks[0], jax.ShapeDtypeStruct)
    flat = [piece for group in weights for piece in group]
    counts = [len(group) for group in weights]
    kept = [] if fresh else list(stacks)
    ahead = len(scalars) + 1 + len(ordinary) + len(flat) + len(reads)
    n = len(stacks)
    cuts = [len(scalars), 1, len(ordinary), len(flat), len(reads), len(kept), n, 1]

    def kernel(*refs):
        parts, at = [], 0
        for cut in cuts:
            parts.append(refs[at : at + cut])
            at += cut
        groups, begin = [], 0
        for c in counts:
            groups.append(parts[3][begin : begin + c])
            begin += c
        for _ in body(
            parts[0], parts[1][0], parts[2], groups, parts[4], parts[6], parts[7][0], refs[at:]
        ):
            pass

    out = pl.pallas_call(
        kernel,
        out_shape=[pltpu.HBM(s.shape, s.dtype) for s in stacks] + [result],
        in_specs=[SM] * (len(scalars) + 1)
        + [VM] * len(ordinary)
        + [HB] * (len(flat) + len(reads) + len(kept)),
        out_specs=[HB] * n + [VM],
        scratch_shapes=scratch,
        input_output_aliases={} if fresh else {ahead + i: i for i in range(n)},
        compiler_params=pltpu.CompilerParams(vmem_limit_bytes=limit * 1024 * 1024),
        cost_estimate=pl.CostEstimate(
            flops=work * 100000000, bytes_accessed=1000000, transcendentals=0
        ),
        name=name,
    )(*scalars, spots, *ordinary, *(in_hbm(a) for a in flat + list(reads) + kept))
    return list(out[:n]), out[n]


V_TAP, V_CBIAS, V_GS, V_SKIP, V_G1, V_G2, V_SBIAS, V_DECAY = 0, 4, 5, 6, 7, 8, 9, 10


def scan_terms(step_raw, vec_ref, heads):
    lane = iota(step_raw.shape, 1)
    pre = step_raw + vec_ref[V_SBIAS : V_SBIAS + 1, :HALF]
    soft = jnp.maximum(pre, 0.0) + jnp.log1p(jnp.exp(-jnp.abs(pre)))
    step = jnp.where(lane < heads, soft, 0.0)
    change = step * vec_ref[V_DECAY : V_DECAY + 1, :HALF]
    length = step.shape[0]
    lower = jnp.where(
        iota((length, length), 0) >= iota((length, length), 1), 1.0, 0.0
    ).astype(BF)
    run = sum(dot(lower, part) for part in split3(change))
    middle = run[HALF - 1 : HALF, :]
    bend = jnp.where(iota(run.shape, 0) < HALF, middle - run, run - middle)
    bend = jnp.exp(jnp.minimum(bend, 0.0))
    return pre, step, change, run, bend


def broadcast_runs(run, run_wide, heads):
    for h in range(heads):
        run_wide[:, h * HALF : (h + 1) * HALF] = jnp.broadcast_to(
            run[:, h : h + 1], (run.shape[0], HALF)
        )


def mix_forward(widths, scalars, spots, ordinary, weights, reads, stacks, hidden_ref, scratch):
    ci, mi, qw, kw, heads = widths
    index_ref, slot_ref = scalars
    base = 4 * index_ref[0]
    x_ref, vec_ref, cos_ref, sin_ref, _ = ordinary
    w_first, w_conv, w_gate, w_out = weights
    (win, wout, normed, conv_raw, z, xbc, gate_raw, qkv, step_raw, probs, branch, mixed_all, y,
     gated, run_wide, run_row, step_two, bend_two, in_sem, out_sem) = scratch
    (s_normed, s_conv, s_z, s_gate, s_qkv, s_step, s_probs, s_ssm, s_mixed, s_y, s_hidden,
     s_x) = stacks
    g0 = ci
    q0 = ci + mi
    total = win.shape[1]
    tail = total - q0
    wait = start_all(
        [
            row_pieces(w_first, spots, win, [(slice(0, tail), slice(q0, total))]),
            row_pieces(w_conv, spots, win, [(slice(0, ci), slice(0, ci))]),
            row_pieces(w_gate, spots, win, [(slice(0, mi), slice(g0, q0))]),
            out_pieces(w_out, spots, wout, mi),
        ],
        in_sem,
    )
    save, finish = saver(slot_ref[base], slot_ref[base + 1] > 0, out_sem)
    yield

    length = x_ref.shape[0]
    x = x_ref[...].astype(F32)
    rate = lax.rsqrt(jnp.mean(x * x, axis=-1, keepdims=True) + EPSILON)
    normed[...] = (x * rate * vec_ref[V_G1 : V_G1 + 1, : x.shape[1]]).astype(BF)
    save(normed, s_normed)
    lane_first = jnp.bitwise_and(iota((length, HALF), 1), HD - 1) < HD // 2
    half_low = iota((length, HALF), 1) < HD

    wait(0)
    cosine, sine = cos_ref[...], sin_ref[...]
    n_rope = (qw + kw) // HALF
    for t in range((total - q0) // HALF // 2):
        raw = dot(normed[...], win[:, q0 + t * TILE : q0 + (t + 1) * TILE])
        for part in range(2):
            c = 2 * t + part
            piece = raw[:, part * HALF : (part + 1) * HALF]
            if c < n_rope:
                piece = rope(piece, cosine, sine, lane_first)
            if c < n_rope + kw // HALF:
                qkv[:, c * HALF : (c + 1) * HALF] = piece.astype(BF)
            else:
                step_raw[...] = piece
    if ((total - q0) // HALF) % 2:
        step_raw[...] = dot(normed[...], win[:, total - HALF : total])
    save(qkv, s_qkv)
    save(step_raw, s_step)

    wait(1)
    row = iota((length, TILE), 0)

    def conv_tile(t, carry):
        cols = lanes(t)
        raw = dot(normed[...], win[:, cols])
        conv_raw[:, cols] = raw.astype(BF)
        total_z = vec_ref[V_CBIAS : V_CBIAS + 1, cols] + raw * vec_ref[3:4, cols]
        for back in range(1, 4):
            moved = jnp.where(row >= back, pltpu.roll(raw, back, 0), 0.0)
            total_z = total_z + moved * vec_ref[3 - back : 4 - back, cols]
        z[:, cols] = total_z.astype(BF)
        xbc[:, cols] = (total_z * sigmoid(total_z)).astype(BF)
        return carry

    lax.fori_loop(0, ci // TILE, conv_tile, 0, unroll=True)
    save(conv_raw, s_conv)
    save(z, s_z)

    wait(2)

    def gate_tile(t, carry):
        raw = dot(normed[...], win[:, pl.ds(pl.multiple_of(g0 + t * TILE, TILE), TILE)])
        gate_raw[:, lanes(t)] = raw.astype(BF)
        return carry

    lax.fori_loop(0, mi // TILE, gate_tile, 0, unroll=True)
    save(gate_raw, s_gate)

    yield

    keys, values = qkv[:, qw : qw + kw], qkv[:, qw + kw : qw + 2 * kw]
    keys_far, values_far = pltpu.roll(keys.astype(F32), HD, 1).astype(BF), pltpu.roll(
        values.astype(F32), HD, 1
    ).astype(BF)
    causal_top = iota((HALF, HALF), 1) <= iota((HALF, HALF), 0)
    causal_low = iota((HALF, length), 1) <= iota((HALF, length), 0) + HALF
    pairs = qw // HALF
    groups = kw // HD
    probs_zero = jnp.zeros((HALF, HALF), BF)
    for pair in range(pairs):
        group = pair // (pairs // groups)
        keep = half_low if group == 0 else jnp.logical_not(half_low)
        keys_two = jnp.where(keep, keys, keys_far)
        values_two = jnp.where(keep, values, values_far)
        query = qkv[:, pair * HALF : (pair + 1) * HALF] * jnp.asarray(HD ** (-0.5), BF)
        results = []
        for side in range(2):
            own = half_low if side == 0 else jnp.logical_not(half_low)
            q = jnp.where(own, query, jnp.zeros_like(query))
            at = (2 * pair + side) * length
            out = []
            for lo, causal in ((0, causal_top), (1, causal_low)):
                width = HALF if lo == 0 else length
                scores = dot_nt(q[lo * HALF : (lo + 1) * HALF], keys_two[:width])
                scores = jnp.where(causal, scores, MASKED)
                top = jnp.max(scores, axis=-1, keepdims=True)
                weights = jnp.exp(scores - top)
                weights = weights / jnp.sum(weights, axis=-1, keepdims=True)
                weights = weights.astype(BF)
                if lo == 0:
                    probs[at : at + HALF, :HALF] = weights
                    probs[at : at + HALF, HALF:] = probs_zero
                else:
                    probs[at + HALF : at + length, :] = weights
                out.append(dot(weights, values_two[:width]))
            results.append(jnp.concatenate(out, axis=0))
        mixed = jnp.where(half_low, results[0], results[1])
        mixed_all[:, pair * HALF : (pair + 1) * HALF] = mixed.astype(BF)
    save(probs, s_probs)
    save(mixed_all, s_mixed)

    pre, step, change, run, bend = scan_terms(step_raw[...], vec_ref, heads)
    turned = run.T
    run_row[:HALF, :] = turned[:, :HALF]
    run_row[HALF:, :] = turned[:, HALF:]
    broadcast_runs(run, run_wide, heads)
    step_two[...] = both(step)
    bend_two[...] = both(bend)
    b_in, c_in = xbc[:, mi : mi + HALF], xbc[:, mi + HALF : mi + 2 * HALF]
    tops = [dot_nt(c_in[c * HALF : (c + 1) * HALF], b_in[c * HALF : (c + 1) * HALF]) for c in (0, 1)]
    cross = dot_nt(c_in[HALF:], b_in[:HALF]).astype(BF)
    pair_low = iota((HALF, HALF), 1) < HD
    tops = [jnp.where(causal_top, t, 0.0) for t in tops]

    def mix_tile(t, squares):
        cols = lanes(t)
        spread = expand_matrix(t)
        x_in = xbc[:, cols].astype(F32)
        scaled = (dot(step_two[...], spread) * x_in).astype(BF)
        bends = dot(bend_two[...], spread)
        u = (bends[:HALF] * scaled[:HALF].astype(F32)).astype(BF)
        far = dot(cross, u) * bends[HALF:]
        parts = []
        for p in range(TILE // HALF):
            block = []
            for c in range(2):
                rows = slice(c * HALF, (c + 1) * HALF)
                weights = []
                for side in range(2):
                    h = t * (TILE // HD) + 2 * p + side
                    wide = run_wide[rows, lanes(h, HALF)]
                    line = run_row[pl.ds(c * HALF + h, 1), :]
                    decay = jnp.exp(jnp.minimum(wide - line, 0.0))
                    weights.append((decay * tops[c]).astype(BF))
                xs = scaled[rows, p * HALF : (p + 1) * HALF]
                zero = jnp.zeros_like(xs)
                right = jnp.concatenate(
                    [jnp.where(pair_low, xs, zero), jnp.where(pair_low, zero, xs)], axis=0
                )
                block.append(dot(jnp.concatenate(weights, axis=1), right))
            parts.append(jnp.concatenate(block, axis=0))
        out = jnp.concatenate(parts, axis=1)
        out = out + jnp.concatenate([jnp.zeros_like(far), far], axis=0)
        out = out + vec_ref[V_SKIP : V_SKIP + 1, cols] * x_in
        y[:, cols] = out.astype(BF)
        g = gate_raw[:, cols].astype(F32)
        out = out * (g * sigmoid(g))
        gated[:, cols] = out
        return squares + jnp.sum(out * out, axis=-1, keepdims=True)

    squares = lax.fori_loop(0, mi // TILE, mix_tile, jnp.zeros((length, 1), F32), unroll=True)
    save(y, s_y)
    rate = lax.rsqrt(squares * (1.0 / mi) + EPSILON)
    branch[...] = (gated[...] * rate * vec_ref[V_GS : V_GS + 1, :mi]).astype(BF)
    save(branch, s_ssm)

    wait(3)

    def out_tile(t, carry):
        cols = lanes(t)
        hidden_ref[:, cols] = (
            x_ref[:, cols].astype(F32)
            + dot(branch[...], wout[:mi, cols])
            + dot(mixed_all[...], wout[mi:, cols])
        )
        return carry

    lax.fori_loop(0, wout.shape[1] // TILE, out_tile, 0, unroll=True)
    save(hidden_ref, s_hidden)
    save(x_ref, s_x)
    yield
    finish()


def mixer_forward_scratch(length, width, widths, total):
    ci, mi, qw, kw, heads = widths
    return [
        pltpu.VMEM((width, total), BF),
        pltpu.VMEM((mi + qw, width), BF),
        pltpu.VMEM((length, width), BF),
        pltpu.VMEM((length, ci), BF),
        pltpu.VMEM((length, ci), BF),
        pltpu.VMEM((length, ci), BF),
        pltpu.VMEM((length, mi), BF),
        pltpu.VMEM((length, qw + 2 * kw), BF),
        pltpu.VMEM((length, HALF), F32),
        pltpu.VMEM((qw // HD * length, length), BF),
        pltpu.VMEM((length, mi), BF),
        pltpu.VMEM((length, qw), BF),
        pltpu.VMEM((length, mi), BF),
        pltpu.VMEM((length, mi), F32),
        pltpu.VMEM((length, heads * HALF), F32),
        pltpu.VMEM((length, HALF), F32),
        pltpu.VMEM((length, 2 * HALF), BF),
        pltpu.VMEM((length, 2 * HALF), BF),
        pltpu.SemaphoreType.DMA((32,)),
        pltpu.SemaphoreType.DMA((12,)),
    ]


def mixer_forward_call(
    index, slot, spots, x, vec, cosine, sine, turn, weights, stacks, widths, total
):
    ci, mi, qw, kw, heads = widths
    length, width = x.shape
    scratch = mixer_forward_scratch(length, width, widths, total)
    return call(
        functools.partial(mix_forward, widths),
        "mixer_forward",
        [index, slot],
        spots,
        [x, vec, cosine, sine, turn],
        weights,
        [],
        stacks,
        jax.ShapeDtypeStruct((length, width), F32),
        scratch,
        44,
        200,
    )


def mlp_forward(scalars, spots, ordinary, weights, reads, stacks, low_ref, scratch):
    index_ref, slot_ref = scalars
    base = 4 * index_ref[0]
    hidden_ref, vec_ref = ordinary
    w_g, w_u, w_down = weights
    wgu, wdown, normed, gate_low, up_low, act, final, in_sem, out_sem = scratch
    s_normed, s_gate, s_up, s_act, s_final, s_low = stacks
    ff = wdown.shape[0]
    parts = 2
    step = ff // parts
    groups = []
    for i in range(parts):
        a = slice(i * step, (i + 1) * step)
        b = slice(ff + i * step, ff + (i + 1) * step)
        groups.append(
            row_pieces(w_g, spots, wgu, [(a, a)]) + row_pieces(w_u, spots, wgu, [(a, b)])
        )
    groups.append(row_pieces(w_down, spots, wdown, [(slice(0, wdown.shape[1]),) * 2]))
    wait = start_all(groups, in_sem)
    save, finish = saver(slot_ref[base], slot_ref[base + 1] > 0, out_sem)
    yield
    valid = jnp.where(iota((hidden_ref.shape[0], 1), 0) < slot_ref[base + 2], 1.0, 0.0)

    hidden = hidden_ref[...]
    rate = lax.rsqrt(jnp.mean(hidden * hidden, axis=-1, keepdims=True) + EPSILON)
    normed[...] = (hidden * rate * vec_ref[V_G2 : V_G2 + 1, : hidden.shape[1]]).astype(BF)
    save(normed, s_normed)
    for i in range(parts):
        wait(i)

        def up_tile(t, carry):
            a = pl.ds(pl.multiple_of(i * step + t * TILE, TILE), TILE)
            b = pl.ds(pl.multiple_of(ff + i * step + t * TILE, TILE), TILE)
            gate = dot(normed[...], wgu[:, a])
            up = dot(normed[...], wgu[:, b])
            gate_low[:, a] = gate.astype(BF)
            up_low[:, a] = up.astype(BF)
            act[:, a] = (gate * sigmoid(gate) * up).astype(BF)
            return carry

        lax.fori_loop(0, step // TILE, up_tile, 0, unroll=True)
    save(gate_low, s_gate)
    save(up_low, s_up)
    save(act, s_act)
    wait(parts)

    def down_tile(t, carry):
        cols = lanes(t)
        out = (hidden_ref[:, cols] + dot(act[...], wdown[:, cols])) * valid
        final[:, cols] = out
        low_ref[:, cols] = out.astype(BF)
        return carry

    lax.fori_loop(0, wdown.shape[1] // TILE, down_tile, 0, unroll=True)
    save(final, s_final)
    save(low_ref, s_low, slot_ref[base + 3])
    yield
    finish()


def mlp_forward_scratch(length, width, ff):
    return [
        pltpu.VMEM((width, 2 * ff), BF),
        pltpu.VMEM((ff, width), BF),
        pltpu.VMEM((length, width), BF),
        pltpu.VMEM((length, ff), BF),
        pltpu.VMEM((length, ff), BF),
        pltpu.VMEM((length, ff), BF),
        pltpu.VMEM((length, width), F32),
        pltpu.SemaphoreType.DMA((32,)),
        pltpu.SemaphoreType.DMA((6,)),
    ]


def mlp_forward_call(index, slot, spots, hidden, vec, weights, stacks, ff):
    length, width = hidden.shape
    scratch = mlp_forward_scratch(length, width, ff)
    return call(
        mlp_forward,
        "mlp_forward",
        [index, slot],
        spots,
        [hidden, vec],
        weights,
        [],
        stacks,
        jax.ShapeDtypeStruct((length, width), BF),
        scratch,
        32,
        3,
    )


def mlp_backward(scalars, spots, ordinary, weights, reads, stacks, d_hidden_ref, scratch):
    index_ref, slot_ref, mix_ref = scalars
    base = 4 * index_ref[0]
    target_ref, vec_ref, _ = ordinary
    w_g, w_u, w_down = weights
    s_final, s_hidden, s_gate, s_up = reads
    (wgu, wdown, final, hidden, gate_low, up_low, d_mlp, d_gu, d_sum, d_normed, small, in_sem,
     out_sem) = scratch
    s_dmlp, s_dgate, s_dup, s_small = stacks
    slot = slot_ref[base]
    ff = wdown.shape[0]
    wait = start_all(
        [
            [(s_final.at[slot], final)],
            [(s_gate.at[slot], gate_low), (s_up.at[slot], up_low)]
            + row_pieces(w_down, spots, wdown, [(slice(0, wdown.shape[1]),) * 2]),
            row_pieces(w_g, spots, wgu, [(slice(0, ff), slice(0, ff))])
            + row_pieces(w_u, spots, wgu, [(slice(0, ff), slice(ff, 2 * ff))]),
            [(s_hidden.at[slot], hidden)],
        ],
        in_sem,
    )
    save, finish = saver(slot, slot_ref[base + 1] > 0, out_sem)
    yield
    wait(0)
    target = target_ref[...].astype(F32)
    valid = jnp.where(iota((target_ref.shape[0], 1), 0) < slot_ref[base + 2], 1.0, 0.0)
    misfit = final[...] - target
    loss = jnp.sum(valid * misfit * misfit, axis=0, keepdims=True)
    seed = valid * jnp.where(mix_ref[0] > 0.5, target, mix_ref[1] * misfit)
    d_sum[...] = seed
    d_mlp[...] = seed.astype(BF)
    save(d_mlp, s_dmlp)
    wait(1)

    def act_tile(t, carry):
        a = lanes(t)
        b = pl.ds(pl.multiple_of(ff + t * TILE, TILE), TILE)
        d_act = dot_nt(d_mlp[...], wdown[a, :])
        gate, up = gate_low[:, a].astype(F32), up_low[:, a].astype(F32)
        s = sigmoid(gate)
        swish = gate * s
        d_gu[:, a] = (d_act * up * (s + swish - swish * s)).astype(BF)
        d_gu[:, b] = (d_act * swish).astype(BF)
        return carry

    lax.fori_loop(0, ff // TILE, act_tile, 0, unroll=True)
    save(d_gu.at[:, :ff], s_dgate)
    save(d_gu.at[:, ff:], s_dup)
    wait(2)
    yield

    def back_tile(t, carry):
        rows = lanes(t)
        d_normed[:, rows] = dot_nt(d_gu[...], wgu[rows, :])
        return carry

    lax.fori_loop(0, wgu.shape[0] // TILE, back_tile, 0, unroll=True)
    wait(3)
    h = hidden[...]
    width = h.shape[1]
    rate = lax.rsqrt(jnp.mean(h * h, axis=-1, keepdims=True) + EPSILON)
    unit = h * rate
    d_n = d_normed[...]
    small[...] = jnp.zeros_like(small)
    small[0:1, :width] = jnp.sum(d_n * unit, axis=0, keepdims=True)
    small[1:2, :width] = loss
    save(small, s_small)
    d_n = d_n * vec_ref[V_G2 : V_G2 + 1, :width]
    d_hidden_ref[...] = d_sum[...] + rate * (
        d_n - unit * jnp.mean(d_n * unit, axis=-1, keepdims=True)
    )
    yield
    finish()


def mlp_backward_scratch(length, width, ff, small):
    return [
        pltpu.VMEM((width, 2 * ff), BF),
        pltpu.VMEM((ff, width), BF),
        pltpu.VMEM((length, width), F32),
        pltpu.VMEM((length, width), F32),
        pltpu.VMEM((length, ff), BF),
        pltpu.VMEM((length, ff), BF),
        pltpu.VMEM((length, width), BF),
        pltpu.VMEM((length, 2 * ff), BF),
        pltpu.VMEM((length, width), F32),
        pltpu.VMEM((length, width), F32),
        pltpu.VMEM(small, F32),
        pltpu.SemaphoreType.DMA((32,)),
        pltpu.SemaphoreType.DMA((4,)),
    ]


def mlp_backward_call(index, slot, mix, spots, target, vec, turn, weights, reads, stacks, ff):
    length, width = target.shape
    scratch = mlp_backward_scratch(length, width, ff, stacks[-1].shape[1:])
    return call(
        mlp_backward,
        "mlp_backward",
        [index, slot, mix],
        spots,
        [target, vec, turn],
        weights,
        reads,
        stacks,
        jax.ShapeDtypeStruct((length, width), F32),
        scratch,
        40,
        3,
    )


def column_sum(v):
    return jnp.sum(v, axis=0, keepdims=True)


def mix_backward(
    widths, scalars, spots, ordinary, weights, reads, stacks, d_input_ref, scratch
):
    ci, mi, qw, kw, heads = widths
    index_ref, slot_ref = scalars
    base = 4 * index_ref[0]
    d_hidden_ref, vec_ref, cos_ref, sin_ref, _ = ordinary
    w_first, w_conv, w_gate, w_out = weights
    s_conv, s_z, s_gate, s_qkv, s_step, s_probs, s_y, s_x = reads
    (win, wout, conv_raw, z, gate_raw, qkv, step_raw, probs, y, x_low, d_branch, d_proj, d_mixed,
     d_ssm, d_z, d_normed, run_wide, run_row, step_two, bend_two, tops, d_tops, run_acc, step_acc,
     small, in_sem, out_sem) = scratch
    s_dbranch, s_dfirst, s_dconv, s_dgate, s_dinput, s_small = stacks
    slot = slot_ref[base]
    g0, q0 = ci, ci + mi
    s0 = q0 + qw + 2 * kw
    total = win.shape[1]
    tail = total - q0
    length, width = d_hidden_ref.shape
    wait = start_all(
        [
            out_pieces(w_out, spots, wout, mi),
            [(s_probs.at[slot], probs), (s_qkv.at[slot], qkv)],
            [(s_step.at[slot], step_raw), (s_gate.at[slot], gate_raw), (s_y.at[slot], y)],
            [(s_z.at[slot], z)],
            [(s_conv.at[slot], conv_raw)],
            row_pieces(w_first, spots, win, [(slice(0, tail), slice(q0, total))])
            + row_pieces(w_conv, spots, win, [(slice(0, ci), slice(0, ci))])
            + row_pieces(w_gate, spots, win, [(slice(0, mi), slice(g0, q0))]),
            [(s_x.at[slot], x_low)],
        ],
        in_sem,
    )
    save, finish = saver(slot, slot_ref[base + 1] > 0, out_sem)
    yield
    small[...] = jnp.zeros_like(small)
    d_branch[...] = d_hidden_ref[...].astype(BF)
    save(d_branch, s_dbranch)
    wait(0)
    for t in range(qw // TILE):
        rows = slice(mi + t * TILE, mi + (t + 1) * TILE)
        d_mixed[:, t * TILE : (t + 1) * TILE] = dot_nt(d_branch[...], wout[rows, :]).astype(BF)

    lane_first = jnp.bitwise_and(iota((length, HALF), 1), HD - 1) < HD // 2
    half_low = iota((length, HALF), 1) < HD
    cosine, sine = cos_ref[...], -sin_ref[...]
    wait(1)
    keys, values = qkv[:, qw : qw + kw], qkv[:, qw + kw : qw + 2 * kw]
    keys_far, values_far = pltpu.roll(keys.astype(F32), HD, 1).astype(BF), pltpu.roll(
        values.astype(F32), HD, 1
    ).astype(BF)
    pairs = qw // HALF
    groups = kw // HD
    scale = HD ** (-0.5)
    d_keys = [jnp.zeros((length, HALF), F32) for _ in range(groups)]
    d_values = [jnp.zeros((length, HALF), F32) for _ in range(groups)]
    for pair in range(pairs):
        group = pair // (pairs // groups)
        keep = half_low if group == 0 else jnp.logical_not(half_low)
        keys_two = jnp.where(keep, keys, keys_far)
        values_two = jnp.where(keep, values, values_far)
        cols = slice(pair * HALF, (pair + 1) * HALF)
        query, d_out = qkv[:, cols], d_mixed[:, cols]
        results = []
        for side in range(2):
            own = half_low if side == 0 else jnp.logical_not(half_low)
            q = jnp.where(own, query, jnp.zeros_like(query))
            d_o = jnp.where(own, d_out, jnp.zeros_like(d_out))
            at = (2 * pair + side) * length
            weights = probs[at : at + length, :]
            wide = weights.astype(F32)
            d_weights = dot_nt(d_o, values_two)
            inner = wide * d_weights
            d_scores = (inner - wide * jnp.sum(inner, axis=-1, keepdims=True)).astype(BF)
            results.append(dot(d_scores, keys_two))
            d_keys[group] = d_keys[group] + dot_tn(d_scores, q)
            d_values[group] = d_values[group] + dot_tn(weights, d_o)
        d_q = jnp.where(half_low, results[0], results[1]) * scale
        d_proj[:, q0 + pair * HALF : q0 + (pair + 1) * HALF] = rope(
            d_q, cosine, sine, lane_first
        ).astype(BF)
    folded = [v + pltpu.roll(v, HD, 1) for v in d_keys]
    d_k = jnp.where(half_low, folded[0], folded[1]) * scale
    d_proj[:, q0 + qw : q0 + qw + kw] = rope(d_k, cosine, sine, lane_first).astype(BF)
    folded = [v + pltpu.roll(v, HD, 1) for v in d_values]
    d_proj[:, q0 + qw + kw : s0] = jnp.where(half_low, folded[0], folded[1]).astype(BF)

    wait(2)

    def norm_tile(t, sums):
        cols = lanes(t)
        d_s = dot_nt(d_branch[...], wout[cols, :])
        d_ssm[:, cols] = d_s
        g = gate_raw[:, cols].astype(F32)
        gated = y[:, cols].astype(F32) * (g * sigmoid(g))
        d_n = d_s * vec_ref[V_GS : V_GS + 1, cols]
        return (
            sums[0] + jnp.sum(gated * gated, axis=-1, keepdims=True),
            sums[1] + jnp.sum(gated * d_n, axis=-1, keepdims=True),
        )

    zero_col = jnp.zeros((length, 1), F32)
    squares, along = lax.fori_loop(0, mi // TILE, norm_tile, (zero_col, zero_col), unroll=True)
    rate = lax.rsqrt(squares * (1.0 / mi) + EPSILON)
    along = along * (rate * rate) * (1.0 / mi)

    pre, step, change, run, bend = scan_terms(step_raw[...], vec_ref, heads)
    turned = run.T
    run_row[:HALF, :] = turned[:, :HALF]
    run_row[HALF:, :] = turned[:, HALF:]
    broadcast_runs(run, run_wide, heads)
    step_two[...] = both(step)
    bend_two[...] = both(bend)
    wait(3)
    zb = z[:, mi : mi + 2 * HALF].astype(F32)
    sb = sigmoid(zb)
    bc = (zb * sb).astype(BF)
    b_in, c_in = bc[:, :HALF], bc[:, HALF:]
    causal = iota((HALF, HALF), 1) <= iota((HALF, HALF), 0)
    for c in range(2):
        rows = slice(c * HALF, (c + 1) * HALF)
        tops[rows, :] = jnp.where(causal, dot_nt(c_in[rows], b_in[rows]), 0.0)
    cross = dot_nt(c_in[HALF:], b_in[:HALF])
    cross_turned = cross.T.astype(BF)
    cross = cross.astype(BF)
    pair_low = iota((HALF, HALF), 1) < HD
    d_tops[...] = jnp.zeros_like(d_tops)
    run_acc[...] = jnp.zeros_like(run_acc)
    step_acc[...] = jnp.zeros_like(step_acc)

    def mix_tile(t, carry):
        cols = lanes(t)
        g = gate_raw[:, cols].astype(F32)
        s = sigmoid(g)
        swish = g * s
        y_in = y[:, cols].astype(F32)
        gated = y_in * swish
        d_s = d_ssm[:, cols]
        small[V_GS : V_GS + 1, cols] = column_sum(d_s * gated * rate)
        d_gated = rate * (d_s * vec_ref[V_GS : V_GS + 1, cols]) - gated * (along * rate)
        d_proj[:, pl.ds(pl.multiple_of(g0 + t * TILE, TILE), TILE)] = (
            d_gated * y_in * (s + swish - swish * s)
        ).astype(BF)
        d_y = d_gated * swish
        z_in = z[:, cols].astype(F32)
        s = sigmoid(z_in)
        x_in = z_in * s
        slope = s + x_in - x_in * s
        spread = expand_matrix(t)
        steps = dot(step_two[...], spread)
        bends = dot(bend_two[...], spread)
        scaled = (steps * x_in).astype(BF)
        d_low = d_y.astype(BF)
        u = (bends[:HALF] * scaled[:HALF].astype(F32)).astype(BF)
        v = (bends[HALF:] * d_y[HALF:]).astype(BF)
        far = dot(cross, u)
        back = dot(cross_turned, v)
        d_tops[2 * HALF :, :] += dot_nt(v, u)
        mixed_parts, back_parts = [], []
        for p in range(TILE // HALF):
            mixed_block, back_block = [], []
            for c in range(2):
                rows = slice(c * HALF, (c + 1) * HALF)
                xs = scaled[rows, p * HALF : (p + 1) * HALF]
                dy = d_low[rows, p * HALF : (p + 1) * HALF]
                zero = jnp.zeros_like(xs)
                xs_two = [jnp.where(pair_low, xs, zero), jnp.where(pair_low, zero, xs)]
                dy_two = [jnp.where(pair_low, dy, zero), jnp.where(pair_low, zero, dy)]
                weights = []
                d_top = jnp.zeros((HALF, HALF), F32)
                for side in range(2):
                    h = t * (TILE // HD) + 2 * p + side
                    wide = run_wide[rows, lanes(h, HALF)]
                    line = run_row[pl.ds(c * HALF + h, 1), :]
                    decay = jnp.exp(jnp.minimum(wide - line, 0.0))
                    weights.append((decay * tops[rows, :]).astype(BF))
                    d_top = d_top + decay * dot_nt(dy_two[side], xs)
                d_tops[rows, :] += d_top
                mixed_block.append(
                    dot(jnp.concatenate(weights, axis=1), jnp.concatenate(xs_two, axis=0))
                )
                back_block.append(
                    dot_tn(jnp.concatenate(weights, axis=0), jnp.concatenate(dy_two, axis=0))
                )
            mixed_parts.append(jnp.concatenate(mixed_block, axis=0))
            back_parts.append(jnp.concatenate(back_block, axis=0))
        mixed = jnp.concatenate(mixed_parts, axis=1)
        d_scaled = jnp.concatenate(back_parts, axis=1)
        crossing = jnp.concatenate(
            [-(u.astype(F32) * back), v.astype(F32) * far], axis=0
        )
        runs = d_low.astype(F32) * mixed - scaled.astype(F32) * d_scaled + crossing
        d_scaled = d_scaled + jnp.concatenate([bends[:HALF] * back, jnp.zeros_like(back)], axis=0)
        gather = reduce_matrix(t)
        run_acc[...] += sum(dot(part, gather) for part in split2(runs))
        step_acc[...] += sum(dot(part, gather) for part in split2(x_in * d_scaled))
        small[V_SKIP : V_SKIP + 1, cols] = column_sum(d_y * x_in)
        d_x = steps * d_scaled + vec_ref[V_SKIP : V_SKIP + 1, cols] * d_y
        d_z[:, cols] = d_x * slope
        return carry

    lax.fori_loop(0, mi // TILE, mix_tile, 0, unroll=True)
    d_top = [
        jnp.where(causal, d_tops[c * HALF : (c + 1) * HALF, :], 0.0).astype(BF) for c in range(2)
    ]
    d_cross = d_tops[2 * HALF :, :].astype(BF)
    d_c = jnp.concatenate(
        [dot(d_top[0], b_in[:HALF]), dot(d_cross, b_in[:HALF]) + dot(d_top[1], b_in[HALF:])], axis=0
    )
    d_b = jnp.concatenate(
        [dot_tn(d_top[0], c_in[:HALF]) + dot_tn(d_cross, c_in[HALF:]), dot_tn(d_top[1], c_in[HALF:])],
        axis=0,
    )
    xb = zb * sb
    d_z[:, mi : mi + 2 * HALF] = jnp.concatenate([d_b, d_c], axis=1) * (sb + xb - xb * sb)
    upper = jnp.where(
        iota((length, length), 0) <= iota((length, length), 1), 1.0, 0.0
    ).astype(BF)
    d_change = sum(dot(upper, part) for part in split3(run_acc[...]))
    d_pre = (step_acc[...] + d_change * vec_ref[V_DECAY : V_DECAY + 1, :HALF]) * sigmoid(pre)
    d_pre = jnp.where(iota(d_pre.shape, 1) < heads, d_pre, 0.0)
    d_proj[:, s0:total] = d_pre.astype(BF)
    small[V_SBIAS : V_SBIAS + 1, :HALF] = column_sum(d_pre)
    small[V_DECAY : V_DECAY + 1, :HALF] = column_sum(d_change * change)

    wait(4)
    row = iota((length, TILE), 0)

    def conv_tile(t, carry):
        cols = lanes(t)
        d = d_z[:, cols]
        raw = conv_raw[:, cols].astype(F32)
        small[V_CBIAS : V_CBIAS + 1, cols] = column_sum(d)
        small[3:4, cols] = column_sum(d * raw)
        out = d * vec_ref[3:4, cols]
        for ahead in range(1, 4):
            moved = jnp.where(row < length - ahead, pltpu.roll(d, length - ahead, 0), 0.0)
            small[3 - ahead : 4 - ahead, cols] = column_sum(moved * raw)
            out = out + moved * vec_ref[3 - ahead : 4 - ahead, cols]
        d_proj[:, cols] = out.astype(BF)
        return carry

    lax.fori_loop(0, ci // TILE, conv_tile, 0, unroll=True)
    save(d_proj.at[:, q0:], s_dfirst)
    save(d_proj.at[:, :ci], s_dconv)
    save(d_proj.at[:, g0:q0], s_dgate)

    wait(5)

    def back_tile(t, carry):
        rows = lanes(t)
        d_normed[:, rows] = dot_nt(d_proj[...], win[rows, :])
        return carry

    lax.fori_loop(0, width // TILE, back_tile, 0, unroll=True)
    wait(6)
    x = x_low[...].astype(F32)
    rate_one = lax.rsqrt(jnp.mean(x * x, axis=-1, keepdims=True) + EPSILON)
    unit = x * rate_one
    d_n = d_normed[...]
    small[V_G1 : V_G1 + 1, :width] = column_sum(d_n * unit)
    save(small, s_small)
    d_n = d_n * vec_ref[V_G1 : V_G1 + 1, :width]
    d_input_ref[...] = (
        d_hidden_ref[...]
        + rate_one * (d_n - unit * jnp.mean(d_n * unit, axis=-1, keepdims=True))
    ).astype(BF)
    save(d_input_ref, s_dinput, slot_ref[base + 3])
    yield
    finish()


def mixer_backward_scratch(length, width, widths, total, small):
    ci, mi, qw, kw, heads = widths
    return [
        pltpu.VMEM((width, total), BF),
        pltpu.VMEM((mi + qw, width), BF),
        pltpu.VMEM((length, ci), BF),
        pltpu.VMEM((length, ci), BF),
        pltpu.VMEM((length, mi), BF),
        pltpu.VMEM((length, qw + 2 * kw), BF),
        pltpu.VMEM((length, HALF), F32),
        pltpu.VMEM((qw // HD * length, length), BF),
        pltpu.VMEM((length, mi), BF),
        pltpu.VMEM((length, width), BF),
        pltpu.VMEM((length, width), BF),
        pltpu.VMEM((length, total), BF),
        pltpu.VMEM((length, qw), BF),
        pltpu.VMEM((length, mi), F32),
        pltpu.VMEM((length, ci), F32),
        pltpu.VMEM((length, width), F32),
        pltpu.VMEM((length, heads * HALF), F32),
        pltpu.VMEM((length, HALF), F32),
        pltpu.VMEM((length, 2 * HALF), BF),
        pltpu.VMEM((length, 2 * HALF), BF),
        pltpu.VMEM((2 * HALF, HALF), F32),
        pltpu.VMEM((3 * HALF, HALF), F32),
        pltpu.VMEM((length, HALF), F32),
        pltpu.VMEM((length, HALF), F32),
        pltpu.VMEM(small, F32),
        pltpu.SemaphoreType.DMA((48,)),
        pltpu.SemaphoreType.DMA((6,)),
    ]


def mixer_backward_call(
    index, slot, spots, d_hidden, vec, cosine, sine, turn, weights, reads, stacks, widths, total
):
    ci, mi, qw, kw, heads = widths
    length, width = d_hidden.shape
    scratch = mixer_backward_scratch(length, width, widths, total, stacks[-1].shape[1:])
    return call(
        functools.partial(mix_backward, widths),
        "mixer_backward",
        [index, slot],
        spots,
        [d_hidden, vec, cosine, sine, turn],
        weights,
        reads,
        stacks,
        jax.ShapeDtypeStruct((length, width), BF),
        scratch,
        48,
        250,
    )


def weight_kernel(core_ref, away_ref, stay_ref, right_ref, out_away, out_stay, turned):
    rows = away_ref.shape[2]
    tokens = away_ref.shape[0] * away_ref.shape[1]

    @pl.when(pl.program_id(1) == 0)
    def _():
        turned[:rows, :] = away_ref[...].reshape(tokens, rows).T
        turned[rows:, :] = stay_ref[...].reshape(tokens, rows).T

    right = right_ref[...].reshape(tokens, right_ref.shape[2])
    out_away[0] = dot(turned[:rows, :], right).astype(BF)
    out_stay[0] = dot(turned[rows:, :], right).astype(BF)


def weight_grad_halves(core, left, right):
    count, length, depth = left.shape
    columns = right.shape[2]
    rows = depth // 4
    tile = max(t for t in (896, 768, 512, 256, 128) if columns % t == 0)
    grid = pltpu.PrefetchScalarGridSpec(
        num_scalar_prefetch=1,
        grid=(2, columns // tile),
        in_specs=[
            pl.BlockSpec((count, length, rows), lambda c, n, core: (0, 0, 2 * c + 1 - core[0])),
            pl.BlockSpec((count, length, rows), lambda c, n, core: (0, 0, 2 * c + core[0])),
            pl.BlockSpec((count, length, tile), lambda c, n, core: (0, 0, n)),
        ],
        out_specs=[pl.BlockSpec((1, rows, tile), lambda c, n, core: (c, 0, n))] * 2,
        scratch_shapes=[pltpu.VMEM((2 * rows, count * length), BF)],
    )
    shape = jax.ShapeDtypeStruct((2, rows, columns), BF)
    return pl.pallas_call(
        weight_kernel,
        out_shape=[shape, shape],
        grid_spec=grid,
        compiler_params=pltpu.CompilerParams(vmem_limit_bytes=40 * 1024 * 1024),
        cost_estimate=pl.CostEstimate(
            flops=100000000, bytes_accessed=1000000, transcendentals=0
        ),
        name="weight_gradient",
    )(core, left, left, right)


def layer_forward_call(
    index, slot, spots, x, vec, cosine, sine, turn, weights, stacks, widths, total, ff
):
    length, width = x.shape
    first = mixer_forward_scratch(length, width, widths, total)
    second = mlp_forward_scratch(length, width, ff)
    n = 12

    def body(scalars, spots, ordinary, weights, reads, stacks, low_ref, scratch):
        hidden = scratch[-1]
        one = mix_forward(
            widths, scalars, spots, ordinary, weights[:4], [], stacks[:n], hidden,
            scratch[: len(first)],
        )
        two = mlp_forward(
            scalars, spots, [hidden, ordinary[1]], weights[4:], [], stacks[n:], low_ref,
            scratch[len(first) : -1],
        )
        for part in (one, one, two, one, two, one, two):
            next(part, None)
        yield

    return call(
        body,
        "layer_forward",
        [index, slot],
        spots,
        [x, vec, cosine, sine, turn],
        weights,
        [],
        stacks,
        jax.ShapeDtypeStruct((length, width), BF),
        first + second + [pltpu.VMEM((length, width), F32)],
        58,
        200,
    )


def layer_backward_call(
    index, slot, mix, spots, target, vec, cosine, sine, turn, weights, reads, stacks, widths, total, ff
):
    length, width = target.shape
    first = mlp_backward_scratch(length, width, ff, stacks[3].shape[1:])
    second = mixer_backward_scratch(length, width, widths, total, stacks[-1].shape[1:])
    n = 4

    def body(scalars, spots, ordinary, weights, reads, stacks, d_input_ref, scratch):
        d_hidden = scratch[-1]
        target_ref, vec_ref, cos_ref, sin_ref, turn_ref = ordinary
        one = mlp_backward(
            scalars, spots, [target_ref, vec_ref, turn_ref], weights[4:], reads[:4],
            stacks[:n], d_hidden, scratch[: len(first)],
        )
        two = mix_backward(
            widths, scalars[:2], spots, [d_hidden, vec_ref, cos_ref, sin_ref, turn_ref],
            weights[:4], reads[4:], stacks[n:], d_input_ref, scratch[len(first) : -1],
        )
        for part in (one, one, two, one, two, one, two):
            next(part, None)
        yield

    return call(
        body,
        "layer_backward",
        [index, slot, mix],
        spots,
        [target, vec, cosine, sine, turn],
        weights,
        reads,
        stacks,
        jax.ShapeDtypeStruct((length, width), BF),
        first + second + [pltpu.VMEM((length, width), F32)],
        60,
        250,
    )


def rope_tables(length):
    halves = HD // 2
    inverse = jnp.exp(jnp.arange(halves, dtype=F32) * (-2.0 * math.log(ROPE_BASE) / HD))
    angles = jnp.arange(length, dtype=F32)[:, None] * inverse[None, :]
    cosine, sine = jnp.cos(angles), jnp.sin(angles)
    return (
        jnp.concatenate([cosine] * 4, axis=1),
        jnp.concatenate([-sine, sine, -sine, sine], axis=1),
    )


def swap(block, axis, bit):
    return lax.ppermute(block, axis, [(i, i ^ bit) for i in range(lax.axis_size(axis))])


def after(value, *others):
    if not others:
        return value
    return lax.optimization_barrier((value,) + others)[0]


def corner(made):
    part = made.reshape(-1, made.shape[-1])[:8, :HALF].astype(BF)
    return jnp.dot(part, jnp.ones((HALF, HALF), BF), preferred_element_type=F32)


def quick_links():
    return lax.axis_size("fsdp") == 4 and lax.axis_size("rep") == 4


def gather_halves(shard, axis, before_y=(), before_z=()):
    parity = lax.axis_index("rep") % 2
    half = shard.shape[axis] // 2
    mine = lax.dynamic_slice_in_dim(shard, parity * half, half, axis)
    near = swap(shard, "fsdp", 1)
    far_one = swap(after(mine, *before_y), "fsdp", 2)
    far_two = swap(after(far_one, *before_z), "rep", 1)
    return [shard, near, far_one, far_two, swap(far_one, "fsdp", 1), swap(far_two, "fsdp", 1)]


def gather_wholes(shard, *before_y):
    far = swap(after(shard, *before_y), "fsdp", 2)
    return [shard, swap(shard, "fsdp", 1), far, swap(far, "fsdp", 1)]


def plus(a, b):
    return (a.astype(F32) + b.astype(F32)).astype(BF)


def weight_grad(left, right):
    return lax.dot_general(
        left, right, (((0, 1), (0, 1)), ((), ())), preferred_element_type=F32
    ).astype(BF)


class Reduction:
    def __init__(self, left, right, riders=None):
        self.left, self.right, self.riders = left, right, riders

    def begin(self, order):
        left, right = order(self.left, self.right)
        core = lax.axis_index("fsdp") % 2
        away, stay = weight_grad_halves(core.astype(jnp.int32)[None], left, right)
        if self.riders is not None:
            blocks, column = self.riders
            away, stay = (
                lax.dynamic_update_slice(
                    grad, lax.dynamic_index_in_dim(blocks, i, 1, keepdims=False), (0, 0, column)
                )
                for grad, i in ((away, 1 - core), (stay, core))
            )
        self.stay = stay
        self.moved = swap(away, "fsdp", 1)
        return stay

    def chips(self, order):
        chip = lax.axis_index("fsdp") // 2
        self.kept = order(self.stay, self.moved)

        def part(i):
            return [lax.dynamic_index_in_dim(v, i, 0, keepdims=False) for v in self.kept]

        away = plus(*part(1 - chip))
        self.moved = swap(away, "fsdp", 2)
        return away

    def line_in(self, order):
        chip = lax.axis_index("fsdp") // 2
        *kept, moved = order(*self.kept, self.moved)
        one, two = (lax.dynamic_index_in_dim(v, chip, 0, keepdims=False) for v in kept)
        self.stay = (one.astype(F32) + two.astype(F32) + moved.astype(F32)).astype(BF)
        self.moved = lax.ppermute(self.stay, "rep", [(0, 1), (3, 2)])
        return self.stay

    def middle(self, order):
        stay, moved = order(self.stay, self.moved)
        self.stay = plus(stay, moved)
        self.moved = lax.ppermute(self.stay, "rep", [(1, 2), (2, 1)])
        return self.stay

    def line_out(self, order):
        stay, moved = order(self.stay, self.moved)
        self.stay = plus(stay, moved)
        self.moved = lax.ppermute(self.stay, "rep", [(1, 0), (2, 3)])
        return self.stay

    def finish(self, order):
        stay, moved = order(self.stay, self.moved)
        rank = lax.axis_index("rep")
        inner = jnp.logical_or(rank == 1, rank == 2)
        self.result = jnp.where(inner, stay, moved).astype(F32)
        return self.result


def body(
    inputs,
    teacher,
    lengths,
    order,
    loss_scale,
    norm_gain1,
    w_query,
    w_key,
    w_value,
    w_attn_out,
    w_ssm_gate,
    w_conv_in,
    w_step,
    conv_kernel,
    conv_bias,
    step_bias,
    decay_log,
    skip_gain,
    ssm_norm_gain,
    w_ssm_out,
    norm_gain2,
    w_gate,
    w_up,
    w_down,
):
    quick = quick_links()
    n_rep = lax.axis_size("rep")
    n_fsdp = lax.axis_size("fsdp")
    rank = lax.axis_index("rep")
    fsdp = lax.axis_index("fsdp")
    section = lax.axis_index("section")
    first = section == 0
    device = fsdp * n_rep + rank
    count, length, width = inputs.shape
    ci, mi, qw, kw = (w.shape[2] for w in (w_conv_in, w_ssm_gate, w_query, w_key))
    heads = w_step.shape[2]
    ff = w_up.shape[2]
    widths = (ci, mi, qw, kw, heads)
    taps = conv_kernel.shape[1]
    rows = width // n_fsdp
    tail = qw + 2 * kw + HALF
    total = ci + mi + tail

    turns = jnp.arange(count, dtype=jnp.int32)
    numbers = jnp.arange(order.shape[0], dtype=jnp.int32)
    mine = device * count + turns
    sources = jnp.sum(jnp.where(order[None, :] == mine[:, None], numbers[None, :], 0), axis=1)
    target = lax.dynamic_slice_in_dim(order, device * count, count) // count % n_rep
    anchor = sources // count % n_rep

    def inverse(key):
        return jnp.sum(jnp.where((key ^ rank)[None, :] == turns[:, None], turns[None, :], 0), axis=1)

    send_at, keep_at = inverse(target), inverse(anchor)
    own_lengths = jnp.take(lengths, jnp.take(sources, keep_at))
    outgoing = [
        jnp.where(
            first,
            lax.dynamic_index_in_dim(inputs, send_at[j], 0, keepdims=False),
            lax.dynamic_index_in_dim(teacher, send_at[j], 0, keepdims=False),
        )
        for j in range(count)
    ]
    dealt = [outgoing[0]]

    def deal(j, *earlier):
        dealt.append(swap(after(outgoing[j], *earlier), "rep", j))

    for j in range(1, count - 1):
        deal(j)

    def columns(flat):
        wide = -(-flat.size // rows)
        return jnp.pad(flat, (0, wide * rows - flat.size)).reshape(rows, wide)

    convs = jnp.concatenate([conv_kernel[0], conv_bias], axis=0)
    riders = jnp.concatenate(
        [
            norm_gain1[0][:, None],
            norm_gain2[0][:, None],
            columns(convs.reshape(-1)),
            columns(ssm_norm_gain[0]),
        ],
        axis=1,
    )
    used = riders.shape[1]
    wide = -(-convs.size // rows)
    shard_first = jnp.concatenate(
        [w_query[0], w_key[0], w_value[0], w_step[0], riders]
        + [jnp.zeros((rows, HALF - heads - used), BF)],
        axis=1,
    )
    at = qw + 2 * kw + heads
    parity = rank % 2
    if quick:
        g_gate = gather_halves(w_ssm_gate[0], 0, (), dealt[1:2])
        g_conv = gather_halves(w_conv_in[0], 0, (), dealt[2:3])
        g_first = gather_halves(shard_first, 0, g_gate[2:3], g_gate[3:4])
        shard_out = jnp.concatenate([w_ssm_out[0], w_attn_out[0]], axis=0)
        g_out = gather_halves(shard_out, 1, g_conv[2:3], g_conv[3:4])
        g_g = gather_halves(w_gate[0], 0, g_first[2:3], g_first[3:4])
        g_u = gather_wholes(w_up[0], g_out[2], g_g[2])
        spots = [2 * fsdp, 2 * (fsdp ^ 1)]
        spots += [2 * (fsdp ^ k) + b for k in (2, 3) for b in (parity, 1 - parity)]
        spots = jnp.stack(spots).astype(jnp.int32)
        cut = [piece[:, at : at + used] for piece in g_first]
        swapped = [jnp.where(parity == 0, cut[i], cut[i + 1]) for i in (2, 4)]
        swapped2 = [jnp.where(parity == 0, cut[i + 1], cut[i]) for i in (2, 4)]
        blocks = jnp.stack(
            [cut[0], cut[1]]
            + [jnp.concatenate([a, b], axis=0) for a, b in zip(swapped, swapped2)]
        )
        ridden = jnp.take(blocks, jnp.arange(4, dtype=jnp.int32) ^ fsdp, axis=0)
    else:

        def whole(shard):
            return lax.all_gather(shard, "fsdp", axis=0, tiled=True)

        g_first, g_conv, g_gate, g_g, g_u, g_down = (
            [whole(w)]
            for w in (shard_first, w_conv_in[0], w_ssm_gate[0], w_gate[0], w_up[0], w_down[0])
        )
        g_out = [jnp.concatenate([whole(w_ssm_out[0]), whole(w_attn_out[0])], axis=0)]
        spots = jnp.zeros((1,), jnp.int32)
        ridden = g_first[0][:, at : at + used].reshape(n_fsdp, rows, used)
    mixer_weights = [g_first, g_conv, g_gate, g_out]
    mlp_weights = None if quick else [g_g, g_u, g_down]

    conv_all = ridden[:, :, 2 : 2 + wide].reshape(n_fsdp, -1)[:, : (taps + 1) * ci // n_fsdp]
    conv_all = conv_all.reshape(n_fsdp, taps + 1, ci // n_fsdp).transpose(1, 0, 2)
    ssm_gain = ridden[:, :, 2 + wide :].reshape(n_fsdp, -1)[:, : mi // n_fsdp].reshape(1, mi)

    def table_row(v):
        v = v.astype(F32)
        return jnp.pad(v, ((0, 0), (0, ci - v.shape[1])))

    vec = jnp.concatenate(
        [
            table_row(v)
            for v in (
                conv_all.reshape(taps + 1, ci),
                ssm_gain,
                jnp.repeat(skip_gain, HD, axis=1),
                ridden[:, :, 0].reshape(1, width),
                ridden[:, :, 1].reshape(1, width),
                step_bias,
                -jnp.exp(decay_log),
                jnp.zeros((16 - taps - 7, 1), F32),
            )
        ],
        axis=0,
    )
    cosine, sine = rope_tables(length)

    valid_count = jnp.sum(lengths).astype(F32)
    factor = loss_scale / (valid_count * width)

    skew = 2
    steps = count + skew
    ticks = jnp.arange(steps, dtype=jnp.int32)
    raw = jnp.concatenate([ticks - skew * section, count - 1 - ticks + skew * (1 - section)])
    inside = jnp.logical_and(raw >= 0, raw < count).astype(jnp.int32)
    slots = jnp.clip(raw, 0, count - 1)
    plan = [slots, inside, jnp.take(own_lengths, slots), jnp.take(keep_at, slots)]
    plan = jnp.stack(plan, axis=1).reshape(-1)
    mix = jnp.stack([jnp.where(first, 1.0, 0.0), 2.0 * factor])

    def stack(*shape, kind=BF):
        return jax.ShapeDtypeStruct((count,) + shape, kind)

    mix_stacks = [
        stack(length, width),
        stack(length, ci),
        stack(length, ci),
        stack(length, mi),
        stack(length, qw + 2 * kw),
        stack(length, HALF, kind=F32),
        stack(qw // HD * length, length),
        stack(length, mi),
        stack(length, qw),
        stack(length, mi),
        stack(length, width, kind=F32),
        stack(length, width),
    ]
    mlp_stacks = [
        stack(length, width),
        stack(length, ff),
        stack(length, ff),
        stack(length, ff),
        stack(length, width, kind=F32),
        stack(length, width),
    ]

    token = []

    def chained(*values):
        if not quick or not token:
            return values
        return lax.optimization_barrier(values + tuple(token))[: len(values)]

    def chain(made):
        token[:] = [made]

    received, hiddens = [], []

    def number(i):
        return jnp.full((1,), i, jnp.int32)

    def mixer_tick(tick, turn, mix_stacks):
        mix_stacks, hidden = mixer_forward_call(
            number(tick),
            plan,
            spots,
            dealt[tick],
            vec,
            cosine,
            sine,
            corner(turn),
            mixer_weights,
            mix_stacks,
            widths,
            total,
        )
        chain(hidden)
        hiddens.append(hidden)
        return mix_stacks

    def mlp_tick(tick, mlp_stacks):
        (hidden,) = chained(hiddens[tick])
        mlp_stacks, low = mlp_forward_call(
            number(tick), plan, spots, hidden, vec, mlp_weights, mlp_stacks, ff
        )
        return mlp_stacks, low

    def layer_tick(tick, turn, stacks):
        if tick < count:
            one, two = chained(dealt[tick], received[tick - skew])
            seq_in = jnp.where(first, one, two)
        else:
            seq_in = received[tick - skew]
        return layer_forward_call(
            number(tick),
            plan,
            spots,
            seq_in,
            vec,
            cosine,
            sine,
            corner(turn),
            mixer_weights + mlp_weights,
            stacks,
            widths,
            total,
            ff,
        )

    mix_stacks = mixer_tick(0, dealt[0], mix_stacks)
    if quick:
        mlp_weights = [g_g, g_u, gather_wholes(w_down[0], hiddens[0])]
    deal(count - 1, hiddens[0])
    mix_stacks = mixer_tick(1, hiddens[0], mix_stacks)
    for tick in range(steps):
        if tick < skew:
            mlp_stacks, low = mlp_tick(tick, mlp_stacks)
        else:
            stacks, low = layer_tick(tick, low, mix_stacks + mlp_stacks)
            mix_stacks, mlp_stacks = stacks[: len(mix_stacks)], stacks[len(mix_stacks) :]
        chain(low)
        if tick < count:
            received.append(lax.ppermute(low, "section", [(0, 1)]))

    (s_normed, s_conv, s_z, s_gate, s_qkv, s_step, s_probs, s_ssm, s_mixed, s_y, s_hidden,
     s_x) = mix_stacks
    s_normed2, s_g, s_u, s_act, s_final, s_low = mlp_stacks
    mlp_grads = [
        stack(length, width),
        stack(length, ff),
        stack(length, ff),
        stack(8, width, kind=F32),
    ]
    mix_grads = [
        stack(length, width),
        stack(length, tail),
        stack(length, ci),
        stack(length, mi),
        stack(length, width),
        stack(16, ci, kind=F32),
    ]
    incoming, returned = [], [None] * count

    hiddens = []

    def mlp_turn(turn, mlp_grads):
        (seed,) = chained(incoming[turn - skew])
        return mlp_backward_call(
            number(steps + turn),
            plan,
            mix,
            spots,
            seed,
            vec,
            corner(hiddens[-1]) if turn > count else jnp.zeros((8, HALF), F32),
            mlp_weights,
            reads,
            mlp_grads,
            ff,
        )

    def mixer_turn(turn, d_hidden, before, mix_grads):
        mix_grads, d_input = mixer_backward_call(
            number(steps + turn),
            plan,
            spots,
            d_hidden,
            vec,
            cosine,
            sine,
            corner(before),
            mixer_weights,
            mix_reads,
            mix_grads,
            widths,
            total,
        )
        send_back(turn, d_input)
        return mix_grads, d_input

    def send_back(turn, d_input):
        if turn < count:
            incoming.append(lax.ppermute(d_input, "section", [(1, 0)]))
        if turn >= skew:
            j = count - 1 - turn + skew
            back = lax.dynamic_index_in_dim(after(s_low, d_input), keep_at[j], 0, keepdims=False)
            back = jnp.where(first, d_input, back)
            returned[j] = swap(back, "rep", j) if j else back

    reads = [s_final, s_hidden, s_g, s_u]
    mix_reads = [s_conv, s_z, s_gate, s_qkv, s_step, s_probs, s_y, s_x]
    d_input = low
    for turn in range(count):
        if turn < skew:
            (seed,) = chained(dealt[count - 1 - turn])
        else:
            one, two = chained(incoming[turn - skew], dealt[count - 1 - turn])
            seed = jnp.where(first, one, two)
        grads, d_input = layer_backward_call(
            number(steps + turn),
            plan,
            mix,
            spots,
            seed,
            vec,
            cosine,
            sine,
            corner(d_input),
            mixer_weights + mlp_weights,
            reads + mix_reads,
            mlp_grads + mix_grads,
            widths,
            total,
            ff,
        )
        mlp_grads, mix_grads = grads[: len(mlp_grads)], grads[len(mlp_grads) :]
        chain(d_input)
        send_back(turn, d_input)

    for turn in range(count, steps):
        mlp_grads, d_hidden = mlp_turn(turn, mlp_grads)
        chain(d_hidden)
        hiddens.append(d_hidden)
    s_dmlp, s_dg, s_du, small_mlp = mlp_grads
    early = [(s_normed2, s_dg), (s_normed2, s_du), (s_act, s_dmlp)]
    chunks = [Reduction(*pair) for pair in early]

    def stages(*words):
        for word in words:
            chain(getattr(chunks[int(word[1])], names[word[0]])(chained))

    names = dict(W="begin", A="chips", L="line_in", M="middle", O="line_out", F="finish")
    if quick:
        stages("W0", "W1", "W2", "A0", "A1", "A2")
    for turn in range(count, steps):
        d_hidden = hiddens[turn - count]
        before = d_hidden
        if quick:
            before = after(token[0], *returned[2:]) if turn > count else token[0]
        mix_grads, d_input = mixer_turn(turn, d_hidden, before, mix_grads)
        if quick:
            chain(d_input)
            if turn == count:
                stages("L0")
    s_dbranch, s_dfirst, s_dconv, s_dgate, s_dinput, small_mix = mix_grads
    late = [
        (s_normed, s_dconv),
        (s_normed, s_dgate),
        (s_ssm, s_dbranch),
        (s_normed, s_dfirst),
        (s_mixed, s_dbranch),
    ]

    mix_sum = jnp.sum(small_mix, axis=0)
    mlp_sum = jnp.sum(small_mlp, axis=0)
    singles = jnp.concatenate(
        [
            mix_sum[V_SBIAS, :heads],
            mix_sum[V_DECAY, :heads],
            jnp.sum(mix_sum[V_SKIP, :mi].reshape(heads, HD), axis=1),
            jnp.sum(mlp_sum[1])[None],
        ]
    )

    def share(v):
        return v.reshape(v.shape[0], n_fsdp, -1).transpose(1, 0, 2).reshape(n_fsdp, -1)

    shares = [
        share(mix_sum[: taps + 1]),
        share(mix_sum[V_GS : V_GS + 1, :mi]),
        share(mix_sum[V_G1 : V_G1 + 1, :width]),
        share(mlp_sum[:1]),
        jnp.broadcast_to(singles[None], (n_fsdp, singles.size)),
    ]
    cuts = [v.shape[1] for v in shares]
    flat = jnp.concatenate(shares, axis=1)

    if quick:
        spare = -(-flat.shape[1] // rows)
        flat = jnp.pad(flat, ((0, 0), (0, spare * rows - flat.shape[1])))
        riders = flat.astype(BF).reshape(2, 2, rows, spare)
        column = tail - HALF + heads
        chunks += [Reduction(*pair) for pair in late]
        chunks[6].riders = (riders, column)
        stages("L1", "M0", "W3", "W4", "W5", "W6", "W7")
        stages("A3", "L2", "M1", "O0")
        stages("A4", "L3", "M2", "O1", "F0")
        token.append(returned[1])
        stages("A5", "L4", "M3", "O2", "F1")
        stages("A6", "L5", "M4", "O3", "F2")
        stages("A7", "L6", "M5", "O4", "F3")
        stages("L7", "M6", "O5", "F4", "M7", "O6", "F5", "O7", "F6", "F7")
        reduced = [chunk.result for chunk in chunks]
        flat = reduced[6][:, column : column + spare].reshape(-1)
        ends = chained(*returned, s_dinput, s_low)
        returned, s_dinput, s_low = ends[:count], ends[-2], ends[-1]
    else:

        def reduce_all(pair):
            grad = weight_grad(*pair)
            own = lax.psum_scatter(grad, "fsdp", scatter_dimension=0, tiled=True)
            return lax.psum(own, "rep").astype(F32)

        reduced = [reduce_all(pair) for pair in early + late]
        flat = lax.psum(lax.psum_scatter(flat, "fsdp", tiled=True), "rep").reshape(-1)
    grad_gate, grad_up, grad_down, grad_conv, grad_sgate, grad_ssm_out, grad_first, grad_attn = reduced

    parts, begin = [], 0
    for cut in cuts[:-1] + [heads] * 3 + [1]:
        parts.append(flat[begin : begin + cut])
        begin += cut
    convs = parts[0].reshape(taps + 1, -1)
    loss = jnp.where(first, lax.ppermute(parts[-1], "section", [(1, 0)]), parts[-1])[0]

    restored = jnp.zeros((count, length, width), BF)
    for j in range(count):
        restored = lax.dynamic_update_index_in_dim(restored, returned[j], send_at[j], 0)
    activations = jnp.where(first, s_low, restored)[None]
    gradients = jnp.where(first, restored, s_dinput)[None]
    s0 = qw + 2 * kw
    return (
        activations,
        gradients,
        loss / (valid_count * width),
        parts[2][None],
        grad_first[None, :, :qw],
        grad_first[None, :, qw : qw + kw],
        grad_first[None, :, qw + kw : s0],
        grad_attn[None],
        grad_sgate[None],
        grad_conv[None],
        grad_first[None, :, s0 : s0 + heads],
        convs[None, :taps],
        convs[None, taps],
        parts[4][None],
        parts[5][None],
        parts[6][None],
        parts[1][None],
        grad_ssm_out[None],
        parts[3][None],
        grad_gate[None],
        grad_up[None],
        grad_down[None],
    )


def solution(mesh):
    rows3 = P("section", "fsdp", None)
    pair = P("section", "fsdp")
    one = P("section", None)
    data = P(("fsdp", "rep"), None, None)
    taps = P("section", None, "fsdp")
    in_specs = (data, data, P(), P(), P(), pair) + (rows3,) * 7
    in_specs += (taps, pair, one, one, one, pair, rows3, pair, rows3, rows3, rows3)
    placed = P("section", ("fsdp", "rep"), None, None)
    out_specs = (placed, placed, P(), pair) + (rows3,) * 7
    out_specs += (taps, pair, one, one, one, pair, rows3, pair, rows3, rows3, rows3)
    return jax.shard_map(body, mesh=mesh, in_specs=in_specs, out_specs=out_specs, check_vma=False)
```

```python
import math
import functools

import jax
import jax.numpy as jnp
from jax import lax
from jax.experimental import pallas as pl
from jax.experimental.pallas import tpu as pltpu
from jax.sharding import PartitionSpec as P

HD = 64
EPSILON = 1e-05
ROPE_BASE = 100000000000.0
MASKED = -1e30
F32 = jnp.float32
BF = jnp.bfloat16
TILE = 256
HALF = 128
HB = pl.BlockSpec(memory_space=pltpu.HBM)
VM = pl.BlockSpec(memory_space=pltpu.VMEM)
SM = pl.BlockSpec(memory_space=pltpu.SMEM)


def dot(a, b):
    return jnp.dot(a, b, preferred_element_type=F32)


def dot_nt(a, b):
    return lax.dot_general(a, b, (((1,), (1,)), ((), ())), preferred_element_type=F32)


def dot_tn(a, b):
    return lax.dot_general(a, b, (((0,), (0,)), ((), ())), preferred_element_type=F32)


def sigmoid(v):
    return 0.5 * jnp.tanh(0.5 * v) + 0.5


def lanes(i, width=TILE):
    return pl.ds(pl.multiple_of(i * width, width), width)


def iota(shape, axis):
    return lax.broadcasted_iota(jnp.int32, shape, axis)


def split2(v):
    hi = v.astype(BF)
    return hi, (v - hi.astype(F32)).astype(BF)


def split3(v):
    hi = v.astype(BF)
    rest = v - hi.astype(F32)
    mid = rest.astype(BF)
    return hi, mid, (rest - mid.astype(F32)).astype(BF)


def expand_matrix(tile):
    row = jnp.bitwise_and(iota((TILE, TILE), 0), HALF - 1)
    col = jnp.right_shift(iota((TILE, TILE), 1), 6) + tile * (TILE // HD)
    return jnp.where(row == col, 1.0, 0.0).astype(BF)


def reduce_matrix(tile):
    row = jnp.right_shift(iota((TILE, HALF), 0), 6) + tile * (TILE // HD)
    col = iota((TILE, HALF), 1)
    return jnp.where(row == col, 1.0, 0.0).astype(BF)


def both(v):
    return jnp.concatenate(split2(v), axis=1)


def rope(v, cosine, sine, first):
    turned = jnp.where(first, pltpu.roll(v, HALF - HD // 2, 1), pltpu.roll(v, HD // 2, 1))
    return v * cosine + turned * sine


def start_all(groups, sems):
    waits, at = [], 0
    for group in groups:
        copies = []
        for source, target in group:
            copies.append(pltpu.make_async_copy(source, target, sems.at[at]))
            at += 1
        for copy in copies:
            copy.start()
        waits.append(copies)

    def wait(i):
        for copy in waits[i]:
            copy.wait()

    return wait


def row_pieces(pieces, spots, scratch, columns):
    if len(pieces) == 1:
        return [(pieces[0].at[:, a], scratch.at[:, b]) for a, b in columns]
    unit = pieces[-1].shape[0]
    if len(pieces) == 4:
        places = [jnp.right_shift(spots[i], 1) for i in (0, 1, 2, 4)]
    else:
        places = [spots[i] for i in range(6)]
    out = []
    for a, b in columns:
        for place, piece in zip(places, pieces):
            rows = pl.ds(pl.multiple_of(place * unit, unit), piece.shape[0])
            out.append((piece.at[:, a], scratch.at[rows, b]))
    return out


def out_pieces(pieces, spots, scratch, inner):
    if len(pieces) == 1:
        return [(pieces[0], scratch)]
    total, width = scratch.shape
    n = total // pieces[0].shape[0]
    cut, rest = inner // n, (total - inner) // n
    out = []
    for i, piece in enumerate(pieces):
        block, side = jnp.right_shift(spots[i], 1), jnp.bitwise_and(spots[i], 1)
        span = piece.shape[1]
        cols = slice(0, width)
        if span < width:
            cols = pl.ds(pl.multiple_of(side * span, span), span)
        upper = pl.ds(pl.multiple_of(block * cut, cut), cut)
        lower = pl.ds(pl.multiple_of(inner + block * rest, rest), rest)
        out.append((piece.at[:cut, :], scratch.at[upper, cols]))
        out.append((piece.at[cut:, :], scratch.at[lower, cols]))
    return out


def saver(slot, active, sems):
    stores = []

    def save(buffer, stack, at=slot):
        copy = pltpu.make_async_copy(buffer, stack.at[at], sems.at[len(stores)])
        pl.when(active)(copy.start)
        stores.append(copy)

    def finish():
        for copy in stores:
            pl.when(active)(copy.wait)

    return save, finish


def in_hbm(a):
    return pltpu.with_memory_space_constraint(a, pltpu.HBM)


def call(body, name, scalars, spots, ordinary, weights, reads, stacks, result, scratch, limit, work):
    fresh = isinstance(stacks[0], jax.ShapeDtypeStruct)
    flat = [piece for group in weights for piece in group]
    counts = [len(group) for group in weights]
    kept = [] if fresh else list(stacks)
    ahead = len(scalars) + 1 + len(ordinary) + len(flat) + len(reads)
    n = len(stacks)
    cuts = [len(scalars), 1, len(ordinary), len(flat), len(reads), len(kept), n, 1]

    def kernel(*refs):
        parts, at = [], 0
        for cut in cuts:
            parts.append(refs[at : at + cut])
            at += cut
        groups, begin = [], 0
        for c in counts:
            groups.append(parts[3][begin : begin + c])
            begin += c
        for _ in body(
            parts[0], parts[1][0], parts[2], groups, parts[4], parts[6], parts[7][0], refs[at:]
        ):
            pass

    out = pl.pallas_call(
        kernel,
        out_shape=[pltpu.HBM(s.shape, s.dtype) for s in stacks] + [result],
        in_specs=[SM] * (len(scalars) + 1)
        + [VM] * len(ordinary)
        + [HB] * (len(flat) + len(reads) + len(kept)),
        out_specs=[HB] * n + [VM],
        scratch_shapes=scratch,
        input_output_aliases={} if fresh else {ahead + i: i for i in range(n)},
        compiler_params=pltpu.CompilerParams(vmem_limit_bytes=limit * 1024 * 1024),
        cost_estimate=pl.CostEstimate(
            flops=work * 100000000, bytes_accessed=1000000, transcendentals=0
        ),
        name=name,
    )(*scalars, spots, *ordinary, *(in_hbm(a) for a in flat + list(reads) + kept))
    return list(out[:n]), out[n]


V_TAP, V_CBIAS, V_GS, V_SKIP, V_G1, V_G2, V_SBIAS, V_DECAY = 0, 4, 5, 6, 7, 8, 9, 10


def scan_terms(step_raw, vec_ref, heads):
    lane = iota(step_raw.shape, 1)
    pre = step_raw + vec_ref[V_SBIAS : V_SBIAS + 1, :HALF]
    soft = jnp.maximum(pre, 0.0) + jnp.log1p(jnp.exp(-jnp.abs(pre)))
    step = jnp.where(lane < heads, soft, 0.0)
    change = step * vec_ref[V_DECAY : V_DECAY + 1, :HALF]
    length = step.shape[0]
    lower = jnp.where(
        iota((length, length), 0) >= iota((length, length), 1), 1.0, 0.0
    ).astype(BF)
    run = sum(dot(lower, part) for part in split3(change))
    middle = run[HALF - 1 : HALF, :]
    bend = jnp.where(iota(run.shape, 0) < HALF, middle - run, run - middle)
    bend = jnp.exp(jnp.minimum(bend, 0.0))
    return pre, step, change, run, bend


def broadcast_runs(run, run_wide, heads):
    for h in range(heads):
        run_wide[:, h * HALF : (h + 1) * HALF] = jnp.broadcast_to(
            run[:, h : h + 1], (run.shape[0], HALF)
        )


def mix_forward(widths, scalars, spots, ordinary, weights, reads, stacks, hidden_ref, scratch):
    ci, mi, qw, kw, heads = widths
    index_ref, slot_ref = scalars
    base = 4 * index_ref[0]
    x_ref, vec_ref, cos_ref, sin_ref, _ = ordinary
    w_first, w_conv, w_gate, w_out = weights
    (win, wout, normed, conv_raw, z, xbc, gate_raw, qkv, step_raw, probs, branch, mixed_all, y,
     gated, run_wide, run_row, step_two, bend_two, in_sem, out_sem) = scratch
    (s_normed, s_conv, s_z, s_gate, s_qkv, s_step, s_probs, s_ssm, s_mixed, s_y, s_hidden,
     s_x) = stacks
    g0 = ci
    q0 = ci + mi
    total = win.shape[1]
    tail = total - q0
    wait = start_all(
        [
            row_pieces(w_first, spots, win, [(slice(0, tail), slice(q0, total))]),
            row_pieces(w_conv, spots, win, [(slice(0, ci), slice(0, ci))]),
            row_pieces(w_gate, spots, win, [(slice(0, mi), slice(g0, q0))]),
            out_pieces(w_out, spots, wout, mi),
        ],
        in_sem,
    )
    save, finish = saver(slot_ref[base], slot_ref[base + 1] > 0, out_sem)
    yield

    length = x_ref.shape[0]
    x = x_ref[...].astype(F32)
    rate = lax.rsqrt(jnp.mean(x * x, axis=-1, keepdims=True) + EPSILON)
    normed[...] = (x * rate * vec_ref[V_G1 : V_G1 + 1, : x.shape[1]]).astype(BF)
    save(normed, s_normed)
    lane_first = jnp.bitwise_and(iota((length, HALF), 1), HD - 1) < HD // 2
    half_low = iota((length, HALF), 1) < HD

    wait(0)
    cosine, sine = cos_ref[...], sin_ref[...]
    n_rope = (qw + kw) // HALF
    for t in range((total - q0) // HALF // 2):
        raw = dot(normed[...], win[:, q0 + t * TILE : q0 + (t + 1) * TILE])
        for part in range(2):
            c = 2 * t + part
            piece = raw[:, part * HALF : (part + 1) * HALF]
            if c < n_rope:
                piece = rope(piece, cosine, sine, lane_first)
            if c < n_rope + kw // HALF:
                qkv[:, c * HALF : (c + 1) * HALF] = piece.astype(BF)
            else:
                step_raw[...] = piece
    if ((total - q0) // HALF) % 2:
        step_raw[...] = dot(normed[...], win[:, total - HALF : total])
    save(qkv, s_qkv)
    save(step_raw, s_step)

    wait(1)
    row = iota((length, TILE), 0)

    def conv_tile(t, carry):
        cols = lanes(t)
        raw = dot(normed[...], win[:, cols])
        conv_raw[:, cols] = raw.astype(BF)
        total_z = vec_ref[V_CBIAS : V_CBIAS + 1, cols] + raw * vec_ref[3:4, cols]
        for back in range(1, 4):
            moved = jnp.where(row >= back, pltpu.roll(raw, back, 0), 0.0)
            total_z = total_z + moved * vec_ref[3 - back : 4 - back, cols]
        z[:, cols] = total_z.astype(BF)
        xbc[:, cols] = (total_z * sigmoid(total_z)).astype(BF)
        return carry

    lax.fori_loop(0, ci // TILE, conv_tile, 0, unroll=True)
    save(conv_raw, s_conv)
    save(z, s_z)

    wait(2)

    def gate_tile(t, carry):
        raw = dot(normed[...], win[:, pl.ds(pl.multiple_of(g0 + t * TILE, TILE), TILE)])
        gate_raw[:, lanes(t)] = raw.astype(BF)
        return carry

    lax.fori_loop(0, mi // TILE, gate_tile, 0, unroll=True)
    save(gate_raw, s_gate)

    yield

    keys, values = qkv[:, qw : qw + kw], qkv[:, qw + kw : qw + 2 * kw]
    keys_far, values_far = pltpu.roll(keys.astype(F32), HD, 1).astype(BF), pltpu.roll(
        values.astype(F32), HD, 1
    ).astype(BF)
    causal_top = iota((HALF, HALF), 1) <= iota((HALF, HALF), 0)
    causal_low = iota((HALF, length), 1) <= iota((HALF, length), 0) + HALF
    pairs = qw // HALF
    groups = kw // HD
    probs_zero = jnp.zeros((HALF, HALF), BF)
    for pair in range(pairs):
        group = pair // (pairs // groups)
        keep = half_low if group == 0 else jnp.logical_not(half_low)
        keys_two = jnp.where(keep, keys, keys_far)
        values_two = jnp.where(keep, values, values_far)
        query = qkv[:, pair * HALF : (pair + 1) * HALF] * jnp.asarray(HD ** (-0.5), BF)
        results = []
        for side in range(2):
            own = half_low if side == 0 else jnp.logical_not(half_low)
            q = jnp.where(own, query, jnp.zeros_like(query))
            at = (2 * pair + side) * length
            out = []
            for lo, causal in ((0, causal_top), (1, causal_low)):
                width = HALF if lo == 0 else length
                scores = dot_nt(q[lo * HALF : (lo + 1) * HALF], keys_two[:width])
                scores = jnp.where(causal, scores, MASKED)
                top = jnp.max(scores, axis=-1, keepdims=True)
                weights = jnp.exp(scores - top)
                weights = weights / jnp.sum(weights, axis=-1, keepdims=True)
                weights = weights.astype(BF)
                if lo == 0:
                    probs[at : at + HALF, :HALF] = weights
                    probs[at : at + HALF, HALF:] = probs_zero
                else:
                    probs[at + HALF : at + length, :] = weights
                out.append(dot(weights, values_two[:width]))
            results.append(jnp.concatenate(out, axis=0))
        mixed = jnp.where(half_low, results[0], results[1])
        mixed_all[:, pair * HALF : (pair + 1) * HALF] = mixed.astype(BF)
    save(probs, s_probs)
    save(mixed_all, s_mixed)

    pre, step, change, run, bend = scan_terms(step_raw[...], vec_ref, heads)
    turned = run.T
    run_row[:HALF, :] = turned[:, :HALF]
    run_row[HALF:, :] = turned[:, HALF:]
    broadcast_runs(run, run_wide, heads)
    step_two[...] = both(step)
    bend_two[...] = both(bend)
    b_in, c_in = xbc[:, mi : mi + HALF], xbc[:, mi + HALF : mi + 2 * HALF]
    tops = [dot_nt(c_in[c * HALF : (c + 1) * HALF], b_in[c * HALF : (c + 1) * HALF]) for c in (0, 1)]
    cross = dot_nt(c_in[HALF:], b_in[:HALF]).astype(BF)
    pair_low = iota((HALF, HALF), 1) < HD
    tops = [jnp.where(causal_top, t, 0.0) for t in tops]

    def mix_tile(t, squares):
        cols = lanes(t)
        spread = expand_matrix(t)
        x_in = xbc[:, cols].astype(F32)
        scaled = (dot(step_two[...], spread) * x_in).astype(BF)
        bends = dot(bend_two[...], spread)
        u = (bends[:HALF] * scaled[:HALF].astype(F32)).astype(BF)
        far = dot(cross, u) * bends[HALF:]
        parts = []
        for p in range(TILE // HALF):
            block = []
            for c in range(2):
                rows = slice(c * HALF, (c + 1) * HALF)
                weights = []
                for side in range(2):
                    h = t * (TILE // HD) + 2 * p + side
                    wide = run_wide[rows, lanes(h, HALF)]
                    line = run_row[pl.ds(c * HALF + h, 1), :]
                    decay = jnp.exp(jnp.minimum(wide - line, 0.0))
                    weights.append((decay * tops[c]).astype(BF))
                xs = scaled[rows, p * HALF : (p + 1) * HALF]
                zero = jnp.zeros_like(xs)
                right = jnp.concatenate(
                    [jnp.where(pair_low, xs, zero), jnp.where(pair_low, zero, xs)], axis=0
                )
                block.append(dot(jnp.concatenate(weights, axis=1), right))
            parts.append(jnp.concatenate(block, axis=0))
        out = jnp.concatenate(parts, axis=1)
        out = out + jnp.concatenate([jnp.zeros_like(far), far], axis=0)
        out = out + vec_ref[V_SKIP : V_SKIP + 1, cols] * x_in
        y[:, cols] = out.astype(BF)
        g = gate_raw[:, cols].astype(F32)
        out = out * (g * sigmoid(g))
        gated[:, cols] = out
        return squares + jnp.sum(out * out, axis=-1, keepdims=True)

    squares = lax.fori_loop(0, mi // TILE, mix_tile, jnp.zeros((length, 1), F32), unroll=True)
    save(y, s_y)
    rate = lax.rsqrt(squares * (1.0 / mi) + EPSILON)
    branch[...] = (gated[...] * rate * vec_ref[V_GS : V_GS + 1, :mi]).astype(BF)
    save(branch, s_ssm)

    wait(3)

    def out_tile(t, carry):
        cols = lanes(t)
        hidden_ref[:, cols] = (
            x_ref[:, cols].astype(F32)
            + dot(branch[...], wout[:mi, cols])
            + dot(mixed_all[...], wout[mi:, cols])
        )
        return carry

    lax.fori_loop(0, wout.shape[1] // TILE, out_tile, 0, unroll=True)
    save(hidden_ref, s_hidden)
    save(x_ref, s_x)
    yield
    finish()


def mixer_forward_scratch(length, width, widths, total):
    ci, mi, qw, kw, heads = widths
    return [
        pltpu.VMEM((width, total), BF),
        pltpu.VMEM((mi + qw, width), BF),
        pltpu.VMEM((length, width), BF),
        pltpu.VMEM((length, ci), BF),
        pltpu.VMEM((length, ci), BF),
        pltpu.VMEM((length, ci), BF),
        pltpu.VMEM((length, mi), BF),
        pltpu.VMEM((length, qw + 2 * kw), BF),
        pltpu.VMEM((length, HALF), F32),
        pltpu.VMEM((qw // HD * length, length), BF),
        pltpu.VMEM((length, mi), BF),
        pltpu.VMEM((length, qw), BF),
        pltpu.VMEM((length, mi), BF),
        pltpu.VMEM((length, mi), F32),
        pltpu.VMEM((length, heads * HALF), F32),
        pltpu.VMEM((length, HALF), F32),
        pltpu.VMEM((length, 2 * HALF), BF),
        pltpu.VMEM((length, 2 * HALF), BF),
        pltpu.SemaphoreType.DMA((32,)),
        pltpu.SemaphoreType.DMA((12,)),
    ]


def mixer_forward_call(
    index, slot, spots, x, vec, cosine, sine, turn, weights, stacks, widths, total
):
    ci, mi, qw, kw, heads = widths
    length, width = x.shape
    scratch = mixer_forward_scratch(length, width, widths, total)
    return call(
        functools.partial(mix_forward, widths),
        "mixer_forward",
        [index, slot],
        spots,
        [x, vec, cosine, sine, turn],
        weights,
        [],
        stacks,
        jax.ShapeDtypeStruct((length, width), F32),
        scratch,
        44,
        200,
    )


def mlp_forward(scalars, spots, ordinary, weights, reads, stacks, low_ref, scratch):
    index_ref, slot_ref = scalars
    base = 4 * index_ref[0]
    hidden_ref, vec_ref = ordinary
    w_g, w_u, w_down = weights
    wgu, wdown, normed, gate_low, up_low, act, final, in_sem, out_sem = scratch
    s_normed, s_gate, s_up, s_act, s_final, s_low = stacks
    ff = wdown.shape[0]
    parts = 2
    step = ff // parts
    groups = []
    for i in range(parts):
        a = slice(i * step, (i + 1) * step)
        b = slice(ff + i * step, ff + (i + 1) * step)
        groups.append(
            row_pieces(w_g, spots, wgu, [(a, a)]) + row_pieces(w_u, spots, wgu, [(a, b)])
        )
    groups.append(row_pieces(w_down, spots, wdown, [(slice(0, wdown.shape[1]),) * 2]))
    wait = start_all(groups, in_sem)
    save, finish = saver(slot_ref[base], slot_ref[base + 1] > 0, out_sem)
    yield
    valid = jnp.where(iota((hidden_ref.shape[0], 1), 0) < slot_ref[base + 2], 1.0, 0.0)

    hidden = hidden_ref[...]
    rate = lax.rsqrt(jnp.mean(hidden * hidden, axis=-1, keepdims=True) + EPSILON)
    normed[...] = (hidden * rate * vec_ref[V_G2 : V_G2 + 1, : hidden.shape[1]]).astype(BF)
    save(normed, s_normed)
    for i in range(parts):
        wait(i)

        def up_tile(t, carry):
            a = pl.ds(pl.multiple_of(i * step + t * TILE, TILE), TILE)
            b = pl.ds(pl.multiple_of(ff + i * step + t * TILE, TILE), TILE)
            gate = dot(normed[...], wgu[:, a])
            up = dot(normed[...], wgu[:, b])
            gate_low[:, a] = gate.astype(BF)
            up_low[:, a] = up.astype(BF)
            act[:, a] = (gate * sigmoid(gate) * up).astype(BF)
            return carry

        lax.fori_loop(0, step // TILE, up_tile, 0, unroll=True)
    save(gate_low, s_gate)
    save(up_low, s_up)
    save(act, s_act)
    wait(parts)

    def down_tile(t, carry):
        cols = lanes(t)
        out = (hidden_ref[:, cols] + dot(act[...], wdown[:, cols])) * valid
        final[:, cols] = out
        low_ref[:, cols] = out.astype(BF)
        return carry

    lax.fori_loop(0, wdown.shape[1] // TILE, down_tile, 0, unroll=True)
    save(final, s_final)
    save(low_ref, s_low, slot_ref[base + 3])
    yield
    finish()


def mlp_forward_scratch(length, width, ff):
    return [
        pltpu.VMEM((width, 2 * ff), BF),
        pltpu.VMEM((ff, width), BF),
        pltpu.VMEM((length, width), BF),
        pltpu.VMEM((length, ff), BF),
        pltpu.VMEM((length, ff), BF),
        pltpu.VMEM((length, ff), BF),
        pltpu.VMEM((length, width), F32),
        pltpu.SemaphoreType.DMA((32,)),
        pltpu.SemaphoreType.DMA((6,)),
    ]


def mlp_forward_call(index, slot, spots, hidden, vec, weights, stacks, ff):
    length, width = hidden.shape
    scratch = mlp_forward_scratch(length, width, ff)
    return call(
        mlp_forward,
        "mlp_forward",
        [index, slot],
        spots,
        [hidden, vec],
        weights,
        [],
        stacks,
        jax.ShapeDtypeStruct((length, width), BF),
        scratch,
        32,
        3,
    )


def mlp_backward(scalars, spots, ordinary, weights, reads, stacks, d_hidden_ref, scratch):
    index_ref, slot_ref, mix_ref = scalars
    base = 4 * index_ref[0]
    target_ref, vec_ref, _ = ordinary
    w_g, w_u, w_down = weights
    s_final, s_hidden, s_gate, s_up = reads
    (wgu, wdown, final, hidden, gate_low, up_low, d_mlp, d_gu, d_sum, d_normed, small, in_sem,
     out_sem) = scratch
    s_dmlp, s_dgate, s_dup, s_small = stacks
    slot = slot_ref[base]
    ff = wdown.shape[0]
    wait = start_all(
        [
            [(s_final.at[slot], final)],
            [(s_gate.at[slot], gate_low), (s_up.at[slot], up_low)]
            + row_pieces(w_down, spots, wdown, [(slice(0, wdown.shape[1]),) * 2]),
            row_pieces(w_g, spots, wgu, [(slice(0, ff), slice(0, ff))])
            + row_pieces(w_u, spots, wgu, [(slice(0, ff), slice(ff, 2 * ff))]),
            [(s_hidden.at[slot], hidden)],
        ],
        in_sem,
    )
    save, finish = saver(slot, slot_ref[base + 1] > 0, out_sem)
    yield
    wait(0)
    target = target_ref[...].astype(F32)
    valid = jnp.where(iota((target_ref.shape[0], 1), 0) < slot_ref[base + 2], 1.0, 0.0)
    misfit = final[...] - target
    loss = jnp.sum(valid * misfit * misfit, axis=0, keepdims=True)
    seed = valid * jnp.where(mix_ref[0] > 0.5, target, mix_ref[1] * misfit)
    d_sum[...] = seed
    d_mlp[...] = seed.astype(BF)
    save(d_mlp, s_dmlp)
    wait(1)

    def act_tile(t, carry):
        a = lanes(t)
        b = pl.ds(pl.multiple_of(ff + t * TILE, TILE), TILE)
        d_act = dot_nt(d_mlp[...], wdown[a, :])
        gate, up = gate_low[:, a].astype(F32), up_low[:, a].astype(F32)
        s = sigmoid(gate)
        swish = gate * s
        d_gu[:, a] = (d_act * up * (s + swish - swish * s)).astype(BF)
        d_gu[:, b] = (d_act * swish).astype(BF)
        return carry

    lax.fori_loop(0, ff // TILE, act_tile, 0, unroll=True)
    save(d_gu.at[:, :ff], s_dgate)
    save(d_gu.at[:, ff:], s_dup)
    wait(2)
    yield

    def back_tile(t, carry):
        rows = lanes(t)
        d_normed[:, rows] = dot_nt(d_gu[...], wgu[rows, :])
        return carry

    lax.fori_loop(0, wgu.shape[0] // TILE, back_tile, 0, unroll=True)
    wait(3)
    h = hidden[...]
    width = h.shape[1]
    rate = lax.rsqrt(jnp.mean(h * h, axis=-1, keepdims=True) + EPSILON)
    unit = h * rate
    d_n = d_normed[...]
    small[...] = jnp.zeros_like(small)
    small[0:1, :width] = jnp.sum(d_n * unit, axis=0, keepdims=True)
    small[1:2, :width] = loss
    save(small, s_small)
    d_n = d_n * vec_ref[V_G2 : V_G2 + 1, :width]
    d_hidden_ref[...] = d_sum[...] + rate * (
        d_n - unit * jnp.mean(d_n * unit, axis=-1, keepdims=True)
    )
    yield
    finish()


def mlp_backward_scratch(length, width, ff, small):
    return [
        pltpu.VMEM((width, 2 * ff), BF),
        pltpu.VMEM((ff, width), BF),
        pltpu.VMEM((length, width), F32),
        pltpu.VMEM((length, width), F32),
        pltpu.VMEM((length, ff), BF),
        pltpu.VMEM((length, ff), BF),
        pltpu.VMEM((length, width), BF),
        pltpu.VMEM((length, 2 * ff), BF),
        pltpu.VMEM((length, width), F32),
        pltpu.VMEM((length, width), F32),
        pltpu.VMEM(small, F32),
        pltpu.SemaphoreType.DMA((32,)),
        pltpu.SemaphoreType.DMA((4,)),
    ]


def mlp_backward_call(index, slot, mix, spots, target, vec, turn, weights, reads, stacks, ff):
    length, width = target.shape
    scratch = mlp_backward_scratch(length, width, ff, stacks[-1].shape[1:])
    return call(
        mlp_backward,
        "mlp_backward",
        [index, slot, mix],
        spots,
        [target, vec, turn],
        weights,
        reads,
        stacks,
        jax.ShapeDtypeStruct((length, width), F32),
        scratch,
        40,
        3,
    )


def column_sum(v):
    return jnp.sum(v, axis=0, keepdims=True)


def mix_backward(
    widths, scalars, spots, ordinary, weights, reads, stacks, d_input_ref, scratch
):
    ci, mi, qw, kw, heads = widths
    index_ref, slot_ref = scalars
    base = 4 * index_ref[0]
    d_hidden_ref, vec_ref, cos_ref, sin_ref, _ = ordinary
    w_first, w_conv, w_gate, w_out = weights
    s_conv, s_z, s_gate, s_qkv, s_step, s_probs, s_y, s_x = reads
    (win, wout, conv_raw, z, gate_raw, qkv, step_raw, probs, y, x_low, d_branch, d_proj, d_mixed,
     d_ssm, d_z, d_normed, run_wide, run_row, step_two, bend_two, tops, d_tops, run_acc, step_acc,
     small, in_sem, out_sem) = scratch
    s_dbranch, s_dfirst, s_dconv, s_dgate, s_dinput, s_small = stacks
    slot = slot_ref[base]
    g0, q0 = ci, ci + mi
    s0 = q0 + qw + 2 * kw
    total = win.shape[1]
    tail = total - q0
    length, width = d_hidden_ref.shape
    wait = start_all(
        [
            out_pieces(w_out, spots, wout, mi),
            [(s_probs.at[slot], probs), (s_qkv.at[slot], qkv)],
            [(s_step.at[slot], step_raw), (s_gate.at[slot], gate_raw), (s_y.at[slot], y)],
            [(s_z.at[slot], z)],
            [(s_conv.at[slot], conv_raw)],
            row_pieces(w_first, spots, win, [(slice(0, tail), slice(q0, total))])
            + row_pieces(w_conv, spots, win, [(slice(0, ci), slice(0, ci))])
            + row_pieces(w_gate, spots, win, [(slice(0, mi), slice(g0, q0))]),
            [(s_x.at[slot], x_low)],
        ],
        in_sem,
    )
    save, finish = saver(slot, slot_ref[base + 1] > 0, out_sem)
    yield
    small[...] = jnp.zeros_like(small)
    d_branch[...] = d_hidden_ref[...].astype(BF)
    save(d_branch, s_dbranch)
    wait(0)
    for t in range(qw // TILE):
        rows = slice(mi + t * TILE, mi + (t + 1) * TILE)
        d_mixed[:, t * TILE : (t + 1) * TILE] = dot_nt(d_branch[...], wout[rows, :]).astype(BF)

    lane_first = jnp.bitwise_and(iota((length, HALF), 1), HD - 1) < HD // 2
    half_low = iota((length, HALF), 1) < HD
    cosine, sine = cos_ref[...], -sin_ref[...]
    wait(1)
    keys, values = qkv[:, qw : qw + kw], qkv[:, qw + kw : qw + 2 * kw]
    keys_far, values_far = pltpu.roll(keys.astype(F32), HD, 1).astype(BF), pltpu.roll(
        values.astype(F32), HD, 1
    ).astype(BF)
    pairs = qw // HALF
    groups = kw // HD
    scale = HD ** (-0.5)
    d_keys = [jnp.zeros((length, HALF), F32) for _ in range(groups)]
    d_values = [jnp.zeros((length, HALF), F32) for _ in range(groups)]
    for pair in range(pairs):
        group = pair // (pairs // groups)
        keep = half_low if group == 0 else jnp.logical_not(half_low)
        keys_two = jnp.where(keep, keys, keys_far)
        values_two = jnp.where(keep, values, values_far)
        cols = slice(pair * HALF, (pair + 1) * HALF)
        query, d_out = qkv[:, cols], d_mixed[:, cols]
        results = []
        for side in range(2):
            own = half_low if side == 0 else jnp.logical_not(half_low)
            q = jnp.where(own, query, jnp.zeros_like(query))
            d_o = jnp.where(own, d_out, jnp.zeros_like(d_out))
            at = (2 * pair + side) * length
            weights = probs[at : at + length, :]
            wide = weights.astype(F32)
            d_weights = dot_nt(d_o, values_two)
            inner = wide * d_weights
            d_scores = (inner - wide * jnp.sum(inner, axis=-1, keepdims=True)).astype(BF)
            results.append(dot(d_scores, keys_two))
            d_keys[group] = d_keys[group] + dot_tn(d_scores, q)
            d_values[group] = d_values[group] + dot_tn(weights, d_o)
        d_q = jnp.where(half_low, results[0], results[1]) * scale
        d_proj[:, q0 + pair * HALF : q0 + (pair + 1) * HALF] = rope(
            d_q, cosine, sine, lane_first
        ).astype(BF)
    folded = [v + pltpu.roll(v, HD, 1) for v in d_keys]
    d_k = jnp.where(half_low, folded[0], folded[1]) * scale
    d_proj[:, q0 + qw : q0 + qw + kw] = rope(d_k, cosine, sine, lane_first).astype(BF)
    folded = [v + pltpu.roll(v, HD, 1) for v in d_values]
    d_proj[:, q0 + qw + kw : s0] = jnp.where(half_low, folded[0], folded[1]).astype(BF)

    wait(2)

    def norm_tile(t, sums):
        cols = lanes(t)
        d_s = dot_nt(d_branch[...], wout[cols, :])
        d_ssm[:, cols] = d_s
        g = gate_raw[:, cols].astype(F32)
        gated = y[:, cols].astype(F32) * (g * sigmoid(g))
        d_n = d_s * vec_ref[V_GS : V_GS + 1, cols]
        return (
            sums[0] + jnp.sum(gated * gated, axis=-1, keepdims=True),
            sums[1] + jnp.sum(gated * d_n, axis=-1, keepdims=True),
        )

    zero_col = jnp.zeros((length, 1), F32)
    squares, along = lax.fori_loop(0, mi // TILE, norm_tile, (zero_col, zero_col), unroll=True)
    rate = lax.rsqrt(squares * (1.0 / mi) + EPSILON)
    along = along * (rate * rate) * (1.0 / mi)

    pre, step, change, run, bend = scan_terms(step_raw[...], vec_ref, heads)
    turned = run.T
    run_row[:HALF, :] = turned[:, :HALF]
    run_row[HALF:, :] = turned[:, HALF:]
    broadcast_runs(run, run_wide, heads)
    step_two[...] = both(step)
    bend_two[...] = both(bend)
    wait(3)
    zb = z[:, mi : mi + 2 * HALF].astype(F32)
    sb = sigmoid(zb)
    bc = (zb * sb).astype(BF)
    b_in, c_in = bc[:, :HALF], bc[:, HALF:]
    causal = iota((HALF, HALF), 1) <= iota((HALF, HALF), 0)
    for c in range(2):
        rows = slice(c * HALF, (c + 1) * HALF)
        tops[rows, :] = jnp.where(causal, dot_nt(c_in[rows], b_in[rows]), 0.0)
    cross = dot_nt(c_in[HALF:], b_in[:HALF])
    cross_turned = cross.T.astype(BF)
    cross = cross.astype(BF)
    pair_low = iota((HALF, HALF), 1) < HD
    d_tops[...] = jnp.zeros_like(d_tops)
    run_acc[...] = jnp.zeros_like(run_acc)
    step_acc[...] = jnp.zeros_like(step_acc)

    def mix_tile(t, carry):
        cols = lanes(t)
        g = gate_raw[:, cols].astype(F32)
        s = sigmoid(g)
        swish = g * s
        y_in = y[:, cols].astype(F32)
        gated = y_in * swish
        d_s = d_ssm[:, cols]
        small[V_GS : V_GS + 1, cols] = column_sum(d_s * gated * rate)
        d_gated = rate * (d_s * vec_ref[V_GS : V_GS + 1, cols]) - gated * (along * rate)
        d_proj[:, pl.ds(pl.multiple_of(g0 + t * TILE, TILE), TILE)] = (
            d_gated * y_in * (s + swish - swish * s)
        ).astype(BF)
        d_y = d_gated * swish
        z_in = z[:, cols].astype(F32)
        s = sigmoid(z_in)
        x_in = z_in * s
        slope = s + x_in - x_in * s
        spread = expand_matrix(t)
        steps = dot(step_two[...], spread)
        bends = dot(bend_two[...], spread)
        scaled = (steps * x_in).astype(BF)
        d_low = d_y.astype(BF)
        u = (bends[:HALF] * scaled[:HALF].astype(F32)).astype(BF)
        v = (bends[HALF:] * d_y[HALF:]).astype(BF)
        far = dot(cross, u)
        back = dot(cross_turned, v)
        d_tops[2 * HALF :, :] += dot_nt(v, u)
        mixed_parts, back_parts = [], []
        for p in range(TILE // HALF):
            mixed_block, back_block = [], []
            for c in range(2):
                rows = slice(c * HALF, (c + 1) * HALF)
                xs = scaled[rows, p * HALF : (p + 1) * HALF]
                dy = d_low[rows, p * HALF : (p + 1) * HALF]
                zero = jnp.zeros_like(xs)
                xs_two = [jnp.where(pair_low, xs, zero), jnp.where(pair_low, zero, xs)]
                dy_two = [jnp.where(pair_low, dy, zero), jnp.where(pair_low, zero, dy)]
                weights = []
                d_top = jnp.zeros((HALF, HALF), F32)
                for side in range(2):
                    h = t * (TILE // HD) + 2 * p + side
                    wide = run_wide[rows, lanes(h, HALF)]
                    line = run_row[pl.ds(c * HALF + h, 1), :]
                    decay = jnp.exp(jnp.minimum(wide - line, 0.0))
                    weights.append((decay * tops[rows, :]).astype(BF))
                    d_top = d_top + decay * dot_nt(dy_two[side], xs)
                d_tops[rows, :] += d_top
                mixed_block.append(
                    dot(jnp.concatenate(weights, axis=1), jnp.concatenate(xs_two, axis=0))
                )
                back_block.append(
                    dot_tn(jnp.concatenate(weights, axis=0), jnp.concatenate(dy_two, axis=0))
                )
            mixed_parts.append(jnp.concatenate(mixed_block, axis=0))
            back_parts.append(jnp.concatenate(back_block, axis=0))
        mixed = jnp.concatenate(mixed_parts, axis=1)
        d_scaled = jnp.concatenate(back_parts, axis=1)
        crossing = jnp.concatenate(
            [-(u.astype(F32) * back), v.astype(F32) * far], axis=0
        )
        runs = d_low.astype(F32) * mixed - scaled.astype(F32) * d_scaled + crossing
        d_scaled = d_scaled + jnp.concatenate([bends[:HALF] * back, jnp.zeros_like(back)], axis=0)
        gather = reduce_matrix(t)
        run_acc[...] += sum(dot(part, gather) for part in split2(runs))
        step_acc[...] += sum(dot(part, gather) for part in split2(x_in * d_scaled))
        small[V_SKIP : V_SKIP + 1, cols] = column_sum(d_y * x_in)
        d_x = steps * d_scaled + vec_ref[V_SKIP : V_SKIP + 1, cols] * d_y
        d_z[:, cols] = d_x * slope
        return carry

    lax.fori_loop(0, mi // TILE, mix_tile, 0, unroll=True)
    d_top = [
        jnp.where(causal, d_tops[c * HALF : (c + 1) * HALF, :], 0.0).astype(BF) for c in range(2)
    ]
    d_cross = d_tops[2 * HALF :, :].astype(BF)
    d_c = jnp.concatenate(
        [dot(d_top[0], b_in[:HALF]), dot(d_cross, b_in[:HALF]) + dot(d_top[1], b_in[HALF:])], axis=0
    )
    d_b = jnp.concatenate(
        [dot_tn(d_top[0], c_in[:HALF]) + dot_tn(d_cross, c_in[HALF:]), dot_tn(d_top[1], c_in[HALF:])],
        axis=0,
    )
    xb = zb * sb
    d_z[:, mi : mi + 2 * HALF] = jnp.concatenate([d_b, d_c], axis=1) * (sb + xb - xb * sb)
    upper = jnp.where(
        iota((length, length), 0) <= iota((length, length), 1), 1.0, 0.0
    ).astype(BF)
    d_change = sum(dot(upper, part) for part in split3(run_acc[...]))
    d_pre = (step_acc[...] + d_change * vec_ref[V_DECAY : V_DECAY + 1, :HALF]) * sigmoid(pre)
    d_pre = jnp.where(iota(d_pre.shape, 1) < heads, d_pre, 0.0)
    d_proj[:, s0:total] = d_pre.astype(BF)
    small[V_SBIAS : V_SBIAS + 1, :HALF] = column_sum(d_pre)
    small[V_DECAY : V_DECAY + 1, :HALF] = column_sum(d_change * change)

    wait(4)
    row = iota((length, TILE), 0)

    def conv_tile(t, carry):
        cols = lanes(t)
        d = d_z[:, cols]
        raw = conv_raw[:, cols].astype(F32)
        small[V_CBIAS : V_CBIAS + 1, cols] = column_sum(d)
        small[3:4, cols] = column_sum(d * raw)
        out = d * vec_ref[3:4, cols]
        for ahead in range(1, 4):
            moved = jnp.where(row < length - ahead, pltpu.roll(d, length - ahead, 0), 0.0)
            small[3 - ahead : 4 - ahead, cols] = column_sum(moved * raw)
            out = out + moved * vec_ref[3 - ahead : 4 - ahead, cols]
        d_proj[:, cols] = out.astype(BF)
        return carry

    lax.fori_loop(0, ci // TILE, conv_tile, 0, unroll=True)
    save(d_proj.at[:, q0:], s_dfirst)
    save(d_proj.at[:, :ci], s_dconv)
    save(d_proj.at[:, g0:q0], s_dgate)

    wait(5)

    def back_tile(t, carry):
        rows = lanes(t)
        d_normed[:, rows] = dot_nt(d_proj[...], win[rows, :])
        return carry

    lax.fori_loop(0, width // TILE, back_tile, 0, unroll=True)
    wait(6)
    x = x_low[...].astype(F32)
    rate_one = lax.rsqrt(jnp.mean(x * x, axis=-1, keepdims=True) + EPSILON)
    unit = x * rate_one
    d_n = d_normed[...]
    small[V_G1 : V_G1 + 1, :width] = column_sum(d_n * unit)
    save(small, s_small)
    d_n = d_n * vec_ref[V_G1 : V_G1 + 1, :width]
    d_input_ref[...] = (
        d_hidden_ref[...]
        + rate_one * (d_n - unit * jnp.mean(d_n * unit, axis=-1, keepdims=True))
    ).astype(BF)
    save(d_input_ref, s_dinput, slot_ref[base + 3])
    yield
    finish()


def mixer_backward_scratch(length, width, widths, total, small):
    ci, mi, qw, kw, heads = widths
    return [
        pltpu.VMEM((width, total), BF),
        pltpu.VMEM((mi + qw, width), BF),
        pltpu.VMEM((length, ci), BF),
        pltpu.VMEM((length, ci), BF),
        pltpu.VMEM((length, mi), BF),
        pltpu.VMEM((length, qw + 2 * kw), BF),
        pltpu.VMEM((length, HALF), F32),
        pltpu.VMEM((qw // HD * length, length), BF),
        pltpu.VMEM((length, mi), BF),
        pltpu.VMEM((length, width), BF),
        pltpu.VMEM((length, width), BF),
        pltpu.VMEM((length, total), BF),
        pltpu.VMEM((length, qw), BF),
        pltpu.VMEM((length, mi), F32),
        pltpu.VMEM((length, ci), F32),
        pltpu.VMEM((length, width), F32),
        pltpu.VMEM((length, heads * HALF), F32),
        pltpu.VMEM((length, HALF), F32),
        pltpu.VMEM((length, 2 * HALF), BF),
        pltpu.VMEM((length, 2 * HALF), BF),
        pltpu.VMEM((2 * HALF, HALF), F32),
        pltpu.VMEM((3 * HALF, HALF), F32),
        pltpu.VMEM((length, HALF), F32),
        pltpu.VMEM((length, HALF), F32),
        pltpu.VMEM(small, F32),
        pltpu.SemaphoreType.DMA((48,)),
        pltpu.SemaphoreType.DMA((6,)),
    ]


def mixer_backward_call(
    index, slot, spots, d_hidden, vec, cosine, sine, turn, weights, reads, stacks, widths, total
):
    ci, mi, qw, kw, heads = widths
    length, width = d_hidden.shape
    scratch = mixer_backward_scratch(length, width, widths, total, stacks[-1].shape[1:])
    return call(
        functools.partial(mix_backward, widths),
        "mixer_backward",
        [index, slot],
        spots,
        [d_hidden, vec, cosine, sine, turn],
        weights,
        reads,
        stacks,
        jax.ShapeDtypeStruct((length, width), BF),
        scratch,
        48,
        250,
    )


def weight_kernel(core_ref, away_ref, stay_ref, right_ref, out_away, out_stay, turned):
    rows = away_ref.shape[2]
    tokens = away_ref.shape[0] * away_ref.shape[1]
    turned[:rows, :] = away_ref[...].reshape(tokens, rows).T
    turned[rows:, :] = stay_ref[...].reshape(tokens, rows).T
    right = right_ref[...].reshape(tokens, right_ref.shape[2])
    out_away[0] = dot(turned[:rows, :], right).astype(BF)
    out_stay[0] = dot(turned[rows:, :], right).astype(BF)


def weight_grad_halves(core, left, right):
    count, length, depth = left.shape
    columns = right.shape[2]
    rows = depth // 4
    grid = pltpu.PrefetchScalarGridSpec(
        num_scalar_prefetch=1,
        grid=(2,),
        in_specs=[
            pl.BlockSpec((count, length, rows), lambda c, core: (0, 0, 2 * c + 1 - core[0])),
            pl.BlockSpec((count, length, rows), lambda c, core: (0, 0, 2 * c + core[0])),
            pl.BlockSpec((count, length, columns), lambda c, core: (0, 0, 0)),
        ],
        out_specs=[pl.BlockSpec((1, rows, columns), lambda c, core: (c, 0, 0))] * 2,
        scratch_shapes=[pltpu.VMEM((2 * rows, count * length), BF)],
    )
    shape = pltpu.HBM((2, rows, columns), BF)
    return pl.pallas_call(
        weight_kernel,
        out_shape=[shape, shape],
        grid_spec=grid,
        compiler_params=pltpu.CompilerParams(vmem_limit_bytes=40 * 1024 * 1024),
        cost_estimate=pl.CostEstimate(
            flops=100000000, bytes_accessed=1000000, transcendentals=0
        ),
        name="weight_gradient",
    )(core, in_hbm(left), in_hbm(left), in_hbm(right))


def layer_forward_call(
    index, slot, spots, x, vec, cosine, sine, turn, weights, stacks, widths, total, ff
):
    length, width = x.shape
    first = mixer_forward_scratch(length, width, widths, total)
    second = mlp_forward_scratch(length, width, ff)
    n = 12

    def body(scalars, spots, ordinary, weights, reads, stacks, low_ref, scratch):
        hidden = scratch[-1]
        one = mix_forward(
            widths, scalars, spots, ordinary, weights[:4], [], stacks[:n], hidden,
            scratch[: len(first)],
        )
        two = mlp_forward(
            scalars, spots, [hidden, ordinary[1]], weights[4:], [], stacks[n:], low_ref,
            scratch[len(first) : -1],
        )
        for part in (one, one, two, one, two, one, two):
            next(part, None)
        yield

    return call(
        body,
        "layer_forward",
        [index, slot],
        spots,
        [x, vec, cosine, sine, turn],
        weights,
        [],
        stacks,
        jax.ShapeDtypeStruct((length, width), BF),
        first + second + [pltpu.VMEM((length, width), F32)],
        58,
        200,
    )


def layer_backward_call(
    index, slot, mix, spots, target, vec, cosine, sine, turn, weights, reads, stacks, widths, total, ff
):
    length, width = target.shape
    first = mlp_backward_scratch(length, width, ff, stacks[3].shape[1:])
    second = mixer_backward_scratch(length, width, widths, total, stacks[-1].shape[1:])
    n = 4

    def body(scalars, spots, ordinary, weights, reads, stacks, d_input_ref, scratch):
        d_hidden = scratch[-1]
        target_ref, vec_ref, cos_ref, sin_ref, turn_ref = ordinary
        one = mlp_backward(
            scalars, spots, [target_ref, vec_ref, turn_ref], weights[4:], reads[:4],
            stacks[:n], d_hidden, scratch[: len(first)],
        )
        two = mix_backward(
            widths, scalars[:2], spots, [d_hidden, vec_ref, cos_ref, sin_ref, turn_ref],
            weights[:4], reads[4:], stacks[n:], d_input_ref, scratch[len(first) : -1],
        )
        for part in (one, one, two, one, two, one, two):
            next(part, None)
        yield

    return call(
        body,
        "layer_backward",
        [index, slot, mix],
        spots,
        [target, vec, cosine, sine, turn],
        weights,
        reads,
        stacks,
        jax.ShapeDtypeStruct((length, width), BF),
        first + second + [pltpu.VMEM((length, width), F32)],
        60,
        250,
    )


def rope_tables(length):
    halves = HD // 2
    inverse = jnp.exp(jnp.arange(halves, dtype=F32) * (-2.0 * math.log(ROPE_BASE) / HD))
    angles = jnp.arange(length, dtype=F32)[:, None] * inverse[None, :]
    cosine, sine = jnp.cos(angles), jnp.sin(angles)
    return (
        jnp.concatenate([cosine] * 4, axis=1),
        jnp.concatenate([-sine, sine, -sine, sine], axis=1),
    )


def swap(block, axis, bit):
    return lax.ppermute(block, axis, [(i, i ^ bit) for i in range(lax.axis_size(axis))])


def after(value, *others):
    if not others:
        return value
    return lax.optimization_barrier((value,) + others)[0]


def corner(made):
    part = made.reshape(-1, made.shape[-1])[:8, :HALF].astype(BF)
    return jnp.dot(part, jnp.ones((HALF, HALF), BF), preferred_element_type=F32)


def quick_links():
    return lax.axis_size("fsdp") == 4 and lax.axis_size("rep") == 4


def gather_halves(shard, axis, before_y=(), before_z=()):
    parity = lax.axis_index("rep") % 2
    half = shard.shape[axis] // 2
    mine = lax.dynamic_slice_in_dim(shard, parity * half, half, axis)
    near = swap(shard, "fsdp", 1)
    far_one = swap(after(mine, *before_y), "fsdp", 2)
    far_two = swap(after(far_one, *before_z), "rep", 1)
    return [shard, near, far_one, far_two]


def gather_wholes(shard, *before_y):
    return [shard, swap(shard, "fsdp", 1), swap(after(shard, *before_y), "fsdp", 2)]


def share_far(pieces, *before):
    return pieces + [swap(after(piece, *before), "fsdp", 1) for piece in pieces[2:]]


def plus(a, b):
    return (a.astype(F32) + b.astype(F32)).astype(BF)


def weight_grad(left, right):
    return lax.dot_general(
        left, right, (((0, 1), (0, 1)), ((), ())), preferred_element_type=F32
    ).astype(BF)


class Reduction:
    def __init__(self, left, right, riders=None):
        self.left, self.right, self.riders = left, right, riders

    def begin(self, order):
        left, right = order(self.left, self.right)
        core = lax.axis_index("fsdp") % 2
        away, stay = weight_grad_halves(core.astype(jnp.int32)[None], left, right)
        if self.riders is not None:
            blocks, column = self.riders
            away, stay = (
                lax.dynamic_update_slice(
                    grad, lax.dynamic_index_in_dim(blocks, i, 1, keepdims=False), (0, 0, column)
                )
                for grad, i in ((away, 1 - core), (stay, core))
            )
        self.stay = stay
        self.moved = swap(away, "fsdp", 1)
        return stay

    def chips(self, order):
        chip = lax.axis_index("fsdp") // 2
        self.kept = order(self.stay, self.moved)

        def part(i):
            return [lax.dynamic_index_in_dim(v, i, 0, keepdims=False) for v in self.kept]

        away = plus(*part(1 - chip))
        self.moved = swap(away, "fsdp", 2)
        return away

    def line_in(self, order):
        chip = lax.axis_index("fsdp") // 2
        *kept, moved = order(*self.kept, self.moved)
        one, two = (lax.dynamic_index_in_dim(v, chip, 0, keepdims=False) for v in kept)
        self.stay = (one.astype(F32) + two.astype(F32) + moved.astype(F32)).astype(BF)
        self.moved = lax.ppermute(self.stay, "rep", [(0, 1), (3, 2)])
        return self.stay

    def middle(self, order):
        stay, moved = order(self.stay, self.moved)
        self.stay = plus(stay, moved)
        self.moved = lax.ppermute(self.stay, "rep", [(1, 2), (2, 1)])
        return self.stay

    def line_out(self, order):
        stay, moved = order(self.stay, self.moved)
        self.stay = plus(stay, moved)
        self.moved = lax.ppermute(self.stay, "rep", [(1, 0), (2, 3)])
        return self.stay

    def finish(self, order):
        stay, moved = order(self.stay, self.moved)
        rank = lax.axis_index("rep")
        inner = jnp.logical_or(rank == 1, rank == 2)
        self.result = jnp.where(inner, stay, moved).astype(F32)
        return self.result


def body(
    inputs,
    teacher,
    lengths,
    order,
    loss_scale,
    norm_gain1,
    w_query,
    w_key,
    w_value,
    w_attn_out,
    w_ssm_gate,
    w_conv_in,
    w_step,
    conv_kernel,
    conv_bias,
    step_bias,
    decay_log,
    skip_gain,
    ssm_norm_gain,
    w_ssm_out,
    norm_gain2,
    w_gate,
    w_up,
    w_down,
):
    quick = quick_links()
    n_rep = lax.axis_size("rep")
    n_fsdp = lax.axis_size("fsdp")
    rank = lax.axis_index("rep")
    fsdp = lax.axis_index("fsdp")
    section = lax.axis_index("section")
    first = section == 0
    device = fsdp * n_rep + rank
    count, length, width = inputs.shape
    ci, mi, qw, kw = (w.shape[2] for w in (w_conv_in, w_ssm_gate, w_query, w_key))
    heads = w_step.shape[2]
    ff = w_up.shape[2]
    widths = (ci, mi, qw, kw, heads)
    taps = conv_kernel.shape[1]
    rows = width // n_fsdp
    tail = qw + 2 * kw + HALF
    total = ci + mi + tail

    turns = jnp.arange(count, dtype=jnp.int32)
    numbers = jnp.arange(order.shape[0], dtype=jnp.int32)
    mine = device * count + turns
    sources = jnp.sum(jnp.where(order[None, :] == mine[:, None], numbers[None, :], 0), axis=1)
    target = lax.dynamic_slice_in_dim(order, device * count, count) // count % n_rep
    anchor = sources // count % n_rep

    def inverse(key):
        return jnp.sum(jnp.where((key ^ rank)[None, :] == turns[:, None], turns[None, :], 0), axis=1)

    send_at, keep_at = inverse(target), inverse(anchor)
    own_lengths = jnp.take(lengths, jnp.take(sources, keep_at))
    outgoing = [
        jnp.where(
            first,
            lax.dynamic_index_in_dim(inputs, send_at[j], 0, keepdims=False),
            lax.dynamic_index_in_dim(teacher, send_at[j], 0, keepdims=False),
        )
        for j in range(count)
    ]
    dealt = [outgoing[0]]

    def deal(j, *earlier):
        dealt.append(swap(after(outgoing[j], *earlier), "rep", j))


    def columns(flat):
        wide = -(-flat.size // rows)
        return jnp.pad(flat, (0, wide * rows - flat.size)).reshape(rows, wide)

    convs = jnp.concatenate([conv_kernel[0], conv_bias], axis=0)
    riders = jnp.concatenate(
        [
            norm_gain1[0][:, None],
            norm_gain2[0][:, None],
            columns(convs.reshape(-1)),
            columns(ssm_norm_gain[0]),
        ],
        axis=1,
    )
    used = riders.shape[1]
    wide = -(-convs.size // rows)
    shard_first = jnp.concatenate(
        [w_query[0], w_key[0], w_value[0], w_step[0], riders]
        + [jnp.zeros((rows, HALF - heads - used), BF)],
        axis=1,
    )
    at = qw + 2 * kw + heads
    parity = rank % 2
    if quick:
        g_gate = gather_halves(w_ssm_gate[0], 0)
        g_conv = gather_halves(w_conv_in[0], 0)
        g_first = gather_halves(shard_first, 0, g_gate[2:3], g_gate[3:4])
        shard_out = jnp.concatenate([w_ssm_out[0], w_attn_out[0]], axis=0)
        g_out = gather_halves(shard_out, 1, g_conv[2:3], g_conv[3:4])
        g_g = gather_halves(w_gate[0], 0, g_first[2:3], g_first[3:4])
        g_u = gather_wholes(w_up[0], g_out[2], g_g[2])
        deal(1, g_out[3])
        deal(2, dealt[1])
        g_gate, g_conv, g_first, g_out = (share_far(g) for g in (g_gate, g_conv, g_first, g_out))
        spots = [2 * fsdp, 2 * (fsdp ^ 1)]
        spots += [2 * (fsdp ^ k) + b for k in (2, 3) for b in (parity, 1 - parity)]
        spots = jnp.stack(spots).astype(jnp.int32)
        cut = [piece[:, at : at + used] for piece in g_first]
        swapped = [jnp.where(parity == 0, cut[i], cut[i + 1]) for i in (2, 4)]
        swapped2 = [jnp.where(parity == 0, cut[i + 1], cut[i]) for i in (2, 4)]
        blocks = jnp.stack(
            [cut[0], cut[1]]
            + [jnp.concatenate([a, b], axis=0) for a, b in zip(swapped, swapped2)]
        )
        ridden = jnp.take(blocks, jnp.arange(4, dtype=jnp.int32) ^ fsdp, axis=0)
    else:

        for j in range(1, count - 1):
            deal(j)

        def whole(shard):
            return lax.all_gather(shard, "fsdp", axis=0, tiled=True)

        g_first, g_conv, g_gate, g_g, g_u, g_down = (
            [whole(w)]
            for w in (shard_first, w_conv_in[0], w_ssm_gate[0], w_gate[0], w_up[0], w_down[0])
        )
        g_out = [jnp.concatenate([whole(w_ssm_out[0]), whole(w_attn_out[0])], axis=0)]
        spots = jnp.zeros((1,), jnp.int32)
        ridden = g_first[0][:, at : at + used].reshape(n_fsdp, rows, used)
    mixer_weights = [g_first, g_conv, g_gate, g_out]
    mlp_weights = None if quick else [g_g, g_u, g_down]

    conv_all = ridden[:, :, 2 : 2 + wide].reshape(n_fsdp, -1)[:, : (taps + 1) * ci // n_fsdp]
    conv_all = conv_all.reshape(n_fsdp, taps + 1, ci // n_fsdp).transpose(1, 0, 2)
    ssm_gain = ridden[:, :, 2 + wide :].reshape(n_fsdp, -1)[:, : mi // n_fsdp].reshape(1, mi)

    def table_row(v):
        v = v.astype(F32)
        return jnp.pad(v, ((0, 0), (0, ci - v.shape[1])))

    vec = jnp.concatenate(
        [
            table_row(v)
            for v in (
                conv_all.reshape(taps + 1, ci),
                ssm_gain,
                jnp.repeat(skip_gain, HD, axis=1),
                ridden[:, :, 0].reshape(1, width),
                ridden[:, :, 1].reshape(1, width),
                step_bias,
                -jnp.exp(decay_log),
                jnp.zeros((16 - taps - 7, 1), F32),
            )
        ],
        axis=0,
    )
    cosine, sine = rope_tables(length)

    valid_count = jnp.sum(lengths).astype(F32)
    factor = loss_scale / (valid_count * width)

    skew = 2
    steps = count + skew
    ticks = jnp.arange(steps, dtype=jnp.int32)
    raw = jnp.concatenate([ticks - skew * section, count - 1 - ticks + skew * (1 - section)])
    inside = jnp.logical_and(raw >= 0, raw < count).astype(jnp.int32)
    slots = jnp.clip(raw, 0, count - 1)
    plan = [slots, inside, jnp.take(own_lengths, slots), jnp.take(keep_at, slots)]
    plan = jnp.stack(plan, axis=1).reshape(-1)
    mix = jnp.stack([jnp.where(first, 1.0, 0.0), 2.0 * factor])

    def stack(*shape, kind=BF):
        return jax.ShapeDtypeStruct((count,) + shape, kind)

    mix_stacks = [
        stack(length, width),
        stack(length, ci),
        stack(length, ci),
        stack(length, mi),
        stack(length, qw + 2 * kw),
        stack(length, HALF, kind=F32),
        stack(qw // HD * length, length),
        stack(length, mi),
        stack(length, qw),
        stack(length, mi),
        stack(length, width, kind=F32),
        stack(length, width),
    ]
    mlp_stacks = [
        stack(length, width),
        stack(length, ff),
        stack(length, ff),
        stack(length, ff),
        stack(length, width, kind=F32),
        stack(length, width),
    ]

    token = []

    def chained(*values):
        if not quick or not token:
            return values
        return lax.optimization_barrier(values + tuple(token))[: len(values)]

    def chain(made):
        token[:] = [made]

    received, hiddens = [], []

    blank = jnp.zeros((8, HALF), F32)

    def number(i):
        return jnp.full((1,), i, jnp.int32)

    def mixer_tick(tick, turn, mix_stacks):
        mix_stacks, hidden = mixer_forward_call(
            number(tick),
            plan,
            spots,
            dealt[tick],
            vec,
            cosine,
            sine,
            corner(turn),
            mixer_weights,
            mix_stacks,
            widths,
            total,
        )
        chain(hidden)
        hiddens.append(hidden)
        return mix_stacks

    def mlp_tick(tick, mlp_stacks):
        (hidden,) = chained(hiddens[tick])
        if tick == 1:
            hidden = after(hidden, dealt[2])
        mlp_stacks, low = mlp_forward_call(
            number(tick), plan, spots, hidden, vec, mlp_weights, mlp_stacks, ff
        )
        return mlp_stacks, low

    def layer_tick(tick, turn, stacks):
        if tick < count:
            one, two = chained(dealt[tick], received[tick - skew])
            seq_in = jnp.where(first, one, two)
        else:
            seq_in = received[tick - skew]
        return layer_forward_call(
            number(tick),
            plan,
            spots,
            seq_in,
            vec,
            cosine,
            sine,
            corner(turn) if tick < steps - 1 else blank,
            mixer_weights + mlp_weights,
            stacks,
            widths,
            total,
            ff,
        )

    mix_stacks = mixer_tick(0, dealt[0], mix_stacks)
    if quick:
        g_down = gather_wholes(w_down[0], hiddens[0])
    deal(count - 1, hiddens[0])
    mix_stacks = mixer_tick(1, hiddens[0], mix_stacks)
    if quick:
        mlp_weights = [share_far(g, hiddens[1]) for g in (g_g, g_u, g_down)]
    for tick in range(steps):
        if tick < skew:
            mlp_stacks, low = mlp_tick(tick, mlp_stacks)
        else:
            stacks, low = layer_tick(tick, low, mix_stacks + mlp_stacks)
            mix_stacks, mlp_stacks = stacks[: len(mix_stacks)], stacks[len(mix_stacks) :]
        chain(low)
        if tick < count:
            received.append(lax.ppermute(low, "section", [(0, 1)]))

    (s_normed, s_conv, s_z, s_gate, s_qkv, s_step, s_probs, s_ssm, s_mixed, s_y, s_hidden,
     s_x) = mix_stacks
    s_normed2, s_g, s_u, s_act, s_final, s_low = mlp_stacks
    mlp_grads = [
        stack(length, width),
        stack(length, ff),
        stack(length, ff),
        stack(8, width, kind=F32),
    ]
    mix_grads = [
        stack(length, width),
        stack(length, tail),
        stack(length, ci),
        stack(length, mi),
        stack(length, width),
        stack(16, ci, kind=F32),
    ]
    incoming, returned = [], [None] * count

    hiddens = []

    def mlp_turn(turn, mlp_grads):
        if turn == count:
            token.append(returned[3])
        (seed,) = chained(incoming[turn - skew])
        return mlp_backward_call(
            number(steps + turn),
            plan,
            mix,
            spots,
            seed,
            vec,
            corner(hiddens[-1]) if turn > count else blank,
            mlp_weights,
            reads,
            mlp_grads,
            ff,
        )

    def mixer_turn(turn, d_hidden, before, mix_grads):
        mix_grads, d_input = mixer_backward_call(
            number(steps + turn),
            plan,
            spots,
            d_hidden,
            vec,
            cosine,
            sine,
            corner(before),
            mixer_weights,
            mix_reads,
            mix_grads,
            widths,
            total,
        )
        send_back(turn, d_input)
        return mix_grads, d_input

    def send_back(turn, d_input):
        if turn < count:
            incoming.append(lax.ppermute(d_input, "section", [(1, 0)]))
        if turn >= skew:
            j = count - 1 - turn + skew
            back = lax.dynamic_index_in_dim(after(s_low, d_input), keep_at[j], 0, keepdims=False)
            back = jnp.where(first, d_input, back)
            returned[j] = swap(back, "rep", j) if j else back

    reads = [s_final, s_hidden, s_g, s_u]
    mix_reads = [s_conv, s_z, s_gate, s_qkv, s_step, s_probs, s_y, s_x]
    d_input = low
    for turn in range(count):
        if turn < skew:
            (seed,) = chained(dealt[count - 1 - turn])
        else:
            one, two = chained(incoming[turn - skew], dealt[count - 1 - turn])
            seed = jnp.where(first, one, two)
        grads, d_input = layer_backward_call(
            number(steps + turn),
            plan,
            mix,
            spots,
            seed,
            vec,
            cosine,
            sine,
            corner(d_input) if turn else blank,
            mixer_weights + mlp_weights,
            reads + mix_reads,
            mlp_grads + mix_grads,
            widths,
            total,
            ff,
        )
        mlp_grads, mix_grads = grads[: len(mlp_grads)], grads[len(mlp_grads) :]
        chain(d_input)
        send_back(turn, d_input)

    for turn in range(count, steps):
        mlp_grads, d_hidden = mlp_turn(turn, mlp_grads)
        chain(d_hidden)
        hiddens.append(d_hidden)
    s_dmlp, s_dg, s_du, small_mlp = mlp_grads
    early = [(s_normed2, s_dg), (s_normed2, s_du), (s_act, s_dmlp)]
    chunks = [Reduction(*pair) for pair in early]

    names = dict(W="begin", A="chips", L="line_in", M="middle", O="line_out", F="finish")
    state = [mix_grads]

    def stages(*words):
        for word in words:
            letter, place = word[0], int(word[1:])
            if letter == "B":
                before = token[0] if quick else hiddens[place - count]
                state[0], made = mixer_turn(place, hiddens[place - count], before, state[0])
            else:
                made = getattr(chunks[place], names[letter])(chained)
            chain(made)

    if quick:
        stages("W1")
        token.append(returned[2])
        stages(
            "W2", "W0", "A2", "B4", "A0", "A1", "L2", "B5"
        )
    else:
        stages("B4", "B5")
    mix_grads = state[0]
    s_dbranch, s_dfirst, s_dconv, s_dgate, s_dinput, small_mix = mix_grads
    late = [
        (s_normed, s_dconv),
        (s_normed, s_dgate),
        (s_ssm, s_dbranch),
        (s_normed, s_dfirst),
        (s_mixed, s_dbranch),
    ]

    mix_sum = jnp.sum(small_mix, axis=0)
    mlp_sum = jnp.sum(small_mlp, axis=0)
    singles = jnp.concatenate(
        [
            mix_sum[V_SBIAS, :heads],
            mix_sum[V_DECAY, :heads],
            jnp.sum(mix_sum[V_SKIP, :mi].reshape(heads, HD), axis=1),
            jnp.sum(mlp_sum[1])[None],
        ]
    )

    def share(v):
        return v.reshape(v.shape[0], n_fsdp, -1).transpose(1, 0, 2).reshape(n_fsdp, -1)

    shares = [
        share(mix_sum[: taps + 1]),
        share(mix_sum[V_GS : V_GS + 1, :mi]),
        share(mix_sum[V_G1 : V_G1 + 1, :width]),
        share(mlp_sum[:1]),
        jnp.broadcast_to(singles[None], (n_fsdp, singles.size)),
    ]
    cuts = [v.shape[1] for v in shares]
    flat = jnp.concatenate(shares, axis=1)

    if quick:
        spare = -(-flat.shape[1] // rows)
        flat = jnp.pad(flat, ((0, 0), (0, spare * rows - flat.shape[1])))
        riders = flat.astype(BF).reshape(2, 2, rows, spare)
        column = tail - HALF + heads
        chunks += [Reduction(*pair) for pair in late]
        chunks[6].riders = (riders, column)
        stages(
            "W4", "M2", "L0", "W5", "W3", "W7", "O2", "A4", "L1", "M0", "A5", "A3", "W6", "A7"
        )
        token.append(returned[1])
        stages(
            "L4", "M1", "O0", "F2", "A6", "L3", "M4", "L7", "O1", "F0", "L6", "M3", "L5", "M7",
            "O4", "F1", "M6", "O3", "M5", "F4", "O7", "O6", "F3", "O5", "F7", "F6", "F5"
        )
        reduced = [chunk.result for chunk in chunks]
        flat = reduced[6][:, column : column + spare].reshape(-1)
        ends = chained(*returned, s_dinput, s_low)
        returned, s_dinput, s_low = ends[:count], ends[-2], ends[-1]
    else:

        def reduce_all(pair):
            grad = weight_grad(*pair)
            own = lax.psum_scatter(grad, "fsdp", scatter_dimension=0, tiled=True)
            return lax.psum(own, "rep").astype(F32)

        reduced = [reduce_all(pair) for pair in early + late]
        flat = lax.psum(lax.psum_scatter(flat, "fsdp", tiled=True), "rep").reshape(-1)
    grad_gate, grad_up, grad_down, grad_conv, grad_sgate, grad_ssm_out, grad_first, grad_attn = reduced

    parts, begin = [], 0
    for cut in cuts[:-1] + [heads] * 3 + [1]:
        parts.append(flat[begin : begin + cut])
        begin += cut
    convs = parts[0].reshape(taps + 1, -1)
    loss = jnp.where(first, lax.ppermute(parts[-1], "section", [(1, 0)]), parts[-1])[0]

    restored = jnp.zeros((count, length, width), BF)
    for j in range(count):
        restored = lax.dynamic_update_index_in_dim(restored, returned[j], send_at[j], 0)
    activations = jnp.where(first, s_low, restored)[None]
    gradients = jnp.where(first, restored, s_dinput)[None]
    s0 = qw + 2 * kw
    return (
        activations,
        gradients,
        loss / (valid_count * width),
        parts[2][None],
        grad_first[None, :, :qw],
        grad_first[None, :, qw : qw + kw],
        grad_first[None, :, qw + kw : s0],
        grad_attn[None],
        grad_sgate[None],
        grad_conv[None],
        grad_first[None, :, s0 : s0 + heads],
        convs[None, :taps],
        convs[None, taps],
        parts[4][None],
        parts[5][None],
        parts[6][None],
        parts[1][None],
        grad_ssm_out[None],
        parts[3][None],
        grad_gate[None],
        grad_up[None],
        grad_down[None],
    )


def solution(mesh):
    rows3 = P("section", "fsdp", None)
    pair = P("section", "fsdp")
    one = P("section", None)
    data = P(("fsdp", "rep"), None, None)
    taps = P("section", None, "fsdp")
    in_specs = (data, data, P(), P(), P(), pair) + (rows3,) * 7
    in_specs += (taps, pair, one, one, one, pair, rows3, pair, rows3, rows3, rows3)
    placed = P("section", ("fsdp", "rep"), None, None)
    out_specs = (placed, placed, P(), pair) + (rows3,) * 7
    out_specs += (taps, pair, one, one, one, pair, rows3, pair, rows3, rows3, rows3)
    return jax.shard_map(body, mesh=mesh, in_specs=in_specs, out_specs=out_specs, check_vma=False)
```

```python
import math
import functools

import jax
import jax.numpy as jnp
from jax import lax
from jax.experimental import pallas as pl
from jax.experimental.pallas import tpu as pltpu
from jax.sharding import PartitionSpec as P

HD = 64
EPSILON = 1e-05
ROPE_BASE = 100000000000.0
MASKED = -1e30
F32 = jnp.float32
BF = jnp.bfloat16
TILE = 256
HALF = 128
HB = pl.BlockSpec(memory_space=pltpu.HBM)
VM = pl.BlockSpec(memory_space=pltpu.VMEM)
SM = pl.BlockSpec(memory_space=pltpu.SMEM)


def dot(a, b):
    return jnp.dot(a, b, preferred_element_type=F32)


def dot_nt(a, b):
    return lax.dot_general(a, b, (((1,), (1,)), ((), ())), preferred_element_type=F32)


def dot_tn(a, b):
    return lax.dot_general(a, b, (((0,), (0,)), ((), ())), preferred_element_type=F32)


def sigmoid(v):
    return 0.5 * jnp.tanh(0.5 * v) + 0.5


def lanes(i, width=TILE):
    return pl.ds(pl.multiple_of(i * width, width), width)


def iota(shape, axis):
    return lax.broadcasted_iota(jnp.int32, shape, axis)


def split2(v):
    hi = v.astype(BF)
    return hi, (v - hi.astype(F32)).astype(BF)


def split3(v):
    hi = v.astype(BF)
    rest = v - hi.astype(F32)
    mid = rest.astype(BF)
    return hi, mid, (rest - mid.astype(F32)).astype(BF)


def expand_matrix(tile):
    row = jnp.bitwise_and(iota((TILE, TILE), 0), HALF - 1)
    col = jnp.right_shift(iota((TILE, TILE), 1), 6) + tile * (TILE // HD)
    return jnp.where(row == col, 1.0, 0.0).astype(BF)


def reduce_matrix(tile):
    row = jnp.right_shift(iota((TILE, HALF), 0), 6) + tile * (TILE // HD)
    col = iota((TILE, HALF), 1)
    return jnp.where(row == col, 1.0, 0.0).astype(BF)


def both(v):
    return jnp.concatenate(split2(v), axis=1)


def rope(v, cosine, sine, first):
    turned = jnp.where(first, pltpu.roll(v, HALF - HD // 2, 1), pltpu.roll(v, HD // 2, 1))
    return v * cosine + turned * sine


def start_all(groups, sems):
    waits, at = [], 0
    for group in groups:
        copies = []
        for source, target in group:
            copies.append(pltpu.make_async_copy(source, target, sems.at[at]))
            at += 1
        for copy in copies:
            copy.start()
        waits.append(copies)

    def wait(i):
        for copy in waits[i]:
            copy.wait()

    return wait


def row_pieces(pieces, spots, scratch, columns):
    if len(pieces) == 1:
        return [(pieces[0].at[:, a], scratch.at[:, b]) for a, b in columns]
    unit = pieces[-1].shape[0]
    if len(pieces) == 4:
        places = [jnp.right_shift(spots[i], 1) for i in (0, 1, 2, 4)]
    else:
        places = [spots[i] for i in range(6)]
    out = []
    for a, b in columns:
        for place, piece in zip(places, pieces):
            rows = pl.ds(pl.multiple_of(place * unit, unit), piece.shape[0])
            out.append((piece.at[:, a], scratch.at[rows, b]))
    return out


def out_pieces(pieces, spots, scratch, inner):
    if len(pieces) == 1:
        return [(pieces[0], scratch)]
    total, width = scratch.shape
    n = total // pieces[0].shape[0]
    cut, rest = inner // n, (total - inner) // n
    out = []
    for i, piece in enumerate(pieces):
        block, side = jnp.right_shift(spots[i], 1), jnp.bitwise_and(spots[i], 1)
        span = piece.shape[1]
        cols = slice(0, width)
        if span < width:
            cols = pl.ds(pl.multiple_of(side * span, span), span)
        upper = pl.ds(pl.multiple_of(block * cut, cut), cut)
        lower = pl.ds(pl.multiple_of(inner + block * rest, rest), rest)
        out.append((piece.at[:cut, :], scratch.at[upper, cols]))
        out.append((piece.at[cut:, :], scratch.at[lower, cols]))
    return out


def saver(slot, active, sems):
    stores = []

    def save(buffer, stack, at=slot):
        copy = pltpu.make_async_copy(buffer, stack.at[at], sems.at[len(stores)])
        pl.when(active)(copy.start)
        stores.append(copy)

    def finish():
        for copy in stores:
            pl.when(active)(copy.wait)

    return save, finish


def in_hbm(a):
    return pltpu.with_memory_space_constraint(a, pltpu.HBM)


def call(body, name, scalars, spots, ordinary, weights, reads, stacks, result, scratch, limit, work):
    fresh = isinstance(stacks[0], jax.ShapeDtypeStruct)
    flat = [piece for group in weights for piece in group]
    counts = [len(group) for group in weights]
    kept = [] if fresh else list(stacks)
    ahead = len(scalars) + 1 + len(ordinary) + len(flat) + len(reads)
    n = len(stacks)
    cuts = [len(scalars), 1, len(ordinary), len(flat), len(reads), len(kept), n, 1]

    def kernel(*refs):
        parts, at = [], 0
        for cut in cuts:
            parts.append(refs[at : at + cut])
            at += cut
        groups, begin = [], 0
        for c in counts:
            groups.append(parts[3][begin : begin + c])
            begin += c
        for _ in body(
            parts[0], parts[1][0], parts[2], groups, parts[4], parts[6], parts[7][0], refs[at:]
        ):
            pass

    out = pl.pallas_call(
        kernel,
        out_shape=[pltpu.HBM(s.shape, s.dtype) for s in stacks] + [result],
        in_specs=[SM] * (len(scalars) + 1)
        + [VM] * len(ordinary)
        + [HB] * (len(flat) + len(reads) + len(kept)),
        out_specs=[HB] * n + [VM],
        scratch_shapes=scratch,
        input_output_aliases={} if fresh else {ahead + i: i for i in range(n)},
        compiler_params=pltpu.CompilerParams(vmem_limit_bytes=limit * 1024 * 1024),
        cost_estimate=pl.CostEstimate(
            flops=work * 100000000, bytes_accessed=1000000, transcendentals=0
        ),
        name=name,
    )(*scalars, spots, *ordinary, *(in_hbm(a) for a in flat + list(reads) + kept))
    return list(out[:n]), out[n]


V_TAP, V_CBIAS, V_GS, V_SKIP, V_G1, V_G2, V_SBIAS, V_DECAY = 0, 4, 5, 6, 7, 8, 9, 10


def scan_terms(step_raw, vec_ref, heads):
    lane = iota(step_raw.shape, 1)
    pre = step_raw + vec_ref[V_SBIAS : V_SBIAS + 1, :HALF]
    soft = jnp.maximum(pre, 0.0) + jnp.log1p(jnp.exp(-jnp.abs(pre)))
    step = jnp.where(lane < heads, soft, 0.0)
    change = step * vec_ref[V_DECAY : V_DECAY + 1, :HALF]
    length = step.shape[0]
    lower = jnp.where(
        iota((length, length), 0) >= iota((length, length), 1), 1.0, 0.0
    ).astype(BF)
    run = sum(dot(lower, part) for part in split3(change))
    middle = run[HALF - 1 : HALF, :]
    bend = jnp.where(iota(run.shape, 0) < HALF, middle - run, run - middle)
    bend = jnp.exp(jnp.minimum(bend, 0.0))
    return pre, step, change, run, bend


def broadcast_runs(run, run_wide, heads):
    for h in range(heads):
        run_wide[:, h * HALF : (h + 1) * HALF] = jnp.broadcast_to(
            run[:, h : h + 1], (run.shape[0], HALF)
        )


def mix_forward(widths, scalars, spots, ordinary, weights, reads, stacks, hidden_ref, scratch):
    ci, mi, qw, kw, heads = widths
    index_ref, slot_ref = scalars
    base = 4 * index_ref[0]
    x_ref, vec_ref, cos_ref, sin_ref, _ = ordinary
    w_first, w_conv, w_gate, w_out = weights
    (win, wout, normed, conv_raw, z, xbc, gate_raw, qkv, step_raw, probs, branch, mixed_all, y,
     gated, run_wide, run_row, step_two, bend_two, in_sem, out_sem) = scratch
    (s_normed, s_conv, s_z, s_gate, s_qkv, s_step, s_probs, s_ssm, s_mixed, s_y, s_hidden,
     s_x) = stacks
    g0 = ci
    q0 = ci + mi
    total = win.shape[1]
    tail = total - q0
    wait = start_all(
        [
            row_pieces(w_first, spots, win, [(slice(0, tail), slice(q0, total))]),
            row_pieces(w_conv, spots, win, [(slice(0, ci), slice(0, ci))]),
            row_pieces(w_gate, spots, win, [(slice(0, mi), slice(g0, q0))]),
            out_pieces(w_out, spots, wout, mi),
        ],
        in_sem,
    )
    save, finish = saver(slot_ref[base], slot_ref[base + 1] > 0, out_sem)
    yield

    length = x_ref.shape[0]
    x = x_ref[...].astype(F32)
    rate = lax.rsqrt(jnp.mean(x * x, axis=-1, keepdims=True) + EPSILON)
    normed[...] = (x * rate * vec_ref[V_G1 : V_G1 + 1, : x.shape[1]]).astype(BF)
    save(normed, s_normed)
    lane_first = jnp.bitwise_and(iota((length, HALF), 1), HD - 1) < HD // 2
    half_low = iota((length, HALF), 1) < HD

    wait(0)
    cosine, sine = cos_ref[...], sin_ref[...]
    n_rope = (qw + kw) // HALF
    for t in range((total - q0) // HALF // 2):
        raw = dot(normed[...], win[:, q0 + t * TILE : q0 + (t + 1) * TILE])
        for part in range(2):
            c = 2 * t + part
            piece = raw[:, part * HALF : (part + 1) * HALF]
            if c < n_rope:
                piece = rope(piece, cosine, sine, lane_first)
            if c < n_rope + kw // HALF:
                qkv[:, c * HALF : (c + 1) * HALF] = piece.astype(BF)
            else:
                step_raw[...] = piece
    if ((total - q0) // HALF) % 2:
        step_raw[...] = dot(normed[...], win[:, total - HALF : total])
    save(qkv, s_qkv)
    save(step_raw, s_step)

    wait(1)
    row = iota((length, TILE), 0)

    def conv_tile(t, carry):
        cols = lanes(t)
        raw = dot(normed[...], win[:, cols])
        conv_raw[:, cols] = raw.astype(BF)
        total_z = vec_ref[V_CBIAS : V_CBIAS + 1, cols] + raw * vec_ref[3:4, cols]
        for back in range(1, 4):
            moved = jnp.where(row >= back, pltpu.roll(raw, back, 0), 0.0)
            total_z = total_z + moved * vec_ref[3 - back : 4 - back, cols]
        z[:, cols] = total_z.astype(BF)
        xbc[:, cols] = (total_z * sigmoid(total_z)).astype(BF)
        return carry

    lax.fori_loop(0, ci // TILE, conv_tile, 0, unroll=True)
    save(conv_raw, s_conv)
    save(z, s_z)

    wait(2)

    def gate_tile(t, carry):
        raw = dot(normed[...], win[:, pl.ds(pl.multiple_of(g0 + t * TILE, TILE), TILE)])
        gate_raw[:, lanes(t)] = raw.astype(BF)
        return carry

    lax.fori_loop(0, mi // TILE, gate_tile, 0, unroll=True)
    save(gate_raw, s_gate)

    yield

    keys, values = qkv[:, qw : qw + kw], qkv[:, qw + kw : qw + 2 * kw]
    keys_far, values_far = pltpu.roll(keys.astype(F32), HD, 1).astype(BF), pltpu.roll(
        values.astype(F32), HD, 1
    ).astype(BF)
    causal_top = iota((HALF, HALF), 1) <= iota((HALF, HALF), 0)
    causal_low = iota((HALF, length), 1) <= iota((HALF, length), 0) + HALF
    pairs = qw // HALF
    groups = kw // HD
    probs_zero = jnp.zeros((HALF, HALF), BF)
    for pair in range(pairs):
        group = pair // (pairs // groups)
        keep = half_low if group == 0 else jnp.logical_not(half_low)
        keys_two = jnp.where(keep, keys, keys_far)
        values_two = jnp.where(keep, values, values_far)
        query = qkv[:, pair * HALF : (pair + 1) * HALF] * jnp.asarray(HD ** (-0.5), BF)
        results = []
        for side in range(2):
            own = half_low if side == 0 else jnp.logical_not(half_low)
            q = jnp.where(own, query, jnp.zeros_like(query))
            at = (2 * pair + side) * length
            out = []
            for lo, causal in ((0, causal_top), (1, causal_low)):
                width = HALF if lo == 0 else length
                scores = dot_nt(q[lo * HALF : (lo + 1) * HALF], keys_two[:width])
                scores = jnp.where(causal, scores, MASKED)
                top = jnp.max(scores, axis=-1, keepdims=True)
                weights = jnp.exp(scores - top)
                weights = weights / jnp.sum(weights, axis=-1, keepdims=True)
                weights = weights.astype(BF)
                if lo == 0:
                    probs[at : at + HALF, :HALF] = weights
                    probs[at : at + HALF, HALF:] = probs_zero
                else:
                    probs[at + HALF : at + length, :] = weights
                out.append(dot(weights, values_two[:width]))
            results.append(jnp.concatenate(out, axis=0))
        mixed = jnp.where(half_low, results[0], results[1])
        mixed_all[:, pair * HALF : (pair + 1) * HALF] = mixed.astype(BF)
    save(probs, s_probs)
    save(mixed_all, s_mixed)

    pre, step, change, run, bend = scan_terms(step_raw[...], vec_ref, heads)
    turned = run.T
    run_row[:HALF, :] = turned[:, :HALF]
    run_row[HALF:, :] = turned[:, HALF:]
    broadcast_runs(run, run_wide, heads)
    step_two[...] = both(step)
    bend_two[...] = both(bend)
    b_in, c_in = xbc[:, mi : mi + HALF], xbc[:, mi + HALF : mi + 2 * HALF]
    tops = [dot_nt(c_in[c * HALF : (c + 1) * HALF], b_in[c * HALF : (c + 1) * HALF]) for c in (0, 1)]
    cross = dot_nt(c_in[HALF:], b_in[:HALF]).astype(BF)
    pair_low = iota((HALF, HALF), 1) < HD
    tops = [jnp.where(causal_top, t, 0.0) for t in tops]

    def mix_tile(t, squares):
        cols = lanes(t)
        spread = expand_matrix(t)
        x_in = xbc[:, cols].astype(F32)
        scaled = (dot(step_two[...], spread) * x_in).astype(BF)
        bends = dot(bend_two[...], spread)
        u = (bends[:HALF] * scaled[:HALF].astype(F32)).astype(BF)
        far = dot(cross, u) * bends[HALF:]
        parts = []
        for p in range(TILE // HALF):
            block = []
            for c in range(2):
                rows = slice(c * HALF, (c + 1) * HALF)
                weights = []
                for side in range(2):
                    h = t * (TILE // HD) + 2 * p + side
                    wide = run_wide[rows, lanes(h, HALF)]
                    line = run_row[pl.ds(c * HALF + h, 1), :]
                    decay = jnp.exp(jnp.minimum(wide - line, 0.0))
                    weights.append((decay * tops[c]).astype(BF))
                xs = scaled[rows, p * HALF : (p + 1) * HALF]
                zero = jnp.zeros_like(xs)
                right = jnp.concatenate(
                    [jnp.where(pair_low, xs, zero), jnp.where(pair_low, zero, xs)], axis=0
                )
                block.append(dot(jnp.concatenate(weights, axis=1), right))
            parts.append(jnp.concatenate(block, axis=0))
        out = jnp.concatenate(parts, axis=1)
        out = out + jnp.concatenate([jnp.zeros_like(far), far], axis=0)
        out = out + vec_ref[V_SKIP : V_SKIP + 1, cols] * x_in
        y[:, cols] = out.astype(BF)
        g = gate_raw[:, cols].astype(F32)
        out = out * (g * sigmoid(g))
        gated[:, cols] = out
        return squares + jnp.sum(out * out, axis=-1, keepdims=True)

    squares = lax.fori_loop(0, mi // TILE, mix_tile, jnp.zeros((length, 1), F32), unroll=True)
    save(y, s_y)
    rate = lax.rsqrt(squares * (1.0 / mi) + EPSILON)
    branch[...] = (gated[...] * rate * vec_ref[V_GS : V_GS + 1, :mi]).astype(BF)
    save(branch, s_ssm)

    wait(3)

    def out_tile(t, carry):
        cols = lanes(t)
        hidden_ref[:, cols] = (
            x_ref[:, cols].astype(F32)
            + dot(branch[...], wout[:mi, cols])
            + dot(mixed_all[...], wout[mi:, cols])
        )
        return carry

    lax.fori_loop(0, wout.shape[1] // TILE, out_tile, 0, unroll=True)
    save(hidden_ref, s_hidden)
    save(x_ref, s_x)
    yield
    finish()


def mixer_forward_scratch(length, width, widths, total):
    ci, mi, qw, kw, heads = widths
    return [
        pltpu.VMEM((width, total), BF),
        pltpu.VMEM((mi + qw, width), BF),
        pltpu.VMEM((length, width), BF),
        pltpu.VMEM((length, ci), BF),
        pltpu.VMEM((length, ci), BF),
        pltpu.VMEM((length, ci), BF),
        pltpu.VMEM((length, mi), BF),
        pltpu.VMEM((length, qw + 2 * kw), BF),
        pltpu.VMEM((length, HALF), F32),
        pltpu.VMEM((qw // HD * length, length), BF),
        pltpu.VMEM((length, mi), BF),
        pltpu.VMEM((length, qw), BF),
        pltpu.VMEM((length, mi), BF),
        pltpu.VMEM((length, mi), F32),
        pltpu.VMEM((length, heads * HALF), F32),
        pltpu.VMEM((length, HALF), F32),
        pltpu.VMEM((length, 2 * HALF), BF),
        pltpu.VMEM((length, 2 * HALF), BF),
        pltpu.SemaphoreType.DMA((32,)),
        pltpu.SemaphoreType.DMA((12,)),
    ]


def mixer_forward_call(
    index, slot, spots, x, vec, cosine, sine, turn, weights, stacks, widths, total
):
    ci, mi, qw, kw, heads = widths
    length, width = x.shape
    scratch = mixer_forward_scratch(length, width, widths, total)
    return call(
        functools.partial(mix_forward, widths),
        "mixer_forward",
        [index, slot],
        spots,
        [x, vec, cosine, sine, turn],
        weights,
        [],
        stacks,
        jax.ShapeDtypeStruct((length, width), F32),
        scratch,
        44,
        200,
    )


def mlp_forward(scalars, spots, ordinary, weights, reads, stacks, low_ref, scratch):
    index_ref, slot_ref = scalars
    base = 4 * index_ref[0]
    hidden_ref, vec_ref = ordinary
    w_g, w_u, w_down = weights
    wgu, wdown, normed, gate_low, up_low, act, final, in_sem, out_sem = scratch
    s_normed, s_gate, s_up, s_act, s_final, s_low = stacks
    ff = wdown.shape[0]
    parts = 2
    step = ff // parts
    groups = []
    for i in range(parts):
        a = slice(i * step, (i + 1) * step)
        b = slice(ff + i * step, ff + (i + 1) * step)
        groups.append(
            row_pieces(w_g, spots, wgu, [(a, a)]) + row_pieces(w_u, spots, wgu, [(a, b)])
        )
    groups.append(row_pieces(w_down, spots, wdown, [(slice(0, wdown.shape[1]),) * 2]))
    wait = start_all(groups, in_sem)
    save, finish = saver(slot_ref[base], slot_ref[base + 1] > 0, out_sem)
    yield
    valid = jnp.where(iota((hidden_ref.shape[0], 1), 0) < slot_ref[base + 2], 1.0, 0.0)

    hidden = hidden_ref[...]
    rate = lax.rsqrt(jnp.mean(hidden * hidden, axis=-1, keepdims=True) + EPSILON)
    normed[...] = (hidden * rate * vec_ref[V_G2 : V_G2 + 1, : hidden.shape[1]]).astype(BF)
    save(normed, s_normed)
    for i in range(parts):
        wait(i)

        def up_tile(t, carry):
            a = pl.ds(pl.multiple_of(i * step + t * TILE, TILE), TILE)
            b = pl.ds(pl.multiple_of(ff + i * step + t * TILE, TILE), TILE)
            gate = dot(normed[...], wgu[:, a])
            up = dot(normed[...], wgu[:, b])
            gate_low[:, a] = gate.astype(BF)
            up_low[:, a] = up.astype(BF)
            act[:, a] = (gate * sigmoid(gate) * up).astype(BF)
            return carry

        lax.fori_loop(0, step // TILE, up_tile, 0, unroll=True)
    save(gate_low, s_gate)
    save(up_low, s_up)
    save(act, s_act)
    wait(parts)

    def down_tile(t, carry):
        cols = lanes(t)
        out = (hidden_ref[:, cols] + dot(act[...], wdown[:, cols])) * valid
        final[:, cols] = out
        low_ref[:, cols] = out.astype(BF)
        return carry

    lax.fori_loop(0, wdown.shape[1] // TILE, down_tile, 0, unroll=True)
    save(final, s_final)
    save(low_ref, s_low, slot_ref[base + 3])
    yield
    finish()


def mlp_forward_scratch(length, width, ff):
    return [
        pltpu.VMEM((width, 2 * ff), BF),
        pltpu.VMEM((ff, width), BF),
        pltpu.VMEM((length, width), BF),
        pltpu.VMEM((length, ff), BF),
        pltpu.VMEM((length, ff), BF),
        pltpu.VMEM((length, ff), BF),
        pltpu.VMEM((length, width), F32),
        pltpu.SemaphoreType.DMA((32,)),
        pltpu.SemaphoreType.DMA((6,)),
    ]


def mlp_forward_call(index, slot, spots, hidden, vec, weights, stacks, ff):
    length, width = hidden.shape
    scratch = mlp_forward_scratch(length, width, ff)
    return call(
        mlp_forward,
        "mlp_forward",
        [index, slot],
        spots,
        [hidden, vec],
        weights,
        [],
        stacks,
        jax.ShapeDtypeStruct((length, width), BF),
        scratch,
        32,
        3,
    )


def mlp_backward(scalars, spots, ordinary, weights, reads, stacks, d_hidden_ref, scratch):
    index_ref, slot_ref, mix_ref = scalars
    base = 4 * index_ref[0]
    target_ref, vec_ref, _ = ordinary
    w_g, w_u, w_down = weights
    s_final, s_hidden, s_gate, s_up = reads
    (wgu, wdown, final, hidden, gate_low, up_low, d_mlp, d_gu, d_sum, d_normed, small, in_sem,
     out_sem) = scratch
    s_dmlp, s_dgate, s_dup, s_small = stacks
    slot = slot_ref[base]
    ff = wdown.shape[0]
    wait = start_all(
        [
            [(s_final.at[slot], final)],
            [(s_gate.at[slot], gate_low), (s_up.at[slot], up_low)]
            + row_pieces(w_down, spots, wdown, [(slice(0, wdown.shape[1]),) * 2]),
            row_pieces(w_g, spots, wgu, [(slice(0, ff), slice(0, ff))])
            + row_pieces(w_u, spots, wgu, [(slice(0, ff), slice(ff, 2 * ff))]),
            [(s_hidden.at[slot], hidden)],
        ],
        in_sem,
    )
    save, finish = saver(slot, slot_ref[base + 1] > 0, out_sem)
    yield
    wait(0)
    target = target_ref[...].astype(F32)
    valid = jnp.where(iota((target_ref.shape[0], 1), 0) < slot_ref[base + 2], 1.0, 0.0)
    misfit = final[...] - target
    loss = jnp.sum(valid * misfit * misfit, axis=0, keepdims=True)
    seed = valid * jnp.where(mix_ref[0] > 0.5, target, mix_ref[1] * misfit)
    d_sum[...] = seed
    d_mlp[...] = seed.astype(BF)
    save(d_mlp, s_dmlp)
    wait(1)

    def act_tile(t, carry):
        a = lanes(t)
        b = pl.ds(pl.multiple_of(ff + t * TILE, TILE), TILE)
        d_act = dot_nt(d_mlp[...], wdown[a, :])
        gate, up = gate_low[:, a].astype(F32), up_low[:, a].astype(F32)
        s = sigmoid(gate)
        swish = gate * s
        d_gu[:, a] = (d_act * up * (s + swish - swish * s)).astype(BF)
        d_gu[:, b] = (d_act * swish).astype(BF)
        return carry

    lax.fori_loop(0, ff // TILE, act_tile, 0, unroll=True)
    save(d_gu.at[:, :ff], s_dgate)
    save(d_gu.at[:, ff:], s_dup)
    wait(2)
    yield

    def back_tile(t, carry):
        rows = lanes(t)
        d_normed[:, rows] = dot_nt(d_gu[...], wgu[rows, :])
        return carry

    lax.fori_loop(0, wgu.shape[0] // TILE, back_tile, 0, unroll=True)
    wait(3)
    h = hidden[...]
    width = h.shape[1]
    rate = lax.rsqrt(jnp.mean(h * h, axis=-1, keepdims=True) + EPSILON)
    unit = h * rate
    d_n = d_normed[...]
    small[...] = jnp.zeros_like(small)
    small[0:1, :width] = jnp.sum(d_n * unit, axis=0, keepdims=True)
    small[1:2, :width] = loss
    save(small, s_small)
    d_n = d_n * vec_ref[V_G2 : V_G2 + 1, :width]
    d_hidden_ref[...] = d_sum[...] + rate * (
        d_n - unit * jnp.mean(d_n * unit, axis=-1, keepdims=True)
    )
    yield
    finish()


def mlp_backward_scratch(length, width, ff, small):
    return [
        pltpu.VMEM((width, 2 * ff), BF),
        pltpu.VMEM((ff, width), BF),
        pltpu.VMEM((length, width), F32),
        pltpu.VMEM((length, width), F32),
        pltpu.VMEM((length, ff), BF),
        pltpu.VMEM((length, ff), BF),
        pltpu.VMEM((length, width), BF),
        pltpu.VMEM((length, 2 * ff), BF),
        pltpu.VMEM((length, width), F32),
        pltpu.VMEM((length, width), F32),
        pltpu.VMEM(small, F32),
        pltpu.SemaphoreType.DMA((32,)),
        pltpu.SemaphoreType.DMA((4,)),
    ]


def mlp_backward_call(index, slot, mix, spots, target, vec, turn, weights, reads, stacks, ff):
    length, width = target.shape
    scratch = mlp_backward_scratch(length, width, ff, stacks[-1].shape[1:])
    return call(
        mlp_backward,
        "mlp_backward",
        [index, slot, mix],
        spots,
        [target, vec, turn],
        weights,
        reads,
        stacks,
        jax.ShapeDtypeStruct((length, width), F32),
        scratch,
        40,
        3,
    )


def column_sum(v):
    return jnp.sum(v, axis=0, keepdims=True)


def mix_backward(
    widths, scalars, spots, ordinary, weights, reads, stacks, d_input_ref, scratch
):
    ci, mi, qw, kw, heads = widths
    index_ref, slot_ref = scalars
    base = 4 * index_ref[0]
    d_hidden_ref, vec_ref, cos_ref, sin_ref, _ = ordinary
    w_first, w_conv, w_gate, w_out = weights
    s_conv, s_z, s_gate, s_qkv, s_step, s_probs, s_y, s_x = reads
    (win, wout, conv_raw, z, gate_raw, qkv, step_raw, probs, y, x_low, d_branch, d_proj, d_mixed,
     d_ssm, d_z, d_normed, run_wide, run_row, step_two, bend_two, tops, d_tops, run_acc, step_acc,
     small, in_sem, out_sem) = scratch
    s_dbranch, s_dfirst, s_dconv, s_dgate, s_dinput, s_small = stacks
    slot = slot_ref[base]
    g0, q0 = ci, ci + mi
    s0 = q0 + qw + 2 * kw
    total = win.shape[1]
    tail = total - q0
    length, width = d_hidden_ref.shape
    wait = start_all(
        [
            out_pieces(w_out, spots, wout, mi),
            [(s_probs.at[slot], probs), (s_qkv.at[slot], qkv)],
            [(s_step.at[slot], step_raw), (s_gate.at[slot], gate_raw), (s_y.at[slot], y)],
            [(s_z.at[slot], z)],
            [(s_conv.at[slot], conv_raw)],
            row_pieces(w_first, spots, win, [(slice(0, tail), slice(q0, total))])
            + row_pieces(w_conv, spots, win, [(slice(0, ci), slice(0, ci))])
            + row_pieces(w_gate, spots, win, [(slice(0, mi), slice(g0, q0))]),
            [(s_x.at[slot], x_low)],
        ],
        in_sem,
    )
    save, finish = saver(slot, slot_ref[base + 1] > 0, out_sem)
    yield
    small[...] = jnp.zeros_like(small)
    d_branch[...] = d_hidden_ref[...].astype(BF)
    save(d_branch, s_dbranch)
    wait(0)
    for t in range(qw // TILE):
        rows = slice(mi + t * TILE, mi + (t + 1) * TILE)
        d_mixed[:, t * TILE : (t + 1) * TILE] = dot_nt(d_branch[...], wout[rows, :]).astype(BF)

    lane_first = jnp.bitwise_and(iota((length, HALF), 1), HD - 1) < HD // 2
    half_low = iota((length, HALF), 1) < HD
    cosine, sine = cos_ref[...], -sin_ref[...]
    wait(1)
    keys, values = qkv[:, qw : qw + kw], qkv[:, qw + kw : qw + 2 * kw]
    keys_far, values_far = pltpu.roll(keys.astype(F32), HD, 1).astype(BF), pltpu.roll(
        values.astype(F32), HD, 1
    ).astype(BF)
    pairs = qw // HALF
    groups = kw // HD
    scale = HD ** (-0.5)
    d_keys = [jnp.zeros((length, HALF), F32) for _ in range(groups)]
    d_values = [jnp.zeros((length, HALF), F32) for _ in range(groups)]
    for pair in range(pairs):
        group = pair // (pairs // groups)
        keep = half_low if group == 0 else jnp.logical_not(half_low)
        keys_two = jnp.where(keep, keys, keys_far)
        values_two = jnp.where(keep, values, values_far)
        cols = slice(pair * HALF, (pair + 1) * HALF)
        query, d_out = qkv[:, cols], d_mixed[:, cols]
        results = []
        for side in range(2):
            own = half_low if side == 0 else jnp.logical_not(half_low)
            q = jnp.where(own, query, jnp.zeros_like(query))
            d_o = jnp.where(own, d_out, jnp.zeros_like(d_out))
            at = (2 * pair + side) * length
            weights = probs[at : at + length, :]
            wide = weights.astype(F32)
            d_weights = dot_nt(d_o, values_two)
            inner = wide * d_weights
            d_scores = (inner - wide * jnp.sum(inner, axis=-1, keepdims=True)).astype(BF)
            results.append(dot(d_scores, keys_two))
            d_keys[group] = d_keys[group] + dot_tn(d_scores, q)
            d_values[group] = d_values[group] + dot_tn(weights, d_o)
        d_q = jnp.where(half_low, results[0], results[1]) * scale
        d_proj[:, q0 + pair * HALF : q0 + (pair + 1) * HALF] = rope(
            d_q, cosine, sine, lane_first
        ).astype(BF)
    folded = [v + pltpu.roll(v, HD, 1) for v in d_keys]
    d_k = jnp.where(half_low, folded[0], folded[1]) * scale
    d_proj[:, q0 + qw : q0 + qw + kw] = rope(d_k, cosine, sine, lane_first).astype(BF)
    folded = [v + pltpu.roll(v, HD, 1) for v in d_values]
    d_proj[:, q0 + qw + kw : s0] = jnp.where(half_low, folded[0], folded[1]).astype(BF)

    wait(2)

    def norm_tile(t, sums):
        cols = lanes(t)
        d_s = dot_nt(d_branch[...], wout[cols, :])
        d_ssm[:, cols] = d_s
        g = gate_raw[:, cols].astype(F32)
        gated = y[:, cols].astype(F32) * (g * sigmoid(g))
        d_n = d_s * vec_ref[V_GS : V_GS + 1, cols]
        return (
            sums[0] + jnp.sum(gated * gated, axis=-1, keepdims=True),
            sums[1] + jnp.sum(gated * d_n, axis=-1, keepdims=True),
        )

    zero_col = jnp.zeros((length, 1), F32)
    squares, along = lax.fori_loop(0, mi // TILE, norm_tile, (zero_col, zero_col), unroll=True)
    rate = lax.rsqrt(squares * (1.0 / mi) + EPSILON)
    along = along * (rate * rate) * (1.0 / mi)

    pre, step, change, run, bend = scan_terms(step_raw[...], vec_ref, heads)
    turned = run.T
    run_row[:HALF, :] = turned[:, :HALF]
    run_row[HALF:, :] = turned[:, HALF:]
    broadcast_runs(run, run_wide, heads)
    step_two[...] = both(step)
    bend_two[...] = both(bend)
    wait(3)
    zb = z[:, mi : mi + 2 * HALF].astype(F32)
    sb = sigmoid(zb)
    bc = (zb * sb).astype(BF)
    b_in, c_in = bc[:, :HALF], bc[:, HALF:]
    causal = iota((HALF, HALF), 1) <= iota((HALF, HALF), 0)
    for c in range(2):
        rows = slice(c * HALF, (c + 1) * HALF)
        tops[rows, :] = jnp.where(causal, dot_nt(c_in[rows], b_in[rows]), 0.0)
    cross = dot_nt(c_in[HALF:], b_in[:HALF])
    cross_turned = cross.T.astype(BF)
    cross = cross.astype(BF)
    pair_low = iota((HALF, HALF), 1) < HD
    d_tops[...] = jnp.zeros_like(d_tops)
    run_acc[...] = jnp.zeros_like(run_acc)
    step_acc[...] = jnp.zeros_like(step_acc)

    def mix_tile(t, carry):
        cols = lanes(t)
        g = gate_raw[:, cols].astype(F32)
        s = sigmoid(g)
        swish = g * s
        y_in = y[:, cols].astype(F32)
        gated = y_in * swish
        d_s = d_ssm[:, cols]
        small[V_GS : V_GS + 1, cols] = column_sum(d_s * gated * rate)
        d_gated = rate * (d_s * vec_ref[V_GS : V_GS + 1, cols]) - gated * (along * rate)
        d_proj[:, pl.ds(pl.multiple_of(g0 + t * TILE, TILE), TILE)] = (
            d_gated * y_in * (s + swish - swish * s)
        ).astype(BF)
        d_y = d_gated * swish
        z_in = z[:, cols].astype(F32)
        s = sigmoid(z_in)
        x_in = z_in * s
        slope = s + x_in - x_in * s
        spread = expand_matrix(t)
        steps = dot(step_two[...], spread)
        bends = dot(bend_two[...], spread)
        scaled = (steps * x_in).astype(BF)
        d_low = d_y.astype(BF)
        u = (bends[:HALF] * scaled[:HALF].astype(F32)).astype(BF)
        v = (bends[HALF:] * d_y[HALF:]).astype(BF)
        far = dot(cross, u)
        back = dot(cross_turned, v)
        d_tops[2 * HALF :, :] += dot_nt(v, u)
        mixed_parts, back_parts = [], []
        for p in range(TILE // HALF):
            mixed_block, back_block = [], []
            for c in range(2):
                rows = slice(c * HALF, (c + 1) * HALF)
                xs = scaled[rows, p * HALF : (p + 1) * HALF]
                dy = d_low[rows, p * HALF : (p + 1) * HALF]
                zero = jnp.zeros_like(xs)
                xs_two = [jnp.where(pair_low, xs, zero), jnp.where(pair_low, zero, xs)]
                dy_two = [jnp.where(pair_low, dy, zero), jnp.where(pair_low, zero, dy)]
                weights = []
                d_top = jnp.zeros((HALF, HALF), F32)
                for side in range(2):
                    h = t * (TILE // HD) + 2 * p + side
                    wide = run_wide[rows, lanes(h, HALF)]
                    line = run_row[pl.ds(c * HALF + h, 1), :]
                    decay = jnp.exp(jnp.minimum(wide - line, 0.0))
                    weights.append((decay * tops[rows, :]).astype(BF))
                    d_top = d_top + decay * dot_nt(dy_two[side], xs)
                d_tops[rows, :] += d_top
                mixed_block.append(
                    dot(jnp.concatenate(weights, axis=1), jnp.concatenate(xs_two, axis=0))
                )
                back_block.append(
                    dot_tn(jnp.concatenate(weights, axis=0), jnp.concatenate(dy_two, axis=0))
                )
            mixed_parts.append(jnp.concatenate(mixed_block, axis=0))
            back_parts.append(jnp.concatenate(back_block, axis=0))
        mixed = jnp.concatenate(mixed_parts, axis=1)
        d_scaled = jnp.concatenate(back_parts, axis=1)
        crossing = jnp.concatenate(
            [-(u.astype(F32) * back), v.astype(F32) * far], axis=0
        )
        runs = d_low.astype(F32) * mixed - scaled.astype(F32) * d_scaled + crossing
        d_scaled = d_scaled + jnp.concatenate([bends[:HALF] * back, jnp.zeros_like(back)], axis=0)
        gather = reduce_matrix(t)
        run_acc[...] += sum(dot(part, gather) for part in split2(runs))
        step_acc[...] += sum(dot(part, gather) for part in split2(x_in * d_scaled))
        small[V_SKIP : V_SKIP + 1, cols] = column_sum(d_y * x_in)
        d_x = steps * d_scaled + vec_ref[V_SKIP : V_SKIP + 1, cols] * d_y
        d_z[:, cols] = d_x * slope
        return carry

    lax.fori_loop(0, mi // TILE, mix_tile, 0, unroll=True)
    d_top = [
        jnp.where(causal, d_tops[c * HALF : (c + 1) * HALF, :], 0.0).astype(BF) for c in range(2)
    ]
    d_cross = d_tops[2 * HALF :, :].astype(BF)
    d_c = jnp.concatenate(
        [dot(d_top[0], b_in[:HALF]), dot(d_cross, b_in[:HALF]) + dot(d_top[1], b_in[HALF:])], axis=0
    )
    d_b = jnp.concatenate(
        [dot_tn(d_top[0], c_in[:HALF]) + dot_tn(d_cross, c_in[HALF:]), dot_tn(d_top[1], c_in[HALF:])],
        axis=0,
    )
    xb = zb * sb
    d_z[:, mi : mi + 2 * HALF] = jnp.concatenate([d_b, d_c], axis=1) * (sb + xb - xb * sb)
    upper = jnp.where(
        iota((length, length), 0) <= iota((length, length), 1), 1.0, 0.0
    ).astype(BF)
    d_change = sum(dot(upper, part) for part in split3(run_acc[...]))
    d_pre = (step_acc[...] + d_change * vec_ref[V_DECAY : V_DECAY + 1, :HALF]) * sigmoid(pre)
    d_pre = jnp.where(iota(d_pre.shape, 1) < heads, d_pre, 0.0)
    d_proj[:, s0:total] = d_pre.astype(BF)
    small[V_SBIAS : V_SBIAS + 1, :HALF] = column_sum(d_pre)
    small[V_DECAY : V_DECAY + 1, :HALF] = column_sum(d_change * change)

    wait(4)
    row = iota((length, TILE), 0)

    def conv_tile(t, carry):
        cols = lanes(t)
        d = d_z[:, cols]
        raw = conv_raw[:, cols].astype(F32)
        small[V_CBIAS : V_CBIAS + 1, cols] = column_sum(d)
        small[3:4, cols] = column_sum(d * raw)
        out = d * vec_ref[3:4, cols]
        for ahead in range(1, 4):
            moved = jnp.where(row < length - ahead, pltpu.roll(d, length - ahead, 0), 0.0)
            small[3 - ahead : 4 - ahead, cols] = column_sum(moved * raw)
            out = out + moved * vec_ref[3 - ahead : 4 - ahead, cols]
        d_proj[:, cols] = out.astype(BF)
        return carry

    lax.fori_loop(0, ci // TILE, conv_tile, 0, unroll=True)
    save(d_proj.at[:, q0:], s_dfirst)
    save(d_proj.at[:, :ci], s_dconv)
    save(d_proj.at[:, g0:q0], s_dgate)

    wait(5)

    def back_tile(t, carry):
        rows = lanes(t)
        d_normed[:, rows] = dot_nt(d_proj[...], win[rows, :])
        return carry

    lax.fori_loop(0, width // TILE, back_tile, 0, unroll=True)
    wait(6)
    x = x_low[...].astype(F32)
    rate_one = lax.rsqrt(jnp.mean(x * x, axis=-1, keepdims=True) + EPSILON)
    unit = x * rate_one
    d_n = d_normed[...]
    small[V_G1 : V_G1 + 1, :width] = column_sum(d_n * unit)
    save(small, s_small)
    d_n = d_n * vec_ref[V_G1 : V_G1 + 1, :width]
    d_input_ref[...] = (
        d_hidden_ref[...]
        + rate_one * (d_n - unit * jnp.mean(d_n * unit, axis=-1, keepdims=True))
    ).astype(BF)
    save(d_input_ref, s_dinput, slot_ref[base + 3])
    yield
    finish()


def mixer_backward_scratch(length, width, widths, total, small):
    ci, mi, qw, kw, heads = widths
    return [
        pltpu.VMEM((width, total), BF),
        pltpu.VMEM((mi + qw, width), BF),
        pltpu.VMEM((length, ci), BF),
        pltpu.VMEM((length, ci), BF),
        pltpu.VMEM((length, mi), BF),
        pltpu.VMEM((length, qw + 2 * kw), BF),
        pltpu.VMEM((length, HALF), F32),
        pltpu.VMEM((qw // HD * length, length), BF),
        pltpu.VMEM((length, mi), BF),
        pltpu.VMEM((length, width), BF),
        pltpu.VMEM((length, width), BF),
        pltpu.VMEM((length, total), BF),
        pltpu.VMEM((length, qw), BF),
        pltpu.VMEM((length, mi), F32),
        pltpu.VMEM((length, ci), F32),
        pltpu.VMEM((length, width), F32),
        pltpu.VMEM((length, heads * HALF), F32),
        pltpu.VMEM((length, HALF), F32),
        pltpu.VMEM((length, 2 * HALF), BF),
        pltpu.VMEM((length, 2 * HALF), BF),
        pltpu.VMEM((2 * HALF, HALF), F32),
        pltpu.VMEM((3 * HALF, HALF), F32),
        pltpu.VMEM((length, HALF), F32),
        pltpu.VMEM((length, HALF), F32),
        pltpu.VMEM(small, F32),
        pltpu.SemaphoreType.DMA((48,)),
        pltpu.SemaphoreType.DMA((6,)),
    ]


def mixer_backward_call(
    index, slot, spots, d_hidden, vec, cosine, sine, turn, weights, reads, stacks, widths, total
):
    ci, mi, qw, kw, heads = widths
    length, width = d_hidden.shape
    scratch = mixer_backward_scratch(length, width, widths, total, stacks[-1].shape[1:])
    return call(
        functools.partial(mix_backward, widths),
        "mixer_backward",
        [index, slot],
        spots,
        [d_hidden, vec, cosine, sine, turn],
        weights,
        reads,
        stacks,
        jax.ShapeDtypeStruct((length, width), BF),
        scratch,
        48,
        250,
    )


def weight_kernel(core_ref, away_ref, stay_ref, right_ref, out_away, out_stay, turned):
    rows = away_ref.shape[2]
    tokens = away_ref.shape[0] * away_ref.shape[1]
    turned[:rows, :] = away_ref[...].reshape(tokens, rows).T
    turned[rows:, :] = stay_ref[...].reshape(tokens, rows).T
    right = right_ref[...].reshape(tokens, right_ref.shape[2])
    out_away[0] = dot(turned[:rows, :], right).astype(BF)
    out_stay[0] = dot(turned[rows:, :], right).astype(BF)


def weight_grad_halves(core, left, right):
    count, length, depth = left.shape
    columns = right.shape[2]
    rows = depth // 4
    grid = pltpu.PrefetchScalarGridSpec(
        num_scalar_prefetch=1,
        grid=(2,),
        in_specs=[
            pl.BlockSpec((count, length, rows), lambda c, core: (0, 0, 2 * c + 1 - core[0])),
            pl.BlockSpec((count, length, rows), lambda c, core: (0, 0, 2 * c + core[0])),
            pl.BlockSpec((count, length, columns), lambda c, core: (0, 0, 0)),
        ],
        out_specs=[pl.BlockSpec((1, rows, columns), lambda c, core: (c, 0, 0))] * 2,
        scratch_shapes=[pltpu.VMEM((2 * rows, count * length), BF)],
    )
    shape = pltpu.HBM((2, rows, columns), BF)
    return pl.pallas_call(
        weight_kernel,
        out_shape=[shape, shape],
        grid_spec=grid,
        compiler_params=pltpu.CompilerParams(vmem_limit_bytes=40 * 1024 * 1024),
        cost_estimate=pl.CostEstimate(
            flops=100000000, bytes_accessed=1000000, transcendentals=0
        ),
        name="weight_gradient",
    )(core, in_hbm(left), in_hbm(left), in_hbm(right))


def layer_forward_call(
    index, slot, spots, x, vec, cosine, sine, turn, weights, stacks, widths, total, ff
):
    length, width = x.shape
    first = mixer_forward_scratch(length, width, widths, total)
    second = mlp_forward_scratch(length, width, ff)
    n = 12

    def body(scalars, spots, ordinary, weights, reads, stacks, low_ref, scratch):
        hidden = scratch[-1]
        one = mix_forward(
            widths, scalars, spots, ordinary, weights[:4], [], stacks[:n], hidden,
            scratch[: len(first)],
        )
        two = mlp_forward(
            scalars, spots, [hidden, ordinary[1]], weights[4:], [], stacks[n:], low_ref,
            scratch[len(first) : -1],
        )
        for part in (one, one, two, one, two, one, two):
            next(part, None)
        yield

    return call(
        body,
        "layer_forward",
        [index, slot],
        spots,
        [x, vec, cosine, sine, turn],
        weights,
        [],
        stacks,
        jax.ShapeDtypeStruct((length, width), BF),
        first + second + [pltpu.VMEM((length, width), F32)],
        58,
        200,
    )


def layer_backward_call(
    index, slot, mix, spots, target, vec, cosine, sine, turn, weights, reads, stacks, widths, total, ff
):
    length, width = target.shape
    first = mlp_backward_scratch(length, width, ff, stacks[3].shape[1:])
    second = mixer_backward_scratch(length, width, widths, total, stacks[-1].shape[1:])
    n = 4

    def body(scalars, spots, ordinary, weights, reads, stacks, d_input_ref, scratch):
        d_hidden = scratch[-1]
        target_ref, vec_ref, cos_ref, sin_ref, turn_ref = ordinary
        one = mlp_backward(
            scalars, spots, [target_ref, vec_ref, turn_ref], weights[4:], reads[:4],
            stacks[:n], d_hidden, scratch[: len(first)],
        )
        two = mix_backward(
            widths, scalars[:2], spots, [d_hidden, vec_ref, cos_ref, sin_ref, turn_ref],
            weights[:4], reads[4:], stacks[n:], d_input_ref, scratch[len(first) : -1],
        )
        for part in (one, one, two, one, two, one, two):
            next(part, None)
        yield

    return call(
        body,
        "layer_backward",
        [index, slot, mix],
        spots,
        [target, vec, cosine, sine, turn],
        weights,
        reads,
        stacks,
        jax.ShapeDtypeStruct((length, width), BF),
        first + second + [pltpu.VMEM((length, width), F32)],
        60,
        250,
    )


def rope_tables(length):
    halves = HD // 2
    inverse = jnp.exp(jnp.arange(halves, dtype=F32) * (-2.0 * math.log(ROPE_BASE) / HD))
    angles = jnp.arange(length, dtype=F32)[:, None] * inverse[None, :]
    cosine, sine = jnp.cos(angles), jnp.sin(angles)
    return (
        jnp.concatenate([cosine] * 4, axis=1),
        jnp.concatenate([-sine, sine, -sine, sine], axis=1),
    )


def swap(block, axis, bit):
    return lax.ppermute(block, axis, [(i, i ^ bit) for i in range(lax.axis_size(axis))])


def after(value, *others):
    if not others:
        return value
    return lax.optimization_barrier((value,) + others)[0]


def corner(made):
    part = made.reshape(-1, made.shape[-1])[:8, :HALF].astype(BF)
    return jnp.dot(part, jnp.ones((HALF, HALF), BF), preferred_element_type=F32)


def quick_links():
    return lax.axis_size("fsdp") == 4 and lax.axis_size("rep") == 4


def gather_halves(shard, axis, before_y=(), before_z=()):
    parity = lax.axis_index("rep") % 2
    half = shard.shape[axis] // 2
    mine = lax.dynamic_slice_in_dim(shard, parity * half, half, axis)
    near = swap(shard, "fsdp", 1)
    far_one = swap(after(mine, *before_y), "fsdp", 2)
    far_two = swap(after(far_one, *before_z), "rep", 1)
    return [shard, near, far_one, far_two]


def gather_wholes(shard, *before_y):
    return [shard, swap(shard, "fsdp", 1), swap(after(shard, *before_y), "fsdp", 2)]


def share_far(pieces, *before):
    return pieces + [swap(after(piece, *before), "fsdp", 1) for piece in pieces[2:]]


def plus(a, b):
    return (a.astype(F32) + b.astype(F32)).astype(BF)


def weight_grad(left, right):
    return lax.dot_general(
        left, right, (((0, 1), (0, 1)), ((), ())), preferred_element_type=F32
    ).astype(BF)


class Reduction:
    def __init__(self, left, right, riders=None):
        self.left, self.right, self.riders = left, right, riders

    def begin(self, order):
        left, right = order(self.left, self.right)
        core = lax.axis_index("fsdp") % 2
        away, stay = weight_grad_halves(core.astype(jnp.int32)[None], left, right)
        if self.riders is not None:
            blocks, column = self.riders
            away, stay = (
                lax.dynamic_update_slice(
                    grad, lax.dynamic_index_in_dim(blocks, i, 1, keepdims=False), (0, 0, column)
                )
                for grad, i in ((away, 1 - core), (stay, core))
            )
        self.stay = stay
        self.moved = swap(away, "fsdp", 1)
        return stay

    def chips(self, order):
        chip = lax.axis_index("fsdp") // 2
        self.kept = order(self.stay, self.moved)

        def part(i):
            return [lax.dynamic_index_in_dim(v, i, 0, keepdims=False) for v in self.kept]

        away = plus(*part(1 - chip))
        self.moved = swap(away, "fsdp", 2)
        return away

    def line_in(self, order):
        chip = lax.axis_index("fsdp") // 2
        *kept, moved = order(*self.kept, self.moved)
        one, two = (lax.dynamic_index_in_dim(v, chip, 0, keepdims=False) for v in kept)
        self.stay = (one.astype(F32) + two.astype(F32) + moved.astype(F32)).astype(BF)
        self.moved = lax.ppermute(self.stay, "rep", [(0, 1), (3, 2)])
        return self.stay

    def middle(self, order):
        stay, moved = order(self.stay, self.moved)
        self.stay = plus(stay, moved)
        self.moved = lax.ppermute(self.stay, "rep", [(1, 2), (2, 1)])
        return self.stay

    def line_out(self, order):
        stay, moved = order(self.stay, self.moved)
        self.stay = plus(stay, moved)
        self.moved = lax.ppermute(self.stay, "rep", [(1, 0), (2, 3)])
        return self.stay

    def finish(self, order):
        stay, moved = order(self.stay, self.moved)
        rank = lax.axis_index("rep")
        inner = jnp.logical_or(rank == 1, rank == 2)
        self.result = jnp.where(inner, stay, moved).astype(F32)
        return self.result


def body(
    inputs,
    teacher,
    lengths,
    order,
    loss_scale,
    norm_gain1,
    w_query,
    w_key,
    w_value,
    w_attn_out,
    w_ssm_gate,
    w_conv_in,
    w_step,
    conv_kernel,
    conv_bias,
    step_bias,
    decay_log,
    skip_gain,
    ssm_norm_gain,
    w_ssm_out,
    norm_gain2,
    w_gate,
    w_up,
    w_down,
):
    quick = quick_links()
    n_rep = lax.axis_size("rep")
    n_fsdp = lax.axis_size("fsdp")
    rank = lax.axis_index("rep")
    fsdp = lax.axis_index("fsdp")
    section = lax.axis_index("section")
    first = section == 0
    device = fsdp * n_rep + rank
    count, length, width = inputs.shape
    ci, mi, qw, kw = (w.shape[2] for w in (w_conv_in, w_ssm_gate, w_query, w_key))
    heads = w_step.shape[2]
    ff = w_up.shape[2]
    widths = (ci, mi, qw, kw, heads)
    taps = conv_kernel.shape[1]
    rows = width // n_fsdp
    tail = qw + 2 * kw + HALF
    total = ci + mi + tail

    def columns(flat):
        wide = -(-flat.size // rows)
        return jnp.pad(flat, (0, wide * rows - flat.size)).reshape(rows, wide)

    convs = jnp.concatenate([conv_kernel[0], conv_bias], axis=0)
    riders = jnp.concatenate(
        [
            norm_gain1[0][:, None],
            norm_gain2[0][:, None],
            columns(convs.reshape(-1)),
            columns(ssm_norm_gain[0]),
        ],
        axis=1,
    )
    used = riders.shape[1]
    wide = -(-convs.size // rows)
    shard_first = jnp.concatenate(
        [w_query[0], w_key[0], w_value[0], w_step[0]] + [jnp.zeros((rows, HALF - heads), BF)],
        axis=1,
    )
    parity = rank % 2
    if quick:
        g_gate = gather_halves(w_ssm_gate[0], 0)
        g_conv = gather_halves(w_conv_in[0], 0)
        g_first = gather_halves(shard_first, 0, (), g_gate[3:4])
        shard_out = jnp.concatenate([w_ssm_out[0], w_attn_out[0]], axis=0)
        g_out = gather_halves(shard_out, 1, g_gate[2:3], g_conv[3:4])
        g_g = gather_halves(w_gate[0], 0, g_conv[2:3], g_first[3:4])
        g_u = gather_wholes(w_up[0], g_out[2], g_g[2])
        g_gate, g_conv, g_first, g_out = (
            share_far(g, g_out[3]) for g in (g_gate, g_conv, g_first, g_out)
        )
        spots = [2 * fsdp, 2 * (fsdp ^ 1)]
        spots += [2 * (fsdp ^ k) + b for k in (2, 3) for b in (parity, 1 - parity)]
        spots = jnp.stack(spots).astype(jnp.int32)
        far = swap(riders, "fsdp", 2)
        blocks = jnp.stack([riders, swap(riders, "fsdp", 1), far, swap(far, "fsdp", 1)])
        ridden = jnp.take(blocks, jnp.arange(4, dtype=jnp.int32) ^ fsdp, axis=0)
    else:

        def whole(shard):
            return lax.all_gather(shard, "fsdp", axis=0, tiled=True)

        g_first, g_conv, g_gate, g_g, g_u, g_down = (
            [whole(w)]
            for w in (shard_first, w_conv_in[0], w_ssm_gate[0], w_gate[0], w_up[0], w_down[0])
        )
        g_out = [jnp.concatenate([whole(w_ssm_out[0]), whole(w_attn_out[0])], axis=0)]
        spots = jnp.zeros((1,), jnp.int32)
        ridden = whole(riders).reshape(n_fsdp, rows, used)
    if quick:
        order = after(order, g_gate[3])

    turns = jnp.arange(count, dtype=jnp.int32)
    numbers = jnp.arange(order.shape[0], dtype=jnp.int32)
    mine = device * count + turns
    sources = jnp.sum(jnp.where(order[None, :] == mine[:, None], numbers[None, :], 0), axis=1)
    target = lax.dynamic_slice_in_dim(order, device * count, count) // count % n_rep
    anchor = sources // count % n_rep

    def inverse(key):
        return jnp.sum(jnp.where((key ^ rank)[None, :] == turns[:, None], turns[None, :], 0), axis=1)

    send_at, keep_at = inverse(target), inverse(anchor)
    own_lengths = jnp.take(lengths, jnp.take(sources, keep_at))
    outgoing = [
        jnp.where(
            first,
            lax.dynamic_index_in_dim(inputs, send_at[j], 0, keepdims=False),
            lax.dynamic_index_in_dim(teacher, send_at[j], 0, keepdims=False),
        )
        for j in range(count)
    ]
    dealt = [outgoing[0]]

    def deal(j, *earlier):
        dealt.append(swap(after(outgoing[j], *earlier), "rep", j))


    if quick:
        deal(1, g_out[3])
        deal(2, dealt[1])
    else:
        for j in range(1, count - 1):
            deal(j)

    mixer_weights = [g_first, g_conv, g_gate, g_out]
    mlp_weights = None if quick else [g_g, g_u, g_down]

    conv_all = ridden[:, :, 2 : 2 + wide].reshape(n_fsdp, -1)[:, : (taps + 1) * ci // n_fsdp]
    conv_all = conv_all.reshape(n_fsdp, taps + 1, ci // n_fsdp).transpose(1, 0, 2)
    ssm_gain = ridden[:, :, 2 + wide :].reshape(n_fsdp, -1)[:, : mi // n_fsdp].reshape(1, mi)

    def table_row(v):
        v = v.astype(F32)
        return jnp.pad(v, ((0, 0), (0, ci - v.shape[1])))

    vec = jnp.concatenate(
        [
            table_row(v)
            for v in (
                conv_all.reshape(taps + 1, ci),
                ssm_gain,
                jnp.repeat(skip_gain, HD, axis=1),
                ridden[:, :, 0].reshape(1, width),
                ridden[:, :, 1].reshape(1, width),
                step_bias,
                -jnp.exp(decay_log),
                jnp.zeros((16 - taps - 7, 1), F32),
            )
        ],
        axis=0,
    )
    cosine, sine = rope_tables(length)

    valid_count = jnp.sum(lengths).astype(F32)
    factor = loss_scale / (valid_count * width)

    skew = 2
    steps = count + skew
    ticks = jnp.arange(steps, dtype=jnp.int32)
    raw = jnp.concatenate([ticks - skew * section, count - 1 - ticks + skew * (1 - section)])
    inside = jnp.logical_and(raw >= 0, raw < count).astype(jnp.int32)
    slots = jnp.clip(raw, 0, count - 1)
    plan = [slots, inside, jnp.take(own_lengths, slots), jnp.take(keep_at, slots)]
    plan = jnp.stack(plan, axis=1).reshape(-1)
    mix = jnp.stack([jnp.where(first, 1.0, 0.0), 2.0 * factor])

    def stack(*shape, kind=BF):
        return jax.ShapeDtypeStruct((count,) + shape, kind)

    mix_stacks = [
        stack(length, width),
        stack(length, ci),
        stack(length, ci),
        stack(length, mi),
        stack(length, qw + 2 * kw),
        stack(length, HALF, kind=F32),
        stack(qw // HD * length, length),
        stack(length, mi),
        stack(length, qw),
        stack(length, mi),
        stack(length, width, kind=F32),
        stack(length, width),
    ]
    mlp_stacks = [
        stack(length, width),
        stack(length, ff),
        stack(length, ff),
        stack(length, ff),
        stack(length, width, kind=F32),
        stack(length, width),
    ]

    token = []

    def chained(*values):
        if not quick or not token:
            return values
        return lax.optimization_barrier(values + tuple(token))[: len(values)]

    def chain(made):
        token[:] = [made]

    received, hiddens = [], []

    blank = jnp.zeros((8, HALF), F32)

    def number(i):
        return jnp.full((1,), i, jnp.int32)

    def mixer_tick(tick, turn, mix_stacks):
        mix_stacks, hidden = mixer_forward_call(
            number(tick),
            plan,
            spots,
            dealt[tick],
            vec,
            cosine,
            sine,
            corner(turn),
            mixer_weights,
            mix_stacks,
            widths,
            total,
        )
        chain(hidden)
        hiddens.append(hidden)
        return mix_stacks

    def mlp_tick(tick, mlp_stacks):
        (hidden,) = chained(hiddens[tick])
        mlp_stacks, low = mlp_forward_call(
            number(tick), plan, spots, hidden, vec, mlp_weights, mlp_stacks, ff
        )
        return mlp_stacks, low

    def layer_tick(tick, turn, stacks):
        if tick < count:
            one, two = chained(dealt[tick], received[tick - skew])
            seq_in = jnp.where(first, one, two)
        else:
            seq_in = received[tick - skew]
        return layer_forward_call(
            number(tick),
            plan,
            spots,
            seq_in,
            vec,
            cosine,
            sine,
            corner(turn) if tick < steps - 1 else blank,
            mixer_weights + mlp_weights,
            stacks,
            widths,
            total,
            ff,
        )

    mix_stacks = mixer_tick(0, dealt[0], mix_stacks)
    if quick:
        g_down = gather_wholes(w_down[0], hiddens[0])
    mix_stacks = mixer_tick(1, hiddens[0], mix_stacks)
    if quick:
        mlp_weights = [share_far(g, hiddens[1], dealt[2]) for g in (g_g, g_u, g_down)]
    for tick in range(steps):
        if tick < skew:
            mlp_stacks, low = mlp_tick(tick, mlp_stacks)
            if tick == 0:
                deal(count - 1, low)
        else:
            stacks, low = layer_tick(tick, low, mix_stacks + mlp_stacks)
            mix_stacks, mlp_stacks = stacks[: len(mix_stacks)], stacks[len(mix_stacks) :]
        chain(low)
        if tick < count:
            received.append(lax.ppermute(low, "section", [(0, 1)]))

    (s_normed, s_conv, s_z, s_gate, s_qkv, s_step, s_probs, s_ssm, s_mixed, s_y, s_hidden,
     s_x) = mix_stacks
    s_normed2, s_g, s_u, s_act, s_final, s_low = mlp_stacks
    mlp_grads = [
        stack(length, width),
        stack(length, ff),
        stack(length, ff),
        stack(8, width, kind=F32),
    ]
    mix_grads = [
        stack(length, width),
        stack(length, tail),
        stack(length, ci),
        stack(length, mi),
        stack(length, width),
        stack(16, ci, kind=F32),
    ]
    incoming, returned = [], [None] * count

    hiddens = []

    def mlp_turn(turn, mlp_grads):
        if turn == count:
            token.append(returned[3])
        (seed,) = chained(incoming[turn - skew])
        return mlp_backward_call(
            number(steps + turn),
            plan,
            mix,
            spots,
            seed,
            vec,
            corner(hiddens[-1]) if turn > count else blank,
            mlp_weights,
            reads,
            mlp_grads,
            ff,
        )

    def mixer_turn(turn, d_hidden, before, mix_grads):
        mix_grads, d_input = mixer_backward_call(
            number(steps + turn),
            plan,
            spots,
            d_hidden,
            vec,
            cosine,
            sine,
            corner(before),
            mixer_weights,
            mix_reads,
            mix_grads,
            widths,
            total,
        )
        send_back(turn, d_input)
        return mix_grads, d_input

    def send_back(turn, d_input):
        if turn < count:
            incoming.append(lax.ppermute(d_input, "section", [(1, 0)]))
        if turn >= skew:
            j = count - 1 - turn + skew
            back = lax.dynamic_index_in_dim(after(s_low, d_input), keep_at[j], 0, keepdims=False)
            back = jnp.where(first, d_input, back)
            returned[j] = swap(back, "rep", j) if j else back

    reads = [s_final, s_hidden, s_g, s_u]
    mix_reads = [s_conv, s_z, s_gate, s_qkv, s_step, s_probs, s_y, s_x]
    d_input = low
    for turn in range(count):
        if turn < skew:
            (seed,) = chained(dealt[count - 1 - turn])
        else:
            one, two = chained(incoming[turn - skew], dealt[count - 1 - turn])
            seed = jnp.where(first, one, two)
        grads, d_input = layer_backward_call(
            number(steps + turn),
            plan,
            mix,
            spots,
            seed,
            vec,
            cosine,
            sine,
            corner(d_input) if turn else blank,
            mixer_weights + mlp_weights,
            reads + mix_reads,
            mlp_grads + mix_grads,
            widths,
            total,
            ff,
        )
        mlp_grads, mix_grads = grads[: len(mlp_grads)], grads[len(mlp_grads) :]
        chain(d_input)
        send_back(turn, d_input)

    for turn in range(count, steps):
        mlp_grads, d_hidden = mlp_turn(turn, mlp_grads)
        chain(d_hidden)
        hiddens.append(d_hidden)
    s_dmlp, s_dg, s_du, small_mlp = mlp_grads
    early = [(s_normed2, s_dg), (s_normed2, s_du), (s_act, s_dmlp)]
    chunks = [Reduction(*pair) for pair in early]

    names = dict(W="begin", A="chips", L="line_in", M="middle", O="line_out", F="finish")
    state = [mix_grads]

    def stages(*words):
        for word in words:
            letter, place = word[0], int(word[1:])
            if letter == "B":
                before = token[0] if quick else hiddens[place - count]
                state[0], made = mixer_turn(place, hiddens[place - count], before, state[0])
            else:
                made = getattr(chunks[place], names[letter])(chained)
            chain(made)

    if quick:
        stages("W0", "W1", "A0", "W2", "B4")
        token.append(returned[2])
        stages("A2", "A1", "L0", "B5")
    else:
        stages("B4", "B5")
    mix_grads = state[0]
    s_dbranch, s_dfirst, s_dconv, s_dgate, s_dinput, small_mix = mix_grads
    late = [
        (s_normed, s_dconv),
        (s_normed, s_dgate),
        (s_ssm, s_dbranch),
        (s_normed, s_dfirst),
        (s_mixed, s_dbranch),
    ]

    mix_sum = jnp.sum(small_mix, axis=0)
    mlp_sum = jnp.sum(small_mlp, axis=0)
    singles = jnp.concatenate(
        [
            mix_sum[V_SBIAS, :heads],
            mix_sum[V_DECAY, :heads],
            jnp.sum(mix_sum[V_SKIP, :mi].reshape(heads, HD), axis=1),
            jnp.sum(mlp_sum[1])[None],
        ]
    )

    def share(v):
        return v.reshape(v.shape[0], n_fsdp, -1).transpose(1, 0, 2).reshape(n_fsdp, -1)

    shares = [
        share(mix_sum[: taps + 1]),
        share(mix_sum[V_GS : V_GS + 1, :mi]),
        share(mix_sum[V_G1 : V_G1 + 1, :width]),
        share(mlp_sum[:1]),
        jnp.broadcast_to(singles[None], (n_fsdp, singles.size)),
    ]
    cuts = [v.shape[1] for v in shares]
    flat = jnp.concatenate(shares, axis=1)

    if quick:
        spare = -(-flat.shape[1] // rows)
        flat = jnp.pad(flat, ((0, 0), (0, spare * rows - flat.shape[1])))
        riders = flat.astype(BF).reshape(2, 2, rows, spare)
        column = tail - HALF + heads
        chunks += [Reduction(*pair) for pair in late]
        chunks[6].riders = (riders, column)
        stages(
            "L1", "M0", "W4", "W7", "W3", "L2", "M1", "O0", "A4", "A7", "A3", "W6", "W5", "F0"
        )
        token.append(returned[1])
        stages(
            "O1", "L3", "M2", "L7", "A5", "L4", "A6", "M3", "O2", "F1", "L5", "M4", "L6", "O3",
            "F2", "M7", "M5", "O4", "M6", "F3", "O7", "O5", "F4", "O6", "F7", "F5", "F6"
        )
        reduced = [chunk.result for chunk in chunks]
        flat = reduced[6][:, column : column + spare].reshape(-1)
        ends = chained(*returned, s_dinput, s_low)
        returned, s_dinput, s_low = ends[:count], ends[-2], ends[-1]
    else:

        def reduce_all(pair):
            grad = weight_grad(*pair)
            own = lax.psum_scatter(grad, "fsdp", scatter_dimension=0, tiled=True)
            return lax.psum(own, "rep").astype(F32)

        reduced = [reduce_all(pair) for pair in early + late]
        flat = lax.psum(lax.psum_scatter(flat, "fsdp", tiled=True), "rep").reshape(-1)
    grad_gate, grad_up, grad_down, grad_conv, grad_sgate, grad_ssm_out, grad_first, grad_attn = reduced

    parts, begin = [], 0
    for cut in cuts[:-1] + [heads] * 3 + [1]:
        parts.append(flat[begin : begin + cut])
        begin += cut
    convs = parts[0].reshape(taps + 1, -1)
    loss = jnp.where(first, lax.ppermute(parts[-1], "section", [(1, 0)]), parts[-1])[0]

    restored = jnp.zeros((count, length, width), BF)
    for j in range(count):
        restored = lax.dynamic_update_index_in_dim(restored, returned[j], send_at[j], 0)
    activations = jnp.where(first, s_low, restored)[None]
    gradients = jnp.where(first, restored, s_dinput)[None]
    s0 = qw + 2 * kw
    return (
        activations,
        gradients,
        loss / (valid_count * width),
        parts[2][None],
        grad_first[None, :, :qw],
        grad_first[None, :, qw : qw + kw],
        grad_first[None, :, qw + kw : s0],
        grad_attn[None],
        grad_sgate[None],
        grad_conv[None],
        grad_first[None, :, s0 : s0 + heads],
        convs[None, :taps],
        convs[None, taps],
        parts[4][None],
        parts[5][None],
        parts[6][None],
        parts[1][None],
        grad_ssm_out[None],
        parts[3][None],
        grad_gate[None],
        grad_up[None],
        grad_down[None],
    )


def solution(mesh):
    rows3 = P("section", "fsdp", None)
    pair = P("section", "fsdp")
    one = P("section", None)
    data = P(("fsdp", "rep"), None, None)
    taps = P("section", None, "fsdp")
    in_specs = (data, data, P(), P(), P(), pair) + (rows3,) * 7
    in_specs += (taps, pair, one, one, one, pair, rows3, pair, rows3, rows3, rows3)
    placed = P("section", ("fsdp", "rep"), None, None)
    out_specs = (placed, placed, P(), pair) + (rows3,) * 7
    out_specs += (taps, pair, one, one, one, pair, rows3, pair, rows3, rows3, rows3)
    return jax.shard_map(body, mesh=mesh, in_specs=in_specs, out_specs=out_specs, check_vma=False)
```

```python
import math
import functools

import jax
import jax.numpy as jnp
from jax import lax
from jax.experimental import pallas as pl
from jax.experimental.pallas import tpu as pltpu
from jax.sharding import PartitionSpec as P

HD = 64
EPSILON = 1e-05
ROPE_BASE = 100000000000.0
MASKED = -1e30
F32 = jnp.float32
BF = jnp.bfloat16
TILE = 256
HALF = 128
HB = pl.BlockSpec(memory_space=pltpu.HBM)
VM = pl.BlockSpec(memory_space=pltpu.VMEM)
SM = pl.BlockSpec(memory_space=pltpu.SMEM)


def dot(a, b):
    return jnp.dot(a, b, preferred_element_type=F32)


def dot_nt(a, b):
    return lax.dot_general(a, b, (((1,), (1,)), ((), ())), preferred_element_type=F32)


def dot_tn(a, b):
    return lax.dot_general(a, b, (((0,), (0,)), ((), ())), preferred_element_type=F32)


def sigmoid(v):
    return 0.5 * jnp.tanh(0.5 * v) + 0.5


def lanes(i, width=TILE):
    return pl.ds(pl.multiple_of(i * width, width), width)


def iota(shape, axis):
    return lax.broadcasted_iota(jnp.int32, shape, axis)


def split2(v):
    hi = v.astype(BF)
    return hi, (v - hi.astype(F32)).astype(BF)


def split3(v):
    hi = v.astype(BF)
    rest = v - hi.astype(F32)
    mid = rest.astype(BF)
    return hi, mid, (rest - mid.astype(F32)).astype(BF)


def expand_matrix(tile):
    row = jnp.bitwise_and(iota((TILE, TILE), 0), HALF - 1)
    col = jnp.right_shift(iota((TILE, TILE), 1), 6) + tile * (TILE // HD)
    return jnp.where(row == col, 1.0, 0.0).astype(BF)


def reduce_matrix(tile):
    row = jnp.right_shift(iota((TILE, HALF), 0), 6) + tile * (TILE // HD)
    col = iota((TILE, HALF), 1)
    return jnp.where(row == col, 1.0, 0.0).astype(BF)


def both(v):
    return jnp.concatenate(split2(v), axis=1)


def rope(v, cosine, sine, first):
    turned = jnp.where(first, pltpu.roll(v, HALF - HD // 2, 1), pltpu.roll(v, HD // 2, 1))
    return v * cosine + turned * sine


def start_all(groups, sems):
    waits, at = [], 0
    for group in groups:
        copies = []
        for source, target in group:
            copies.append(pltpu.make_async_copy(source, target, sems.at[at]))
            at += 1
        for copy in copies:
            copy.start()
        waits.append(copies)

    def wait(i):
        for copy in waits[i]:
            copy.wait()

    return wait


def row_pieces(pieces, spots, scratch, columns):
    if len(pieces) == 1:
        return [(pieces[0].at[:, a], scratch.at[:, b]) for a, b in columns]
    unit = pieces[-1].shape[0]
    if len(pieces) == 4:
        places = [jnp.right_shift(spots[i], 1) for i in (0, 1, 2, 4)]
    else:
        places = [spots[i] for i in range(6)]
    out = []
    for a, b in columns:
        for place, piece in zip(places, pieces):
            rows = pl.ds(pl.multiple_of(place * unit, unit), piece.shape[0])
            out.append((piece.at[:, a], scratch.at[rows, b]))
    return out


def out_pieces(pieces, spots, scratch, inner):
    if len(pieces) == 1:
        return [(pieces[0], scratch)]
    total, width = scratch.shape
    n = total // pieces[0].shape[0]
    cut, rest = inner // n, (total - inner) // n
    out = []
    for i, piece in enumerate(pieces):
        block, side = jnp.right_shift(spots[i], 1), jnp.bitwise_and(spots[i], 1)
        span = piece.shape[1]
        cols = slice(0, width)
        if span < width:
            cols = pl.ds(pl.multiple_of(side * span, span), span)
        upper = pl.ds(pl.multiple_of(block * cut, cut), cut)
        lower = pl.ds(pl.multiple_of(inner + block * rest, rest), rest)
        out.append((piece.at[:cut, :], scratch.at[upper, cols]))
        out.append((piece.at[cut:, :], scratch.at[lower, cols]))
    return out


def saver(slot, active, sems):
    stores = []

    def save(buffer, stack, at=slot):
        copy = pltpu.make_async_copy(buffer, stack.at[at], sems.at[len(stores)])
        pl.when(active)(copy.start)
        stores.append(copy)

    def finish():
        for copy in stores:
            pl.when(active)(copy.wait)

    return save, finish


def in_hbm(a):
    return pltpu.with_memory_space_constraint(a, pltpu.HBM)


def call(body, name, scalars, spots, ordinary, weights, reads, stacks, result, scratch, limit, work):
    fresh = isinstance(stacks[0], jax.ShapeDtypeStruct)
    flat = [piece for group in weights for piece in group]
    counts = [len(group) for group in weights]
    kept = [] if fresh else list(stacks)
    ahead = len(scalars) + 1 + len(ordinary) + len(flat) + len(reads)
    n = len(stacks)
    cuts = [len(scalars), 1, len(ordinary), len(flat), len(reads), len(kept), n, 1]

    def kernel(*refs):
        parts, at = [], 0
        for cut in cuts:
            parts.append(refs[at : at + cut])
            at += cut
        groups, begin = [], 0
        for c in counts:
            groups.append(parts[3][begin : begin + c])
            begin += c
        for _ in body(
            parts[0], parts[1][0], parts[2], groups, parts[4], parts[6], parts[7][0], refs[at:]
        ):
            pass

    out = pl.pallas_call(
        kernel,
        out_shape=[pltpu.HBM(s.shape, s.dtype) for s in stacks] + [result],
        in_specs=[SM] * (len(scalars) + 1)
        + [VM] * len(ordinary)
        + [HB] * (len(flat) + len(reads) + len(kept)),
        out_specs=[HB] * n + [VM],
        scratch_shapes=scratch,
        input_output_aliases={} if fresh else {ahead + i: i for i in range(n)},
        compiler_params=pltpu.CompilerParams(vmem_limit_bytes=limit * 1024 * 1024),
        cost_estimate=pl.CostEstimate(
            flops=work * 100000000, bytes_accessed=1000000, transcendentals=0
        ),
        name=name,
    )(*scalars, spots, *ordinary, *(in_hbm(a) for a in flat + list(reads) + kept))
    return list(out[:n]), out[n]


V_TAP, V_CBIAS, V_GS, V_SKIP, V_G1, V_G2, V_SBIAS, V_DECAY = 0, 4, 5, 6, 7, 8, 9, 10


def scan_terms(step_raw, vec_ref, heads):
    lane = iota(step_raw.shape, 1)
    pre = step_raw + vec_ref[V_SBIAS : V_SBIAS + 1, :HALF]
    soft = jnp.maximum(pre, 0.0) + jnp.log1p(jnp.exp(-jnp.abs(pre)))
    step = jnp.where(lane < heads, soft, 0.0)
    change = step * vec_ref[V_DECAY : V_DECAY + 1, :HALF]
    length = step.shape[0]
    lower = jnp.where(
        iota((length, length), 0) >= iota((length, length), 1), 1.0, 0.0
    ).astype(BF)
    run = sum(dot(lower, part) for part in split3(change))
    middle = run[HALF - 1 : HALF, :]
    bend = jnp.where(iota(run.shape, 0) < HALF, middle - run, run - middle)
    bend = jnp.exp(jnp.minimum(bend, 0.0))
    return pre, step, change, run, bend


def broadcast_runs(run, run_wide, heads):
    for h in range(heads):
        run_wide[:, h * HALF : (h + 1) * HALF] = jnp.broadcast_to(
            run[:, h : h + 1], (run.shape[0], HALF)
        )


def mix_forward(widths, scalars, spots, ordinary, weights, reads, stacks, hidden_ref, scratch):
    ci, mi, qw, kw, heads = widths
    index_ref, slot_ref = scalars
    base = 4 * index_ref[0]
    x_ref, vec_ref, cos_ref, sin_ref, _ = ordinary
    w_first, w_conv, w_gate, w_out = weights
    (win, wout, normed, conv_raw, z, xbc, gate_raw, qkv, step_raw, probs, branch, mixed_all, y,
     gated, run_wide, run_row, step_two, bend_two, in_sem, out_sem) = scratch
    (s_normed, s_conv, s_z, s_gate, s_qkv, s_step, s_probs, s_ssm, s_mixed, s_y, s_hidden,
     s_x) = stacks
    g0 = ci
    q0 = ci + mi
    total = win.shape[1]
    tail = total - q0
    wait = start_all(
        [
            row_pieces(w_first, spots, win, [(slice(0, tail), slice(q0, total))]),
            row_pieces(w_conv, spots, win, [(slice(0, ci), slice(0, ci))]),
            row_pieces(w_gate, spots, win, [(slice(0, mi), slice(g0, q0))]),
            out_pieces(w_out, spots, wout, mi),
        ],
        in_sem,
    )
    save, finish = saver(slot_ref[base], slot_ref[base + 1] > 0, out_sem)
    yield

    length = x_ref.shape[0]
    x = x_ref[...].astype(F32)
    rate = lax.rsqrt(jnp.mean(x * x, axis=-1, keepdims=True) + EPSILON)
    normed[...] = (x * rate * vec_ref[V_G1 : V_G1 + 1, : x.shape[1]]).astype(BF)
    save(normed, s_normed)
    lane_first = jnp.bitwise_and(iota((length, HALF), 1), HD - 1) < HD // 2
    half_low = iota((length, HALF), 1) < HD

    wait(0)
    cosine, sine = cos_ref[...], sin_ref[...]
    n_rope = (qw + kw) // HALF
    for t in range((total - q0) // HALF // 2):
        raw = dot(normed[...], win[:, q0 + t * TILE : q0 + (t + 1) * TILE])
        for part in range(2):
            c = 2 * t + part
            piece = raw[:, part * HALF : (part + 1) * HALF]
            if c < n_rope:
                piece = rope(piece, cosine, sine, lane_first)
            if c < n_rope + kw // HALF:
                qkv[:, c * HALF : (c + 1) * HALF] = piece.astype(BF)
            else:
                step_raw[...] = piece
    if ((total - q0) // HALF) % 2:
        step_raw[...] = dot(normed[...], win[:, total - HALF : total])
    save(qkv, s_qkv)
    save(step_raw, s_step)

    wait(1)
    row = iota((length, TILE), 0)

    def conv_tile(t, carry):
        cols = lanes(t)
        raw = dot(normed[...], win[:, cols])
        conv_raw[:, cols] = raw.astype(BF)
        total_z = vec_ref[V_CBIAS : V_CBIAS + 1, cols] + raw * vec_ref[3:4, cols]
        for back in range(1, 4):
            moved = jnp.where(row >= back, pltpu.roll(raw, back, 0), 0.0)
            total_z = total_z + moved * vec_ref[3 - back : 4 - back, cols]
        z[:, cols] = total_z.astype(BF)
        xbc[:, cols] = (total_z * sigmoid(total_z)).astype(BF)
        return carry

    lax.fori_loop(0, ci // TILE, conv_tile, 0, unroll=True)
    save(conv_raw, s_conv)
    save(z, s_z)

    wait(2)

    def gate_tile(t, carry):
        raw = dot(normed[...], win[:, pl.ds(pl.multiple_of(g0 + t * TILE, TILE), TILE)])
        gate_raw[:, lanes(t)] = raw.astype(BF)
        return carry

    lax.fori_loop(0, mi // TILE, gate_tile, 0, unroll=True)
    save(gate_raw, s_gate)

    yield

    keys, values = qkv[:, qw : qw + kw], qkv[:, qw + kw : qw + 2 * kw]
    keys_far, values_far = pltpu.roll(keys.astype(F32), HD, 1).astype(BF), pltpu.roll(
        values.astype(F32), HD, 1
    ).astype(BF)
    causal_top = iota((HALF, HALF), 1) <= iota((HALF, HALF), 0)
    causal_low = iota((HALF, length), 1) <= iota((HALF, length), 0) + HALF
    pairs = qw // HALF
    groups = kw // HD
    probs_zero = jnp.zeros((HALF, HALF), BF)
    for pair in range(pairs):
        group = pair // (pairs // groups)
        keep = half_low if group == 0 else jnp.logical_not(half_low)
        keys_two = jnp.where(keep, keys, keys_far)
        values_two = jnp.where(keep, values, values_far)
        query = qkv[:, pair * HALF : (pair + 1) * HALF] * jnp.asarray(HD ** (-0.5), BF)
        results = []
        for side in range(2):
            own = half_low if side == 0 else jnp.logical_not(half_low)
            q = jnp.where(own, query, jnp.zeros_like(query))
            at = (2 * pair + side) * length
            out = []
            for lo, causal in ((0, causal_top), (1, causal_low)):
                width = HALF if lo == 0 else length
                scores = dot_nt(q[lo * HALF : (lo + 1) * HALF], keys_two[:width])
                scores = jnp.where(causal, scores, MASKED)
                top = jnp.max(scores, axis=-1, keepdims=True)
                weights = jnp.exp(scores - top)
                weights = weights / jnp.sum(weights, axis=-1, keepdims=True)
                weights = weights.astype(BF)
                if lo == 0:
                    probs[at : at + HALF, :HALF] = weights
                    probs[at : at + HALF, HALF:] = probs_zero
                else:
                    probs[at + HALF : at + length, :] = weights
                out.append(dot(weights, values_two[:width]))
            results.append(jnp.concatenate(out, axis=0))
        mixed = jnp.where(half_low, results[0], results[1])
        mixed_all[:, pair * HALF : (pair + 1) * HALF] = mixed.astype(BF)
    save(probs, s_probs)
    save(mixed_all, s_mixed)

    pre, step, change, run, bend = scan_terms(step_raw[...], vec_ref, heads)
    turned = run.T
    run_row[:HALF, :] = turned[:, :HALF]
    run_row[HALF:, :] = turned[:, HALF:]
    broadcast_runs(run, run_wide, heads)
    step_two[...] = both(step)
    bend_two[...] = both(bend)
    b_in, c_in = xbc[:, mi : mi + HALF], xbc[:, mi + HALF : mi + 2 * HALF]
    tops = [dot_nt(c_in[c * HALF : (c + 1) * HALF], b_in[c * HALF : (c + 1) * HALF]) for c in (0, 1)]
    cross = dot_nt(c_in[HALF:], b_in[:HALF]).astype(BF)
    pair_low = iota((HALF, HALF), 1) < HD
    tops = [jnp.where(causal_top, t, 0.0) for t in tops]

    def mix_tile(t, squares):
        cols = lanes(t)
        spread = expand_matrix(t)
        x_in = xbc[:, cols].astype(F32)
        scaled = (dot(step_two[...], spread) * x_in).astype(BF)
        bends = dot(bend_two[...], spread)
        u = (bends[:HALF] * scaled[:HALF].astype(F32)).astype(BF)
        far = dot(cross, u) * bends[HALF:]
        parts = []
        for p in range(TILE // HALF):
            block = []
            for c in range(2):
                rows = slice(c * HALF, (c + 1) * HALF)
                weights = []
                for side in range(2):
                    h = t * (TILE // HD) + 2 * p + side
                    wide = run_wide[rows, lanes(h, HALF)]
                    line = run_row[pl.ds(c * HALF + h, 1), :]
                    decay = jnp.exp(jnp.minimum(wide - line, 0.0))
                    weights.append((decay * tops[c]).astype(BF))
                xs = scaled[rows, p * HALF : (p + 1) * HALF]
                zero = jnp.zeros_like(xs)
                right = jnp.concatenate(
                    [jnp.where(pair_low, xs, zero), jnp.where(pair_low, zero, xs)], axis=0
                )
                block.append(dot(jnp.concatenate(weights, axis=1), right))
            parts.append(jnp.concatenate(block, axis=0))
        out = jnp.concatenate(parts, axis=1)
        out = out + jnp.concatenate([jnp.zeros_like(far), far], axis=0)
        out = out + vec_ref[V_SKIP : V_SKIP + 1, cols] * x_in
        y[:, cols] = out.astype(BF)
        g = gate_raw[:, cols].astype(F32)
        out = out * (g * sigmoid(g))
        gated[:, cols] = out
        return squares + jnp.sum(out * out, axis=-1, keepdims=True)

    squares = lax.fori_loop(0, mi // TILE, mix_tile, jnp.zeros((length, 1), F32), unroll=True)
    save(y, s_y)
    rate = lax.rsqrt(squares * (1.0 / mi) + EPSILON)
    branch[...] = (gated[...] * rate * vec_ref[V_GS : V_GS + 1, :mi]).astype(BF)
    save(branch, s_ssm)

    wait(3)

    def out_tile(t, carry):
        cols = lanes(t)
        hidden_ref[:, cols] = (
            x_ref[:, cols].astype(F32)
            + dot(branch[...], wout[:mi, cols])
            + dot(mixed_all[...], wout[mi:, cols])
        )
        return carry

    lax.fori_loop(0, wout.shape[1] // TILE, out_tile, 0, unroll=True)
    save(hidden_ref, s_hidden)
    save(x_ref, s_x)
    yield
    finish()


def mixer_forward_scratch(length, width, widths, total):
    ci, mi, qw, kw, heads = widths
    return [
        pltpu.VMEM((width, total), BF),
        pltpu.VMEM((mi + qw, width), BF),
        pltpu.VMEM((length, width), BF),
        pltpu.VMEM((length, ci), BF),
        pltpu.VMEM((length, ci), BF),
        pltpu.VMEM((length, ci), BF),
        pltpu.VMEM((length, mi), BF),
        pltpu.VMEM((length, qw + 2 * kw), BF),
        pltpu.VMEM((length, HALF), F32),
        pltpu.VMEM((qw // HD * length, length), BF),
        pltpu.VMEM((length, mi), BF),
        pltpu.VMEM((length, qw), BF),
        pltpu.VMEM((length, mi), BF),
        pltpu.VMEM((length, mi), F32),
        pltpu.VMEM((length, heads * HALF), F32),
        pltpu.VMEM((length, HALF), F32),
        pltpu.VMEM((length, 2 * HALF), BF),
        pltpu.VMEM((length, 2 * HALF), BF),
        pltpu.SemaphoreType.DMA((32,)),
        pltpu.SemaphoreType.DMA((12,)),
    ]


def mixer_forward_call(
    index, slot, spots, x, vec, cosine, sine, turn, weights, stacks, widths, total
):
    ci, mi, qw, kw, heads = widths
    length, width = x.shape
    scratch = mixer_forward_scratch(length, width, widths, total)
    return call(
        functools.partial(mix_forward, widths),
        "mixer_forward",
        [index, slot],
        spots,
        [x, vec, cosine, sine, turn],
        weights,
        [],
        stacks,
        jax.ShapeDtypeStruct((length, width), F32),
        scratch,
        44,
        200,
    )


def mlp_forward(scalars, spots, ordinary, weights, reads, stacks, low_ref, scratch):
    index_ref, slot_ref = scalars
    base = 4 * index_ref[0]
    hidden_ref, vec_ref = ordinary
    w_g, w_u, w_down = weights
    wgu, wdown, normed, gate_low, up_low, act, final, in_sem, out_sem = scratch
    s_normed, s_gate, s_up, s_act, s_final, s_low = stacks
    ff = wdown.shape[0]
    parts = 2
    step = ff // parts
    groups = []
    for i in range(parts):
        a = slice(i * step, (i + 1) * step)
        b = slice(ff + i * step, ff + (i + 1) * step)
        groups.append(
            row_pieces(w_g, spots, wgu, [(a, a)]) + row_pieces(w_u, spots, wgu, [(a, b)])
        )
    groups.append(row_pieces(w_down, spots, wdown, [(slice(0, wdown.shape[1]),) * 2]))
    wait = start_all(groups, in_sem)
    save, finish = saver(slot_ref[base], slot_ref[base + 1] > 0, out_sem)
    yield
    valid = jnp.where(iota((hidden_ref.shape[0], 1), 0) < slot_ref[base + 2], 1.0, 0.0)

    hidden = hidden_ref[...]
    rate = lax.rsqrt(jnp.mean(hidden * hidden, axis=-1, keepdims=True) + EPSILON)
    normed[...] = (hidden * rate * vec_ref[V_G2 : V_G2 + 1, : hidden.shape[1]]).astype(BF)
    save(normed, s_normed)
    for i in range(parts):
        wait(i)

        def up_tile(t, carry):
            a = pl.ds(pl.multiple_of(i * step + t * TILE, TILE), TILE)
            b = pl.ds(pl.multiple_of(ff + i * step + t * TILE, TILE), TILE)
            gate = dot(normed[...], wgu[:, a])
            up = dot(normed[...], wgu[:, b])
            gate_low[:, a] = gate.astype(BF)
            up_low[:, a] = up.astype(BF)
            act[:, a] = (gate * sigmoid(gate) * up).astype(BF)
            return carry

        lax.fori_loop(0, step // TILE, up_tile, 0, unroll=True)
    save(gate_low, s_gate)
    save(up_low, s_up)
    save(act, s_act)
    wait(parts)

    def down_tile(t, carry):
        cols = lanes(t)
        out = (hidden_ref[:, cols] + dot(act[...], wdown[:, cols])) * valid
        final[:, cols] = out
        low_ref[:, cols] = out.astype(BF)
        return carry

    lax.fori_loop(0, wdown.shape[1] // TILE, down_tile, 0, unroll=True)
    save(final, s_final)
    save(low_ref, s_low, slot_ref[base + 3])
    yield
    finish()


def mlp_forward_scratch(length, width, ff):
    return [
        pltpu.VMEM((width, 2 * ff), BF),
        pltpu.VMEM((ff, width), BF),
        pltpu.VMEM((length, width), BF),
        pltpu.VMEM((length, ff), BF),
        pltpu.VMEM((length, ff), BF),
        pltpu.VMEM((length, ff), BF),
        pltpu.VMEM((length, width), F32),
        pltpu.SemaphoreType.DMA((32,)),
        pltpu.SemaphoreType.DMA((6,)),
    ]


def mlp_forward_call(index, slot, spots, hidden, vec, weights, stacks, ff):
    length, width = hidden.shape
    scratch = mlp_forward_scratch(length, width, ff)
    return call(
        mlp_forward,
        "mlp_forward",
        [index, slot],
        spots,
        [hidden, vec],
        weights,
        [],
        stacks,
        jax.ShapeDtypeStruct((length, width), BF),
        scratch,
        32,
        3,
    )


def mlp_backward(scalars, spots, ordinary, weights, reads, stacks, d_hidden_ref, scratch):
    index_ref, slot_ref, mix_ref = scalars
    base = 4 * index_ref[0]
    target_ref, vec_ref, _ = ordinary
    w_g, w_u, w_down = weights
    s_final, s_hidden, s_gate, s_up = reads
    (wgu, wdown, final, hidden, gate_low, up_low, d_mlp, d_gu, d_sum, d_normed, small, in_sem,
     out_sem) = scratch
    s_dmlp, s_dgate, s_dup, s_small = stacks
    slot = slot_ref[base]
    ff = wdown.shape[0]
    wait = start_all(
        [
            [(s_final.at[slot], final)],
            [(s_gate.at[slot], gate_low), (s_up.at[slot], up_low)]
            + row_pieces(w_down, spots, wdown, [(slice(0, wdown.shape[1]),) * 2]),
            row_pieces(w_g, spots, wgu, [(slice(0, ff), slice(0, ff))])
            + row_pieces(w_u, spots, wgu, [(slice(0, ff), slice(ff, 2 * ff))]),
            [(s_hidden.at[slot], hidden)],
        ],
        in_sem,
    )
    save, finish = saver(slot, slot_ref[base + 1] > 0, out_sem)
    yield
    wait(0)
    target = target_ref[...].astype(F32)
    valid = jnp.where(iota((target_ref.shape[0], 1), 0) < slot_ref[base + 2], 1.0, 0.0)
    misfit = final[...] - target
    loss = jnp.sum(valid * misfit * misfit, axis=0, keepdims=True)
    seed = valid * jnp.where(mix_ref[0] > 0.5, target, mix_ref[1] * misfit)
    d_sum[...] = seed
    d_mlp[...] = seed.astype(BF)
    save(d_mlp, s_dmlp)
    wait(1)

    def act_tile(t, carry):
        a = lanes(t)
        b = pl.ds(pl.multiple_of(ff + t * TILE, TILE), TILE)
        d_act = dot_nt(d_mlp[...], wdown[a, :])
        gate, up = gate_low[:, a].astype(F32), up_low[:, a].astype(F32)
        s = sigmoid(gate)
        swish = gate * s
        d_gu[:, a] = (d_act * up * (s + swish - swish * s)).astype(BF)
        d_gu[:, b] = (d_act * swish).astype(BF)
        return carry

    lax.fori_loop(0, ff // TILE, act_tile, 0, unroll=True)
    save(d_gu.at[:, :ff], s_dgate)
    save(d_gu.at[:, ff:], s_dup)
    wait(2)
    yield

    def back_tile(t, carry):
        rows = lanes(t)
        d_normed[:, rows] = dot_nt(d_gu[...], wgu[rows, :])
        return carry

    lax.fori_loop(0, wgu.shape[0] // TILE, back_tile, 0, unroll=True)
    wait(3)
    h = hidden[...]
    width = h.shape[1]
    rate = lax.rsqrt(jnp.mean(h * h, axis=-1, keepdims=True) + EPSILON)
    unit = h * rate
    d_n = d_normed[...]
    small[...] = jnp.zeros_like(small)
    small[0:1, :width] = jnp.sum(d_n * unit, axis=0, keepdims=True)
    small[1:2, :width] = loss
    save(small, s_small)
    d_n = d_n * vec_ref[V_G2 : V_G2 + 1, :width]
    d_hidden_ref[...] = d_sum[...] + rate * (
        d_n - unit * jnp.mean(d_n * unit, axis=-1, keepdims=True)
    )
    yield
    finish()


def mlp_backward_scratch(length, width, ff, small):
    return [
        pltpu.VMEM((width, 2 * ff), BF),
        pltpu.VMEM((ff, width), BF),
        pltpu.VMEM((length, width), F32),
        pltpu.VMEM((length, width), F32),
        pltpu.VMEM((length, ff), BF),
        pltpu.VMEM((length, ff), BF),
        pltpu.VMEM((length, width), BF),
        pltpu.VMEM((length, 2 * ff), BF),
        pltpu.VMEM((length, width), F32),
        pltpu.VMEM((length, width), F32),
        pltpu.VMEM(small, F32),
        pltpu.SemaphoreType.DMA((32,)),
        pltpu.SemaphoreType.DMA((4,)),
    ]


def mlp_backward_call(index, slot, mix, spots, target, vec, turn, weights, reads, stacks, ff):
    length, width = target.shape
    scratch = mlp_backward_scratch(length, width, ff, stacks[-1].shape[1:])
    return call(
        mlp_backward,
        "mlp_backward",
        [index, slot, mix],
        spots,
        [target, vec, turn],
        weights,
        reads,
        stacks,
        jax.ShapeDtypeStruct((length, width), F32),
        scratch,
        40,
        3,
    )


def column_sum(v):
    return jnp.sum(v, axis=0, keepdims=True)


def mix_backward(
    widths, scalars, spots, ordinary, weights, reads, stacks, d_input_ref, scratch
):
    ci, mi, qw, kw, heads = widths
    index_ref, slot_ref = scalars
    base = 4 * index_ref[0]
    d_hidden_ref, vec_ref, cos_ref, sin_ref, _ = ordinary
    w_first, w_conv, w_gate, w_out = weights
    s_conv, s_z, s_gate, s_qkv, s_step, s_probs, s_y, s_x = reads
    (win, wout, conv_raw, z, gate_raw, qkv, step_raw, probs, y, x_low, d_branch, d_proj, d_mixed,
     d_ssm, d_z, d_normed, run_wide, run_row, step_two, bend_two, tops, d_tops, run_acc, step_acc,
     small, in_sem, out_sem) = scratch
    s_dbranch, s_dfirst, s_dconv, s_dgate, s_dinput, s_small = stacks
    slot = slot_ref[base]
    g0, q0 = ci, ci + mi
    s0 = q0 + qw + 2 * kw
    total = win.shape[1]
    tail = total - q0
    length, width = d_hidden_ref.shape
    wait = start_all(
        [
            out_pieces(w_out, spots, wout, mi),
            [(s_probs.at[slot], probs), (s_qkv.at[slot], qkv)],
            [(s_step.at[slot], step_raw), (s_gate.at[slot], gate_raw), (s_y.at[slot], y)],
            [(s_z.at[slot], z)],
            [(s_conv.at[slot], conv_raw)],
            row_pieces(w_first, spots, win, [(slice(0, tail), slice(q0, total))])
            + row_pieces(w_conv, spots, win, [(slice(0, ci), slice(0, ci))])
            + row_pieces(w_gate, spots, win, [(slice(0, mi), slice(g0, q0))]),
            [(s_x.at[slot], x_low)],
        ],
        in_sem,
    )
    save, finish = saver(slot, slot_ref[base + 1] > 0, out_sem)
    yield
    small[...] = jnp.zeros_like(small)
    d_branch[...] = d_hidden_ref[...].astype(BF)
    save(d_branch, s_dbranch)
    wait(0)
    for t in range(qw // TILE):
        rows = slice(mi + t * TILE, mi + (t + 1) * TILE)
        d_mixed[:, t * TILE : (t + 1) * TILE] = dot_nt(d_branch[...], wout[rows, :]).astype(BF)

    lane_first = jnp.bitwise_and(iota((length, HALF), 1), HD - 1) < HD // 2
    half_low = iota((length, HALF), 1) < HD
    cosine, sine = cos_ref[...], -sin_ref[...]
    wait(1)
    keys, values = qkv[:, qw : qw + kw], qkv[:, qw + kw : qw + 2 * kw]
    keys_far, values_far = pltpu.roll(keys.astype(F32), HD, 1).astype(BF), pltpu.roll(
        values.astype(F32), HD, 1
    ).astype(BF)
    pairs = qw // HALF
    groups = kw // HD
    scale = HD ** (-0.5)
    d_keys = [jnp.zeros((length, HALF), F32) for _ in range(groups)]
    d_values = [jnp.zeros((length, HALF), F32) for _ in range(groups)]
    for pair in range(pairs):
        group = pair // (pairs // groups)
        keep = half_low if group == 0 else jnp.logical_not(half_low)
        keys_two = jnp.where(keep, keys, keys_far)
        values_two = jnp.where(keep, values, values_far)
        cols = slice(pair * HALF, (pair + 1) * HALF)
        query, d_out = qkv[:, cols], d_mixed[:, cols]
        results = []
        for side in range(2):
            own = half_low if side == 0 else jnp.logical_not(half_low)
            q = jnp.where(own, query, jnp.zeros_like(query))
            d_o = jnp.where(own, d_out, jnp.zeros_like(d_out))
            at = (2 * pair + side) * length
            weights = probs[at : at + length, :]
            wide = weights.astype(F32)
            d_weights = dot_nt(d_o, values_two)
            inner = wide * d_weights
            d_scores = (inner - wide * jnp.sum(inner, axis=-1, keepdims=True)).astype(BF)
            results.append(dot(d_scores, keys_two))
            d_keys[group] = d_keys[group] + dot_tn(d_scores, q)
            d_values[group] = d_values[group] + dot_tn(weights, d_o)
        d_q = jnp.where(half_low, results[0], results[1]) * scale
        d_proj[:, q0 + pair * HALF : q0 + (pair + 1) * HALF] = rope(
            d_q, cosine, sine, lane_first
        ).astype(BF)
    folded = [v + pltpu.roll(v, HD, 1) for v in d_keys]
    d_k = jnp.where(half_low, folded[0], folded[1]) * scale
    d_proj[:, q0 + qw : q0 + qw + kw] = rope(d_k, cosine, sine, lane_first).astype(BF)
    folded = [v + pltpu.roll(v, HD, 1) for v in d_values]
    d_proj[:, q0 + qw + kw : s0] = jnp.where(half_low, folded[0], folded[1]).astype(BF)

    wait(2)

    def norm_tile(t, sums):
        cols = lanes(t)
        d_s = dot_nt(d_branch[...], wout[cols, :])
        d_ssm[:, cols] = d_s
        g = gate_raw[:, cols].astype(F32)
        gated = y[:, cols].astype(F32) * (g * sigmoid(g))
        d_n = d_s * vec_ref[V_GS : V_GS + 1, cols]
        return (
            sums[0] + jnp.sum(gated * gated, axis=-1, keepdims=True),
            sums[1] + jnp.sum(gated * d_n, axis=-1, keepdims=True),
        )

    zero_col = jnp.zeros((length, 1), F32)
    squares, along = lax.fori_loop(0, mi // TILE, norm_tile, (zero_col, zero_col), unroll=True)
    rate = lax.rsqrt(squares * (1.0 / mi) + EPSILON)
    along = along * (rate * rate) * (1.0 / mi)

    pre, step, change, run, bend = scan_terms(step_raw[...], vec_ref, heads)
    turned = run.T
    run_row[:HALF, :] = turned[:, :HALF]
    run_row[HALF:, :] = turned[:, HALF:]
    broadcast_runs(run, run_wide, heads)
    step_two[...] = both(step)
    bend_two[...] = both(bend)
    wait(3)
    zb = z[:, mi : mi + 2 * HALF].astype(F32)
    sb = sigmoid(zb)
    bc = (zb * sb).astype(BF)
    b_in, c_in = bc[:, :HALF], bc[:, HALF:]
    causal = iota((HALF, HALF), 1) <= iota((HALF, HALF), 0)
    for c in range(2):
        rows = slice(c * HALF, (c + 1) * HALF)
        tops[rows, :] = jnp.where(causal, dot_nt(c_in[rows], b_in[rows]), 0.0)
    cross = dot_nt(c_in[HALF:], b_in[:HALF])
    cross_turned = cross.T.astype(BF)
    cross = cross.astype(BF)
    pair_low = iota((HALF, HALF), 1) < HD
    d_tops[...] = jnp.zeros_like(d_tops)
    run_acc[...] = jnp.zeros_like(run_acc)
    step_acc[...] = jnp.zeros_like(step_acc)

    def mix_tile(t, carry):
        cols = lanes(t)
        g = gate_raw[:, cols].astype(F32)
        s = sigmoid(g)
        swish = g * s
        y_in = y[:, cols].astype(F32)
        gated = y_in * swish
        d_s = d_ssm[:, cols]
        small[V_GS : V_GS + 1, cols] = column_sum(d_s * gated * rate)
        d_gated = rate * (d_s * vec_ref[V_GS : V_GS + 1, cols]) - gated * (along * rate)
        d_proj[:, pl.ds(pl.multiple_of(g0 + t * TILE, TILE), TILE)] = (
            d_gated * y_in * (s + swish - swish * s)
        ).astype(BF)
        d_y = d_gated * swish
        z_in = z[:, cols].astype(F32)
        s = sigmoid(z_in)
        x_in = z_in * s
        slope = s + x_in - x_in * s
        spread = expand_matrix(t)
        steps = dot(step_two[...], spread)
        bends = dot(bend_two[...], spread)
        scaled = (steps * x_in).astype(BF)
        d_low = d_y.astype(BF)
        u = (bends[:HALF] * scaled[:HALF].astype(F32)).astype(BF)
        v = (bends[HALF:] * d_y[HALF:]).astype(BF)
        far = dot(cross, u)
        back = dot(cross_turned, v)
        d_tops[2 * HALF :, :] += dot_nt(v, u)
        mixed_parts, back_parts = [], []
        for p in range(TILE // HALF):
            mixed_block, back_block = [], []
            for c in range(2):
                rows = slice(c * HALF, (c + 1) * HALF)
                xs = scaled[rows, p * HALF : (p + 1) * HALF]
                dy = d_low[rows, p * HALF : (p + 1) * HALF]
                zero = jnp.zeros_like(xs)
                xs_two = [jnp.where(pair_low, xs, zero), jnp.where(pair_low, zero, xs)]
                dy_two = [jnp.where(pair_low, dy, zero), jnp.where(pair_low, zero, dy)]
                weights = []
                d_top = jnp.zeros((HALF, HALF), F32)
                for side in range(2):
                    h = t * (TILE // HD) + 2 * p + side
                    wide = run_wide[rows, lanes(h, HALF)]
                    line = run_row[pl.ds(c * HALF + h, 1), :]
                    decay = jnp.exp(jnp.minimum(wide - line, 0.0))
                    weights.append((decay * tops[rows, :]).astype(BF))
                    d_top = d_top + decay * dot_nt(dy_two[side], xs)
                d_tops[rows, :] += d_top
                mixed_block.append(
                    dot(jnp.concatenate(weights, axis=1), jnp.concatenate(xs_two, axis=0))
                )
                back_block.append(
                    dot_tn(jnp.concatenate(weights, axis=0), jnp.concatenate(dy_two, axis=0))
                )
            mixed_parts.append(jnp.concatenate(mixed_block, axis=0))
            back_parts.append(jnp.concatenate(back_block, axis=0))
        mixed = jnp.concatenate(mixed_parts, axis=1)
        d_scaled = jnp.concatenate(back_parts, axis=1)
        crossing = jnp.concatenate(
            [-(u.astype(F32) * back), v.astype(F32) * far], axis=0
        )
        runs = d_low.astype(F32) * mixed - scaled.astype(F32) * d_scaled + crossing
        d_scaled = d_scaled + jnp.concatenate([bends[:HALF] * back, jnp.zeros_like(back)], axis=0)
        gather = reduce_matrix(t)
        run_acc[...] += sum(dot(part, gather) for part in split2(runs))
        step_acc[...] += sum(dot(part, gather) for part in split2(x_in * d_scaled))
        small[V_SKIP : V_SKIP + 1, cols] = column_sum(d_y * x_in)
        d_x = steps * d_scaled + vec_ref[V_SKIP : V_SKIP + 1, cols] * d_y
        d_z[:, cols] = d_x * slope
        return carry

    lax.fori_loop(0, mi // TILE, mix_tile, 0, unroll=True)
    d_top = [
        jnp.where(causal, d_tops[c * HALF : (c + 1) * HALF, :], 0.0).astype(BF) for c in range(2)
    ]
    d_cross = d_tops[2 * HALF :, :].astype(BF)
    d_c = jnp.concatenate(
        [dot(d_top[0], b_in[:HALF]), dot(d_cross, b_in[:HALF]) + dot(d_top[1], b_in[HALF:])], axis=0
    )
    d_b = jnp.concatenate(
        [dot_tn(d_top[0], c_in[:HALF]) + dot_tn(d_cross, c_in[HALF:]), dot_tn(d_top[1], c_in[HALF:])],
        axis=0,
    )
    xb = zb * sb
    d_z[:, mi : mi + 2 * HALF] = jnp.concatenate([d_b, d_c], axis=1) * (sb + xb - xb * sb)
    upper = jnp.where(
        iota((length, length), 0) <= iota((length, length), 1), 1.0, 0.0
    ).astype(BF)
    d_change = sum(dot(upper, part) for part in split3(run_acc[...]))
    d_pre = (step_acc[...] + d_change * vec_ref[V_DECAY : V_DECAY + 1, :HALF]) * sigmoid(pre)
    d_pre = jnp.where(iota(d_pre.shape, 1) < heads, d_pre, 0.0)
    d_proj[:, s0:total] = d_pre.astype(BF)
    small[V_SBIAS : V_SBIAS + 1, :HALF] = column_sum(d_pre)
    small[V_DECAY : V_DECAY + 1, :HALF] = column_sum(d_change * change)

    wait(4)
    row = iota((length, TILE), 0)

    def conv_tile(t, carry):
        cols = lanes(t)
        d = d_z[:, cols]
        raw = conv_raw[:, cols].astype(F32)
        small[V_CBIAS : V_CBIAS + 1, cols] = column_sum(d)
        small[3:4, cols] = column_sum(d * raw)
        out = d * vec_ref[3:4, cols]
        for ahead in range(1, 4):
            moved = jnp.where(row < length - ahead, pltpu.roll(d, length - ahead, 0), 0.0)
            small[3 - ahead : 4 - ahead, cols] = column_sum(moved * raw)
            out = out + moved * vec_ref[3 - ahead : 4 - ahead, cols]
        d_proj[:, cols] = out.astype(BF)
        return carry

    lax.fori_loop(0, ci // TILE, conv_tile, 0, unroll=True)
    save(d_proj.at[:, q0:], s_dfirst)
    save(d_proj.at[:, :ci], s_dconv)
    save(d_proj.at[:, g0:q0], s_dgate)

    wait(5)

    def back_tile(t, carry):
        rows = lanes(t)
        d_normed[:, rows] = dot_nt(d_proj[...], win[rows, :])
        return carry

    lax.fori_loop(0, width // TILE, back_tile, 0, unroll=True)
    wait(6)
    x = x_low[...].astype(F32)
    rate_one = lax.rsqrt(jnp.mean(x * x, axis=-1, keepdims=True) + EPSILON)
    unit = x * rate_one
    d_n = d_normed[...]
    small[V_G1 : V_G1 + 1, :width] = column_sum(d_n * unit)
    save(small, s_small)
    d_n = d_n * vec_ref[V_G1 : V_G1 + 1, :width]
    d_input_ref[...] = (
        d_hidden_ref[...]
        + rate_one * (d_n - unit * jnp.mean(d_n * unit, axis=-1, keepdims=True))
    ).astype(BF)
    save(d_input_ref, s_dinput, slot_ref[base + 3])
    yield
    finish()


def mixer_backward_scratch(length, width, widths, total, small):
    ci, mi, qw, kw, heads = widths
    return [
        pltpu.VMEM((width, total), BF),
        pltpu.VMEM((mi + qw, width), BF),
        pltpu.VMEM((length, ci), BF),
        pltpu.VMEM((length, ci), BF),
        pltpu.VMEM((length, mi), BF),
        pltpu.VMEM((length, qw + 2 * kw), BF),
        pltpu.VMEM((length, HALF), F32),
        pltpu.VMEM((qw // HD * length, length), BF),
        pltpu.VMEM((length, mi), BF),
        pltpu.VMEM((length, width), BF),
        pltpu.VMEM((length, width), BF),
        pltpu.VMEM((length, total), BF),
        pltpu.VMEM((length, qw), BF),
        pltpu.VMEM((length, mi), F32),
        pltpu.VMEM((length, ci), F32),
        pltpu.VMEM((length, width), F32),
        pltpu.VMEM((length, heads * HALF), F32),
        pltpu.VMEM((length, HALF), F32),
        pltpu.VMEM((length, 2 * HALF), BF),
        pltpu.VMEM((length, 2 * HALF), BF),
        pltpu.VMEM((2 * HALF, HALF), F32),
        pltpu.VMEM((3 * HALF, HALF), F32),
        pltpu.VMEM((length, HALF), F32),
        pltpu.VMEM((length, HALF), F32),
        pltpu.VMEM(small, F32),
        pltpu.SemaphoreType.DMA((48,)),
        pltpu.SemaphoreType.DMA((6,)),
    ]


def mixer_backward_call(
    index, slot, spots, d_hidden, vec, cosine, sine, turn, weights, reads, stacks, widths, total
):
    ci, mi, qw, kw, heads = widths
    length, width = d_hidden.shape
    scratch = mixer_backward_scratch(length, width, widths, total, stacks[-1].shape[1:])
    return call(
        functools.partial(mix_backward, widths),
        "mixer_backward",
        [index, slot],
        spots,
        [d_hidden, vec, cosine, sine, turn],
        weights,
        reads,
        stacks,
        jax.ShapeDtypeStruct((length, width), BF),
        scratch,
        48,
        250,
    )


def weight_kernel(core_ref, away_ref, stay_ref, right_ref, out_away, out_stay, turned):
    rows = away_ref.shape[2]
    tokens = away_ref.shape[0] * away_ref.shape[1]
    turned[:rows, :] = away_ref[...].reshape(tokens, rows).T
    turned[rows:, :] = stay_ref[...].reshape(tokens, rows).T
    right = right_ref[...].reshape(tokens, right_ref.shape[2])
    out_away[0] = dot(turned[:rows, :], right).astype(BF)
    out_stay[0] = dot(turned[rows:, :], right).astype(BF)


def weight_grad_halves(core, left, right):
    count, length, depth = left.shape
    columns = right.shape[2]
    rows = depth // 4
    grid = pltpu.PrefetchScalarGridSpec(
        num_scalar_prefetch=1,
        grid=(2,),
        in_specs=[
            pl.BlockSpec((count, length, rows), lambda c, core: (0, 0, 2 * c + 1 - core[0])),
            pl.BlockSpec((count, length, rows), lambda c, core: (0, 0, 2 * c + core[0])),
            pl.BlockSpec((count, length, columns), lambda c, core: (0, 0, 0)),
        ],
        out_specs=[pl.BlockSpec((1, rows, columns), lambda c, core: (c, 0, 0))] * 2,
        scratch_shapes=[pltpu.VMEM((2 * rows, count * length), BF)],
    )
    shape = pltpu.HBM((2, rows, columns), BF)
    return pl.pallas_call(
        weight_kernel,
        out_shape=[shape, shape],
        grid_spec=grid,
        compiler_params=pltpu.CompilerParams(vmem_limit_bytes=40 * 1024 * 1024),
        cost_estimate=pl.CostEstimate(
            flops=100000000, bytes_accessed=1000000, transcendentals=0
        ),
        name="weight_gradient",
    )(core, in_hbm(left), in_hbm(left), in_hbm(right))


def layer_forward_call(
    index, slot, spots, x, vec, cosine, sine, turn, weights, stacks, widths, total, ff
):
    length, width = x.shape
    first = mixer_forward_scratch(length, width, widths, total)
    second = mlp_forward_scratch(length, width, ff)
    n = 12

    def body(scalars, spots, ordinary, weights, reads, stacks, low_ref, scratch):
        hidden = scratch[-1]
        one = mix_forward(
            widths, scalars, spots, ordinary, weights[:4], [], stacks[:n], hidden,
            scratch[: len(first)],
        )
        two = mlp_forward(
            scalars, spots, [hidden, ordinary[1]], weights[4:], [], stacks[n:], low_ref,
            scratch[len(first) : -1],
        )
        for part in (one, one, two, one, two, one, two):
            next(part, None)
        yield

    return call(
        body,
        "layer_forward",
        [index, slot],
        spots,
        [x, vec, cosine, sine, turn],
        weights,
        [],
        stacks,
        jax.ShapeDtypeStruct((length, width), BF),
        first + second + [pltpu.VMEM((length, width), F32)],
        58,
        200,
    )


def layer_backward_call(
    index, slot, mix, spots, target, vec, cosine, sine, turn, weights, reads, stacks, widths, total, ff
):
    length, width = target.shape
    first = mlp_backward_scratch(length, width, ff, stacks[3].shape[1:])
    second = mixer_backward_scratch(length, width, widths, total, stacks[-1].shape[1:])
    n = 4

    def body(scalars, spots, ordinary, weights, reads, stacks, d_input_ref, scratch):
        d_hidden = scratch[-1]
        target_ref, vec_ref, cos_ref, sin_ref, turn_ref = ordinary
        one = mlp_backward(
            scalars, spots, [target_ref, vec_ref, turn_ref], weights[4:], reads[:4],
            stacks[:n], d_hidden, scratch[: len(first)],
        )
        two = mix_backward(
            widths, scalars[:2], spots, [d_hidden, vec_ref, cos_ref, sin_ref, turn_ref],
            weights[:4], reads[4:], stacks[n:], d_input_ref, scratch[len(first) : -1],
        )
        for part in (one, one, two, one, two, one, two):
            next(part, None)
        yield

    return call(
        body,
        "layer_backward",
        [index, slot, mix],
        spots,
        [target, vec, cosine, sine, turn],
        weights,
        reads,
        stacks,
        jax.ShapeDtypeStruct((length, width), BF),
        first + second + [pltpu.VMEM((length, width), F32)],
        60,
        250,
    )


def rope_tables(length):
    halves = HD // 2
    inverse = jnp.exp(jnp.arange(halves, dtype=F32) * (-2.0 * math.log(ROPE_BASE) / HD))
    angles = jnp.arange(length, dtype=F32)[:, None] * inverse[None, :]
    cosine, sine = jnp.cos(angles), jnp.sin(angles)
    return (
        jnp.concatenate([cosine] * 4, axis=1),
        jnp.concatenate([-sine, sine, -sine, sine], axis=1),
    )


def swap(block, axis, bit):
    return lax.ppermute(block, axis, [(i, i ^ bit) for i in range(lax.axis_size(axis))])


def after(value, *others):
    if not others:
        return value
    return lax.optimization_barrier((value,) + others)[0]


def corner(made):
    part = made.reshape(-1, made.shape[-1])[:8, :HALF].astype(BF)
    return jnp.dot(part, jnp.ones((HALF, HALF), BF), preferred_element_type=F32)


def quick_links():
    return lax.axis_size("fsdp") == 4 and lax.axis_size("rep") == 4


def gather_halves(shard, axis, before_y=(), before_z=()):
    parity = lax.axis_index("rep") % 2
    half = shard.shape[axis] // 2
    mine = lax.dynamic_slice_in_dim(shard, parity * half, half, axis)
    near = swap(shard, "fsdp", 1)
    far_one = swap(after(mine, *before_y), "fsdp", 2)
    far_two = swap(after(far_one, *before_z), "rep", 1)
    return [shard, near, far_one, far_two]


def gather_wholes(shard, *before_y):
    return [shard, swap(shard, "fsdp", 1), swap(after(shard, *before_y), "fsdp", 2)]


def share_far(pieces, *before):
    return pieces + [swap(after(piece, *before), "fsdp", 1) for piece in pieces[2:]]


def plus(a, b):
    return (a.astype(F32) + b.astype(F32)).astype(BF)


def weight_grad(left, right):
    return lax.dot_general(
        left, right, (((0, 1), (0, 1)), ((), ())), preferred_element_type=F32
    ).astype(BF)


class Reduction:
    def __init__(self, left, right, riders=None):
        self.left, self.right, self.riders = left, right, riders

    def begin(self, order):
        left, right = order(self.left, self.right)
        core = lax.axis_index("fsdp") % 2
        away, stay = weight_grad_halves(core.astype(jnp.int32)[None], left, right)
        if self.riders is not None:
            blocks, column = self.riders
            away, stay = (
                lax.dynamic_update_slice(
                    grad, lax.dynamic_index_in_dim(blocks, i, 1, keepdims=False), (0, 0, column)
                )
                for grad, i in ((away, 1 - core), (stay, core))
            )
        self.stay = stay
        self.moved = swap(away, "fsdp", 1)
        return stay

    def chips(self, order):
        chip = lax.axis_index("fsdp") // 2
        self.kept = order(self.stay, self.moved)

        def part(i):
            return [lax.dynamic_index_in_dim(v, i, 0, keepdims=False) for v in self.kept]

        away = plus(*part(1 - chip))
        self.moved = swap(away, "fsdp", 2)
        return away

    def line_in(self, order):
        chip = lax.axis_index("fsdp") // 2
        *kept, moved = order(*self.kept, self.moved)
        one, two = (lax.dynamic_index_in_dim(v, chip, 0, keepdims=False) for v in kept)
        self.stay = (one.astype(F32) + two.astype(F32) + moved.astype(F32)).astype(BF)
        self.moved = lax.ppermute(self.stay, "rep", [(0, 1), (3, 2)])
        return self.stay

    def middle(self, order):
        stay, moved = order(self.stay, self.moved)
        self.stay = plus(stay, moved)
        self.moved = lax.ppermute(self.stay, "rep", [(1, 2), (2, 1)])
        return self.stay

    def line_out(self, order):
        stay, moved = order(self.stay, self.moved)
        self.stay = plus(stay, moved)
        self.moved = lax.ppermute(self.stay, "rep", [(1, 0), (2, 3)])
        return self.stay

    def finish(self, order):
        stay, moved = order(self.stay, self.moved)
        rank = lax.axis_index("rep")
        inner = jnp.logical_or(rank == 1, rank == 2)
        self.result = jnp.where(inner, stay, moved).astype(F32)
        return self.result


def body(
    inputs,
    teacher,
    lengths,
    order,
    loss_scale,
    norm_gain1,
    w_query,
    w_key,
    w_value,
    w_attn_out,
    w_ssm_gate,
    w_conv_in,
    w_step,
    conv_kernel,
    conv_bias,
    step_bias,
    decay_log,
    skip_gain,
    ssm_norm_gain,
    w_ssm_out,
    norm_gain2,
    w_gate,
    w_up,
    w_down,
):
    quick = quick_links()
    n_rep = lax.axis_size("rep")
    n_fsdp = lax.axis_size("fsdp")
    rank = lax.axis_index("rep")
    fsdp = lax.axis_index("fsdp")
    section = lax.axis_index("section")
    first = section == 0
    device = fsdp * n_rep + rank
    count, length, width = inputs.shape
    ci, mi, qw, kw = (w.shape[2] for w in (w_conv_in, w_ssm_gate, w_query, w_key))
    heads = w_step.shape[2]
    ff = w_up.shape[2]
    widths = (ci, mi, qw, kw, heads)
    taps = conv_kernel.shape[1]
    rows = width // n_fsdp
    tail = qw + 2 * kw + HALF
    total = ci + mi + tail

    def columns(flat):
        wide = -(-flat.size // rows)
        return jnp.pad(flat, (0, wide * rows - flat.size)).reshape(rows, wide)

    convs = jnp.concatenate([conv_kernel[0], conv_bias], axis=0)
    riders = jnp.concatenate(
        [
            norm_gain1[0][:, None],
            norm_gain2[0][:, None],
            columns(convs.reshape(-1)),
            columns(ssm_norm_gain[0]),
        ],
        axis=1,
    )
    used = riders.shape[1]
    wide = -(-convs.size // rows)
    shard_first = jnp.concatenate(
        [w_query[0], w_key[0], w_value[0], w_step[0]] + [jnp.zeros((rows, HALF - heads), BF)],
        axis=1,
    )
    parity = rank % 2
    if quick:
        g_gate = gather_halves(w_ssm_gate[0], 0)
        g_conv = gather_halves(w_conv_in[0], 0)
        g_first = gather_halves(shard_first, 0, (), g_gate[3:4])
        shard_out = jnp.concatenate([w_ssm_out[0], w_attn_out[0]], axis=0)
        g_out = gather_halves(shard_out, 1, g_gate[2:3], g_conv[3:4])
        g_g = gather_halves(w_gate[0], 0, g_conv[2:3], g_first[3:4])
        g_u = gather_wholes(w_up[0], g_out[2])
        g_gate, g_conv, g_first, g_out = (
            share_far(g, g_out[3]) for g in (g_gate, g_conv, g_first, g_out)
        )
        spots = [2 * fsdp, 2 * (fsdp ^ 1)]
        spots += [2 * (fsdp ^ k) + b for k in (2, 3) for b in (parity, 1 - parity)]
        spots = jnp.stack(spots).astype(jnp.int32)
        far = swap(riders, "fsdp", 2)
        blocks = jnp.stack([riders, swap(riders, "fsdp", 1), far, swap(far, "fsdp", 1)])
        ridden = jnp.take(blocks, jnp.arange(4, dtype=jnp.int32) ^ fsdp, axis=0)
    else:

        def whole(shard):
            return lax.all_gather(shard, "fsdp", axis=0, tiled=True)

        g_first, g_conv, g_gate, g_g, g_u, g_down = (
            [whole(w)]
            for w in (shard_first, w_conv_in[0], w_ssm_gate[0], w_gate[0], w_up[0], w_down[0])
        )
        g_out = [jnp.concatenate([whole(w_ssm_out[0]), whole(w_attn_out[0])], axis=0)]
        spots = jnp.zeros((1,), jnp.int32)
        ridden = whole(riders).reshape(n_fsdp, rows, used)
    if quick:
        order = after(order, g_gate[3])

    turns = jnp.arange(count, dtype=jnp.int32)
    numbers = jnp.arange(order.shape[0], dtype=jnp.int32)
    mine = device * count + turns
    sources = jnp.sum(jnp.where(order[None, :] == mine[:, None], numbers[None, :], 0), axis=1)
    target = lax.dynamic_slice_in_dim(order, device * count, count) // count % n_rep
    anchor = sources // count % n_rep

    def inverse(key):
        return jnp.sum(jnp.where((key ^ rank)[None, :] == turns[:, None], turns[None, :], 0), axis=1)

    send_at, keep_at = inverse(target), inverse(anchor)
    own_lengths = jnp.take(lengths, jnp.take(sources, keep_at))
    outgoing = [
        jnp.where(
            first,
            lax.dynamic_index_in_dim(inputs, send_at[j], 0, keepdims=False),
            lax.dynamic_index_in_dim(teacher, send_at[j], 0, keepdims=False),
        )
        for j in range(count)
    ]
    dealt = [outgoing[0]]

    def deal(j, *earlier):
        dealt.append(swap(after(outgoing[j], *earlier), "rep", j))


    if quick:
        deal(1, g_out[3])
        deal(2, dealt[1])
    else:
        for j in range(1, count - 1):
            deal(j)

    mixer_weights = [g_first, g_conv, g_gate, g_out]
    mlp_weights = None if quick else [g_g, g_u, g_down]

    conv_all = ridden[:, :, 2 : 2 + wide].reshape(n_fsdp, -1)[:, : (taps + 1) * ci // n_fsdp]
    conv_all = conv_all.reshape(n_fsdp, taps + 1, ci // n_fsdp).transpose(1, 0, 2)
    ssm_gain = ridden[:, :, 2 + wide :].reshape(n_fsdp, -1)[:, : mi // n_fsdp].reshape(1, mi)

    def table_row(v):
        v = v.astype(F32)
        return jnp.pad(v, ((0, 0), (0, ci - v.shape[1])))

    vec = jnp.concatenate(
        [
            table_row(v)
            for v in (
                conv_all.reshape(taps + 1, ci),
                ssm_gain,
                jnp.repeat(skip_gain, HD, axis=1),
                ridden[:, :, 0].reshape(1, width),
                ridden[:, :, 1].reshape(1, width),
                step_bias,
                -jnp.exp(decay_log),
                jnp.zeros((16 - taps - 7, 1), F32),
            )
        ],
        axis=0,
    )
    cosine, sine = rope_tables(length)

    valid_count = jnp.sum(lengths).astype(F32)
    factor = loss_scale / (valid_count * width)

    skew = 2
    steps = count + skew
    ticks = jnp.arange(steps, dtype=jnp.int32)
    raw = jnp.concatenate([ticks - skew * section, count - 1 - ticks + skew * (1 - section)])
    inside = jnp.logical_and(raw >= 0, raw < count).astype(jnp.int32)
    slots = jnp.clip(raw, 0, count - 1)
    plan = [slots, inside, jnp.take(own_lengths, slots), jnp.take(keep_at, slots)]
    plan = jnp.stack(plan, axis=1).reshape(-1)
    mix = jnp.stack([jnp.where(first, 1.0, 0.0), 2.0 * factor])

    def stack(*shape, kind=BF):
        return jax.ShapeDtypeStruct((count,) + shape, kind)

    mix_stacks = [
        stack(length, width),
        stack(length, ci),
        stack(length, ci),
        stack(length, mi),
        stack(length, qw + 2 * kw),
        stack(length, HALF, kind=F32),
        stack(qw // HD * length, length),
        stack(length, mi),
        stack(length, qw),
        stack(length, mi),
        stack(length, width, kind=F32),
        stack(length, width),
    ]
    mlp_stacks = [
        stack(length, width),
        stack(length, ff),
        stack(length, ff),
        stack(length, ff),
        stack(length, width, kind=F32),
        stack(length, width),
    ]

    token = []

    def chained(*values):
        if not quick or not token:
            return values
        return lax.optimization_barrier(values + tuple(token))[: len(values)]

    def chain(made):
        token[:] = [made]

    received, hiddens = [], []

    blank = jnp.zeros((8, HALF), F32)

    def number(i):
        return jnp.full((1,), i, jnp.int32)

    def mixer_tick(tick, turn, mix_stacks):
        mix_stacks, hidden = mixer_forward_call(
            number(tick),
            plan,
            spots,
            dealt[tick],
            vec,
            cosine,
            sine,
            corner(turn),
            mixer_weights,
            mix_stacks,
            widths,
            total,
        )
        chain(hidden)
        hiddens.append(hidden)
        return mix_stacks

    def mlp_tick(tick, mlp_stacks):
        (hidden,) = chained(hiddens[tick])
        mlp_stacks, low = mlp_forward_call(
            number(tick), plan, spots, hidden, vec, mlp_weights, mlp_stacks, ff
        )
        return mlp_stacks, low

    def layer_tick(tick, turn, stacks):
        if tick < count:
            one, two = chained(dealt[tick], received[tick - skew])
            seq_in = jnp.where(first, one, two)
        else:
            seq_in = received[tick - skew]
        return layer_forward_call(
            number(tick),
            plan,
            spots,
            seq_in,
            vec,
            cosine,
            sine,
            corner(turn) if tick < steps - 1 else blank,
            mixer_weights + mlp_weights,
            stacks,
            widths,
            total,
            ff,
        )

    if quick:
        dealt[0] = after(dealt[0], dealt[1])
    mix_stacks = mixer_tick(0, dealt[0], mix_stacks)
    if quick:
        g_down = gather_wholes(w_down[0], hiddens[0])
    mix_stacks = mixer_tick(1, hiddens[0], mix_stacks)
    if quick:
        mlp_weights = [share_far(g, hiddens[1], dealt[2]) for g in (g_g, g_u, g_down)]
    for tick in range(steps):
        if tick < skew:
            mlp_stacks, low = mlp_tick(tick, mlp_stacks)
            if tick == 0:
                deal(count - 1, low)
        else:
            stacks, low = layer_tick(tick, low, mix_stacks + mlp_stacks)
            mix_stacks, mlp_stacks = stacks[: len(mix_stacks)], stacks[len(mix_stacks) :]
        chain(low)
        if tick < count:
            received.append(lax.ppermute(low, "section", [(0, 1)]))

    (s_normed, s_conv, s_z, s_gate, s_qkv, s_step, s_probs, s_ssm, s_mixed, s_y, s_hidden,
     s_x) = mix_stacks
    s_normed2, s_g, s_u, s_act, s_final, s_low = mlp_stacks
    mlp_grads = [
        stack(length, width),
        stack(length, ff),
        stack(length, ff),
        stack(8, width, kind=F32),
    ]
    mix_grads = [
        stack(length, width),
        stack(length, tail),
        stack(length, ci),
        stack(length, mi),
        stack(length, width),
        stack(16, ci, kind=F32),
    ]
    incoming, returned = [], [None] * count

    hiddens = []

    def mlp_turn(turn, mlp_grads):
        if turn == count:
            token.append(returned[3])
        (seed,) = chained(incoming[turn - skew])
        return mlp_backward_call(
            number(steps + turn),
            plan,
            mix,
            spots,
            seed,
            vec,
            corner(hiddens[-1]) if turn > count else blank,
            mlp_weights,
            reads,
            mlp_grads,
            ff,
        )

    def mixer_turn(turn, d_hidden, before, mix_grads):
        mix_grads, d_input = mixer_backward_call(
            number(steps + turn),
            plan,
            spots,
            d_hidden,
            vec,
            cosine,
            sine,
            corner(before),
            mixer_weights,
            mix_reads,
            mix_grads,
            widths,
            total,
        )
        send_back(turn, d_input)
        return mix_grads, d_input

    def send_back(turn, d_input):
        if turn < count:
            incoming.append(lax.ppermute(d_input, "section", [(1, 0)]))
        if turn >= skew:
            j = count - 1 - turn + skew
            back = lax.dynamic_index_in_dim(after(s_low, d_input), keep_at[j], 0, keepdims=False)
            back = jnp.where(first, d_input, back)
            returned[j] = swap(back, "rep", j) if j else back

    reads = [s_final, s_hidden, s_g, s_u]
    mix_reads = [s_conv, s_z, s_gate, s_qkv, s_step, s_probs, s_y, s_x]
    d_input = low
    for turn in range(count):
        if turn < skew:
            (seed,) = chained(dealt[count - 1 - turn])
        else:
            one, two = chained(incoming[turn - skew], dealt[count - 1 - turn])
            seed = jnp.where(first, one, two)
        grads, d_input = layer_backward_call(
            number(steps + turn),
            plan,
            mix,
            spots,
            seed,
            vec,
            cosine,
            sine,
            corner(d_input) if turn else blank,
            mixer_weights + mlp_weights,
            reads + mix_reads,
            mlp_grads + mix_grads,
            widths,
            total,
            ff,
        )
        mlp_grads, mix_grads = grads[: len(mlp_grads)], grads[len(mlp_grads) :]
        chain(d_input)
        send_back(turn, d_input)

    loss_part = jnp.sum(mlp_grads[3][:, 1])[None]
    loss_part = jnp.where(first, lax.ppermute(loss_part, "section", [(1, 0)]), loss_part)

    for turn in range(count, steps):
        mlp_grads, d_hidden = mlp_turn(turn, mlp_grads)
        chain(d_hidden)
        hiddens.append(d_hidden)
    s_dmlp, s_dg, s_du, small_mlp = mlp_grads
    early = [(s_normed2, s_dg), (s_normed2, s_du), (s_act, s_dmlp)]
    chunks = [Reduction(*pair) for pair in early]

    names = dict(W="begin", A="chips", L="line_in", M="middle", O="line_out", F="finish")
    state = [mix_grads]

    def stages(*words):
        for word in words:
            letter, place = word[0], int(word[1:])
            if letter == "B":
                before = token[0] if quick else hiddens[place - count]
                state[0], made = mixer_turn(place, hiddens[place - count], before, state[0])
            else:
                made = getattr(chunks[place], names[letter])(chained)
            chain(made)

    if quick:
        stages(
            "W2", "W0", "W1", "A0", "B4"
        )
        token.append(returned[2])
        stages(
            "A1", "A2", "L0", "B5"
        )
    else:
        stages("B4", "B5")
    mix_grads = state[0]
    s_dbranch, s_dfirst, s_dconv, s_dgate, s_dinput, small_mix = mix_grads
    late = [
        (s_normed, s_dconv),
        (s_normed, s_dgate),
        (s_ssm, s_dbranch),
        (s_normed, s_dfirst),
        (s_mixed, s_dbranch),
    ]

    mix_sum = jnp.sum(small_mix, axis=0)
    mlp_sum = jnp.sum(small_mlp, axis=0)
    singles = jnp.concatenate(
        [
            mix_sum[V_SBIAS, :heads],
            mix_sum[V_DECAY, :heads],
            jnp.sum(mix_sum[V_SKIP, :mi].reshape(heads, HD), axis=1),
            loss_part,
        ]
    )

    def share(v):
        return v.reshape(v.shape[0], n_fsdp, -1).transpose(1, 0, 2).reshape(n_fsdp, -1)

    shares = [
        share(mix_sum[: taps + 1]),
        share(mix_sum[V_GS : V_GS + 1, :mi]),
        share(mix_sum[V_G1 : V_G1 + 1, :width]),
        share(mlp_sum[:1]),
        jnp.broadcast_to(singles[None], (n_fsdp, singles.size)),
    ]
    cuts = [v.shape[1] for v in shares]
    flat = jnp.concatenate(shares, axis=1)

    if quick:
        spare = -(-flat.shape[1] // rows)
        flat = jnp.pad(flat, ((0, 0), (0, spare * rows - flat.shape[1])))
        riders = flat.astype(BF).reshape(2, 2, rows, spare)
        column = tail - HALF + heads
        chunks += [Reduction(*pair) for pair in late]
        chunks[6].riders = (riders, column)
        stages(
            "L1", "M0", "W7", "W4", "W3", "L2", "M1", "O0", "A4", "A3", "A7", "W6", "O1", "W5"
        )
        token.append(returned[1])
        stages(
            "F0", "M2", "L3", "A6", "A5", "L4", "O2", "F1", "M3", "L5", "M4", "F2", "L7", "O3",
            "M5", "L6", "O4", "F3", "O5", "M7", "F4", "M6", "F5", "O7", "O6", "F7", "F6"
        )
        reduced = [chunk.result for chunk in chunks]
        flat = reduced[6][:, column : column + spare].reshape(-1)
        ends = chained(*returned, s_dinput, s_low)
        returned, s_dinput, s_low = ends[:count], ends[-2], ends[-1]
    else:

        def reduce_all(pair):
            grad = weight_grad(*pair)
            own = lax.psum_scatter(grad, "fsdp", scatter_dimension=0, tiled=True)
            return lax.psum(own, "rep").astype(F32)

        reduced = [reduce_all(pair) for pair in early + late]
        flat = lax.psum(lax.psum_scatter(flat, "fsdp", tiled=True), "rep").reshape(-1)
    grad_gate, grad_up, grad_down, grad_conv, grad_sgate, grad_ssm_out, grad_first, grad_attn = reduced

    parts, begin = [], 0
    for cut in cuts[:-1] + [heads] * 3 + [1]:
        parts.append(flat[begin : begin + cut])
        begin += cut
    convs = parts[0].reshape(taps + 1, -1)
    loss = parts[-1][0]

    restored = jnp.zeros((count, length, width), BF)
    for j in range(count):
        restored = lax.dynamic_update_index_in_dim(restored, returned[j], send_at[j], 0)
    activations = jnp.where(first, s_low, restored)[None]
    gradients = jnp.where(first, restored, s_dinput)[None]
    s0 = qw + 2 * kw
    return (
        activations,
        gradients,
        loss / (valid_count * width),
        parts[2][None],
        grad_first[None, :, :qw],
        grad_first[None, :, qw : qw + kw],
        grad_first[None, :, qw + kw : s0],
        grad_attn[None],
        grad_sgate[None],
        grad_conv[None],
        grad_first[None, :, s0 : s0 + heads],
        convs[None, :taps],
        convs[None, taps],
        parts[4][None],
        parts[5][None],
        parts[6][None],
        parts[1][None],
        grad_ssm_out[None],
        parts[3][None],
        grad_gate[None],
        grad_up[None],
        grad_down[None],
    )


def solution(mesh):
    rows3 = P("section", "fsdp", None)
    pair = P("section", "fsdp")
    one = P("section", None)
    data = P(("fsdp", "rep"), None, None)
    taps = P("section", None, "fsdp")
    in_specs = (data, data, P(), P(), P(), pair) + (rows3,) * 7
    in_specs += (taps, pair, one, one, one, pair, rows3, pair, rows3, rows3, rows3)
    placed = P("section", ("fsdp", "rep"), None, None)
    out_specs = (placed, placed, P(), pair) + (rows3,) * 7
    out_specs += (taps, pair, one, one, one, pair, rows3, pair, rows3, rows3, rows3)
    return jax.shard_map(body, mesh=mesh, in_specs=in_specs, out_specs=out_specs, check_vma=False)
```

```python
import math
import functools

import jax
import jax.numpy as jnp
from jax import lax
from jax.experimental import pallas as pl
from jax.experimental.pallas import tpu as pltpu
from jax.sharding import PartitionSpec as P

HD = 64
EPSILON = 1e-05
ROPE_BASE = 100000000000.0
MASKED = -1e30
F32 = jnp.float32
BF = jnp.bfloat16
TILE = 256
HALF = 128
HB = pl.BlockSpec(memory_space=pltpu.HBM)
VM = pl.BlockSpec(memory_space=pltpu.VMEM)
SM = pl.BlockSpec(memory_space=pltpu.SMEM)


def dot(a, b):
    return jnp.dot(a, b, preferred_element_type=F32)


def dot_nt(a, b):
    return lax.dot_general(a, b, (((1,), (1,)), ((), ())), preferred_element_type=F32)


def dot_tn(a, b):
    return lax.dot_general(a, b, (((0,), (0,)), ((), ())), preferred_element_type=F32)


def sigmoid(v):
    return 0.5 * jnp.tanh(0.5 * v) + 0.5


def lanes(i, width=TILE):
    return pl.ds(pl.multiple_of(i * width, width), width)


def iota(shape, axis):
    return lax.broadcasted_iota(jnp.int32, shape, axis)


def split2(v):
    hi = v.astype(BF)
    return hi, (v - hi.astype(F32)).astype(BF)


def split3(v):
    hi = v.astype(BF)
    rest = v - hi.astype(F32)
    mid = rest.astype(BF)
    return hi, mid, (rest - mid.astype(F32)).astype(BF)


def expand_matrix(tile):
    row = jnp.bitwise_and(iota((TILE, TILE), 0), HALF - 1)
    col = jnp.right_shift(iota((TILE, TILE), 1), 6) + tile * (TILE // HD)
    return jnp.where(row == col, 1.0, 0.0).astype(BF)


def reduce_matrix(tile):
    row = jnp.right_shift(iota((TILE, HALF), 0), 6) + tile * (TILE // HD)
    col = iota((TILE, HALF), 1)
    return jnp.where(row == col, 1.0, 0.0).astype(BF)


def both(v):
    return jnp.concatenate(split2(v), axis=1)


def rope(v, cosine, sine, first):
    turned = jnp.where(first, pltpu.roll(v, HALF - HD // 2, 1), pltpu.roll(v, HD // 2, 1))
    return v * cosine + turned * sine


def start_all(groups, sems):
    waits, at = [], 0
    for group in groups:
        copies = []
        for source, target in group:
            copies.append(pltpu.make_async_copy(source, target, sems.at[at]))
            at += 1
        for copy in copies:
            copy.start()
        waits.append(copies)

    def wait(i):
        for copy in waits[i]:
            copy.wait()

    return wait


def row_pieces(pieces, spots, scratch, columns):
    if len(pieces) == 1:
        return [(pieces[0].at[:, a], scratch.at[:, b]) for a, b in columns]
    unit = pieces[-1].shape[0]
    if len(pieces) == 4:
        places = [jnp.right_shift(spots[i], 1) for i in (0, 1, 2, 4)]
    else:
        places = [spots[i] for i in range(6)]
    out = []
    for a, b in columns:
        for place, piece in zip(places, pieces):
            rows = pl.ds(pl.multiple_of(place * unit, unit), piece.shape[0])
            out.append((piece.at[:, a], scratch.at[rows, b]))
    return out


def out_pieces(pieces, spots, scratch, inner):
    if len(pieces) == 1:
        return [(pieces[0], scratch)]
    total, width = scratch.shape
    n = total // pieces[0].shape[0]
    cut, rest = inner // n, (total - inner) // n
    out = []
    for i, piece in enumerate(pieces):
        block, side = jnp.right_shift(spots[i], 1), jnp.bitwise_and(spots[i], 1)
        span = piece.shape[1]
        cols = slice(0, width)
        if span < width:
            cols = pl.ds(pl.multiple_of(side * span, span), span)
        upper = pl.ds(pl.multiple_of(block * cut, cut), cut)
        lower = pl.ds(pl.multiple_of(inner + block * rest, rest), rest)
        out.append((piece.at[:cut, :], scratch.at[upper, cols]))
        out.append((piece.at[cut:, :], scratch.at[lower, cols]))
    return out


def saver(slot, active, sems):
    stores = []

    def save(buffer, stack, at=slot):
        copy = pltpu.make_async_copy(buffer, stack.at[at], sems.at[len(stores)])
        pl.when(active)(copy.start)
        stores.append(copy)

    def finish():
        for copy in stores:
            pl.when(active)(copy.wait)

    return save, finish


def in_hbm(a):
    return pltpu.with_memory_space_constraint(a, pltpu.HBM)


def call(body, name, scalars, spots, ordinary, weights, reads, stacks, result, scratch, limit, work):
    fresh = isinstance(stacks[0], jax.ShapeDtypeStruct)
    flat = [piece for group in weights for piece in group]
    counts = [len(group) for group in weights]
    kept = [] if fresh else list(stacks)
    ahead = len(scalars) + 1 + len(ordinary) + len(flat) + len(reads)
    n = len(stacks)
    cuts = [len(scalars), 1, len(ordinary), len(flat), len(reads), len(kept), n, 1]

    def kernel(*refs):
        parts, at = [], 0
        for cut in cuts:
            parts.append(refs[at : at + cut])
            at += cut
        groups, begin = [], 0
        for c in counts:
            groups.append(parts[3][begin : begin + c])
            begin += c
        for _ in body(
            parts[0], parts[1][0], parts[2], groups, parts[4], parts[6], parts[7][0], refs[at:]
        ):
            pass

    out = pl.pallas_call(
        kernel,
        out_shape=[pltpu.HBM(s.shape, s.dtype) for s in stacks] + [result],
        in_specs=[SM] * (len(scalars) + 1)
        + [VM] * len(ordinary)
        + [HB] * (len(flat) + len(reads) + len(kept)),
        out_specs=[HB] * n + [VM],
        scratch_shapes=scratch,
        input_output_aliases={} if fresh else {ahead + i: i for i in range(n)},
        compiler_params=pltpu.CompilerParams(vmem_limit_bytes=limit * 1024 * 1024),
        cost_estimate=pl.CostEstimate(
            flops=work * 100000000, bytes_accessed=1000000, transcendentals=0
        ),
        name=name,
    )(*scalars, spots, *ordinary, *(in_hbm(a) for a in flat + list(reads) + kept))
    return list(out[:n]), out[n]


V_TAP, V_CBIAS, V_GS, V_SKIP, V_G1, V_G2, V_SBIAS, V_DECAY = 0, 4, 5, 6, 7, 8, 9, 10


def scan_terms(step_raw, vec_ref, heads):
    lane = iota(step_raw.shape, 1)
    pre = step_raw + vec_ref[V_SBIAS : V_SBIAS + 1, :HALF]
    soft = jnp.maximum(pre, 0.0) + jnp.log1p(jnp.exp(-jnp.abs(pre)))
    step = jnp.where(lane < heads, soft, 0.0)
    change = step * vec_ref[V_DECAY : V_DECAY + 1, :HALF]
    length = step.shape[0]
    lower = jnp.where(
        iota((length, length), 0) >= iota((length, length), 1), 1.0, 0.0
    ).astype(BF)
    run = sum(dot(lower, part) for part in split3(change))
    middle = run[HALF - 1 : HALF, :]
    bend = jnp.where(iota(run.shape, 0) < HALF, middle - run, run - middle)
    bend = jnp.exp(jnp.minimum(bend, 0.0))
    return pre, step, change, run, bend


def broadcast_runs(run, run_wide, heads):
    for h in range(heads):
        run_wide[:, h * HALF : (h + 1) * HALF] = jnp.broadcast_to(
            run[:, h : h + 1], (run.shape[0], HALF)
        )


def mix_forward(widths, scalars, spots, ordinary, weights, reads, stacks, hidden_ref, scratch):
    ci, mi, qw, kw, heads = widths
    index_ref, slot_ref = scalars
    base = 4 * index_ref[0]
    x_ref, vec_ref, cos_ref, sin_ref, _ = ordinary
    w_first, w_conv, w_gate, w_out = weights
    (win, wout, normed, conv_raw, z, xbc, gate_raw, qkv, step_raw, probs, branch, mixed_all, y,
     gated, run_wide, run_row, step_two, bend_two, in_sem, out_sem) = scratch
    (s_normed, s_conv, s_z, s_gate, s_qkv, s_step, s_probs, s_ssm, s_mixed, s_y, s_hidden,
     s_x) = stacks
    g0 = ci
    q0 = ci + mi
    total = win.shape[1]
    tail = total - q0
    wait = start_all(
        [
            row_pieces(w_first, spots, win, [(slice(0, tail), slice(q0, total))]),
            row_pieces(w_conv, spots, win, [(slice(0, ci), slice(0, ci))]),
            row_pieces(w_gate, spots, win, [(slice(0, mi), slice(g0, q0))]),
            out_pieces(w_out, spots, wout, mi),
        ],
        in_sem,
    )
    save, finish = saver(slot_ref[base], slot_ref[base + 1] > 0, out_sem)
    yield

    length = x_ref.shape[0]
    x = x_ref[...].astype(F32)
    rate = lax.rsqrt(jnp.mean(x * x, axis=-1, keepdims=True) + EPSILON)
    normed[...] = (x * rate * vec_ref[V_G1 : V_G1 + 1, : x.shape[1]]).astype(BF)
    save(normed, s_normed)
    lane_first = jnp.bitwise_and(iota((length, HALF), 1), HD - 1) < HD // 2
    half_low = iota((length, HALF), 1) < HD

    wait(0)
    cosine, sine = cos_ref[...], sin_ref[...]
    n_rope = (qw + kw) // HALF
    for t in range((total - q0) // HALF // 2):
        raw = dot(normed[...], win[:, q0 + t * TILE : q0 + (t + 1) * TILE])
        for part in range(2):
            c = 2 * t + part
            piece = raw[:, part * HALF : (part + 1) * HALF]
            if c < n_rope:
                piece = rope(piece, cosine, sine, lane_first)
            if c < n_rope + kw // HALF:
                qkv[:, c * HALF : (c + 1) * HALF] = piece.astype(BF)
            else:
                step_raw[...] = piece
    if ((total - q0) // HALF) % 2:
        step_raw[...] = dot(normed[...], win[:, total - HALF : total])
    save(qkv, s_qkv)
    save(step_raw, s_step)

    wait(1)
    row = iota((length, TILE), 0)

    def conv_tile(t, carry):
        cols = lanes(t)
        raw = dot(normed[...], win[:, cols])
        conv_raw[:, cols] = raw.astype(BF)
        total_z = vec_ref[V_CBIAS : V_CBIAS + 1, cols] + raw * vec_ref[3:4, cols]
        for back in range(1, 4):
            moved = jnp.where(row >= back, pltpu.roll(raw, back, 0), 0.0)
            total_z = total_z + moved * vec_ref[3 - back : 4 - back, cols]
        z[:, cols] = total_z.astype(BF)
        xbc[:, cols] = (total_z * sigmoid(total_z)).astype(BF)
        return carry

    lax.fori_loop(0, ci // TILE, conv_tile, 0, unroll=True)
    save(conv_raw, s_conv)
    save(z, s_z)

    wait(2)

    def gate_tile(t, carry):
        raw = dot(normed[...], win[:, pl.ds(pl.multiple_of(g0 + t * TILE, TILE), TILE)])
        gate_raw[:, lanes(t)] = raw.astype(BF)
        return carry

    lax.fori_loop(0, mi // TILE, gate_tile, 0, unroll=True)
    save(gate_raw, s_gate)

    yield

    keys, values = qkv[:, qw : qw + kw], qkv[:, qw + kw : qw + 2 * kw]
    keys_far, values_far = pltpu.roll(keys.astype(F32), HD, 1).astype(BF), pltpu.roll(
        values.astype(F32), HD, 1
    ).astype(BF)
    causal_top = iota((HALF, HALF), 1) <= iota((HALF, HALF), 0)
    causal_low = iota((HALF, length), 1) <= iota((HALF, length), 0) + HALF
    pairs = qw // HALF
    groups = kw // HD
    probs_zero = jnp.zeros((HALF, HALF), BF)
    for pair in range(pairs):
        group = pair // (pairs // groups)
        keep = half_low if group == 0 else jnp.logical_not(half_low)
        keys_two = jnp.where(keep, keys, keys_far)
        values_two = jnp.where(keep, values, values_far)
        query = qkv[:, pair * HALF : (pair + 1) * HALF] * jnp.asarray(HD ** (-0.5), BF)
        results = []
        for side in range(2):
            own = half_low if side == 0 else jnp.logical_not(half_low)
            q = jnp.where(own, query, jnp.zeros_like(query))
            at = (2 * pair + side) * length
            out = []
            for lo, causal in ((0, causal_top), (1, causal_low)):
                width = HALF if lo == 0 else length
                scores = dot_nt(q[lo * HALF : (lo + 1) * HALF], keys_two[:width])
                scores = jnp.where(causal, scores, MASKED)
                top = jnp.max(scores, axis=-1, keepdims=True)
                weights = jnp.exp(scores - top)
                weights = weights / jnp.sum(weights, axis=-1, keepdims=True)
                weights = weights.astype(BF)
                if lo == 0:
                    probs[at : at + HALF, :HALF] = weights
                    probs[at : at + HALF, HALF:] = probs_zero
                else:
                    probs[at + HALF : at + length, :] = weights
                out.append(dot(weights, values_two[:width]))
            results.append(jnp.concatenate(out, axis=0))
        mixed = jnp.where(half_low, results[0], results[1])
        mixed_all[:, pair * HALF : (pair + 1) * HALF] = mixed.astype(BF)
    save(probs, s_probs)
    save(mixed_all, s_mixed)

    pre, step, change, run, bend = scan_terms(step_raw[...], vec_ref, heads)
    turned = run.T
    run_row[:HALF, :] = turned[:, :HALF]
    run_row[HALF:, :] = turned[:, HALF:]
    broadcast_runs(run, run_wide, heads)
    step_two[...] = both(step)
    bend_two[...] = both(bend)
    b_in, c_in = xbc[:, mi : mi + HALF], xbc[:, mi + HALF : mi + 2 * HALF]
    tops = [dot_nt(c_in[c * HALF : (c + 1) * HALF], b_in[c * HALF : (c + 1) * HALF]) for c in (0, 1)]
    cross = dot_nt(c_in[HALF:], b_in[:HALF]).astype(BF)
    pair_low = iota((HALF, HALF), 1) < HD
    tops = [jnp.where(causal_top, t, 0.0) for t in tops]

    def mix_tile(t, squares):
        cols = lanes(t)
        spread = expand_matrix(t)
        x_in = xbc[:, cols].astype(F32)
        scaled = (dot(step_two[...], spread) * x_in).astype(BF)
        bends = dot(bend_two[...], spread)
        u = (bends[:HALF] * scaled[:HALF].astype(F32)).astype(BF)
        far = dot(cross, u) * bends[HALF:]
        parts = []
        for p in range(TILE // HALF):
            block = []
            for c in range(2):
                rows = slice(c * HALF, (c + 1) * HALF)
                weights = []
                for side in range(2):
                    h = t * (TILE // HD) + 2 * p + side
                    wide = run_wide[rows, lanes(h, HALF)]
                    line = run_row[pl.ds(c * HALF + h, 1), :]
                    decay = jnp.exp(jnp.minimum(wide - line, 0.0))
                    weights.append((decay * tops[c]).astype(BF))
                xs = scaled[rows, p * HALF : (p + 1) * HALF]
                zero = jnp.zeros_like(xs)
                right = jnp.concatenate(
                    [jnp.where(pair_low, xs, zero), jnp.where(pair_low, zero, xs)], axis=0
                )
                block.append(dot(jnp.concatenate(weights, axis=1), right))
            parts.append(jnp.concatenate(block, axis=0))
        out = jnp.concatenate(parts, axis=1)
        out = out + jnp.concatenate([jnp.zeros_like(far), far], axis=0)
        out = out + vec_ref[V_SKIP : V_SKIP + 1, cols] * x_in
        y[:, cols] = out.astype(BF)
        g = gate_raw[:, cols].astype(F32)
        out = out * (g * sigmoid(g))
        gated[:, cols] = out
        return squares + jnp.sum(out * out, axis=-1, keepdims=True)

    squares = lax.fori_loop(0, mi // TILE, mix_tile, jnp.zeros((length, 1), F32), unroll=True)
    save(y, s_y)
    rate = lax.rsqrt(squares * (1.0 / mi) + EPSILON)
    branch[...] = (gated[...] * rate * vec_ref[V_GS : V_GS + 1, :mi]).astype(BF)
    save(branch, s_ssm)

    wait(3)

    def out_tile(t, carry):
        cols = lanes(t)
        hidden_ref[:, cols] = (
            x_ref[:, cols].astype(F32)
            + dot(branch[...], wout[:mi, cols])
            + dot(mixed_all[...], wout[mi:, cols])
        )
        return carry

    lax.fori_loop(0, wout.shape[1] // TILE, out_tile, 0, unroll=True)
    save(hidden_ref, s_hidden)
    save(x_ref, s_x)
    yield
    finish()


def mixer_forward_scratch(length, width, widths, total):
    ci, mi, qw, kw, heads = widths
    return [
        pltpu.VMEM((width, total), BF),
        pltpu.VMEM((mi + qw, width), BF),
        pltpu.VMEM((length, width), BF),
        pltpu.VMEM((length, ci), BF),
        pltpu.VMEM((length, ci), BF),
        pltpu.VMEM((length, ci), BF),
        pltpu.VMEM((length, mi), BF),
        pltpu.VMEM((length, qw + 2 * kw), BF),
        pltpu.VMEM((length, HALF), F32),
        pltpu.VMEM((qw // HD * length, length), BF),
        pltpu.VMEM((length, mi), BF),
        pltpu.VMEM((length, qw), BF),
        pltpu.VMEM((length, mi), BF),
        pltpu.VMEM((length, mi), F32),
        pltpu.VMEM((length, heads * HALF), F32),
        pltpu.VMEM((length, HALF), F32),
        pltpu.VMEM((length, 2 * HALF), BF),
        pltpu.VMEM((length, 2 * HALF), BF),
        pltpu.SemaphoreType.DMA((32,)),
        pltpu.SemaphoreType.DMA((12,)),
    ]


def mixer_forward_call(
    index, slot, spots, x, vec, cosine, sine, turn, weights, stacks, widths, total
):
    ci, mi, qw, kw, heads = widths
    length, width = x.shape
    scratch = mixer_forward_scratch(length, width, widths, total)
    return call(
        functools.partial(mix_forward, widths),
        "mixer_forward",
        [index, slot],
        spots,
        [x, vec, cosine, sine, turn],
        weights,
        [],
        stacks,
        jax.ShapeDtypeStruct((length, width), F32),
        scratch,
        44,
        200,
    )


def mlp_forward(scalars, spots, ordinary, weights, reads, stacks, low_ref, scratch):
    index_ref, slot_ref = scalars
    base = 4 * index_ref[0]
    hidden_ref, vec_ref = ordinary
    w_g, w_u, w_down = weights
    wgu, wdown, normed, gate_low, up_low, act, final, in_sem, out_sem = scratch
    s_normed, s_gate, s_up, s_act, s_final, s_low = stacks
    ff = wdown.shape[0]
    parts = 2
    step = ff // parts
    groups = []
    for i in range(parts):
        a = slice(i * step, (i + 1) * step)
        b = slice(ff + i * step, ff + (i + 1) * step)
        groups.append(
            row_pieces(w_g, spots, wgu, [(a, a)]) + row_pieces(w_u, spots, wgu, [(a, b)])
        )
    groups.append(row_pieces(w_down, spots, wdown, [(slice(0, wdown.shape[1]),) * 2]))
    wait = start_all(groups, in_sem)
    save, finish = saver(slot_ref[base], slot_ref[base + 1] > 0, out_sem)
    yield
    valid = jnp.where(iota((hidden_ref.shape[0], 1), 0) < slot_ref[base + 2], 1.0, 0.0)

    hidden = hidden_ref[...]
    rate = lax.rsqrt(jnp.mean(hidden * hidden, axis=-1, keepdims=True) + EPSILON)
    normed[...] = (hidden * rate * vec_ref[V_G2 : V_G2 + 1, : hidden.shape[1]]).astype(BF)
    save(normed, s_normed)
    for i in range(parts):
        wait(i)

        def up_tile(t, carry):
            a = pl.ds(pl.multiple_of(i * step + t * TILE, TILE), TILE)
            b = pl.ds(pl.multiple_of(ff + i * step + t * TILE, TILE), TILE)
            gate = dot(normed[...], wgu[:, a])
            up = dot(normed[...], wgu[:, b])
            gate_low[:, a] = gate.astype(BF)
            up_low[:, a] = up.astype(BF)
            act[:, a] = (gate * sigmoid(gate) * up).astype(BF)
            return carry

        lax.fori_loop(0, step // TILE, up_tile, 0, unroll=True)
    save(gate_low, s_gate)
    save(up_low, s_up)
    save(act, s_act)
    wait(parts)

    def down_tile(t, carry):
        cols = lanes(t)
        out = (hidden_ref[:, cols] + dot(act[...], wdown[:, cols])) * valid
        final[:, cols] = out
        low_ref[:, cols] = out.astype(BF)
        return carry

    lax.fori_loop(0, wdown.shape[1] // TILE, down_tile, 0, unroll=True)
    save(final, s_final)
    save(low_ref, s_low, slot_ref[base + 3])
    yield
    finish()


def mlp_forward_scratch(length, width, ff):
    return [
        pltpu.VMEM((width, 2 * ff), BF),
        pltpu.VMEM((ff, width), BF),
        pltpu.VMEM((length, width), BF),
        pltpu.VMEM((length, ff), BF),
        pltpu.VMEM((length, ff), BF),
        pltpu.VMEM((length, ff), BF),
        pltpu.VMEM((length, width), F32),
        pltpu.SemaphoreType.DMA((32,)),
        pltpu.SemaphoreType.DMA((6,)),
    ]


def mlp_forward_call(index, slot, spots, hidden, vec, weights, stacks, ff):
    length, width = hidden.shape
    scratch = mlp_forward_scratch(length, width, ff)
    return call(
        mlp_forward,
        "mlp_forward",
        [index, slot],
        spots,
        [hidden, vec],
        weights,
        [],
        stacks,
        jax.ShapeDtypeStruct((length, width), BF),
        scratch,
        32,
        3,
    )


def mlp_backward(scalars, spots, ordinary, weights, reads, stacks, d_hidden_ref, scratch):
    index_ref, slot_ref, mix_ref = scalars
    base = 4 * index_ref[0]
    target_ref, vec_ref, _ = ordinary
    w_g, w_u, w_down = weights
    s_final, s_hidden, s_gate, s_up = reads
    (wgu, wdown, final, hidden, gate_low, up_low, d_mlp, d_gu, d_sum, d_normed, small, in_sem,
     out_sem) = scratch
    s_dmlp, s_dgate, s_dup, s_small = stacks
    slot = slot_ref[base]
    ff = wdown.shape[0]
    wait = start_all(
        [
            [(s_final.at[slot], final)],
            [(s_gate.at[slot], gate_low), (s_up.at[slot], up_low)]
            + row_pieces(w_down, spots, wdown, [(slice(0, wdown.shape[1]),) * 2]),
            row_pieces(w_g, spots, wgu, [(slice(0, ff), slice(0, ff))])
            + row_pieces(w_u, spots, wgu, [(slice(0, ff), slice(ff, 2 * ff))]),
            [(s_hidden.at[slot], hidden)],
        ],
        in_sem,
    )
    save, finish = saver(slot, slot_ref[base + 1] > 0, out_sem)
    yield
    wait(0)
    target = target_ref[...].astype(F32)
    valid = jnp.where(iota((target_ref.shape[0], 1), 0) < slot_ref[base + 2], 1.0, 0.0)
    misfit = final[...] - target
    loss = jnp.sum(valid * misfit * misfit, axis=0, keepdims=True)
    seed = valid * jnp.where(mix_ref[0] > 0.5, target, mix_ref[1] * misfit)
    d_sum[...] = seed
    d_mlp[...] = seed.astype(BF)
    save(d_mlp, s_dmlp)
    wait(1)

    def act_tile(t, carry):
        a = lanes(t)
        b = pl.ds(pl.multiple_of(ff + t * TILE, TILE), TILE)
        d_act = dot_nt(d_mlp[...], wdown[a, :])
        gate, up = gate_low[:, a].astype(F32), up_low[:, a].astype(F32)
        s = sigmoid(gate)
        swish = gate * s
        d_gu[:, a] = (d_act * up * (s + swish - swish * s)).astype(BF)
        d_gu[:, b] = (d_act * swish).astype(BF)
        return carry

    lax.fori_loop(0, ff // TILE, act_tile, 0, unroll=True)
    save(d_gu.at[:, :ff], s_dgate)
    save(d_gu.at[:, ff:], s_dup)
    wait(2)
    yield

    def back_tile(t, carry):
        rows = lanes(t)
        d_normed[:, rows] = dot_nt(d_gu[...], wgu[rows, :])
        return carry

    lax.fori_loop(0, wgu.shape[0] // TILE, back_tile, 0, unroll=True)
    wait(3)
    h = hidden[...]
    width = h.shape[1]
    rate = lax.rsqrt(jnp.mean(h * h, axis=-1, keepdims=True) + EPSILON)
    unit = h * rate
    d_n = d_normed[...]
    small[...] = jnp.zeros_like(small)
    small[0:1, :width] = jnp.sum(d_n * unit, axis=0, keepdims=True)
    small[1:2, :width] = loss
    save(small, s_small)
    d_n = d_n * vec_ref[V_G2 : V_G2 + 1, :width]
    d_hidden_ref[...] = d_sum[...] + rate * (
        d_n - unit * jnp.mean(d_n * unit, axis=-1, keepdims=True)
    )
    yield
    finish()


def mlp_backward_scratch(length, width, ff, small):
    return [
        pltpu.VMEM((width, 2 * ff), BF),
        pltpu.VMEM((ff, width), BF),
        pltpu.VMEM((length, width), F32),
        pltpu.VMEM((length, width), F32),
        pltpu.VMEM((length, ff), BF),
        pltpu.VMEM((length, ff), BF),
        pltpu.VMEM((length, width), BF),
        pltpu.VMEM((length, 2 * ff), BF),
        pltpu.VMEM((length, width), F32),
        pltpu.VMEM((length, width), F32),
        pltpu.VMEM(small, F32),
        pltpu.SemaphoreType.DMA((32,)),
        pltpu.SemaphoreType.DMA((4,)),
    ]


def mlp_backward_call(index, slot, mix, spots, target, vec, turn, weights, reads, stacks, ff):
    length, width = target.shape
    scratch = mlp_backward_scratch(length, width, ff, stacks[-1].shape[1:])
    return call(
        mlp_backward,
        "mlp_backward",
        [index, slot, mix],
        spots,
        [target, vec, turn],
        weights,
        reads,
        stacks,
        jax.ShapeDtypeStruct((length, width), F32),
        scratch,
        40,
        3,
    )


def column_sum(v):
    return jnp.sum(v, axis=0, keepdims=True)


def mix_backward(
    widths, scalars, spots, ordinary, weights, reads, stacks, d_input_ref, scratch
):
    ci, mi, qw, kw, heads = widths
    index_ref, slot_ref = scalars
    base = 4 * index_ref[0]
    d_hidden_ref, vec_ref, cos_ref, sin_ref, _ = ordinary
    w_first, w_conv, w_gate, w_out = weights
    s_conv, s_z, s_gate, s_qkv, s_step, s_probs, s_y, s_x = reads
    (win, wout, conv_raw, z, gate_raw, qkv, step_raw, probs, y, x_low, d_branch, d_proj, d_mixed,
     d_ssm, d_z, d_normed, run_wide, run_row, step_two, bend_two, tops, d_tops, run_acc, step_acc,
     small, in_sem, out_sem) = scratch
    s_dbranch, s_dfirst, s_dconv, s_dgate, s_dinput, s_small = stacks
    slot = slot_ref[base]
    g0, q0 = ci, ci + mi
    s0 = q0 + qw + 2 * kw
    total = win.shape[1]
    tail = total - q0
    length, width = d_hidden_ref.shape
    wait = start_all(
        [
            out_pieces(w_out, spots, wout, mi),
            [(s_probs.at[slot], probs), (s_qkv.at[slot], qkv)],
            [(s_step.at[slot], step_raw), (s_gate.at[slot], gate_raw), (s_y.at[slot], y)],
            [(s_z.at[slot], z)],
            [(s_conv.at[slot], conv_raw)],
            row_pieces(w_first, spots, win, [(slice(0, tail), slice(q0, total))])
            + row_pieces(w_conv, spots, win, [(slice(0, ci), slice(0, ci))])
            + row_pieces(w_gate, spots, win, [(slice(0, mi), slice(g0, q0))]),
            [(s_x.at[slot], x_low)],
        ],
        in_sem,
    )
    save, finish = saver(slot, slot_ref[base + 1] > 0, out_sem)
    yield
    small[...] = jnp.zeros_like(small)
    d_branch[...] = d_hidden_ref[...].astype(BF)
    save(d_branch, s_dbranch)
    wait(0)
    for t in range(qw // TILE):
        rows = slice(mi + t * TILE, mi + (t + 1) * TILE)
        d_mixed[:, t * TILE : (t + 1) * TILE] = dot_nt(d_branch[...], wout[rows, :]).astype(BF)

    lane_first = jnp.bitwise_and(iota((length, HALF), 1), HD - 1) < HD // 2
    half_low = iota((length, HALF), 1) < HD
    cosine, sine = cos_ref[...], -sin_ref[...]
    wait(1)
    keys, values = qkv[:, qw : qw + kw], qkv[:, qw + kw : qw + 2 * kw]
    keys_far, values_far = pltpu.roll(keys.astype(F32), HD, 1).astype(BF), pltpu.roll(
        values.astype(F32), HD, 1
    ).astype(BF)
    pairs = qw // HALF
    groups = kw // HD
    scale = HD ** (-0.5)
    d_keys = [jnp.zeros((length, HALF), F32) for _ in range(groups)]
    d_values = [jnp.zeros((length, HALF), F32) for _ in range(groups)]
    for pair in range(pairs):
        group = pair // (pairs // groups)
        keep = half_low if group == 0 else jnp.logical_not(half_low)
        keys_two = jnp.where(keep, keys, keys_far)
        values_two = jnp.where(keep, values, values_far)
        cols = slice(pair * HALF, (pair + 1) * HALF)
        query, d_out = qkv[:, cols], d_mixed[:, cols]
        results = []
        for side in range(2):
            own = half_low if side == 0 else jnp.logical_not(half_low)
            q = jnp.where(own, query, jnp.zeros_like(query))
            d_o = jnp.where(own, d_out, jnp.zeros_like(d_out))
            at = (2 * pair + side) * length
            weights = probs[at : at + length, :]
            wide = weights.astype(F32)
            d_weights = dot_nt(d_o, values_two)
            inner = wide * d_weights
            d_scores = (inner - wide * jnp.sum(inner, axis=-1, keepdims=True)).astype(BF)
            results.append(dot(d_scores, keys_two))
            d_keys[group] = d_keys[group] + dot_tn(d_scores, q)
            d_values[group] = d_values[group] + dot_tn(weights, d_o)
        d_q = jnp.where(half_low, results[0], results[1]) * scale
        d_proj[:, q0 + pair * HALF : q0 + (pair + 1) * HALF] = rope(
            d_q, cosine, sine, lane_first
        ).astype(BF)
    folded = [v + pltpu.roll(v, HD, 1) for v in d_keys]
    d_k = jnp.where(half_low, folded[0], folded[1]) * scale
    d_proj[:, q0 + qw : q0 + qw + kw] = rope(d_k, cosine, sine, lane_first).astype(BF)
    folded = [v + pltpu.roll(v, HD, 1) for v in d_values]
    d_proj[:, q0 + qw + kw : s0] = jnp.where(half_low, folded[0], folded[1]).astype(BF)

    wait(2)

    def norm_tile(t, sums):
        cols = lanes(t)
        d_s = dot_nt(d_branch[...], wout[cols, :])
        d_ssm[:, cols] = d_s
        g = gate_raw[:, cols].astype(F32)
        gated = y[:, cols].astype(F32) * (g * sigmoid(g))
        d_n = d_s * vec_ref[V_GS : V_GS + 1, cols]
        return (
            sums[0] + jnp.sum(gated * gated, axis=-1, keepdims=True),
            sums[1] + jnp.sum(gated * d_n, axis=-1, keepdims=True),
        )

    zero_col = jnp.zeros((length, 1), F32)
    squares, along = lax.fori_loop(0, mi // TILE, norm_tile, (zero_col, zero_col), unroll=True)
    rate = lax.rsqrt(squares * (1.0 / mi) + EPSILON)
    along = along * (rate * rate) * (1.0 / mi)

    pre, step, change, run, bend = scan_terms(step_raw[...], vec_ref, heads)
    turned = run.T
    run_row[:HALF, :] = turned[:, :HALF]
    run_row[HALF:, :] = turned[:, HALF:]
    broadcast_runs(run, run_wide, heads)
    step_two[...] = both(step)
    bend_two[...] = both(bend)
    wait(3)
    zb = z[:, mi : mi + 2 * HALF].astype(F32)
    sb = sigmoid(zb)
    bc = (zb * sb).astype(BF)
    b_in, c_in = bc[:, :HALF], bc[:, HALF:]
    causal = iota((HALF, HALF), 1) <= iota((HALF, HALF), 0)
    for c in range(2):
        rows = slice(c * HALF, (c + 1) * HALF)
        tops[rows, :] = jnp.where(causal, dot_nt(c_in[rows], b_in[rows]), 0.0)
    cross = dot_nt(c_in[HALF:], b_in[:HALF])
    cross_turned = cross.T.astype(BF)
    cross = cross.astype(BF)
    pair_low = iota((HALF, HALF), 1) < HD
    d_tops[...] = jnp.zeros_like(d_tops)
    run_acc[...] = jnp.zeros_like(run_acc)
    step_acc[...] = jnp.zeros_like(step_acc)

    def mix_tile(t, carry):
        cols = lanes(t)
        g = gate_raw[:, cols].astype(F32)
        s = sigmoid(g)
        swish = g * s
        y_in = y[:, cols].astype(F32)
        gated = y_in * swish
        d_s = d_ssm[:, cols]
        small[V_GS : V_GS + 1, cols] = column_sum(d_s * gated * rate)
        d_gated = rate * (d_s * vec_ref[V_GS : V_GS + 1, cols]) - gated * (along * rate)
        d_proj[:, pl.ds(pl.multiple_of(g0 + t * TILE, TILE), TILE)] = (
            d_gated * y_in * (s + swish - swish * s)
        ).astype(BF)
        d_y = d_gated * swish
        z_in = z[:, cols].astype(F32)
        s = sigmoid(z_in)
        x_in = z_in * s
        slope = s + x_in - x_in * s
        spread = expand_matrix(t)
        steps = dot(step_two[...], spread)
        bends = dot(bend_two[...], spread)
        scaled = (steps * x_in).astype(BF)
        d_low = d_y.astype(BF)
        u = (bends[:HALF] * scaled[:HALF].astype(F32)).astype(BF)
        v = (bends[HALF:] * d_y[HALF:]).astype(BF)
        far = dot(cross, u)
        back = dot(cross_turned, v)
        d_tops[2 * HALF :, :] += dot_nt(v, u)
        mixed_parts, back_parts = [], []
        for p in range(TILE // HALF):
            mixed_block, back_block = [], []
            for c in range(2):
                rows = slice(c * HALF, (c + 1) * HALF)
                xs = scaled[rows, p * HALF : (p + 1) * HALF]
                dy = d_low[rows, p * HALF : (p + 1) * HALF]
                zero = jnp.zeros_like(xs)
                xs_two = [jnp.where(pair_low, xs, zero), jnp.where(pair_low, zero, xs)]
                dy_two = [jnp.where(pair_low, dy, zero), jnp.where(pair_low, zero, dy)]
                weights = []
                d_top = jnp.zeros((HALF, HALF), F32)
                for side in range(2):
                    h = t * (TILE // HD) + 2 * p + side
                    wide = run_wide[rows, lanes(h, HALF)]
                    line = run_row[pl.ds(c * HALF + h, 1), :]
                    decay = jnp.exp(jnp.minimum(wide - line, 0.0))
                    weights.append((decay * tops[rows, :]).astype(BF))
                    d_top = d_top + decay * dot_nt(dy_two[side], xs)
                d_tops[rows, :] += d_top
                mixed_block.append(
                    dot(jnp.concatenate(weights, axis=1), jnp.concatenate(xs_two, axis=0))
                )
                back_block.append(
                    dot_tn(jnp.concatenate(weights, axis=0), jnp.concatenate(dy_two, axis=0))
                )
            mixed_parts.append(jnp.concatenate(mixed_block, axis=0))
            back_parts.append(jnp.concatenate(back_block, axis=0))
        mixed = jnp.concatenate(mixed_parts, axis=1)
        d_scaled = jnp.concatenate(back_parts, axis=1)
        crossing = jnp.concatenate(
            [-(u.astype(F32) * back), v.astype(F32) * far], axis=0
        )
        runs = d_low.astype(F32) * mixed - scaled.astype(F32) * d_scaled + crossing
        d_scaled = d_scaled + jnp.concatenate([bends[:HALF] * back, jnp.zeros_like(back)], axis=0)
        gather = reduce_matrix(t)
        run_acc[...] += sum(dot(part, gather) for part in split2(runs))
        step_acc[...] += sum(dot(part, gather) for part in split2(x_in * d_scaled))
        small[V_SKIP : V_SKIP + 1, cols] = column_sum(d_y * x_in)
        d_x = steps * d_scaled + vec_ref[V_SKIP : V_SKIP + 1, cols] * d_y
        d_z[:, cols] = d_x * slope
        return carry

    lax.fori_loop(0, mi // TILE, mix_tile, 0, unroll=True)
    d_top = [
        jnp.where(causal, d_tops[c * HALF : (c + 1) * HALF, :], 0.0).astype(BF) for c in range(2)
    ]
    d_cross = d_tops[2 * HALF :, :].astype(BF)
    d_c = jnp.concatenate(
        [dot(d_top[0], b_in[:HALF]), dot(d_cross, b_in[:HALF]) + dot(d_top[1], b_in[HALF:])], axis=0
    )
    d_b = jnp.concatenate(
        [dot_tn(d_top[0], c_in[:HALF]) + dot_tn(d_cross, c_in[HALF:]), dot_tn(d_top[1], c_in[HALF:])],
        axis=0,
    )
    xb = zb * sb
    d_z[:, mi : mi + 2 * HALF] = jnp.concatenate([d_b, d_c], axis=1) * (sb + xb - xb * sb)
    upper = jnp.where(
        iota((length, length), 0) <= iota((length, length), 1), 1.0, 0.0
    ).astype(BF)
    d_change = sum(dot(upper, part) for part in split3(run_acc[...]))
    d_pre = (step_acc[...] + d_change * vec_ref[V_DECAY : V_DECAY + 1, :HALF]) * sigmoid(pre)
    d_pre = jnp.where(iota(d_pre.shape, 1) < heads, d_pre, 0.0)
    d_proj[:, s0:total] = d_pre.astype(BF)
    small[V_SBIAS : V_SBIAS + 1, :HALF] = column_sum(d_pre)
    small[V_DECAY : V_DECAY + 1, :HALF] = column_sum(d_change * change)

    wait(4)
    row = iota((length, TILE), 0)

    def conv_tile(t, carry):
        cols = lanes(t)
        d = d_z[:, cols]
        raw = conv_raw[:, cols].astype(F32)
        small[V_CBIAS : V_CBIAS + 1, cols] = column_sum(d)
        small[3:4, cols] = column_sum(d * raw)
        out = d * vec_ref[3:4, cols]
        for ahead in range(1, 4):
            moved = jnp.where(row < length - ahead, pltpu.roll(d, length - ahead, 0), 0.0)
            small[3 - ahead : 4 - ahead, cols] = column_sum(moved * raw)
            out = out + moved * vec_ref[3 - ahead : 4 - ahead, cols]
        d_proj[:, cols] = out.astype(BF)
        return carry

    lax.fori_loop(0, ci // TILE, conv_tile, 0, unroll=True)
    save(d_proj.at[:, q0:], s_dfirst)
    save(d_proj.at[:, :ci], s_dconv)
    save(d_proj.at[:, g0:q0], s_dgate)

    wait(5)

    def back_tile(t, carry):
        rows = lanes(t)
        d_normed[:, rows] = dot_nt(d_proj[...], win[rows, :])
        return carry

    lax.fori_loop(0, width // TILE, back_tile, 0, unroll=True)
    wait(6)
    x = x_low[...].astype(F32)
    rate_one = lax.rsqrt(jnp.mean(x * x, axis=-1, keepdims=True) + EPSILON)
    unit = x * rate_one
    d_n = d_normed[...]
    small[V_G1 : V_G1 + 1, :width] = column_sum(d_n * unit)
    save(small, s_small)
    d_n = d_n * vec_ref[V_G1 : V_G1 + 1, :width]
    d_input_ref[...] = (
        d_hidden_ref[...]
        + rate_one * (d_n - unit * jnp.mean(d_n * unit, axis=-1, keepdims=True))
    ).astype(BF)
    save(d_input_ref, s_dinput, slot_ref[base + 3])
    yield
    finish()


def mixer_backward_scratch(length, width, widths, total, small):
    ci, mi, qw, kw, heads = widths
    return [
        pltpu.VMEM((width, total), BF),
        pltpu.VMEM((mi + qw, width), BF),
        pltpu.VMEM((length, ci), BF),
        pltpu.VMEM((length, ci), BF),
        pltpu.VMEM((length, mi), BF),
        pltpu.VMEM((length, qw + 2 * kw), BF),
        pltpu.VMEM((length, HALF), F32),
        pltpu.VMEM((qw // HD * length, length), BF),
        pltpu.VMEM((length, mi), BF),
        pltpu.VMEM((length, width), BF),
        pltpu.VMEM((length, width), BF),
        pltpu.VMEM((length, total), BF),
        pltpu.VMEM((length, qw), BF),
        pltpu.VMEM((length, mi), F32),
        pltpu.VMEM((length, ci), F32),
        pltpu.VMEM((length, width), F32),
        pltpu.VMEM((length, heads * HALF), F32),
        pltpu.VMEM((length, HALF), F32),
        pltpu.VMEM((length, 2 * HALF), BF),
        pltpu.VMEM((length, 2 * HALF), BF),
        pltpu.VMEM((2 * HALF, HALF), F32),
        pltpu.VMEM((3 * HALF, HALF), F32),
        pltpu.VMEM((length, HALF), F32),
        pltpu.VMEM((length, HALF), F32),
        pltpu.VMEM(small, F32),
        pltpu.SemaphoreType.DMA((48,)),
        pltpu.SemaphoreType.DMA((6,)),
    ]


def mixer_backward_call(
    index, slot, spots, d_hidden, vec, cosine, sine, turn, weights, reads, stacks, widths, total
):
    ci, mi, qw, kw, heads = widths
    length, width = d_hidden.shape
    scratch = mixer_backward_scratch(length, width, widths, total, stacks[-1].shape[1:])
    return call(
        functools.partial(mix_backward, widths),
        "mixer_backward",
        [index, slot],
        spots,
        [d_hidden, vec, cosine, sine, turn],
        weights,
        reads,
        stacks,
        jax.ShapeDtypeStruct((length, width), BF),
        scratch,
        48,
        250,
    )


def weight_kernel(core_ref, away_ref, stay_ref, right_ref, out_away, out_stay, turned):
    rows = away_ref.shape[2]
    tokens = away_ref.shape[0] * away_ref.shape[1]
    turned[:rows, :] = away_ref[...].reshape(tokens, rows).T
    turned[rows:, :] = stay_ref[...].reshape(tokens, rows).T
    right = right_ref[...].reshape(tokens, right_ref.shape[2])
    out_away[0] = dot(turned[:rows, :], right).astype(BF)
    out_stay[0] = dot(turned[rows:, :], right).astype(BF)


def weight_grad_halves(core, left, right):
    count, length, depth = left.shape
    columns = right.shape[2]
    rows = depth // 4
    grid = pltpu.PrefetchScalarGridSpec(
        num_scalar_prefetch=1,
        grid=(2,),
        in_specs=[
            pl.BlockSpec((count, length, rows), lambda c, core: (0, 0, 2 * c + 1 - core[0])),
            pl.BlockSpec((count, length, rows), lambda c, core: (0, 0, 2 * c + core[0])),
            pl.BlockSpec((count, length, columns), lambda c, core: (0, 0, 0)),
        ],
        out_specs=[pl.BlockSpec((1, rows, columns), lambda c, core: (c, 0, 0))] * 2,
        scratch_shapes=[pltpu.VMEM((2 * rows, count * length), BF)],
    )
    shape = pltpu.HBM((2, rows, columns), BF)
    return pl.pallas_call(
        weight_kernel,
        out_shape=[shape, shape],
        grid_spec=grid,
        compiler_params=pltpu.CompilerParams(vmem_limit_bytes=40 * 1024 * 1024),
        cost_estimate=pl.CostEstimate(
            flops=100000000, bytes_accessed=1000000, transcendentals=0
        ),
        name="weight_gradient",
    )(core, in_hbm(left), in_hbm(left), in_hbm(right))


def layer_forward_call(
    index, slot, spots, x, vec, cosine, sine, turn, weights, stacks, widths, total, ff
):
    length, width = x.shape
    first = mixer_forward_scratch(length, width, widths, total)
    second = mlp_forward_scratch(length, width, ff)
    n = 12

    def body(scalars, spots, ordinary, weights, reads, stacks, low_ref, scratch):
        hidden = scratch[-1]
        one = mix_forward(
            widths, scalars, spots, ordinary, weights[:4], [], stacks[:n], hidden,
            scratch[: len(first)],
        )
        two = mlp_forward(
            scalars, spots, [hidden, ordinary[1]], weights[4:], [], stacks[n:], low_ref,
            scratch[len(first) : -1],
        )
        for part in (one, one, two, one, two, one, two):
            next(part, None)
        yield

    return call(
        body,
        "layer_forward",
        [index, slot],
        spots,
        [x, vec, cosine, sine, turn],
        weights,
        [],
        stacks,
        jax.ShapeDtypeStruct((length, width), BF),
        first + second + [pltpu.VMEM((length, width), F32)],
        58,
        200,
    )


def layer_backward_call(
    index, slot, mix, spots, target, vec, cosine, sine, turn, weights, reads, stacks, widths, total, ff
):
    length, width = target.shape
    first = mlp_backward_scratch(length, width, ff, stacks[3].shape[1:])
    second = mixer_backward_scratch(length, width, widths, total, stacks[-1].shape[1:])
    n = 4

    def body(scalars, spots, ordinary, weights, reads, stacks, d_input_ref, scratch):
        d_hidden = scratch[-1]
        target_ref, vec_ref, cos_ref, sin_ref, turn_ref = ordinary
        one = mlp_backward(
            scalars, spots, [target_ref, vec_ref, turn_ref], weights[4:], reads[:4],
            stacks[:n], d_hidden, scratch[: len(first)],
        )
        two = mix_backward(
            widths, scalars[:2], spots, [d_hidden, vec_ref, cos_ref, sin_ref, turn_ref],
            weights[:4], reads[4:], stacks[n:], d_input_ref, scratch[len(first) : -1],
        )
        for part in (one, one, two, one, two, one, two):
            next(part, None)
        yield

    return call(
        body,
        "layer_backward",
        [index, slot, mix],
        spots,
        [target, vec, cosine, sine, turn],
        weights,
        reads,
        stacks,
        jax.ShapeDtypeStruct((length, width), BF),
        first + second + [pltpu.VMEM((length, width), F32)],
        60,
        250,
    )


def rope_tables(length):
    halves = HD // 2
    inverse = jnp.exp(jnp.arange(halves, dtype=F32) * (-2.0 * math.log(ROPE_BASE) / HD))
    angles = jnp.arange(length, dtype=F32)[:, None] * inverse[None, :]
    cosine, sine = jnp.cos(angles), jnp.sin(angles)
    return (
        jnp.concatenate([cosine] * 4, axis=1),
        jnp.concatenate([-sine, sine, -sine, sine], axis=1),
    )


def swap(block, axis, bit):
    return lax.ppermute(block, axis, [(i, i ^ bit) for i in range(lax.axis_size(axis))])


def after(value, *others):
    if not others:
        return value
    return lax.optimization_barrier((value,) + others)[0]


def corner(made):
    part = made.reshape(-1, made.shape[-1])[:8, :HALF].astype(BF)
    return jnp.dot(part, jnp.ones((HALF, HALF), BF), preferred_element_type=F32)


def quick_links():
    return lax.axis_size("fsdp") == 4 and lax.axis_size("rep") == 4


def gather_halves(shard, axis, before_y=(), before_z=()):
    parity = lax.axis_index("rep") % 2
    half = shard.shape[axis] // 2
    mine = lax.dynamic_slice_in_dim(shard, parity * half, half, axis)
    near = swap(shard, "fsdp", 1)
    far_one = swap(after(mine, *before_y), "fsdp", 2)
    far_two = swap(after(far_one, *before_z), "rep", 1)
    return [shard, near, far_one, far_two]


def gather_wholes(shard, *before_y):
    return [shard, swap(shard, "fsdp", 1), swap(after(shard, *before_y), "fsdp", 2)]


def share_far(pieces, *before):
    return pieces + [swap(after(piece, *before), "fsdp", 1) for piece in pieces[2:]]


def plus(a, b):
    return (a.astype(F32) + b.astype(F32)).astype(BF)


def weight_grad(left, right):
    return lax.dot_general(
        left, right, (((0, 1), (0, 1)), ((), ())), preferred_element_type=F32
    ).astype(BF)


class Reduction:
    def __init__(self, left, right, riders=None):
        self.left, self.right, self.riders = left, right, riders

    def begin(self, order):
        left, right = order(self.left, self.right)
        core = lax.axis_index("fsdp") % 2
        away, stay = weight_grad_halves(core.astype(jnp.int32)[None], left, right)
        if self.riders is not None:
            blocks, column = self.riders
            away, stay = (
                lax.dynamic_update_slice(
                    grad, lax.dynamic_index_in_dim(blocks, i, 1, keepdims=False), (0, 0, column)
                )
                for grad, i in ((away, 1 - core), (stay, core))
            )
        self.stay = stay
        self.moved = swap(away, "fsdp", 1)
        return stay

    def chips(self, order):
        chip = lax.axis_index("fsdp") // 2
        self.kept = order(self.stay, self.moved)

        def part(i):
            return [lax.dynamic_index_in_dim(v, i, 0, keepdims=False) for v in self.kept]

        away = plus(*part(1 - chip))
        self.moved = swap(away, "fsdp", 2)
        return away

    def line_in(self, order):
        chip = lax.axis_index("fsdp") // 2
        *kept, moved = order(*self.kept, self.moved)
        one, two = (lax.dynamic_index_in_dim(v, chip, 0, keepdims=False) for v in kept)
        self.stay = (one.astype(F32) + two.astype(F32) + moved.astype(F32)).astype(BF)
        self.moved = lax.ppermute(self.stay, "rep", [(0, 1), (3, 2)])
        return self.stay

    def middle(self, order):
        stay, moved = order(self.stay, self.moved)
        self.stay = plus(stay, moved)
        self.moved = lax.ppermute(self.stay, "rep", [(1, 2), (2, 1)])
        return self.stay

    def line_out(self, order):
        stay, moved = order(self.stay, self.moved)
        self.stay = plus(stay, moved)
        self.moved = lax.ppermute(self.stay, "rep", [(1, 0), (2, 3)])
        return self.stay

    def finish(self, order):
        stay, moved = order(self.stay, self.moved)
        rank = lax.axis_index("rep")
        inner = jnp.logical_or(rank == 1, rank == 2)
        self.result = jnp.where(inner, stay, moved).astype(F32)
        return self.result


def body(
    inputs,
    teacher,
    lengths,
    order,
    loss_scale,
    norm_gain1,
    w_query,
    w_key,
    w_value,
    w_attn_out,
    w_ssm_gate,
    w_conv_in,
    w_step,
    conv_kernel,
    conv_bias,
    step_bias,
    decay_log,
    skip_gain,
    ssm_norm_gain,
    w_ssm_out,
    norm_gain2,
    w_gate,
    w_up,
    w_down,
):
    quick = quick_links()
    n_rep = lax.axis_size("rep")
    n_fsdp = lax.axis_size("fsdp")
    rank = lax.axis_index("rep")
    fsdp = lax.axis_index("fsdp")
    section = lax.axis_index("section")
    first = section == 0
    device = fsdp * n_rep + rank
    count, length, width = inputs.shape
    ci, mi, qw, kw = (w.shape[2] for w in (w_conv_in, w_ssm_gate, w_query, w_key))
    heads = w_step.shape[2]
    ff = w_up.shape[2]
    widths = (ci, mi, qw, kw, heads)
    taps = conv_kernel.shape[1]
    rows = width // n_fsdp
    tail = qw + 2 * kw + HALF
    total = ci + mi + tail

    def columns(flat):
        wide = -(-flat.size // rows)
        return jnp.pad(flat, (0, wide * rows - flat.size)).reshape(rows, wide)

    convs = jnp.concatenate([conv_kernel[0], conv_bias], axis=0)
    riders = jnp.concatenate(
        [
            norm_gain1[0][:, None],
            norm_gain2[0][:, None],
            columns(convs.reshape(-1)),
            columns(ssm_norm_gain[0]),
        ],
        axis=1,
    )
    used = riders.shape[1]
    wide = -(-convs.size // rows)
    shard_first = jnp.concatenate(
        [w_query[0], w_key[0], w_value[0], w_step[0]] + [jnp.zeros((rows, HALF - heads), BF)],
        axis=1,
    )
    parity = rank % 2
    if quick:
        g_gate = gather_halves(w_ssm_gate[0], 0)
        g_conv = gather_halves(w_conv_in[0], 0)
        g_first = gather_halves(shard_first, 0, (), g_gate[3:4])
        shard_out = jnp.concatenate([w_ssm_out[0], w_attn_out[0]], axis=0)
        g_out = gather_halves(shard_out, 1, g_gate[2:3], g_conv[3:4])
        g_g = gather_halves(w_gate[0], 0, g_conv[2:3], g_first[3:4])
        g_u = gather_wholes(w_up[0], g_out[2])
        g_gate, g_conv, g_first, g_out = (
            share_far(g, g_out[3]) for g in (g_gate, g_conv, g_first, g_out)
        )
        spots = [2 * fsdp, 2 * (fsdp ^ 1)]
        spots += [2 * (fsdp ^ k) + b for k in (2, 3) for b in (parity, 1 - parity)]
        spots = jnp.stack(spots).astype(jnp.int32)
        far = swap(riders, "fsdp", 2)
        blocks = jnp.stack([riders, swap(riders, "fsdp", 1), far, swap(far, "fsdp", 1)])
        ridden = jnp.take(blocks, jnp.arange(4, dtype=jnp.int32) ^ fsdp, axis=0)
    else:

        def whole(shard):
            return lax.all_gather(shard, "fsdp", axis=0, tiled=True)

        g_first, g_conv, g_gate, g_g, g_u, g_down = (
            [whole(w)]
            for w in (shard_first, w_conv_in[0], w_ssm_gate[0], w_gate[0], w_up[0], w_down[0])
        )
        g_out = [jnp.concatenate([whole(w_ssm_out[0]), whole(w_attn_out[0])], axis=0)]
        spots = jnp.zeros((1,), jnp.int32)
        ridden = whole(riders).reshape(n_fsdp, rows, used)
    if quick:
        order = after(order, g_gate[3])

    turns = jnp.arange(count, dtype=jnp.int32)
    numbers = jnp.arange(order.shape[0], dtype=jnp.int32)
    mine = device * count + turns
    sources = jnp.sum(jnp.where(order[None, :] == mine[:, None], numbers[None, :], 0), axis=1)
    target = lax.dynamic_slice_in_dim(order, device * count, count) // count % n_rep
    anchor = sources // count % n_rep

    def inverse(key):
        return jnp.sum(jnp.where((key ^ rank)[None, :] == turns[:, None], turns[None, :], 0), axis=1)

    send_at, keep_at = inverse(target), inverse(anchor)
    own_lengths = jnp.take(lengths, jnp.take(sources, keep_at))
    outgoing = [
        jnp.where(
            first,
            lax.dynamic_index_in_dim(inputs, send_at[j], 0, keepdims=False),
            lax.dynamic_index_in_dim(teacher, send_at[j], 0, keepdims=False),
        )
        for j in range(count)
    ]
    dealt = [outgoing[0]]

    def deal(j, *earlier):
        dealt.append(swap(after(outgoing[j], *earlier), "rep", j))


    if quick:
        deal(1, g_out[3])
        deal(2, dealt[1])
    else:
        for j in range(1, count - 1):
            deal(j)

    mixer_weights = [g_first, g_conv, g_gate, g_out]
    mlp_weights = None if quick else [g_g, g_u, g_down]

    conv_all = ridden[:, :, 2 : 2 + wide].reshape(n_fsdp, -1)[:, : (taps + 1) * ci // n_fsdp]
    conv_all = conv_all.reshape(n_fsdp, taps + 1, ci // n_fsdp).transpose(1, 0, 2)
    ssm_gain = ridden[:, :, 2 + wide :].reshape(n_fsdp, -1)[:, : mi // n_fsdp].reshape(1, mi)

    def table_row(v):
        v = v.astype(F32)
        return jnp.pad(v, ((0, 0), (0, ci - v.shape[1])))

    vec = jnp.concatenate(
        [
            table_row(v)
            for v in (
                conv_all.reshape(taps + 1, ci),
                ssm_gain,
                jnp.repeat(skip_gain, HD, axis=1),
                ridden[:, :, 0].reshape(1, width),
                ridden[:, :, 1].reshape(1, width),
                step_bias,
                -jnp.exp(decay_log),
                jnp.zeros((16 - taps - 7, 1), F32),
            )
        ],
        axis=0,
    )
    cosine, sine = rope_tables(length)

    valid_count = jnp.sum(lengths).astype(F32)
    factor = loss_scale / (valid_count * width)

    skew = 2
    steps = count + skew
    ticks = jnp.arange(steps, dtype=jnp.int32)
    raw = jnp.concatenate([ticks - skew * section, count - 1 - ticks + skew * (1 - section)])
    inside = jnp.logical_and(raw >= 0, raw < count).astype(jnp.int32)
    slots = jnp.clip(raw, 0, count - 1)
    plan = [slots, inside, jnp.take(own_lengths, slots), jnp.take(keep_at, slots)]
    plan = jnp.stack(plan, axis=1).reshape(-1)
    mix = jnp.stack([jnp.where(first, 1.0, 0.0), 2.0 * factor])

    def stack(*shape, kind=BF):
        return jax.ShapeDtypeStruct((count,) + shape, kind)

    mix_stacks = [
        stack(length, width),
        stack(length, ci),
        stack(length, ci),
        stack(length, mi),
        stack(length, qw + 2 * kw),
        stack(length, HALF, kind=F32),
        stack(qw // HD * length, length),
        stack(length, mi),
        stack(length, qw),
        stack(length, mi),
        stack(length, width, kind=F32),
        stack(length, width),
    ]
    mlp_stacks = [
        stack(length, width),
        stack(length, ff),
        stack(length, ff),
        stack(length, ff),
        stack(length, width, kind=F32),
        stack(length, width),
    ]

    token = []

    def chained(*values):
        if not quick or not token:
            return values
        return lax.optimization_barrier(values + tuple(token))[: len(values)]

    def chain(made):
        token[:] = [made]

    received, hiddens = [], []

    blank = jnp.zeros((8, HALF), F32)

    def number(i):
        return jnp.full((1,), i, jnp.int32)

    def mixer_tick(tick, turn, mix_stacks):
        mix_stacks, hidden = mixer_forward_call(
            number(tick),
            plan,
            spots,
            dealt[tick],
            vec,
            cosine,
            sine,
            corner(turn),
            mixer_weights,
            mix_stacks,
            widths,
            total,
        )
        chain(hidden)
        hiddens.append(hidden)
        return mix_stacks

    def mlp_tick(tick, mlp_stacks):
        (hidden,) = chained(hiddens[tick])
        mlp_stacks, low = mlp_forward_call(
            number(tick), plan, spots, hidden, vec, mlp_weights, mlp_stacks, ff
        )
        return mlp_stacks, low

    def layer_tick(tick, turn, stacks):
        if tick < count:
            one, two = chained(dealt[tick], received[tick - skew])
            seq_in = jnp.where(first, one, two)
        else:
            seq_in = received[tick - skew]
        return layer_forward_call(
            number(tick),
            plan,
            spots,
            seq_in,
            vec,
            cosine,
            sine,
            corner(turn) if tick < steps - 1 else blank,
            mixer_weights + mlp_weights,
            stacks,
            widths,
            total,
            ff,
        )

    if quick:
        dealt[0] = after(dealt[0], dealt[1])
    mix_stacks = mixer_tick(0, dealt[0], mix_stacks)
    if quick:
        g_down = gather_wholes(w_down[0], hiddens[0])
    mix_stacks = mixer_tick(1, hiddens[0], mix_stacks)
    if quick:
        mlp_weights = [share_far(g, hiddens[1], dealt[2]) for g in (g_g, g_u, g_down)]
    for tick in range(steps):
        if tick < skew:
            mlp_stacks, low = mlp_tick(tick, mlp_stacks)
            if tick == 0:
                deal(count - 1, low)
        else:
            stacks, low = layer_tick(tick, low, mix_stacks + mlp_stacks)
            mix_stacks, mlp_stacks = stacks[: len(mix_stacks)], stacks[len(mix_stacks) :]
        chain(low)
        if tick < count:
            received.append(lax.ppermute(low, "section", [(0, 1)]))

    (s_normed, s_conv, s_z, s_gate, s_qkv, s_step, s_probs, s_ssm, s_mixed, s_y, s_hidden,
     s_x) = mix_stacks
    s_normed2, s_g, s_u, s_act, s_final, s_low = mlp_stacks
    mlp_grads = [
        stack(length, width),
        stack(length, ff),
        stack(length, ff),
        stack(8, width, kind=F32),
    ]
    mix_grads = [
        stack(length, width),
        stack(length, tail),
        stack(length, ci),
        stack(length, mi),
        stack(length, width),
        stack(16, ci, kind=F32),
    ]
    incoming, returned = [], [None] * count

    hiddens = []

    def mlp_turn(turn, mlp_grads):
        if turn == count:
            token.append(returned[3])
        (seed,) = chained(incoming[turn - skew])
        return mlp_backward_call(
            number(steps + turn),
            plan,
            mix,
            spots,
            seed,
            vec,
            corner(hiddens[-1]) if turn > count else blank,
            mlp_weights,
            reads,
            mlp_grads,
            ff,
        )

    def mixer_turn(turn, d_hidden, before, mix_grads):
        mix_grads, d_input = mixer_backward_call(
            number(steps + turn),
            plan,
            spots,
            d_hidden,
            vec,
            cosine,
            sine,
            corner(before),
            mixer_weights,
            mix_reads,
            mix_grads,
            widths,
            total,
        )
        send_back(turn, d_input)
        return mix_grads, d_input

    def send_back(turn, d_input):
        if turn < count:
            incoming.append(lax.ppermute(d_input, "section", [(1, 0)]))
        if turn >= skew:
            j = count - 1 - turn + skew
            back = lax.dynamic_index_in_dim(after(s_low, d_input), keep_at[j], 0, keepdims=False)
            back = jnp.where(first, d_input, back)
            returned[j] = swap(back, "rep", j) if j else back

    reads = [s_final, s_hidden, s_g, s_u]
    mix_reads = [s_conv, s_z, s_gate, s_qkv, s_step, s_probs, s_y, s_x]
    d_input = low
    for turn in range(count):
        if turn < skew:
            (seed,) = chained(dealt[count - 1 - turn])
        else:
            one, two = chained(incoming[turn - skew], dealt[count - 1 - turn])
            seed = jnp.where(first, one, two)
        grads, d_input = layer_backward_call(
            number(steps + turn),
            plan,
            mix,
            spots,
            seed,
            vec,
            cosine,
            sine,
            corner(d_input) if turn else blank,
            mixer_weights + mlp_weights,
            reads + mix_reads,
            mlp_grads + mix_grads,
            widths,
            total,
            ff,
        )
        mlp_grads, mix_grads = grads[: len(mlp_grads)], grads[len(mlp_grads) :]
        chain(d_input)
        send_back(turn, d_input)

    loss_part = jnp.sum(mlp_grads[3][:, 1])[None]
    loss_part = jnp.where(first, lax.ppermute(loss_part, "section", [(1, 0)]), loss_part)

    for turn in range(count, steps):
        mlp_grads, d_hidden = mlp_turn(turn, mlp_grads)
        chain(d_hidden)
        hiddens.append(d_hidden)
    s_dmlp, s_dg, s_du, small_mlp = mlp_grads
    early = [(s_normed2, s_dg), (s_normed2, s_du), (s_act, s_dmlp)]
    chunks = [Reduction(*pair) for pair in early]

    names = dict(W="begin", A="chips", L="line_in", M="middle", O="line_out", F="finish")
    state = [mix_grads]

    def stages(*words):
        for word in words:
            letter, place = word[0], int(word[1:])
            if letter == "B":
                before = token[0] if quick else hiddens[place - count]
                state[0], made = mixer_turn(place, hiddens[place - count], before, state[0])
            else:
                made = getattr(chunks[place], names[letter])(chained)
            chain(made)

    if quick:
        stages(
            "W0", "W1", "A0", "W2", "B4"
        )
        token.append(returned[2])
        stages(
            "A2", "A1", "L0", "B5"
        )
    else:
        stages("B4", "B5")
    mix_grads = state[0]
    s_dbranch, s_dfirst, s_dconv, s_dgate, s_dinput, small_mix = mix_grads
    late = [
        (s_normed, s_dconv),
        (s_normed, s_dgate),
        (s_ssm, s_dbranch),
        (s_normed, s_dfirst),
        (s_mixed, s_dbranch),
    ]

    mix_sum = jnp.sum(small_mix, axis=0)
    mlp_sum = jnp.sum(small_mlp, axis=0)
    singles = jnp.concatenate(
        [
            mix_sum[V_SBIAS, :heads],
            mix_sum[V_DECAY, :heads],
            jnp.sum(mix_sum[V_SKIP, :mi].reshape(heads, HD), axis=1),
            loss_part,
        ]
    )

    def share(v):
        return v.reshape(v.shape[0], n_fsdp, -1).transpose(1, 0, 2).reshape(n_fsdp, -1)

    shares = [
        share(mix_sum[: taps + 1]),
        share(mix_sum[V_GS : V_GS + 1, :mi]),
        share(mix_sum[V_G1 : V_G1 + 1, :width]),
        share(mlp_sum[:1]),
        jnp.broadcast_to(singles[None], (n_fsdp, singles.size)),
    ]
    cuts = [v.shape[1] for v in shares]
    flat = jnp.concatenate(shares, axis=1)

    def split_ends(values):
        return values[:count], values[-2], values[-1]

    def own_outputs(returned, s_dinput, s_low):
        restored = jnp.zeros((count, length, width), BF)
        for j in range(count):
            restored = lax.dynamic_update_index_in_dim(restored, returned[j], send_at[j], 0)
        return jnp.where(first, s_low, restored)[None], jnp.where(first, restored, s_dinput)[None]

    if quick:
        spare = -(-flat.shape[1] // rows)
        flat = jnp.pad(flat, ((0, 0), (0, spare * rows - flat.shape[1])))
        riders = flat.astype(BF).reshape(2, 2, rows, spare)
        column = tail - HALF + heads
        chunks += [Reduction(*pair) for pair in late]
        chunks[6].riders = (riders, column)
        stages(
            "L1", "M0", "W4", "W7", "W3", "L2", "M1", "O0", "A4", "A7", "A3", "W6", "W5", "F0"
        )
        token.append(returned[1])
        stages(
            "O1", "L3", "M2", "L7", "A5", "L4", "A6", "M3", "O2", "F1", "L5", "M4", "L6", "O3",
            "F2", "M7", "M5", "O4"
        )
        returned, s_dinput, s_low = split_ends(chained(*returned, s_dinput, s_low))
        activations, gradients = own_outputs(returned, s_dinput, s_low)
        token.extend([activations, gradients])
        stages(
            "M6", "F3", "O7", "O5", "F4", "O6", "F7", "F5", "F6"
        )
        reduced = [chunk.result for chunk in chunks]
        flat = reduced[6][:, column : column + spare].reshape(-1)
    else:

        def reduce_all(pair):
            grad = weight_grad(*pair)
            own = lax.psum_scatter(grad, "fsdp", scatter_dimension=0, tiled=True)
            return lax.psum(own, "rep").astype(F32)

        reduced = [reduce_all(pair) for pair in early + late]
        flat = lax.psum(lax.psum_scatter(flat, "fsdp", tiled=True), "rep").reshape(-1)
    grad_gate, grad_up, grad_down, grad_conv, grad_sgate, grad_ssm_out, grad_first, grad_attn = reduced

    parts, begin = [], 0
    for cut in cuts[:-1] + [heads] * 3 + [1]:
        parts.append(flat[begin : begin + cut])
        begin += cut
    convs = parts[0].reshape(taps + 1, -1)
    loss = parts[-1][0]

    if not quick:
        activations, gradients = own_outputs(returned, s_dinput, s_low)
    s0 = qw + 2 * kw
    return (
        activations,
        gradients,
        loss / (valid_count * width),
        parts[2][None],
        grad_first[None, :, :qw],
        grad_first[None, :, qw : qw + kw],
        grad_first[None, :, qw + kw : s0],
        grad_attn[None],
        grad_sgate[None],
        grad_conv[None],
        grad_first[None, :, s0 : s0 + heads],
        convs[None, :taps],
        convs[None, taps],
        parts[4][None],
        parts[5][None],
        parts[6][None],
        parts[1][None],
        grad_ssm_out[None],
        parts[3][None],
        grad_gate[None],
        grad_up[None],
        grad_down[None],
    )


def solution(mesh):
    rows3 = P("section", "fsdp", None)
    pair = P("section", "fsdp")
    one = P("section", None)
    data = P(("fsdp", "rep"), None, None)
    taps = P("section", None, "fsdp")
    in_specs = (data, data, P(), P(), P(), pair) + (rows3,) * 7
    in_specs += (taps, pair, one, one, one, pair, rows3, pair, rows3, rows3, rows3)
    placed = P("section", ("fsdp", "rep"), None, None)
    out_specs = (placed, placed, P(), pair) + (rows3,) * 7
    out_specs += (taps, pair, one, one, one, pair, rows3, pair, rows3, rows3, rows3)
    return jax.shard_map(body, mesh=mesh, in_specs=in_specs, out_specs=out_specs, check_vma=False)
```

```python
import math
import functools

import jax
import jax.numpy as jnp
from jax import lax
from jax.experimental import pallas as pl
from jax.experimental.pallas import tpu as pltpu
from jax.sharding import PartitionSpec as P

HD = 64
EPSILON = 1e-05
ROPE_BASE = 100000000000.0
MASKED = -1e30
F32 = jnp.float32
BF = jnp.bfloat16
TILE = 256
HALF = 128
HB = pl.BlockSpec(memory_space=pltpu.HBM)
VM = pl.BlockSpec(memory_space=pltpu.VMEM)
SM = pl.BlockSpec(memory_space=pltpu.SMEM)


def dot(a, b):
    return jnp.dot(a, b, preferred_element_type=F32)


def dot_nt(a, b):
    return lax.dot_general(a, b, (((1,), (1,)), ((), ())), preferred_element_type=F32)


def dot_tn(a, b):
    return lax.dot_general(a, b, (((0,), (0,)), ((), ())), preferred_element_type=F32)


def sigmoid(v):
    return 0.5 * jnp.tanh(0.5 * v) + 0.5


def lanes(i, width=TILE):
    return pl.ds(pl.multiple_of(i * width, width), width)


def iota(shape, axis):
    return lax.broadcasted_iota(jnp.int32, shape, axis)


def split2(v):
    hi = v.astype(BF)
    return hi, (v - hi.astype(F32)).astype(BF)


def split3(v):
    hi = v.astype(BF)
    rest = v - hi.astype(F32)
    mid = rest.astype(BF)
    return hi, mid, (rest - mid.astype(F32)).astype(BF)


def expand_matrix(tile):
    row = jnp.bitwise_and(iota((TILE, TILE), 0), HALF - 1)
    col = jnp.right_shift(iota((TILE, TILE), 1), 6) + tile * (TILE // HD)
    return jnp.where(row == col, 1.0, 0.0).astype(BF)


def reduce_matrix(tile):
    row = jnp.right_shift(iota((TILE, HALF), 0), 6) + tile * (TILE // HD)
    col = iota((TILE, HALF), 1)
    return jnp.where(row == col, 1.0, 0.0).astype(BF)


def both(v):
    return jnp.concatenate(split2(v), axis=1)


def rope(v, cosine, sine, first):
    turned = jnp.where(first, pltpu.roll(v, HALF - HD // 2, 1), pltpu.roll(v, HD // 2, 1))
    return v * cosine + turned * sine


def start_all(groups, sems):
    waits, at = [], 0
    for group in groups:
        copies = []
        for source, target in group:
            copies.append(pltpu.make_async_copy(source, target, sems.at[at]))
            at += 1
        for copy in copies:
            copy.start()
        waits.append(copies)

    def wait(i):
        for copy in waits[i]:
            copy.wait()

    return wait


def row_pieces(pieces, spots, scratch, columns):
    if len(pieces) == 1:
        return [(pieces[0].at[:, a], scratch.at[:, b]) for a, b in columns]
    unit = pieces[-1].shape[0]
    if len(pieces) == 4:
        places = [jnp.right_shift(spots[i], 1) for i in (0, 1, 2, 4)]
    else:
        places = [spots[i] for i in range(6)]
    out = []
    for a, b in columns:
        for place, piece in zip(places, pieces):
            rows = pl.ds(pl.multiple_of(place * unit, unit), piece.shape[0])
            out.append((piece.at[:, a], scratch.at[rows, b]))
    return out


def out_pieces(pieces, spots, scratch, inner):
    if len(pieces) == 1:
        return [(pieces[0], scratch)]
    total, width = scratch.shape
    n = total // pieces[0].shape[0]
    cut, rest = inner // n, (total - inner) // n
    out = []
    for i, piece in enumerate(pieces):
        block, side = jnp.right_shift(spots[i], 1), jnp.bitwise_and(spots[i], 1)
        span = piece.shape[1]
        cols = slice(0, width)
        if span < width:
            cols = pl.ds(pl.multiple_of(side * span, span), span)
        upper = pl.ds(pl.multiple_of(block * cut, cut), cut)
        lower = pl.ds(pl.multiple_of(inner + block * rest, rest), rest)
        out.append((piece.at[:cut, :], scratch.at[upper, cols]))
        out.append((piece.at[cut:, :], scratch.at[lower, cols]))
    return out


def saver(slot, active, sems):
    stores = []

    def save(buffer, stack, at=slot):
        copy = pltpu.make_async_copy(buffer, stack.at[at], sems.at[len(stores)])
        pl.when(active)(copy.start)
        stores.append(copy)

    def finish():
        for copy in stores:
            pl.when(active)(copy.wait)

    return save, finish


def in_hbm(a):
    return pltpu.with_memory_space_constraint(a, pltpu.HBM)


def call(body, name, scalars, spots, ordinary, weights, reads, stacks, result, scratch, limit, work):
    fresh = isinstance(stacks[0], jax.ShapeDtypeStruct)
    flat = [piece for group in weights for piece in group]
    counts = [len(group) for group in weights]
    kept = [] if fresh else list(stacks)
    ahead = len(scalars) + 1 + len(ordinary) + len(flat) + len(reads)
    n = len(stacks)
    cuts = [len(scalars), 1, len(ordinary), len(flat), len(reads), len(kept), n, 1]

    def kernel(*refs):
        parts, at = [], 0
        for cut in cuts:
            parts.append(refs[at : at + cut])
            at += cut
        groups, begin = [], 0
        for c in counts:
            groups.append(parts[3][begin : begin + c])
            begin += c
        for _ in body(
            parts[0], parts[1][0], parts[2], groups, parts[4], parts[6], parts[7][0], refs[at:]
        ):
            pass

    out = pl.pallas_call(
        kernel,
        out_shape=[pltpu.HBM(s.shape, s.dtype) for s in stacks] + [result],
        in_specs=[SM] * (len(scalars) + 1)
        + [VM] * len(ordinary)
        + [HB] * (len(flat) + len(reads) + len(kept)),
        out_specs=[HB] * n + [VM],
        scratch_shapes=scratch,
        input_output_aliases={} if fresh else {ahead + i: i for i in range(n)},
        compiler_params=pltpu.CompilerParams(vmem_limit_bytes=limit * 1024 * 1024),
        cost_estimate=pl.CostEstimate(
            flops=work * 100000000, bytes_accessed=1000000, transcendentals=0
        ),
        name=name,
    )(*scalars, spots, *ordinary, *(in_hbm(a) for a in flat + list(reads) + kept))
    return list(out[:n]), out[n]


V_TAP, V_CBIAS, V_GS, V_SKIP, V_G1, V_G2, V_SBIAS, V_DECAY = 0, 4, 5, 6, 7, 8, 9, 10


def scan_terms(step_raw, vec_ref, heads):
    lane = iota(step_raw.shape, 1)
    pre = step_raw + vec_ref[V_SBIAS : V_SBIAS + 1, :HALF]
    soft = jnp.maximum(pre, 0.0) + jnp.log1p(jnp.exp(-jnp.abs(pre)))
    step = jnp.where(lane < heads, soft, 0.0)
    change = step * vec_ref[V_DECAY : V_DECAY + 1, :HALF]
    length = step.shape[0]
    lower = jnp.where(
        iota((length, length), 0) >= iota((length, length), 1), 1.0, 0.0
    ).astype(BF)
    run = sum(dot(lower, part) for part in split3(change))
    middle = run[HALF - 1 : HALF, :]
    bend = jnp.where(iota(run.shape, 0) < HALF, middle - run, run - middle)
    bend = jnp.exp(jnp.minimum(bend, 0.0))
    return pre, step, change, run, bend


def broadcast_runs(run, run_wide, heads):
    for h in range(heads):
        run_wide[:, h * HALF : (h + 1) * HALF] = jnp.broadcast_to(
            run[:, h : h + 1], (run.shape[0], HALF)
        )


def mix_forward(widths, scalars, spots, ordinary, weights, reads, stacks, hidden_ref, scratch):
    ci, mi, qw, kw, heads = widths
    index_ref, slot_ref = scalars
    base = 4 * index_ref[0]
    x_ref, vec_ref, cos_ref, sin_ref, _ = ordinary
    w_first, w_conv, w_gate, w_out = weights
    (win, wout, normed, conv_raw, z, xbc, gate_raw, qkv, step_raw, probs, branch, mixed_all, y,
     gated, run_wide, run_row, step_two, bend_two, in_sem, out_sem) = scratch
    (s_normed, s_conv, s_z, s_gate, s_qkv, s_step, s_probs, s_ssm, s_mixed, s_y, s_hidden,
     s_x) = stacks
    g0 = ci
    q0 = ci + mi
    total = win.shape[1]
    tail = total - q0
    wait = start_all(
        [
            row_pieces(w_first, spots, win, [(slice(0, tail), slice(q0, total))]),
            row_pieces(w_conv, spots, win, [(slice(0, ci), slice(0, ci))]),
            row_pieces(w_gate, spots, win, [(slice(0, mi), slice(g0, q0))]),
            out_pieces(w_out, spots, wout, mi),
        ],
        in_sem,
    )
    save, finish = saver(slot_ref[base], slot_ref[base + 1] > 0, out_sem)
    yield

    length = x_ref.shape[0]
    x = x_ref[...].astype(F32)
    rate = lax.rsqrt(jnp.mean(x * x, axis=-1, keepdims=True) + EPSILON)
    normed[...] = (x * rate * vec_ref[V_G1 : V_G1 + 1, : x.shape[1]]).astype(BF)
    save(normed, s_normed)
    lane_first = jnp.bitwise_and(iota((length, HALF), 1), HD - 1) < HD // 2
    half_low = iota((length, HALF), 1) < HD

    wait(0)
    cosine, sine = cos_ref[...], sin_ref[...]
    n_rope = (qw + kw) // HALF
    for t in range((total - q0) // HALF // 2):
        raw = dot(normed[...], win[:, q0 + t * TILE : q0 + (t + 1) * TILE])
        for part in range(2):
            c = 2 * t + part
            piece = raw[:, part * HALF : (part + 1) * HALF]
            if c < n_rope:
                piece = rope(piece, cosine, sine, lane_first)
            if c < n_rope + kw // HALF:
                qkv[:, c * HALF : (c + 1) * HALF] = piece.astype(BF)
            else:
                step_raw[...] = piece
    if ((total - q0) // HALF) % 2:
        step_raw[...] = dot(normed[...], win[:, total - HALF : total])
    save(qkv, s_qkv)
    save(step_raw, s_step)

    wait(1)
    row = iota((length, TILE), 0)

    def conv_tile(t, carry):
        cols = lanes(t)
        raw = dot(normed[...], win[:, cols])
        conv_raw[:, cols] = raw.astype(BF)
        total_z = vec_ref[V_CBIAS : V_CBIAS + 1, cols] + raw * vec_ref[3:4, cols]
        for back in range(1, 4):
            moved = jnp.where(row >= back, pltpu.roll(raw, back, 0), 0.0)
            total_z = total_z + moved * vec_ref[3 - back : 4 - back, cols]
        z[:, cols] = total_z.astype(BF)
        xbc[:, cols] = (total_z * sigmoid(total_z)).astype(BF)
        return carry

    lax.fori_loop(0, ci // TILE, conv_tile, 0, unroll=True)
    save(conv_raw, s_conv)
    save(z, s_z)

    wait(2)

    def gate_tile(t, carry):
        raw = dot(normed[...], win[:, pl.ds(pl.multiple_of(g0 + t * TILE, TILE), TILE)])
        gate_raw[:, lanes(t)] = raw.astype(BF)
        return carry

    lax.fori_loop(0, mi // TILE, gate_tile, 0, unroll=True)
    save(gate_raw, s_gate)

    yield

    keys, values = qkv[:, qw : qw + kw], qkv[:, qw + kw : qw + 2 * kw]
    keys_far, values_far = pltpu.roll(keys.astype(F32), HD, 1).astype(BF), pltpu.roll(
        values.astype(F32), HD, 1
    ).astype(BF)
    causal_top = iota((HALF, HALF), 1) <= iota((HALF, HALF), 0)
    causal_low = iota((HALF, length), 1) <= iota((HALF, length), 0) + HALF
    pairs = qw // HALF
    groups = kw // HD
    probs_zero = jnp.zeros((HALF, HALF), BF)
    for pair in range(pairs):
        group = pair // (pairs // groups)
        keep = half_low if group == 0 else jnp.logical_not(half_low)
        keys_two = jnp.where(keep, keys, keys_far)
        values_two = jnp.where(keep, values, values_far)
        query = qkv[:, pair * HALF : (pair + 1) * HALF] * jnp.asarray(HD ** (-0.5), BF)
        results = []
        for side in range(2):
            own = half_low if side == 0 else jnp.logical_not(half_low)
            q = jnp.where(own, query, jnp.zeros_like(query))
            at = (2 * pair + side) * length
            out = []
            for lo, causal in ((0, causal_top), (1, causal_low)):
                width = HALF if lo == 0 else length
                scores = dot_nt(q[lo * HALF : (lo + 1) * HALF], keys_two[:width])
                scores = jnp.where(causal, scores, MASKED)
                top = jnp.max(scores, axis=-1, keepdims=True)
                weights = jnp.exp(scores - top)
                weights = weights / jnp.sum(weights, axis=-1, keepdims=True)
                weights = weights.astype(BF)
                if lo == 0:
                    probs[at : at + HALF, :HALF] = weights
                    probs[at : at + HALF, HALF:] = probs_zero
                else:
                    probs[at + HALF : at + length, :] = weights
                out.append(dot(weights, values_two[:width]))
            results.append(jnp.concatenate(out, axis=0))
        mixed = jnp.where(half_low, results[0], results[1])
        mixed_all[:, pair * HALF : (pair + 1) * HALF] = mixed.astype(BF)
    save(probs, s_probs)
    save(mixed_all, s_mixed)

    pre, step, change, run, bend = scan_terms(step_raw[...], vec_ref, heads)
    turned = run.T
    run_row[:HALF, :] = turned[:, :HALF]
    run_row[HALF:, :] = turned[:, HALF:]
    broadcast_runs(run, run_wide, heads)
    step_two[...] = both(step)
    bend_two[...] = both(bend)
    b_in, c_in = xbc[:, mi : mi + HALF], xbc[:, mi + HALF : mi + 2 * HALF]
    tops = [dot_nt(c_in[c * HALF : (c + 1) * HALF], b_in[c * HALF : (c + 1) * HALF]) for c in (0, 1)]
    cross = dot_nt(c_in[HALF:], b_in[:HALF]).astype(BF)
    pair_low = iota((HALF, HALF), 1) < HD
    tops = [jnp.where(causal_top, t, 0.0) for t in tops]

    def mix_tile(t, squares):
        cols = lanes(t)
        spread = expand_matrix(t)
        x_in = xbc[:, cols].astype(F32)
        scaled = (dot(step_two[...], spread) * x_in).astype(BF)
        bends = dot(bend_two[...], spread)
        u = (bends[:HALF] * scaled[:HALF].astype(F32)).astype(BF)
        far = dot(cross, u) * bends[HALF:]
        parts = []
        for p in range(TILE // HALF):
            block = []
            for c in range(2):
                rows = slice(c * HALF, (c + 1) * HALF)
                weights = []
                for side in range(2):
                    h = t * (TILE // HD) + 2 * p + side
                    wide = run_wide[rows, lanes(h, HALF)]
                    line = run_row[pl.ds(c * HALF + h, 1), :]
                    decay = jnp.exp(jnp.minimum(wide - line, 0.0))
                    weights.append((decay * tops[c]).astype(BF))
                xs = scaled[rows, p * HALF : (p + 1) * HALF]
                zero = jnp.zeros_like(xs)
                right = jnp.concatenate(
                    [jnp.where(pair_low, xs, zero), jnp.where(pair_low, zero, xs)], axis=0
                )
                block.append(dot(jnp.concatenate(weights, axis=1), right))
            parts.append(jnp.concatenate(block, axis=0))
        out = jnp.concatenate(parts, axis=1)
        out = out + jnp.concatenate([jnp.zeros_like(far), far], axis=0)
        out = out + vec_ref[V_SKIP : V_SKIP + 1, cols] * x_in
        y[:, cols] = out.astype(BF)
        g = gate_raw[:, cols].astype(F32)
        out = out * (g * sigmoid(g))
        gated[:, cols] = out
        return squares + jnp.sum(out * out, axis=-1, keepdims=True)

    squares = lax.fori_loop(0, mi // TILE, mix_tile, jnp.zeros((length, 1), F32), unroll=True)
    save(y, s_y)
    rate = lax.rsqrt(squares * (1.0 / mi) + EPSILON)
    branch[...] = (gated[...] * rate * vec_ref[V_GS : V_GS + 1, :mi]).astype(BF)
    save(branch, s_ssm)

    wait(3)

    def out_tile(t, carry):
        cols = lanes(t)
        hidden_ref[:, cols] = (
            x_ref[:, cols].astype(F32)
            + dot(branch[...], wout[:mi, cols])
            + dot(mixed_all[...], wout[mi:, cols])
        )
        return carry

    lax.fori_loop(0, wout.shape[1] // TILE, out_tile, 0, unroll=True)
    save(hidden_ref, s_hidden)
    save(x_ref, s_x)
    yield
    finish()


def mixer_forward_scratch(length, width, widths, total):
    ci, mi, qw, kw, heads = widths
    return [
        pltpu.VMEM((width, total), BF),
        pltpu.VMEM((mi + qw, width), BF),
        pltpu.VMEM((length, width), BF),
        pltpu.VMEM((length, ci), BF),
        pltpu.VMEM((length, ci), BF),
        pltpu.VMEM((length, ci), BF),
        pltpu.VMEM((length, mi), BF),
        pltpu.VMEM((length, qw + 2 * kw), BF),
        pltpu.VMEM((length, HALF), F32),
        pltpu.VMEM((qw // HD * length, length), BF),
        pltpu.VMEM((length, mi), BF),
        pltpu.VMEM((length, qw), BF),
        pltpu.VMEM((length, mi), BF),
        pltpu.VMEM((length, mi), F32),
        pltpu.VMEM((length, heads * HALF), F32),
        pltpu.VMEM((length, HALF), F32),
        pltpu.VMEM((length, 2 * HALF), BF),
        pltpu.VMEM((length, 2 * HALF), BF),
        pltpu.SemaphoreType.DMA((32,)),
        pltpu.SemaphoreType.DMA((12,)),
    ]


def mixer_forward_call(
    index, slot, spots, x, vec, cosine, sine, turn, weights, stacks, widths, total
):
    ci, mi, qw, kw, heads = widths
    length, width = x.shape
    scratch = mixer_forward_scratch(length, width, widths, total)
    return call(
        functools.partial(mix_forward, widths),
        "mixer_forward",
        [index, slot],
        spots,
        [x, vec, cosine, sine, turn],
        weights,
        [],
        stacks,
        jax.ShapeDtypeStruct((length, width), F32),
        scratch,
        44,
        200,
    )


def mlp_forward(scalars, spots, ordinary, weights, reads, stacks, low_ref, scratch):
    index_ref, slot_ref = scalars
    base = 4 * index_ref[0]
    hidden_ref, vec_ref = ordinary
    w_g, w_u, w_down = weights
    wgu, wdown, normed, gate_low, up_low, act, final, in_sem, out_sem = scratch
    s_normed, s_gate, s_up, s_act, s_final, s_low = stacks
    ff = wdown.shape[0]
    parts = 2
    step = ff // parts
    groups = []
    for i in range(parts):
        a = slice(i * step, (i + 1) * step)
        b = slice(ff + i * step, ff + (i + 1) * step)
        groups.append(
            row_pieces(w_g, spots, wgu, [(a, a)]) + row_pieces(w_u, spots, wgu, [(a, b)])
        )
    groups.append(row_pieces(w_down, spots, wdown, [(slice(0, wdown.shape[1]),) * 2]))
    wait = start_all(groups, in_sem)
    save, finish = saver(slot_ref[base], slot_ref[base + 1] > 0, out_sem)
    yield
    valid = jnp.where(iota((hidden_ref.shape[0], 1), 0) < slot_ref[base + 2], 1.0, 0.0)

    hidden = hidden_ref[...]
    rate = lax.rsqrt(jnp.mean(hidden * hidden, axis=-1, keepdims=True) + EPSILON)
    normed[...] = (hidden * rate * vec_ref[V_G2 : V_G2 + 1, : hidden.shape[1]]).astype(BF)
    save(normed, s_normed)
    for i in range(parts):
        wait(i)

        def up_tile(t, carry):
            a = pl.ds(pl.multiple_of(i * step + t * TILE, TILE), TILE)
            b = pl.ds(pl.multiple_of(ff + i * step + t * TILE, TILE), TILE)
            gate = dot(normed[...], wgu[:, a])
            up = dot(normed[...], wgu[:, b])
            gate_low[:, a] = gate.astype(BF)
            up_low[:, a] = up.astype(BF)
            act[:, a] = (gate * sigmoid(gate) * up).astype(BF)
            return carry

        lax.fori_loop(0, step // TILE, up_tile, 0, unroll=True)
    save(gate_low, s_gate)
    save(up_low, s_up)
    save(act, s_act)
    wait(parts)

    def down_tile(t, carry):
        cols = lanes(t)
        out = (hidden_ref[:, cols] + dot(act[...], wdown[:, cols])) * valid
        final[:, cols] = out
        low_ref[:, cols] = out.astype(BF)
        return carry

    lax.fori_loop(0, wdown.shape[1] // TILE, down_tile, 0, unroll=True)
    save(final, s_final)
    save(low_ref, s_low, slot_ref[base + 3])
    yield
    finish()


def mlp_forward_scratch(length, width, ff):
    return [
        pltpu.VMEM((width, 2 * ff), BF),
        pltpu.VMEM((ff, width), BF),
        pltpu.VMEM((length, width), BF),
        pltpu.VMEM((length, ff), BF),
        pltpu.VMEM((length, ff), BF),
        pltpu.VMEM((length, ff), BF),
        pltpu.VMEM((length, width), F32),
        pltpu.SemaphoreType.DMA((32,)),
        pltpu.SemaphoreType.DMA((6,)),
    ]


def mlp_forward_call(index, slot, spots, hidden, vec, weights, stacks, ff):
    length, width = hidden.shape
    scratch = mlp_forward_scratch(length, width, ff)
    return call(
        mlp_forward,
        "mlp_forward",
        [index, slot],
        spots,
        [hidden, vec],
        weights,
        [],
        stacks,
        jax.ShapeDtypeStruct((length, width), BF),
        scratch,
        32,
        3,
    )


def mlp_backward(scalars, spots, ordinary, weights, reads, stacks, d_hidden_ref, scratch):
    index_ref, slot_ref, mix_ref = scalars
    base = 4 * index_ref[0]
    target_ref, vec_ref, _ = ordinary
    w_g, w_u, w_down = weights
    s_final, s_hidden, s_gate, s_up = reads
    (wgu, wdown, final, hidden, gate_low, up_low, d_mlp, d_gu, d_sum, d_normed, small, in_sem,
     out_sem) = scratch
    s_dmlp, s_dgate, s_dup, s_small = stacks
    slot = slot_ref[base]
    ff = wdown.shape[0]
    wait = start_all(
        [
            [(s_final.at[slot], final)],
            [(s_gate.at[slot], gate_low), (s_up.at[slot], up_low)]
            + row_pieces(w_down, spots, wdown, [(slice(0, wdown.shape[1]),) * 2]),
            row_pieces(w_g, spots, wgu, [(slice(0, ff), slice(0, ff))])
            + row_pieces(w_u, spots, wgu, [(slice(0, ff), slice(ff, 2 * ff))]),
            [(s_hidden.at[slot], hidden)],
        ],
        in_sem,
    )
    save, finish = saver(slot, slot_ref[base + 1] > 0, out_sem)
    yield
    wait(0)
    target = target_ref[...].astype(F32)
    valid = jnp.where(iota((target_ref.shape[0], 1), 0) < slot_ref[base + 2], 1.0, 0.0)
    misfit = final[...] - target
    loss = jnp.sum(valid * misfit * misfit, axis=0, keepdims=True)
    seed = valid * jnp.where(mix_ref[0] > 0.5, target, mix_ref[1] * misfit)
    d_sum[...] = seed
    d_mlp[...] = seed.astype(BF)
    save(d_mlp, s_dmlp)
    wait(1)

    def act_tile(t, carry):
        a = lanes(t)
        b = pl.ds(pl.multiple_of(ff + t * TILE, TILE), TILE)
        d_act = dot_nt(d_mlp[...], wdown[a, :])
        gate, up = gate_low[:, a].astype(F32), up_low[:, a].astype(F32)
        s = sigmoid(gate)
        swish = gate * s
        d_gu[:, a] = (d_act * up * (s + swish - swish * s)).astype(BF)
        d_gu[:, b] = (d_act * swish).astype(BF)
        return carry

    lax.fori_loop(0, ff // TILE, act_tile, 0, unroll=True)
    save(d_gu.at[:, :ff], s_dgate)
    save(d_gu.at[:, ff:], s_dup)
    wait(2)
    yield

    def back_tile(t, carry):
        rows = lanes(t)
        d_normed[:, rows] = dot_nt(d_gu[...], wgu[rows, :])
        return carry

    lax.fori_loop(0, wgu.shape[0] // TILE, back_tile, 0, unroll=True)
    wait(3)
    h = hidden[...]
    width = h.shape[1]
    rate = lax.rsqrt(jnp.mean(h * h, axis=-1, keepdims=True) + EPSILON)
    unit = h * rate
    d_n = d_normed[...]
    small[...] = jnp.zeros_like(small)
    small[0:1, :width] = jnp.sum(d_n * unit, axis=0, keepdims=True)
    small[1:2, :width] = loss
    save(small, s_small)
    d_n = d_n * vec_ref[V_G2 : V_G2 + 1, :width]
    d_hidden_ref[...] = d_sum[...] + rate * (
        d_n - unit * jnp.mean(d_n * unit, axis=-1, keepdims=True)
    )
    yield
    finish()


def mlp_backward_scratch(length, width, ff, small):
    return [
        pltpu.VMEM((width, 2 * ff), BF),
        pltpu.VMEM((ff, width), BF),
        pltpu.VMEM((length, width), F32),
        pltpu.VMEM((length, width), F32),
        pltpu.VMEM((length, ff), BF),
        pltpu.VMEM((length, ff), BF),
        pltpu.VMEM((length, width), BF),
        pltpu.VMEM((length, 2 * ff), BF),
        pltpu.VMEM((length, width), F32),
        pltpu.VMEM((length, width), F32),
        pltpu.VMEM(small, F32),
        pltpu.SemaphoreType.DMA((32,)),
        pltpu.SemaphoreType.DMA((4,)),
    ]


def mlp_backward_call(index, slot, mix, spots, target, vec, turn, weights, reads, stacks, ff):
    length, width = target.shape
    scratch = mlp_backward_scratch(length, width, ff, stacks[-1].shape[1:])
    return call(
        mlp_backward,
        "mlp_backward",
        [index, slot, mix],
        spots,
        [target, vec, turn],
        weights,
        reads,
        stacks,
        jax.ShapeDtypeStruct((length, width), F32),
        scratch,
        40,
        3,
    )


def column_sum(v):
    return jnp.sum(v, axis=0, keepdims=True)


def mix_backward(
    widths, scalars, spots, ordinary, weights, reads, stacks, d_input_ref, scratch
):
    ci, mi, qw, kw, heads = widths
    index_ref, slot_ref = scalars
    base = 4 * index_ref[0]
    d_hidden_ref, vec_ref, cos_ref, sin_ref, _ = ordinary
    w_first, w_conv, w_gate, w_out = weights
    s_conv, s_z, s_gate, s_qkv, s_step, s_probs, s_y, s_x = reads
    (win, wout, conv_raw, z, gate_raw, qkv, step_raw, probs, y, x_low, d_branch, d_proj, d_mixed,
     d_ssm, d_z, d_normed, run_wide, run_row, step_two, bend_two, tops, d_tops, run_acc, step_acc,
     small, in_sem, out_sem) = scratch
    s_dbranch, s_dfirst, s_dconv, s_dgate, s_dinput, s_small = stacks
    slot = slot_ref[base]
    g0, q0 = ci, ci + mi
    s0 = q0 + qw + 2 * kw
    total = win.shape[1]
    tail = total - q0
    length, width = d_hidden_ref.shape
    wait = start_all(
        [
            out_pieces(w_out, spots, wout, mi),
            [(s_probs.at[slot], probs), (s_qkv.at[slot], qkv)],
            [(s_step.at[slot], step_raw), (s_gate.at[slot], gate_raw), (s_y.at[slot], y)],
            [(s_z.at[slot], z)],
            [(s_conv.at[slot], conv_raw)],
            row_pieces(w_first, spots, win, [(slice(0, tail), slice(q0, total))])
            + row_pieces(w_conv, spots, win, [(slice(0, ci), slice(0, ci))])
            + row_pieces(w_gate, spots, win, [(slice(0, mi), slice(g0, q0))]),
            [(s_x.at[slot], x_low)],
        ],
        in_sem,
    )
    save, finish = saver(slot, slot_ref[base + 1] > 0, out_sem)
    yield
    small[...] = jnp.zeros_like(small)
    d_branch[...] = d_hidden_ref[...].astype(BF)
    save(d_branch, s_dbranch)
    wait(0)
    for t in range(qw // TILE):
        rows = slice(mi + t * TILE, mi + (t + 1) * TILE)
        d_mixed[:, t * TILE : (t + 1) * TILE] = dot_nt(d_branch[...], wout[rows, :]).astype(BF)

    lane_first = jnp.bitwise_and(iota((length, HALF), 1), HD - 1) < HD // 2
    half_low = iota((length, HALF), 1) < HD
    cosine, sine = cos_ref[...], -sin_ref[...]
    wait(1)
    keys, values = qkv[:, qw : qw + kw], qkv[:, qw + kw : qw + 2 * kw]
    keys_far, values_far = pltpu.roll(keys.astype(F32), HD, 1).astype(BF), pltpu.roll(
        values.astype(F32), HD, 1
    ).astype(BF)
    pairs = qw // HALF
    groups = kw // HD
    scale = HD ** (-0.5)
    d_keys = [jnp.zeros((length, HALF), F32) for _ in range(groups)]
    d_values = [jnp.zeros((length, HALF), F32) for _ in range(groups)]
    for pair in range(pairs):
        group = pair // (pairs // groups)
        keep = half_low if group == 0 else jnp.logical_not(half_low)
        keys_two = jnp.where(keep, keys, keys_far)
        values_two = jnp.where(keep, values, values_far)
        cols = slice(pair * HALF, (pair + 1) * HALF)
        query, d_out = qkv[:, cols], d_mixed[:, cols]
        results = []
        for side in range(2):
            own = half_low if side == 0 else jnp.logical_not(half_low)
            q = jnp.where(own, query, jnp.zeros_like(query))
            d_o = jnp.where(own, d_out, jnp.zeros_like(d_out))
            at = (2 * pair + side) * length
            weights = probs[at : at + length, :]
            wide = weights.astype(F32)
            d_weights = dot_nt(d_o, values_two)
            inner = wide * d_weights
            d_scores = (inner - wide * jnp.sum(inner, axis=-1, keepdims=True)).astype(BF)
            results.append(dot(d_scores, keys_two))
            d_keys[group] = d_keys[group] + dot_tn(d_scores, q)
            d_values[group] = d_values[group] + dot_tn(weights, d_o)
        d_q = jnp.where(half_low, results[0], results[1]) * scale
        d_proj[:, q0 + pair * HALF : q0 + (pair + 1) * HALF] = rope(
            d_q, cosine, sine, lane_first
        ).astype(BF)
    folded = [v + pltpu.roll(v, HD, 1) for v in d_keys]
    d_k = jnp.where(half_low, folded[0], folded[1]) * scale
    d_proj[:, q0 + qw : q0 + qw + kw] = rope(d_k, cosine, sine, lane_first).astype(BF)
    folded = [v + pltpu.roll(v, HD, 1) for v in d_values]
    d_proj[:, q0 + qw + kw : s0] = jnp.where(half_low, folded[0], folded[1]).astype(BF)

    wait(2)

    def norm_tile(t, sums):
        cols = lanes(t)
        d_s = dot_nt(d_branch[...], wout[cols, :])
        d_ssm[:, cols] = d_s
        g = gate_raw[:, cols].astype(F32)
        gated = y[:, cols].astype(F32) * (g * sigmoid(g))
        d_n = d_s * vec_ref[V_GS : V_GS + 1, cols]
        return (
            sums[0] + jnp.sum(gated * gated, axis=-1, keepdims=True),
            sums[1] + jnp.sum(gated * d_n, axis=-1, keepdims=True),
        )

    zero_col = jnp.zeros((length, 1), F32)
    squares, along = lax.fori_loop(0, mi // TILE, norm_tile, (zero_col, zero_col), unroll=True)
    rate = lax.rsqrt(squares * (1.0 / mi) + EPSILON)
    along = along * (rate * rate) * (1.0 / mi)

    pre, step, change, run, bend = scan_terms(step_raw[...], vec_ref, heads)
    turned = run.T
    run_row[:HALF, :] = turned[:, :HALF]
    run_row[HALF:, :] = turned[:, HALF:]
    broadcast_runs(run, run_wide, heads)
    step_two[...] = both(step)
    bend_two[...] = both(bend)
    wait(3)
    zb = z[:, mi : mi + 2 * HALF].astype(F32)
    sb = sigmoid(zb)
    bc = (zb * sb).astype(BF)
    b_in, c_in = bc[:, :HALF], bc[:, HALF:]
    causal = iota((HALF, HALF), 1) <= iota((HALF, HALF), 0)
    for c in range(2):
        rows = slice(c * HALF, (c + 1) * HALF)
        tops[rows, :] = jnp.where(causal, dot_nt(c_in[rows], b_in[rows]), 0.0)
    cross = dot_nt(c_in[HALF:], b_in[:HALF])
    cross_turned = cross.T.astype(BF)
    cross = cross.astype(BF)
    pair_low = iota((HALF, HALF), 1) < HD
    d_tops[...] = jnp.zeros_like(d_tops)
    run_acc[...] = jnp.zeros_like(run_acc)
    step_acc[...] = jnp.zeros_like(step_acc)

    def mix_tile(t, carry):
        cols = lanes(t)
        g = gate_raw[:, cols].astype(F32)
        s = sigmoid(g)
        swish = g * s
        y_in = y[:, cols].astype(F32)
        gated = y_in * swish
        d_s = d_ssm[:, cols]
        small[V_GS : V_GS + 1, cols] = column_sum(d_s * gated * rate)
        d_gated = rate * (d_s * vec_ref[V_GS : V_GS + 1, cols]) - gated * (along * rate)
        d_proj[:, pl.ds(pl.multiple_of(g0 + t * TILE, TILE), TILE)] = (
            d_gated * y_in * (s + swish - swish * s)
        ).astype(BF)
        d_y = d_gated * swish
        z_in = z[:, cols].astype(F32)
        s = sigmoid(z_in)
        x_in = z_in * s
        slope = s + x_in - x_in * s
        spread = expand_matrix(t)
        steps = dot(step_two[...], spread)
        bends = dot(bend_two[...], spread)
        scaled = (steps * x_in).astype(BF)
        d_low = d_y.astype(BF)
        u = (bends[:HALF] * scaled[:HALF].astype(F32)).astype(BF)
        v = (bends[HALF:] * d_y[HALF:]).astype(BF)
        far = dot(cross, u)
        back = dot(cross_turned, v)
        d_tops[2 * HALF :, :] += dot_nt(v, u)
        mixed_parts, back_parts = [], []
        for p in range(TILE // HALF):
            mixed_block, back_block = [], []
            for c in range(2):
                rows = slice(c * HALF, (c + 1) * HALF)
                xs = scaled[rows, p * HALF : (p + 1) * HALF]
                dy = d_low[rows, p * HALF : (p + 1) * HALF]
                zero = jnp.zeros_like(xs)
                xs_two = [jnp.where(pair_low, xs, zero), jnp.where(pair_low, zero, xs)]
                dy_two = [jnp.where(pair_low, dy, zero), jnp.where(pair_low, zero, dy)]
                weights = []
                d_top = jnp.zeros((HALF, HALF), F32)
                for side in range(2):
                    h = t * (TILE // HD) + 2 * p + side
                    wide = run_wide[rows, lanes(h, HALF)]
                    line = run_row[pl.ds(c * HALF + h, 1), :]
                    decay = jnp.exp(jnp.minimum(wide - line, 0.0))
                    weights.append((decay * tops[rows, :]).astype(BF))
                    d_top = d_top + decay * dot_nt(dy_two[side], xs)
                d_tops[rows, :] += d_top
                mixed_block.append(
                    dot(jnp.concatenate(weights, axis=1), jnp.concatenate(xs_two, axis=0))
                )
                back_block.append(
                    dot_tn(jnp.concatenate(weights, axis=0), jnp.concatenate(dy_two, axis=0))
                )
            mixed_parts.append(jnp.concatenate(mixed_block, axis=0))
            back_parts.append(jnp.concatenate(back_block, axis=0))
        mixed = jnp.concatenate(mixed_parts, axis=1)
        d_scaled = jnp.concatenate(back_parts, axis=1)
        crossing = jnp.concatenate(
            [-(u.astype(F32) * back), v.astype(F32) * far], axis=0
        )
        runs = d_low.astype(F32) * mixed - scaled.astype(F32) * d_scaled + crossing
        d_scaled = d_scaled + jnp.concatenate([bends[:HALF] * back, jnp.zeros_like(back)], axis=0)
        gather = reduce_matrix(t)
        run_acc[...] += sum(dot(part, gather) for part in split2(runs))
        step_acc[...] += sum(dot(part, gather) for part in split2(x_in * d_scaled))
        small[V_SKIP : V_SKIP + 1, cols] = column_sum(d_y * x_in)
        d_x = steps * d_scaled + vec_ref[V_SKIP : V_SKIP + 1, cols] * d_y
        d_z[:, cols] = d_x * slope
        return carry

    lax.fori_loop(0, mi // TILE, mix_tile, 0, unroll=True)
    d_top = [
        jnp.where(causal, d_tops[c * HALF : (c + 1) * HALF, :], 0.0).astype(BF) for c in range(2)
    ]
    d_cross = d_tops[2 * HALF :, :].astype(BF)
    d_c = jnp.concatenate(
        [dot(d_top[0], b_in[:HALF]), dot(d_cross, b_in[:HALF]) + dot(d_top[1], b_in[HALF:])], axis=0
    )
    d_b = jnp.concatenate(
        [dot_tn(d_top[0], c_in[:HALF]) + dot_tn(d_cross, c_in[HALF:]), dot_tn(d_top[1], c_in[HALF:])],
        axis=0,
    )
    xb = zb * sb
    d_z[:, mi : mi + 2 * HALF] = jnp.concatenate([d_b, d_c], axis=1) * (sb + xb - xb * sb)
    upper = jnp.where(
        iota((length, length), 0) <= iota((length, length), 1), 1.0, 0.0
    ).astype(BF)
    d_change = sum(dot(upper, part) for part in split3(run_acc[...]))
    d_pre = (step_acc[...] + d_change * vec_ref[V_DECAY : V_DECAY + 1, :HALF]) * sigmoid(pre)
    d_pre = jnp.where(iota(d_pre.shape, 1) < heads, d_pre, 0.0)
    d_proj[:, s0:total] = d_pre.astype(BF)
    small[V_SBIAS : V_SBIAS + 1, :HALF] = column_sum(d_pre)
    small[V_DECAY : V_DECAY + 1, :HALF] = column_sum(d_change * change)

    wait(4)
    row = iota((length, TILE), 0)

    def conv_tile(t, carry):
        cols = lanes(t)
        d = d_z[:, cols]
        raw = conv_raw[:, cols].astype(F32)
        small[V_CBIAS : V_CBIAS + 1, cols] = column_sum(d)
        small[3:4, cols] = column_sum(d * raw)
        out = d * vec_ref[3:4, cols]
        for ahead in range(1, 4):
            moved = jnp.where(row < length - ahead, pltpu.roll(d, length - ahead, 0), 0.0)
            small[3 - ahead : 4 - ahead, cols] = column_sum(moved * raw)
            out = out + moved * vec_ref[3 - ahead : 4 - ahead, cols]
        d_proj[:, cols] = out.astype(BF)
        return carry

    lax.fori_loop(0, ci // TILE, conv_tile, 0, unroll=True)
    save(d_proj.at[:, q0:], s_dfirst)
    save(d_proj.at[:, :ci], s_dconv)
    save(d_proj.at[:, g0:q0], s_dgate)

    wait(5)

    def back_tile(t, carry):
        rows = lanes(t)
        d_normed[:, rows] = dot_nt(d_proj[...], win[rows, :])
        return carry

    lax.fori_loop(0, width // TILE, back_tile, 0, unroll=True)
    wait(6)
    x = x_low[...].astype(F32)
    rate_one = lax.rsqrt(jnp.mean(x * x, axis=-1, keepdims=True) + EPSILON)
    unit = x * rate_one
    d_n = d_normed[...]
    small[V_G1 : V_G1 + 1, :width] = column_sum(d_n * unit)
    save(small, s_small)
    d_n = d_n * vec_ref[V_G1 : V_G1 + 1, :width]
    d_input_ref[...] = (
        d_hidden_ref[...]
        + rate_one * (d_n - unit * jnp.mean(d_n * unit, axis=-1, keepdims=True))
    ).astype(BF)
    save(d_input_ref, s_dinput, slot_ref[base + 3])
    yield
    finish()


def mixer_backward_scratch(length, width, widths, total, small):
    ci, mi, qw, kw, heads = widths
    return [
        pltpu.VMEM((width, total), BF),
        pltpu.VMEM((mi + qw, width), BF),
        pltpu.VMEM((length, ci), BF),
        pltpu.VMEM((length, ci), BF),
        pltpu.VMEM((length, mi), BF),
        pltpu.VMEM((length, qw + 2 * kw), BF),
        pltpu.VMEM((length, HALF), F32),
        pltpu.VMEM((qw // HD * length, length), BF),
        pltpu.VMEM((length, mi), BF),
        pltpu.VMEM((length, width), BF),
        pltpu.VMEM((length, width), BF),
        pltpu.VMEM((length, total), BF),
        pltpu.VMEM((length, qw), BF),
        pltpu.VMEM((length, mi), F32),
        pltpu.VMEM((length, ci), F32),
        pltpu.VMEM((length, width), F32),
        pltpu.VMEM((length, heads * HALF), F32),
        pltpu.VMEM((length, HALF), F32),
        pltpu.VMEM((length, 2 * HALF), BF),
        pltpu.VMEM((length, 2 * HALF), BF),
        pltpu.VMEM((2 * HALF, HALF), F32),
        pltpu.VMEM((3 * HALF, HALF), F32),
        pltpu.VMEM((length, HALF), F32),
        pltpu.VMEM((length, HALF), F32),
        pltpu.VMEM(small, F32),
        pltpu.SemaphoreType.DMA((48,)),
        pltpu.SemaphoreType.DMA((6,)),
    ]


def mixer_backward_call(
    index, slot, spots, d_hidden, vec, cosine, sine, turn, weights, reads, stacks, widths, total
):
    ci, mi, qw, kw, heads = widths
    length, width = d_hidden.shape
    scratch = mixer_backward_scratch(length, width, widths, total, stacks[-1].shape[1:])
    return call(
        functools.partial(mix_backward, widths),
        "mixer_backward",
        [index, slot],
        spots,
        [d_hidden, vec, cosine, sine, turn],
        weights,
        reads,
        stacks,
        jax.ShapeDtypeStruct((length, width), BF),
        scratch,
        48,
        250,
    )


def weight_kernel(core_ref, away_ref, stay_ref, right_ref, out_away, out_stay, turned):
    rows = away_ref.shape[2]
    tokens = away_ref.shape[0] * away_ref.shape[1]
    turned[:rows, :] = away_ref[...].reshape(tokens, rows).T
    turned[rows:, :] = stay_ref[...].reshape(tokens, rows).T
    right = right_ref[...].reshape(tokens, right_ref.shape[2])
    out_away[0] = dot(turned[:rows, :], right).astype(BF)
    out_stay[0] = dot(turned[rows:, :], right).astype(BF)


def weight_grad_halves(core, left, right):
    count, length, depth = left.shape
    columns = right.shape[2]
    rows = depth // 4
    grid = pltpu.PrefetchScalarGridSpec(
        num_scalar_prefetch=1,
        grid=(2,),
        in_specs=[
            pl.BlockSpec((count, length, rows), lambda c, core: (0, 0, 2 * c + 1 - core[0])),
            pl.BlockSpec((count, length, rows), lambda c, core: (0, 0, 2 * c + core[0])),
            pl.BlockSpec((count, length, columns), lambda c, core: (0, 0, 0)),
        ],
        out_specs=[pl.BlockSpec((1, rows, columns), lambda c, core: (c, 0, 0))] * 2,
        scratch_shapes=[pltpu.VMEM((2 * rows, count * length), BF)],
    )
    shape = pltpu.HBM((2, rows, columns), BF)
    return pl.pallas_call(
        weight_kernel,
        out_shape=[shape, shape],
        grid_spec=grid,
        compiler_params=pltpu.CompilerParams(vmem_limit_bytes=40 * 1024 * 1024),
        cost_estimate=pl.CostEstimate(
            flops=100000000, bytes_accessed=1000000, transcendentals=0
        ),
        name="weight_gradient",
    )(core, in_hbm(left), in_hbm(left), in_hbm(right))


def layer_forward_call(
    index, slot, spots, x, vec, cosine, sine, turn, weights, stacks, widths, total, ff
):
    length, width = x.shape
    first = mixer_forward_scratch(length, width, widths, total)
    second = mlp_forward_scratch(length, width, ff)
    n = 12

    def body(scalars, spots, ordinary, weights, reads, stacks, low_ref, scratch):
        hidden = scratch[-1]
        one = mix_forward(
            widths, scalars, spots, ordinary, weights[:4], [], stacks[:n], hidden,
            scratch[: len(first)],
        )
        two = mlp_forward(
            scalars, spots, [hidden, ordinary[1]], weights[4:], [], stacks[n:], low_ref,
            scratch[len(first) : -1],
        )
        for part in (one, one, two, one, two, one, two):
            next(part, None)
        yield

    return call(
        body,
        "layer_forward",
        [index, slot],
        spots,
        [x, vec, cosine, sine, turn],
        weights,
        [],
        stacks,
        jax.ShapeDtypeStruct((length, width), BF),
        first + second + [pltpu.VMEM((length, width), F32)],
        58,
        200,
    )


def layer_backward_call(
    index, slot, mix, spots, target, vec, cosine, sine, turn, weights, reads, stacks, widths, total, ff
):
    length, width = target.shape
    first = mlp_backward_scratch(length, width, ff, stacks[3].shape[1:])
    second = mixer_backward_scratch(length, width, widths, total, stacks[-1].shape[1:])
    n = 4

    def body(scalars, spots, ordinary, weights, reads, stacks, d_input_ref, scratch):
        d_hidden = scratch[-1]
        target_ref, vec_ref, cos_ref, sin_ref, turn_ref = ordinary
        one = mlp_backward(
            scalars, spots, [target_ref, vec_ref, turn_ref], weights[4:], reads[:4],
            stacks[:n], d_hidden, scratch[: len(first)],
        )
        two = mix_backward(
            widths, scalars[:2], spots, [d_hidden, vec_ref, cos_ref, sin_ref, turn_ref],
            weights[:4], reads[4:], stacks[n:], d_input_ref, scratch[len(first) : -1],
        )
        for part in (one, one, two, one, two, one, two):
            next(part, None)
        yield

    return call(
        body,
        "layer_backward",
        [index, slot, mix],
        spots,
        [target, vec, cosine, sine, turn],
        weights,
        reads,
        stacks,
        jax.ShapeDtypeStruct((length, width), BF),
        first + second + [pltpu.VMEM((length, width), F32)],
        60,
        250,
    )


def rope_tables(length):
    halves = HD // 2
    inverse = jnp.exp(jnp.arange(halves, dtype=F32) * (-2.0 * math.log(ROPE_BASE) / HD))
    angles = jnp.arange(length, dtype=F32)[:, None] * inverse[None, :]
    cosine, sine = jnp.cos(angles), jnp.sin(angles)
    return (
        jnp.concatenate([cosine] * 4, axis=1),
        jnp.concatenate([-sine, sine, -sine, sine], axis=1),
    )


def swap(block, axis, bit):
    return lax.ppermute(block, axis, [(i, i ^ bit) for i in range(lax.axis_size(axis))])


def after(value, *others):
    if not others:
        return value
    return lax.optimization_barrier((value,) + others)[0]


def corner(made):
    part = made.reshape(-1, made.shape[-1])[:8, :HALF].astype(BF)
    return jnp.dot(part, jnp.ones((HALF, HALF), BF), preferred_element_type=F32)


def quick_links():
    return lax.axis_size("fsdp") == 4 and lax.axis_size("rep") == 4


def gather_halves(shard, axis, before_y=(), before_z=()):
    parity = lax.axis_index("rep") % 2
    half = shard.shape[axis] // 2
    mine = lax.dynamic_slice_in_dim(shard, parity * half, half, axis)
    near = swap(shard, "fsdp", 1)
    far_one = swap(after(mine, *before_y), "fsdp", 2)
    far_two = swap(after(far_one, *before_z), "rep", 1)
    return [shard, near, far_one, far_two]


def gather_wholes(shard, *before_y):
    return [shard, swap(shard, "fsdp", 1), swap(after(shard, *before_y), "fsdp", 2)]


def share_far(pieces, *before):
    return pieces + [swap(after(piece, *before), "fsdp", 1) for piece in pieces[2:]]


def plus(a, b):
    return (a.astype(F32) + b.astype(F32)).astype(BF)


def weight_grad(left, right):
    return lax.dot_general(
        left, right, (((0, 1), (0, 1)), ((), ())), preferred_element_type=F32
    ).astype(BF)


class Reduction:
    def __init__(self, left, right, riders=None):
        self.left, self.right, self.riders = left, right, riders

    def begin(self, order):
        left, right = order(self.left, self.right)
        core = lax.axis_index("fsdp") % 2
        away, stay = weight_grad_halves(core.astype(jnp.int32)[None], left, right)
        if self.riders is not None:
            blocks, column = self.riders
            away, stay = (
                lax.dynamic_update_slice(
                    grad, lax.dynamic_index_in_dim(blocks, i, 1, keepdims=False), (0, 0, column)
                )
                for grad, i in ((away, 1 - core), (stay, core))
            )
        self.stay = stay
        self.moved = swap(away, "fsdp", 1)
        return stay

    def chips(self, order):
        chip = lax.axis_index("fsdp") // 2
        self.kept = order(self.stay, self.moved)

        def part(i):
            return [lax.dynamic_index_in_dim(v, i, 0, keepdims=False) for v in self.kept]

        away = plus(*part(1 - chip))
        self.moved = swap(away, "fsdp", 2)
        return away

    def line_in(self, order):
        chip = lax.axis_index("fsdp") // 2
        *kept, moved = order(*self.kept, self.moved)
        one, two = (lax.dynamic_index_in_dim(v, chip, 0, keepdims=False) for v in kept)
        self.stay = (one.astype(F32) + two.astype(F32) + moved.astype(F32)).astype(BF)
        self.moved = lax.ppermute(self.stay, "rep", [(0, 1), (3, 2)])
        return self.stay

    def middle(self, order):
        stay, moved = order(self.stay, self.moved)
        self.stay = plus(stay, moved)
        self.moved = lax.ppermute(self.stay, "rep", [(1, 2), (2, 1)])
        return self.stay

    def line_out(self, order):
        stay, moved = order(self.stay, self.moved)
        self.stay = plus(stay, moved)
        self.moved = lax.ppermute(self.stay, "rep", [(1, 0), (2, 3)])
        return self.stay

    def finish(self, order):
        stay, moved = order(self.stay, self.moved)
        rank = lax.axis_index("rep")
        inner = jnp.logical_or(rank == 1, rank == 2)
        self.result = jnp.where(inner, stay, moved).astype(F32)
        return self.result


def body(
    inputs,
    teacher,
    lengths,
    order,
    loss_scale,
    norm_gain1,
    w_query,
    w_key,
    w_value,
    w_attn_out,
    w_ssm_gate,
    w_conv_in,
    w_step,
    conv_kernel,
    conv_bias,
    step_bias,
    decay_log,
    skip_gain,
    ssm_norm_gain,
    w_ssm_out,
    norm_gain2,
    w_gate,
    w_up,
    w_down,
):
    quick = quick_links()
    n_rep = lax.axis_size("rep")
    n_fsdp = lax.axis_size("fsdp")
    rank = lax.axis_index("rep")
    fsdp = lax.axis_index("fsdp")
    section = lax.axis_index("section")
    first = section == 0
    device = fsdp * n_rep + rank
    count, length, width = inputs.shape
    ci, mi, qw, kw = (w.shape[2] for w in (w_conv_in, w_ssm_gate, w_query, w_key))
    heads = w_step.shape[2]
    ff = w_up.shape[2]
    widths = (ci, mi, qw, kw, heads)
    taps = conv_kernel.shape[1]
    rows = width // n_fsdp
    tail = qw + 2 * kw + HALF
    total = ci + mi + tail

    def columns(flat):
        wide = -(-flat.size // rows)
        return jnp.pad(flat, (0, wide * rows - flat.size)).reshape(rows, wide)

    convs = jnp.concatenate([conv_kernel[0], conv_bias], axis=0)
    riders = jnp.concatenate(
        [
            norm_gain1[0][:, None],
            norm_gain2[0][:, None],
            columns(convs.reshape(-1)),
            columns(ssm_norm_gain[0]),
        ],
        axis=1,
    )
    used = riders.shape[1]
    wide = -(-convs.size // rows)
    shard_first = jnp.concatenate(
        [w_query[0], w_key[0], w_value[0], w_step[0]] + [jnp.zeros((rows, HALF - heads), BF)],
        axis=1,
    )
    parity = rank % 2
    if quick:
        g_gate = gather_halves(w_ssm_gate[0], 0)
        g_conv = gather_halves(w_conv_in[0], 0)
        g_first = gather_halves(shard_first, 0, (), g_gate[3:4])
        shard_out = jnp.concatenate([w_ssm_out[0], w_attn_out[0]], axis=0)
        g_out = gather_halves(shard_out, 1, g_gate[2:3], g_conv[3:4])
        g_g = gather_halves(w_gate[0], 0, g_conv[2:3], g_first[3:4])
        g_u = gather_wholes(w_up[0], g_out[2])
        g_gate, g_conv, g_first, g_out = (
            share_far(g, g_out[3]) for g in (g_gate, g_conv, g_first, g_out)
        )
        spots = [2 * fsdp, 2 * (fsdp ^ 1)]
        spots += [2 * (fsdp ^ k) + b for k in (2, 3) for b in (parity, 1 - parity)]
        spots = jnp.stack(spots).astype(jnp.int32)
        far = swap(riders, "fsdp", 2)
        blocks = jnp.stack([riders, swap(riders, "fsdp", 1), far, swap(far, "fsdp", 1)])
        ridden = jnp.take(blocks, jnp.arange(4, dtype=jnp.int32) ^ fsdp, axis=0)
    else:

        def whole(shard):
            return lax.all_gather(shard, "fsdp", axis=0, tiled=True)

        g_first, g_conv, g_gate, g_g, g_u, g_down = (
            [whole(w)]
            for w in (shard_first, w_conv_in[0], w_ssm_gate[0], w_gate[0], w_up[0], w_down[0])
        )
        g_out = [jnp.concatenate([whole(w_ssm_out[0]), whole(w_attn_out[0])], axis=0)]
        spots = jnp.zeros((1,), jnp.int32)
        ridden = whole(riders).reshape(n_fsdp, rows, used)
    if quick:
        order = after(order, g_gate[3])

    turns = jnp.arange(count, dtype=jnp.int32)
    numbers = jnp.arange(order.shape[0], dtype=jnp.int32)
    mine = device * count + turns
    sources = jnp.sum(jnp.where(order[None, :] == mine[:, None], numbers[None, :], 0), axis=1)
    target = lax.dynamic_slice_in_dim(order, device * count, count) // count % n_rep
    anchor = sources // count % n_rep

    def inverse(key):
        return jnp.sum(jnp.where((key ^ rank)[None, :] == turns[:, None], turns[None, :], 0), axis=1)

    send_at, keep_at = inverse(target), inverse(anchor)
    own_lengths = jnp.take(lengths, jnp.take(sources, keep_at))
    outgoing = [
        jnp.where(
            first,
            lax.dynamic_index_in_dim(inputs, send_at[j], 0, keepdims=False),
            lax.dynamic_index_in_dim(teacher, send_at[j], 0, keepdims=False),
        )
        for j in range(count)
    ]
    dealt = [outgoing[0]]

    def deal(j, *earlier):
        dealt.append(swap(after(outgoing[j], *earlier), "rep", j))


    if quick:
        deal(1, g_out[3])
        deal(2, dealt[1])
    else:
        for j in range(1, count - 1):
            deal(j)

    mixer_weights = [g_first, g_conv, g_gate, g_out]
    mlp_weights = None if quick else [g_g, g_u, g_down]

    conv_all = ridden[:, :, 2 : 2 + wide].reshape(n_fsdp, -1)[:, : (taps + 1) * ci // n_fsdp]
    conv_all = conv_all.reshape(n_fsdp, taps + 1, ci // n_fsdp).transpose(1, 0, 2)
    ssm_gain = ridden[:, :, 2 + wide :].reshape(n_fsdp, -1)[:, : mi // n_fsdp].reshape(1, mi)

    def table_row(v):
        v = v.astype(F32)
        return jnp.pad(v, ((0, 0), (0, ci - v.shape[1])))

    vec = jnp.concatenate(
        [
            table_row(v)
            for v in (
                conv_all.reshape(taps + 1, ci),
                ssm_gain,
                jnp.repeat(skip_gain, HD, axis=1),
                ridden[:, :, 0].reshape(1, width),
                ridden[:, :, 1].reshape(1, width),
                step_bias,
                -jnp.exp(decay_log),
                jnp.zeros((16 - taps - 7, 1), F32),
            )
        ],
        axis=0,
    )
    cosine, sine = rope_tables(length)

    valid_count = jnp.sum(lengths).astype(F32)
    factor = loss_scale / (valid_count * width)

    skew = 2
    steps = count + skew
    ticks = jnp.arange(steps, dtype=jnp.int32)
    raw = jnp.concatenate([ticks - skew * section, count - 1 - ticks + skew * (1 - section)])
    inside = jnp.logical_and(raw >= 0, raw < count).astype(jnp.int32)
    slots = jnp.clip(raw, 0, count - 1)
    plan = [slots, inside, jnp.take(own_lengths, slots), jnp.take(keep_at, slots)]
    plan = jnp.stack(plan, axis=1).reshape(-1)
    mix = jnp.stack([jnp.where(first, 1.0, 0.0), 2.0 * factor])

    def stack(*shape, kind=BF):
        return jax.ShapeDtypeStruct((count,) + shape, kind)

    mix_stacks = [
        stack(length, width),
        stack(length, ci),
        stack(length, ci),
        stack(length, mi),
        stack(length, qw + 2 * kw),
        stack(length, HALF, kind=F32),
        stack(qw // HD * length, length),
        stack(length, mi),
        stack(length, qw),
        stack(length, mi),
        stack(length, width, kind=F32),
        stack(length, width),
    ]
    mlp_stacks = [
        stack(length, width),
        stack(length, ff),
        stack(length, ff),
        stack(length, ff),
        stack(length, width, kind=F32),
        stack(length, width),
    ]

    token = []

    def chained(*values):
        if not quick or not token:
            return values
        return lax.optimization_barrier(values + tuple(token))[: len(values)]

    def chain(made):
        token[:] = [made]

    received, hiddens = [], []

    blank = jnp.zeros((8, HALF), F32)

    def number(i):
        return jnp.full((1,), i, jnp.int32)

    def mixer_tick(tick, turn, mix_stacks):
        mix_stacks, hidden = mixer_forward_call(
            number(tick),
            plan,
            spots,
            dealt[tick],
            vec,
            cosine,
            sine,
            corner(turn),
            mixer_weights,
            mix_stacks,
            widths,
            total,
        )
        chain(hidden)
        hiddens.append(hidden)
        return mix_stacks

    def mlp_tick(tick, mlp_stacks):
        (hidden,) = chained(hiddens[tick])
        mlp_stacks, low = mlp_forward_call(
            number(tick), plan, spots, hidden, vec, mlp_weights, mlp_stacks, ff
        )
        return mlp_stacks, low

    def layer_tick(tick, turn, stacks):
        if tick < count:
            one, two = chained(dealt[tick], received[tick - skew])
            seq_in = jnp.where(first, one, two)
        else:
            seq_in = received[tick - skew]
        return layer_forward_call(
            number(tick),
            plan,
            spots,
            seq_in,
            vec,
            cosine,
            sine,
            corner(turn) if tick < steps - 1 else blank,
            mixer_weights + mlp_weights,
            stacks,
            widths,
            total,
            ff,
        )

    if quick:
        dealt[0] = after(dealt[0], dealt[1])
    mix_stacks = mixer_tick(0, dealt[0], mix_stacks)
    if quick:
        g_down = gather_wholes(w_down[0], hiddens[0])
    mix_stacks = mixer_tick(1, hiddens[0], mix_stacks)
    if quick:
        mlp_weights = [share_far(g, hiddens[1], dealt[2]) for g in (g_g, g_u, g_down)]
    for tick in range(steps):
        if tick < skew:
            mlp_stacks, low = mlp_tick(tick, mlp_stacks)
            if tick == 0:
                deal(count - 1, low)
        else:
            stacks, low = layer_tick(tick, low, mix_stacks + mlp_stacks)
            mix_stacks, mlp_stacks = stacks[: len(mix_stacks)], stacks[len(mix_stacks) :]
        chain(low)
        if tick < count:
            received.append(lax.ppermute(low, "section", [(0, 1)]))

    (s_normed, s_conv, s_z, s_gate, s_qkv, s_step, s_probs, s_ssm, s_mixed, s_y, s_hidden,
     s_x) = mix_stacks
    s_normed2, s_g, s_u, s_act, s_final, s_low = mlp_stacks
    mlp_grads = [
        stack(length, width),
        stack(length, ff),
        stack(length, ff),
        stack(8, width, kind=F32),
    ]
    mix_grads = [
        stack(length, width),
        stack(length, tail),
        stack(length, ci),
        stack(length, mi),
        stack(length, width),
        stack(16, ci, kind=F32),
    ]
    incoming, returned = [], [None] * count

    hiddens = []

    def mlp_turn(turn, mlp_grads):
        if turn == count:
            token.append(returned[3])
        (seed,) = chained(incoming[turn - skew])
        return mlp_backward_call(
            number(steps + turn),
            plan,
            mix,
            spots,
            seed,
            vec,
            corner(hiddens[-1]) if turn > count else blank,
            mlp_weights,
            reads,
            mlp_grads,
            ff,
        )

    def mixer_turn(turn, d_hidden, before, mix_grads):
        mix_grads, d_input = mixer_backward_call(
            number(steps + turn),
            plan,
            spots,
            d_hidden,
            vec,
            cosine,
            sine,
            corner(before),
            mixer_weights,
            mix_reads,
            mix_grads,
            widths,
            total,
        )
        send_back(turn, d_input)
        return mix_grads, d_input

    def send_back(turn, d_input):
        if turn < count:
            incoming.append(lax.ppermute(d_input, "section", [(1, 0)]))
        if turn >= skew:
            j = count - 1 - turn + skew
            back = lax.dynamic_index_in_dim(after(s_low, d_input), keep_at[j], 0, keepdims=False)
            back = jnp.where(first, d_input, back)
            returned[j] = swap(back, "rep", j) if j else back

    reads = [s_final, s_hidden, s_g, s_u]
    mix_reads = [s_conv, s_z, s_gate, s_qkv, s_step, s_probs, s_y, s_x]
    d_input = low
    for turn in range(count):
        if turn < skew:
            (seed,) = chained(dealt[count - 1 - turn])
        else:
            one, two = chained(incoming[turn - skew], dealt[count - 1 - turn])
            seed = jnp.where(first, one, two)
        grads, d_input = layer_backward_call(
            number(steps + turn),
            plan,
            mix,
            spots,
            seed,
            vec,
            cosine,
            sine,
            corner(d_input) if turn else blank,
            mixer_weights + mlp_weights,
            reads + mix_reads,
            mlp_grads + mix_grads,
            widths,
            total,
            ff,
        )
        mlp_grads, mix_grads = grads[: len(mlp_grads)], grads[len(mlp_grads) :]
        chain(d_input)
        send_back(turn, d_input)

    for turn in range(count, steps):
        mlp_grads, d_hidden = mlp_turn(turn, mlp_grads)
        chain(d_hidden)
        hiddens.append(d_hidden)
    s_dmlp, s_dg, s_du, small_mlp = mlp_grads
    early = [(s_normed2, s_dg), (s_normed2, s_du), (s_act, s_dmlp)]
    chunks = [Reduction(*pair) for pair in early]

    names = dict(W="begin", A="chips", L="line_in", M="middle", O="line_out", F="finish")
    state = [mix_grads]

    def stages(*words):
        for word in words:
            letter, place = word[0], int(word[1:])
            if letter == "B":
                before = token[0] if quick else hiddens[place - count]
                state[0], made = mixer_turn(place, hiddens[place - count], before, state[0])
            else:
                made = getattr(chunks[place], names[letter])(chained)
            chain(made)

    if quick:
        stages(
            "W0", "W1", "A0", "W2", "B4"
        )
        token.append(returned[2])
        stages(
            "A2", "A1", "L0", "B5"
        )
    else:
        stages("B4", "B5")
    mix_grads = state[0]
    s_dbranch, s_dfirst, s_dconv, s_dgate, s_dinput, small_mix = mix_grads
    late = [
        (s_normed, s_dconv),
        (s_normed, s_dgate),
        (s_ssm, s_dbranch),
        (s_normed, s_dfirst),
        (s_mixed, s_dbranch),
    ]

    mix_sum = jnp.sum(small_mix, axis=0)
    mlp_sum = jnp.sum(small_mlp, axis=0)
    loss_part = jnp.sum(mlp_sum[1])[None]
    loss_part = jnp.where(first, lax.ppermute(loss_part, "section", [(1, 0)]), loss_part)
    singles = jnp.concatenate(
        [
            mix_sum[V_SBIAS, :heads],
            mix_sum[V_DECAY, :heads],
            jnp.sum(mix_sum[V_SKIP, :mi].reshape(heads, HD), axis=1),
            loss_part,
        ]
    )

    def share(v):
        return v.reshape(v.shape[0], n_fsdp, -1).transpose(1, 0, 2).reshape(n_fsdp, -1)

    shares = [
        share(mix_sum[: taps + 1]),
        share(mix_sum[V_GS : V_GS + 1, :mi]),
        share(mix_sum[V_G1 : V_G1 + 1, :width]),
        share(mlp_sum[:1]),
        jnp.broadcast_to(singles[None], (n_fsdp, singles.size)),
    ]
    cuts = [v.shape[1] for v in shares]
    flat = jnp.concatenate(shares, axis=1)

    def split_ends(values):
        return values[:count], values[-2], values[-1]

    def own_outputs(returned, s_dinput, s_low):
        restored = jnp.zeros((count, length, width), BF)
        for j in range(count):
            restored = lax.dynamic_update_index_in_dim(restored, returned[j], send_at[j], 0)
        return jnp.where(first, s_low, restored)[None], jnp.where(first, restored, s_dinput)[None]

    if quick:
        spare = -(-flat.shape[1] // rows)
        flat = jnp.pad(flat, ((0, 0), (0, spare * rows - flat.shape[1])))
        riders = flat.astype(BF).reshape(2, 2, rows, spare)
        column = tail - HALF + heads
        chunks += [Reduction(*pair) for pair in late]
        chunks[6].riders = (riders, column)
        stages(
            "L1", "M0", "W4", "W7", "W3", "L2", "M1", "O0", "A4", "A7", "A3", "W6", "W5", "F0"
        )
        token.append(returned[1])
        stages(
            "O1", "L3", "M2", "L7", "A5", "L4", "A6", "M3", "O2", "F1", "L5", "M4", "L6", "O3",
            "F2", "M7", "M5", "O4"
        )
        returned, s_dinput, s_low = split_ends(chained(*returned, s_dinput, s_low))
        activations, gradients = own_outputs(returned, s_dinput, s_low)
        token.extend([activations, gradients])
        stages(
            "M6", "F3", "O7", "O5", "F4", "O6", "F7", "F5", "F6"
        )
        reduced = [chunk.result for chunk in chunks]
        flat = reduced[6][:, column : column + spare].reshape(-1)
    else:

        def reduce_all(pair):
            grad = weight_grad(*pair)
            own = lax.psum_scatter(grad, "fsdp", scatter_dimension=0, tiled=True)
            return lax.psum(own, "rep").astype(F32)

        reduced = [reduce_all(pair) for pair in early + late]
        flat = lax.psum(lax.psum_scatter(flat, "fsdp", tiled=True), "rep").reshape(-1)
    grad_gate, grad_up, grad_down, grad_conv, grad_sgate, grad_ssm_out, grad_first, grad_attn = reduced

    parts, begin = [], 0
    for cut in cuts[:-1] + [heads] * 3 + [1]:
        parts.append(flat[begin : begin + cut])
        begin += cut
    convs = parts[0].reshape(taps + 1, -1)
    loss = parts[-1][0]

    if not quick:
        activations, gradients = own_outputs(returned, s_dinput, s_low)
    s0 = qw + 2 * kw
    return (
        activations,
        gradients,
        loss / (valid_count * width),
        parts[2][None],
        grad_first[None, :, :qw],
        grad_first[None, :, qw : qw + kw],
        grad_first[None, :, qw + kw : s0],
        grad_attn[None],
        grad_sgate[None],
        grad_conv[None],
        grad_first[None, :, s0 : s0 + heads],
        convs[None, :taps],
        convs[None, taps],
        parts[4][None],
        parts[5][None],
        parts[6][None],
        parts[1][None],
        grad_ssm_out[None],
        parts[3][None],
        grad_gate[None],
        grad_up[None],
        grad_down[None],
    )


def solution(mesh):
    rows3 = P("section", "fsdp", None)
    pair = P("section", "fsdp")
    one = P("section", None)
    data = P(("fsdp", "rep"), None, None)
    taps = P("section", None, "fsdp")
    in_specs = (data, data, P(), P(), P(), pair) + (rows3,) * 7
    in_specs += (taps, pair, one, one, one, pair, rows3, pair, rows3, rows3, rows3)
    placed = P("section", ("fsdp", "rep"), None, None)
    out_specs = (placed, placed, P(), pair) + (rows3,) * 7
    out_specs += (taps, pair, one, one, one, pair, rows3, pair, rows3, rows3, rows3)
    return jax.shard_map(body, mesh=mesh, in_specs=in_specs, out_specs=out_specs, check_vma=False)
```
